128 devices in a mesh: dp: 64 (over x_lo, z, y, core), mod: 2 (over x_hi).
Axes of the slice: x: 4 (x_hi: 2, x_lo: 2; x = x_hi * 2 + x_lo), y: 4, z: 4, core: 2. Of those that a mesh axis runs over, the one named last changes fastest.
Arguments:
- tokens: bfloat16 [18432, 1152], P(('dp', 'mod')), may hold values from -6 to 6
- condition: bfloat16 [512, 1152], P(('dp', 'mod')), may hold values from -6 to 6
- segments: int32 [18432], P(('dp', 'mod')), may hold values from 0 to 3, as said below
- mod_weight: bfloat16 [1152, 6912], P(None, 'mod'), may hold values from -0.1875 to 0.1875
- mod_bias: bfloat16 [6912], P('mod'), may hold values from -3 to 3
- qkv_weight: bfloat16 [1152, 3456], replicated, may hold values from -0.1875 to 0.1875
- query_gain: float32 [72], replicated, may hold values from 0.1 to 1.9
- key_gain: float32 [72], replicated, may hold values from 0.1 to 1.9
- out_weight: bfloat16 [1152, 1152], replicated, may hold values from -1.5 to 1.5
- gate_weight: bfloat16 [1152, 3072], replicated, may hold values from -0.1875 to 0.1875
- up_weight: bfloat16 [1152, 3072], replicated, may hold values from -0.1875 to 0.1875
- down_weight: bfloat16 [3072, 1152], replicated, may hold values from -0.109375 to 0.109375
- cotangent: bfloat16 [18432, 1152], P(('dp', 'mod')), may hold values from -6 to 6
Outputs:
- layer_out: bfloat16 [18432, 1152], P(('dp', 'mod'))
- grad_tokens: float32 [18432, 1152], P(('dp', 'mod'))
- grad_condition: float32 [512, 1152], P(('dp', 'mod'))
- grad_mod_weight: float32 [1152, 6912], P('dp', 'mod')
- grad_mod_bias: float32 [6912], replicated
- grad_qkv_weight: float32 [1152, 3456], P(('dp', 'mod'))
- grad_query_gain: float32 [72], replicated
- grad_key_gain: float32 [72], replicated
- grad_out_weight: float32 [1152, 1152], P(('dp', 'mod'))
- grad_gate_weight: float32 [1152, 3072], P(('dp', 'mod'))
- grad_up_weight: float32 [1152, 3072], P(('dp', 'mod'))
- grad_down_weight: float32 [3072, 1152], P(('dp', 'mod'))
The draws below stay inside these ranges and needn't reach their ends.
Inputs may be any that keep to these rules, and one draw needn't show every extreme that they name: On each device the 144 tokens are either one image (all segment 0, a 12 x 12 grid of patches in row-major order) or 4 images of 36 tokens each (6 on a side), segments 0 to 3 in order; both kinds of device occur in every draw.
All inputs are finite; a program needn't handle non-finite values.
Results may differ from the reference program's by a relative error of at most 0.013.
The reference program's roundings to bfloat16 on the way count: a program that leaves them out, or rounds other values in their place, can miss the bound.
Values may be sent and summed in bfloat16 or wider, within the bound.
A program may use at most 384 MiB of HBM per device.

```python
import jax
import jax.numpy as jnp
from jax import lax

D = 1152
H = 16
HD = 72
FF = 3072
SIDE = 12
IMG_DEV = 4
TOK_DEV = 144
TOKENS = 18432
IMAGES = 512
N_DP = 64
N_MOD = 2


def draw_segments(key, part):
    key = jax.random.fold_in(key, 11)
    devices = TOKENS // TOK_DEV
    kind_key, small_key, large_key = jax.random.split(key, 3)
    device_kind = jax.random.randint(kind_key, (devices,), 0, 3)
    small_at = jax.random.randint(small_key, (), 0, devices)
    large_at = (small_at + 1 + jax.random.randint(large_key, (), 0, devices - 1)) % devices
    device_ids = jnp.arange(devices)
    device_kind = jnp.where(device_ids == small_at, 0, device_kind)
    device_kind = jnp.where(device_ids == large_at, 1, device_kind)
    positions = jnp.arange(TOK_DEV)
    small_slots = positions // (TOK_DEV // IMG_DEV)
    slot_table = jnp.where(device_kind[:, None] > 0, 0, small_slots[None, :])
    return slot_table.reshape(-1).astype(jnp.int32)


def levels(rng, shape, cuts, smallest, largest):
    def one(dim, blocks):
        heights = jax.random.uniform(jax.random.fold_in(jax.random.fold_in(rng, 6), dim), (blocks,), jnp.float32, smallest / len(cuts), largest / len(cuts))
        return jnp.repeat(jnp.exp(heights), shape[dim] // blocks).reshape((-1,) + (1,) * (len(shape) - dim - 1))

    loudness = one(*cuts[0])
    for cut in cuts[1:]:
        loudness = loudness * one(*cut)
    return loudness


def gaussian(rng, shape, width, limit, cuts=(), kind=jnp.bfloat16):
    factor_of = levels(rng, shape, cuts, -0.22, 0.18) if cuts else 1.0
    values = jax.random.normal(rng, shape, jnp.float32) * width * factor_of
    return jnp.minimum(jnp.maximum(values, -limit), limit).astype(kind)


def setup_inputs(seed: int = 0) -> dict:
    arg_keys = jax.random.split(jax.random.key(seed), 14)
    return {
        "tokens": gaussian(arg_keys[0], (TOKENS, D), 1.0, 6.0, ((0, 128),)),
        "condition": gaussian(arg_keys[1], (IMAGES, D), 1.0, 6.0, ((0, 128),)),
        "segments": draw_segments(jax.random.fold_in(arg_keys[13], 71), 0),
        "mod_weight": gaussian(arg_keys[3], (D, 6 * D), D ** -0.5, 0.1875, ((1, 2),)),
        "mod_bias": gaussian(arg_keys[4], (6 * D,), 0.5, 3.0, ((0, 2),)),
        "qkv_weight": gaussian(arg_keys[5], (D, 3 * D), D ** -0.5, 0.1875),
        "query_gain": jnp.clip(1.0 + 0.18 * jax.random.normal(arg_keys[6], (HD,), jnp.float32), 0.1, 1.9),
        "key_gain": jnp.clip(1.0 + 0.18 * jax.random.normal(arg_keys[7], (HD,), jnp.float32), 0.1, 1.9),
        "out_weight": gaussian(arg_keys[8], (D, D), (max(1, D * 2 // TOK_DEV)) ** -0.5, 1.5),
        "gate_weight": gaussian(arg_keys[9], (D, FF), D ** -0.5, 0.1875),
        "up_weight": gaussian(arg_keys[10], (D, FF), D ** -0.5, 0.1875),
        "down_weight": gaussian(arg_keys[11], (FF, D), FF ** -0.5, 0.109375),
        "cotangent": gaussian(arg_keys[12], (TOKENS, D), 1.0, 6.0, ((0, 128),)),
    }


EPSILON = 1e-06
HIGHEST = lax.Precision.HIGHEST

@jax.custom_vjp
def low(v):
    return lax.optimization_barrier(v.astype(jnp.bfloat16)).astype(jnp.float32)

@jax.custom_vjp
def low_back(v):
    return v

def low_keep(v):
    return (low(v), None)

def low_pass(kept, grad):
    return (grad,)

def back_keep(v):
    return (v, None)

def back_low(kept, grad):
    return (low(grad),)
low.defvjp(low_keep, low_pass)
low_back.defvjp(back_keep, back_low)

def matmul_high(left, right):
    return jnp.dot(left, right, precision=HIGHEST, preferred_element_type=jnp.float32)

def rms_norm(values):
    return values * lax.rsqrt(lax.optimization_barrier(jnp.mean(values * values, axis=-1, keepdims=True)) + EPSILON)

def rotate(values, cosine, sine):
    half_dim = values.shape[-1] // 2
    leading = values[..., :half_dim]
    trailing = values[..., half_dim:]
    cosine = cosine[:, None, :]
    sine = sine[:, None, :]
    return jnp.concatenate([leading * cosine - trailing * sine, trailing * cosine + leading * sine], axis=-1)

def rope_tables(segments, slot_count, side_big, head_dim):
    tok_count = segments.shape[0]
    onehot = (segments[:, None] == jnp.arange(slot_count, dtype=jnp.int32)[None, :]).astype(jnp.int32)
    counts = lax.optimization_barrier(jnp.sum(onehot, axis=0)).astype(jnp.int32)
    starts = (jnp.cumsum(counts) - counts).astype(jnp.int32)
    first_tok = lax.optimization_barrier(jnp.sum(onehot * starts[None, :], axis=1)).astype(jnp.int32)
    extent = lax.optimization_barrier(jnp.sum(onehot * counts[None, :], axis=1)).astype(jnp.int32)
    position = jnp.arange(tok_count, dtype=jnp.int32) - first_tok
    side_len = jnp.where(extent == tok_count, side_big, side_big // 2).astype(jnp.int32)
    row_pos = (position // side_len).astype(jnp.float32)
    col_pos = (position % side_len).astype(jnp.float32)
    quarter = head_dim // 4
    frequency = 10000.0 ** (-jnp.arange(quarter, dtype=jnp.float32) / quarter)
    angles = jnp.concatenate([row_pos[:, None] * frequency[None, :], col_pos[:, None] * frequency[None, :]], axis=1)
    return (jnp.cos(angles), jnp.sin(angles))

def device_attention(queries, memory_keys, memory_values, segments):
    scores = jnp.einsum('thd,shd->hts', queries, memory_keys, precision=HIGHEST) * queries.shape[-1] ** (-0.5)
    scores = low_back(scores)
    allowed = segments[:, None] == segments[None, :]
    attention = jax.nn.softmax(jnp.where(allowed[None], scores, -1e+30), axis=-1)
    return jnp.einsum('hts,shd->thd', low(attention), memory_values, precision=HIGHEST)

def grouped_attention(queries, memory_keys, memory_values, segments):
    devices = N_DP * N_MOD
    per_group = 1
    while per_group * 2 * TOK_DEV <= 4096 and devices % (per_group * 2) == 0:
        per_group = per_group * 2
    blocks = devices // per_group
    block_shape = (blocks, per_group, TOK_DEV, H, HD)
    runner = jax.checkpoint(jax.vmap(device_attention))
    result = lax.map(lambda members: runner(*members), (queries.reshape(block_shape), memory_keys.reshape(block_shape), memory_values.reshape(block_shape), segments.reshape(blocks, per_group, TOK_DEV)))
    return result.reshape(TOKENS, H, HD)

def forward(tokens, condition, mod_weight, mod_bias, qkv_weight, query_gain, key_gain, out_weight, gate_weight, up_weight, down_weight, segments, image_of, cosine, sine):
    modulation = low_back(low(matmul_high(low(jax.nn.silu(condition)), mod_weight) + mod_bias))
    per_token = modulation[image_of]
    pieces = [per_token[:, column * D:(column + 1) * D] for column in range(6)]
    shift_first, scale_first, gate_first, shift_second, scale_second, gate_second = pieces
    first_input = low(rms_norm(tokens) * (1.0 + scale_first) + shift_first)
    projected = low_back(matmul_high(first_input, qkv_weight))
    split_shape = (TOKENS, H, HD)
    queries = low(rotate(rms_norm(projected[:, :D].reshape(split_shape)) * query_gain, cosine, sine))
    memory_keys = low(rotate(rms_norm(projected[:, D:2 * D].reshape(split_shape)) * key_gain, cosine, sine))
    memory_values = low(projected[:, 2 * D:].reshape(split_shape))
    context = grouped_attention(queries, memory_keys, memory_values, segments)
    context = low_back(low(context)).reshape(TOKENS, D)
    attended = low_back(matmul_high(context, out_weight))
    middle = tokens + gate_first * attended
    second_input = low(rms_norm(middle) * (1.0 + scale_second) + shift_second)
    gate_linear = low_back(matmul_high(second_input, gate_weight))
    up_linear = low_back(matmul_high(second_input, up_weight))
    hidden = low(jax.nn.silu(gate_linear) * up_linear)
    branch = low_back(matmul_high(hidden, down_weight))
    return middle + gate_second * branch

def reference(tokens, condition, segments, mod_weight, mod_bias, qkv_weight, query_gain, key_gain, out_weight, gate_weight, up_weight, down_weight, cotangent):
    devices = N_DP * N_MOD
    by_device = segments.reshape(devices, TOK_DEV)
    cosine, sine = jax.vmap(lambda device_rows: rope_tables(device_rows, IMG_DEV, SIDE, HD))(by_device)
    cosine = cosine.reshape(TOKENS, HD // 2)
    sine = sine.reshape(TOKENS, HD // 2)
    image_of = (jnp.arange(devices, dtype=jnp.int32)[:, None] * IMG_DEV + by_device).reshape(TOKENS).astype(jnp.int32)
    floats = tuple((member.astype(jnp.float32) for member in (tokens, condition, mod_weight, mod_bias, qkv_weight, query_gain, key_gain, out_weight, gate_weight, up_weight, down_weight)))

    def closed(*params):
        return forward(*params, segments, image_of, cosine, sine)
    result, pullback = jax.vjp(closed, *floats)
    gradients = pullback(cotangent.astype(jnp.float32))
    return (result.astype(jnp.bfloat16), gradients[0], gradients[1], gradients[2], gradients[3], gradients[4], gradients[5], gradients[6], gradients[7], gradients[8], gradients[9], gradients[10])
```

```python
import jax
import jax.numpy as jnp
import numpy as np
from jax import lax
from jax.experimental import pallas as pl
from jax.experimental.pallas import tpu as pltpu
from jax.sharding import PartitionSpec as P

SIDE = 12


EPSILON = 1e-06
HIGHEST = lax.Precision.HIGHEST


def rms_norm(values):
    inverse = lax.rsqrt(jnp.mean(values * values, axis=-1, keepdims=True) + EPSILON)
    return (values * inverse, inverse)


def norm_back(upstream, normed, inverse):
    return inverse * (upstream - normed * jnp.mean(upstream * normed, axis=-1, keepdims=True))


def rotate(values, cosine, sine):
    half_dim = values.shape[-1] // 2
    leading = values[..., :half_dim]
    trailing = values[..., half_dim:]
    cosine = cosine[:, None, :]
    sine = sine[:, None, :]
    return jnp.concatenate(
        [leading * cosine - trailing * sine, trailing * cosine + leading * sine], axis=-1
    )


def rope_tables(segments, slot_count, side_big, head_dim):
    tok_count = segments.shape[0]
    onehot = (segments[:, None] == jnp.arange(slot_count, dtype=jnp.int32)[None, :]).astype(
        jnp.int32
    )
    counts = jnp.sum(onehot, axis=0)
    starts = jnp.cumsum(counts) - counts
    first_tok = jnp.sum(onehot * starts[None, :], axis=1)
    extent = jnp.sum(onehot * counts[None, :], axis=1)
    position = jnp.arange(tok_count, dtype=jnp.int32) - first_tok
    side_len = jnp.where(extent == tok_count, side_big, side_big // 2).astype(jnp.int32)
    row_pos = (position // side_len).astype(jnp.float32)
    col_pos = (position % side_len).astype(jnp.float32)
    quarter = head_dim // 4
    frequency = 10000.0 ** (-jnp.arange(quarter, dtype=jnp.float32) / quarter)
    angles = jnp.concatenate(
        [row_pos[:, None] * frequency[None, :], col_pos[:, None] * frequency[None, :]], axis=1
    )
    return (jnp.cos(angles), jnp.sin(angles))


def silu_slope(values):
    logistic = jax.nn.sigmoid(values)
    return logistic * (1.0 + values * (1.0 - logistic))


def inner_rows(left, right):
    return lax.dot_general(
        left, right, (((0,), (0,)), ((), ())), preferred_element_type=jnp.float32
    )


def inner_cols(left, right):
    return lax.dot_general(
        left, right, (((1,), (1,)), ((), ())), preferred_element_type=jnp.float32
    )


def masked_scores(queries, memory_keys, allowed, score_scale):
    scores = (
        jnp.einsum("thd,shd->hts", queries, memory_keys, preferred_element_type=jnp.float32)
        * score_scale
    )
    return jnp.where(allowed[None], scores, -1e30)


TOK = 144
PAIR = 2 * TOK
WIDE = 1152
HID = 3072
RING = 4
AXES = ((0, 1, 2), (1, 2, 0), (2, 0, 1))
JOBS = (
    ("down", 24, 384, 384, 256),
    ("gate", 9, 1024, 256, 512),
    ("up", 9, 1024, 256, 512),
    ("out", 9, 384, 384, 256),
    ("qkv", 9, 1152, 384, 640),
)
COPIES = 15
PARTNER_COPIES = 9


def sixteen(rows):
    return (rows + 15) // 16 * 16


def position():
    dp = lax.axis_index("dp")
    x_hi = lax.axis_index("mod")
    core = lax.rem(dp, 2)
    y = lax.rem(dp // 2, 4)
    z = lax.rem(dp // 8, 4)
    return (x_hi * 2 + dp // 32, y, z), core


def device_at(place, core):
    x, y, z = place
    return (((lax.rem(x, 2) * 4 + z) * 4 + y) * 2 + core, x // 2)


def moved(place, axis, value):
    return tuple(value if index == axis else kept for index, kept in enumerate(place))


def row_sources():
    tables = []
    for order in AXES:
        table = np.zeros((4, 4, 4, 9), np.int32)
        for first in range(4):
            for second in range(4):
                for third in range(4):
                    place = [0, 0, 0]
                    for axis, value in zip(order, (first, second, third)):
                        place[axis] = value
                    x, y, z = place
                    owner = (x % 2) * 64 + z * 16 + y * 4 + x // 2
                    table[first, second, third] = owner * 9 + np.arange(9)
        tables.append(table.reshape(576, 1))
    return np.stack(tables)


def reduce_kernel(
    src9_ref,
    src24_ref,
    hidden_in,
    second_in,
    context_in,
    first_in,
    gbranch_in,
    ggate_in,
    gup_in,
    gatt_in,
    gproj_in,
    down_out,
    gate_out,
    up_out,
    out_out,
    qkv_out,
    hidden_s,
    second_s,
    context_s,
    first_s,
    gbranch_s,
    ggate_s,
    gup_s,
    gatt_s,
    gproj_s,
    perm9,
    xt9,
    perm24,
    t32,
    xt24,
    acc,
    *rest,
):
    bufs = [rest[7 * index : 7 * index + 7] for index in range(len(JOBS))]
    send_sem, recv_sem, local_sem = rest[7 * len(JOBS) :]
    place, core = position()
    partner = device_at(place, 1 - core)
    near = []
    for axis in range(3):
        here = place[axis]
        near.append(
            (here, lax.rem(here + 1, 4), lax.rem(here + 3, 4), lax.rem(here + 2, 4))
        )

    barrier = pltpu.get_barrier_semaphore()
    pl.semaphore_signal(barrier, inc=1, device_id=partner, device_id_type=pl.DeviceIdType.MESH)
    for axis in range(3):
        for value in near[axis][1:]:
            pl.semaphore_signal(
                barrier,
                inc=1,
                device_id=device_at(moved(place, axis, value), core),
                device_id_type=pl.DeviceIdType.MESH,
            )
    pl.semaphore_wait(barrier, 10)

    def remote(src, dst, index, target):
        return pltpu.make_async_remote_copy(
            src_ref=src,
            dst_ref=dst,
            send_sem=send_sem.at[index],
            recv_sem=recv_sem.at[index],
            device_id=target,
            device_id_type=pl.DeviceIdType.MESH,
        )

    sent = []
    pairs = {}
    ins = (gbranch_in, hidden_in, second_in, ggate_in, gup_in, context_in, gatt_in, first_in, gproj_in)
    stacks = (gbranch_s, hidden_s, second_s, ggate_s, gup_s, context_s, gatt_s, first_s, gproj_s)
    for index, (own, stack) in enumerate(zip(ins, stacks)):
        local = pltpu.make_async_copy(own, stack.at[pl.ds(0, TOK)], local_sem.at[index])
        local.start()
        across = remote(own, stack.at[pl.ds(TOK, TOK)], index, partner)
        across.start()
        sent.append(across)
        pairs[index] = (local, across)

    def arrived(*indices):
        for index in indices:
            local, across = pairs[index]
            local.wait()
            across.wait_recv()

    lane = lax.broadcasted_iota(jnp.int32, (192, 384), 1)
    perm24[...] = (lane == src24_ref[...] + core * 48).astype(jnp.float32).astype(jnp.bfloat16)

    def pick9(part, stack):
        lanes = lax.broadcasted_iota(jnp.int32, (576, 1), 1)

        @pl.loop(0, 9)
        def _(block):
            columns = lax.broadcasted_iota(jnp.int32, (576, 128), 1) + block * 128
            perm9[:, pl.ds(pl.multiple_of(block * 128, 128), 128)] = (
                (columns == src9_ref[part] + core * 18).astype(jnp.float32).astype(jnp.bfloat16)
            )

        xt9[...] = inner_cols(perm9[...], stack[...]).astype(jnp.bfloat16)

    def pick24(part):
        order = AXES[part]
        weight = [0, 0, 0]
        for axis, value in zip(order, (16, 4, 1)):
            weight[axis] = value

        @pl.loop(0, 8)
        def _(block):
            columns = pl.ds(pl.multiple_of(block * 384, 128), 384)
            rows = inner_cols(perm24[...], hidden_s[:, columns])
            base = (block // 4) * weight[0] + lax.rem(block, 4) * weight[2]
            for y in range(4):
                for x_hi in range(2):
                    unit = base + y * weight[1] + x_hi * 2 * weight[0]
                    at = (y * 2 + x_hi) * 24
                    t32[pl.ds(pl.multiple_of(unit * 24, 8), 24), :] = rows[at : at + 24]

        xt24[...] = t32[...].astype(jnp.bfloat16)

    def multiply(job, part, left, right):
        _, _, width, lanes, _ = JOBS[job]
        target = bufs[job][0]

        @pl.loop(0, width // lanes)
        def _(step):
            to = pl.multiple_of(step * lanes, 128)
            columns = pl.ds(pl.multiple_of(part * width + to, 128), lanes)
            target[part, :, pl.ds(to, lanes)] = jnp.dot(
                left[...], right[:, columns], preferred_element_type=jnp.float32
            ).astype(jnp.bfloat16)

    copies = {}

    def begin(job, part, slot, src, dst, target):
        index = PARTNER_COPIES + (job * 3 + part) * COPIES + slot
        copy = remote(src, dst, index, target)
        copy.start()
        sent.append(copy)
        copies[job, part, slot] = copy

    def arrive(job, part, *slots):
        for slot in slots:
            copies[job, part, slot].wait_recv()

    def ring(part, phase):
        axis = AXES[part][phase]
        here, right, left, opposite = near[axis]
        return (
            here,
            right,
            left,
            opposite,
            device_at(moved(place, axis, right), core),
            device_at(moved(place, axis, left), core),
            device_at(moved(place, axis, opposite), core),
        )

    def first_send(job, part):
        own, half, whole = bufs[job][:3]
        big = 16 * JOBS[job][1]
        cut = sixteen(big // 2)
        here, right, left, opposite, to_right, to_left, _ = ring(part, 0)

        def rows(chunk, start, count):
            return own.at[part, pl.ds(pl.multiple_of(chunk * big + start, 16), count)]

        begin(job, part, 0, rows(opposite, 0, cut), half.at[part, pl.ds(0, cut)], to_right)
        begin(job, part, 1, rows(opposite, cut, big - cut), half.at[part, pl.ds(cut, big - cut)], to_left)
        begin(job, part, 2, rows(right, cut, big - cut), whole.at[part, 0, pl.ds(cut, big - cut)], to_right)
        begin(job, part, 3, rows(left, 0, cut), whole.at[part, 1, pl.ds(0, cut)], to_left)

    def first_add(job, part):
        own, half, whole = bufs[job][:3]
        _, each, width, lanes, _ = JOBS[job]
        big = 16 * each
        cut = sixteen(big // 2)
        here, right, left, opposite, to_right, to_left, _ = ring(part, 0)
        for slot, chunk, start, count, target, side in (
            (0, right, 0, cut, to_right, 0),
            (1, left, cut, big - cut, to_left, 1),
        ):
            arrive(job, part, slot)
            rows = pl.ds(pl.multiple_of(chunk * big + start, 16), count)

            @pl.loop(0, width // 128)
            def _(step):
                columns = pl.ds(pl.multiple_of(step * 128, 128), 128)
                total = own[part, rows, columns].astype(jnp.float32) + half[
                    part, pl.ds(start, count), columns
                ].astype(jnp.float32)
                own[part, rows, columns] = total.astype(jnp.bfloat16)

            begin(
                job,
                part,
                4 + side,
                own.at[part, rows],
                whole.at[part, side, pl.ds(start, count)],
                target,
            )

    def second_send(job, part):
        own, _, whole, mid, mid_half, mid_whole, _ = bufs[job]
        _, each, width, lanes, cut = JOBS[job]
        big, small = 16 * each, 4 * each
        padded = sixteen(small)
        here, right, left, opposite, to_right, to_left, _ = ring(part, 0)
        arrive(job, part, 2, 3, 4, 5)
        rows = pl.ds(pl.multiple_of(here * big, 16), big)

        @pl.loop(0, width // 128)
        def _(step):
            columns = pl.ds(pl.multiple_of(step * 128, 128), 128)
            acc[pl.ds(0, big), :] = (
                own[part, rows, columns].astype(jnp.float32)
                + whole[part, 0, :, columns].astype(jnp.float32)
                + whole[part, 1, :, columns].astype(jnp.float32)
            )
            for chunk in range(4):
                mid[part, chunk, :, columns] = acc[pl.ds(chunk * small, padded), :].astype(jnp.bfloat16)

        here, right, left, opposite, to_right, to_left, _ = ring(part, 1)
        low, high = pl.ds(0, cut), pl.ds(cut, width - cut)
        begin(job, part, 6, mid.at[part, opposite, :, low], mid_half.at[part, :, low], to_right)
        begin(job, part, 7, mid.at[part, opposite, :, high], mid_half.at[part, :, high], to_left)
        begin(job, part, 8, mid.at[part, right, :, high], mid_whole.at[part, 0, :, high], to_right)
        begin(job, part, 9, mid.at[part, left, :, low], mid_whole.at[part, 1, :, low], to_left)

    def second_add(job, part):
        _, _, _, mid, mid_half, mid_whole, _ = bufs[job]
        _, each, width, lanes, cut = JOBS[job]
        here, right, left, opposite, to_right, to_left, _ = ring(part, 1)
        for slot, chunk, start, count, target, side in (
            (6, right, 0, cut, to_right, 0),
            (7, left, cut, width - cut, to_left, 1),
        ):
            arrive(job, part, slot)

            @pl.loop(0, count // 128)
            def _(step):
                columns = pl.ds(pl.multiple_of(start + step * 128, 128), 128)
                total = mid[part, chunk, :, columns].astype(jnp.float32) + mid_half[
                    part, :, columns
                ].astype(jnp.float32)
                mid[part, chunk, :, columns] = total.astype(jnp.bfloat16)

            columns = pl.ds(start, count)
            begin(
                job,
                part,
                10 + side,
                mid.at[part, chunk, :, columns],
                mid_whole.at[part, side, :, columns],
                target,
            )

    def third_send(job, part):
        _, _, _, mid, _, mid_whole, last = bufs[job]
        _, each, width, lanes, cut = JOBS[job]
        small = sixteen(4 * each)
        padded = sixteen(each)
        here = ring(part, 1)[0]
        arrive(job, part, 8, 9, 10, 11)

        @pl.loop(0, width // 128)
        def _(step):
            columns = pl.ds(pl.multiple_of(step * 128, 128), 128)
            acc[pl.ds(0, small), :] = (
                mid[part, here, :, columns].astype(jnp.float32)
                + mid_whole[part, 0, :, columns].astype(jnp.float32)
                + mid_whole[part, 1, :, columns].astype(jnp.float32)
            )
            for chunk in range(4):
                last[part, chunk, :, columns] = acc[pl.ds(chunk * each, padded), :].astype(jnp.bfloat16)

        here, right, left, opposite, to_right, to_left, to_opposite = ring(part, 2)
        for slot, chunk, target in ((0, right, to_right), (1, left, to_left), (2, opposite, to_opposite)):
            begin(job, part, 12 + slot, last.at[part, chunk], last.at[part, 4 + slot], target)

    outs = (down_out, gate_out, up_out, out_out, qkv_out)

    def finish(job, part):
        last = bufs[job][6]
        _, each, width, lanes, cut = JOBS[job]
        here = ring(part, 2)[0]
        arrive(job, part, 12, 13, 14)

        @pl.loop(0, width // 128)
        def _(step):
            to = pl.multiple_of(step * 128, 128)
            columns = pl.ds(to, 128)
            total = last[part, here, :, columns].astype(jnp.float32)
            for slot in range(3):
                total = total + last[part, 4 + slot, :, columns].astype(jnp.float32)
            outs[job][:, pl.ds(pl.multiple_of(part * width + to, 128), 128)] = total[:each]

    def products(job):
        name = JOBS[job][0]
        if name == "down":
            arrived(0, 1)
            for part in range(3):
                pick24(part)
                multiply(job, part, xt24, gbranch_s)
                first_send(job, part)
            return
        stack, right, indices = {
            "gate": (second_s, ggate_s, (2, 3)),
            "up": (second_s, gup_s, (4,)),
            "out": (context_s, gatt_s, (5, 6)),
            "qkv": (first_s, gproj_s, (7, 8)),
        }[name]
        arrived(*indices)
        for part in range(3):
            pick9(part, stack)
            multiply(job, part, xt9, right)
            first_send(job, part)

    stages = (products, first_add, second_send, second_add, third_send, finish)
    for step in range(len(JOBS) + len(stages) - 1):
        for number, stage in enumerate(stages):
            job = step - number
            if 0 <= job < len(JOBS):
                if number == 0:
                    stage(job)
                else:
                    for part in range(3):
                        stage(job, part)
    for copy in sent:
        copy.wait_send()


def reduce_products(first, context, second, hidden, gproj, gatt, ggate, gup, gbranch):
    src9 = jnp.asarray(row_sources())
    src24 = np.arange(192)
    src24 = jnp.asarray((src24 // 48 * 96 + src24 % 48).reshape(192, 1).astype(np.int32))
    vmem = pl.BlockSpec(memory_space=pltpu.VMEM)
    anywhere = pl.BlockSpec(memory_space=pl.ANY)
    scratch = [
        pltpu.VMEM((PAIR, HID), jnp.bfloat16),
        pltpu.VMEM((PAIR, WIDE), jnp.bfloat16),
        pltpu.VMEM((PAIR, WIDE), jnp.bfloat16),
        pltpu.VMEM((PAIR, WIDE), jnp.bfloat16),
        pltpu.VMEM((PAIR, WIDE), jnp.bfloat16),
        pltpu.VMEM((PAIR, HID), jnp.bfloat16),
        pltpu.VMEM((PAIR, HID), jnp.bfloat16),
        pltpu.VMEM((PAIR, WIDE), jnp.bfloat16),
        pltpu.VMEM((PAIR, 3 * WIDE), jnp.bfloat16),
        pltpu.VMEM((576, WIDE), jnp.bfloat16),
        pltpu.VMEM((576, PAIR), jnp.bfloat16),
        pltpu.VMEM((192, 384), jnp.bfloat16),
        pltpu.VMEM((1536, PAIR), jnp.float32),
        pltpu.VMEM((1536, PAIR), jnp.bfloat16),
        pltpu.VMEM((400, 128), jnp.float32),
    ]
    for _, each, width, _, _ in JOBS:
        big, small, tiny = 16 * each, sixteen(4 * each), sixteen(each)
        scratch += [
            pltpu.VMEM((3, 4 * big, width), jnp.bfloat16),
            pltpu.VMEM((3, big, width), jnp.bfloat16),
            pltpu.VMEM((3, 2, big, width), jnp.bfloat16),
            pltpu.VMEM((3, 4, small, width), jnp.bfloat16),
            pltpu.VMEM((3, small, width), jnp.bfloat16),
            pltpu.VMEM((3, 2, small, width), jnp.bfloat16),
            pltpu.VMEM((3, 7, tiny, width), jnp.bfloat16),
        ]
    count = PARTNER_COPIES + 3 * COPIES * len(JOBS)
    scratch += [
        pltpu.SemaphoreType.DMA((count,)),
        pltpu.SemaphoreType.DMA((count,)),
        pltpu.SemaphoreType.DMA((PARTNER_COPIES,)),
    ]
    return pl.pallas_call(
        reduce_kernel,
        out_shape=[
            jax.ShapeDtypeStruct((each, 3 * width), jnp.float32) for _, each, width, _, _ in JOBS
        ],
        in_specs=[vmem, vmem] + [anywhere] * 9,
        out_specs=[vmem] * 5,
        scratch_shapes=scratch,
        compiler_params=pltpu.CompilerParams(
            collective_id=1, has_side_effects=True, vmem_limit_bytes=62 * 1024 * 1024
        ),
        cost_estimate=pl.CostEstimate(
            flops=5_000_000_000, bytes_accessed=10_000_000, transcendentals=0
        ),
    )(src9, src24, hidden, second, context, first, gbranch, ggate, gup, gatt, gproj)


def body(
    tokens,
    condition,
    segments,
    mod_weight,
    mod_bias,
    qkv_weight,
    query_gain,
    key_gain,
    out_weight,
    gate_weight,
    up_weight,
    down_weight,
    cotangent,
):
    tok_count, model_width = tokens.shape
    slot_count = condition.shape[0]
    head_dim = query_gain.shape[0]
    head_count = model_width // head_dim
    split_shape = (tok_count, head_count, head_dim)
    score_scale = head_dim ** (-0.5)
    inputs_float = tokens.astype(jnp.float32)
    condition_pair = lax.all_gather(condition, "mod", axis=0, tiled=True)
    condition_act = jax.nn.silu(condition_pair.astype(jnp.float32)).astype(jnp.bfloat16)
    mod_half = (
        jnp.dot(condition_act, mod_weight, preferred_element_type=jnp.float32)
        + mod_bias.astype(jnp.float32)
    ).astype(jnp.bfloat16)
    modulation = lax.all_to_all(mod_half, "mod", split_axis=0, concat_axis=1, tiled=True)
    onehot = segments[:, None] == jnp.arange(slot_count, dtype=jnp.int32)[None, :]
    per_token = jnp.dot(onehot.astype(jnp.bfloat16), modulation, preferred_element_type=jnp.float32)
    pieces = [
        per_token[:, column * model_width : (column + 1) * model_width] for column in range(6)
    ]
    shift_first, scale_first, gate_first, shift_second, scale_second, gate_second = pieces
    norm_first, inverse_first = rms_norm(inputs_float)
    first_input = (norm_first * (1.0 + scale_first) + shift_first).astype(jnp.bfloat16)
    projected = jnp.dot(first_input, qkv_weight, preferred_element_type=jnp.float32)
    cosine, sine = rope_tables(segments, slot_count, SIDE, head_dim)
    query_hat, query_inverse = rms_norm(projected[:, :model_width].reshape(split_shape))
    key_hat, key_inverse = rms_norm(
        projected[:, model_width : 2 * model_width].reshape(split_shape)
    )
    queries = rotate(query_hat * query_gain, cosine, sine).astype(jnp.bfloat16)
    memory_keys = rotate(key_hat * key_gain, cosine, sine).astype(jnp.bfloat16)
    memory_values = projected[:, 2 * model_width :].reshape(split_shape).astype(jnp.bfloat16)
    allowed = segments[:, None] == segments[None, :]
    scores = masked_scores(queries, memory_keys, allowed, score_scale)
    row_top = jnp.max(scores, axis=-1, keepdims=True)
    log_total = row_top + jnp.log(jnp.sum(jnp.exp(scores - row_top), axis=-1, keepdims=True))
    attention_lo = jnp.exp(scores - log_total).astype(jnp.bfloat16)
    context = (
        jnp.einsum("hts,shd->thd", attention_lo, memory_values, preferred_element_type=jnp.float32)
        .astype(jnp.bfloat16)
        .reshape(tok_count, model_width)
    )
    attended = jnp.dot(context, out_weight, preferred_element_type=jnp.float32)
    middle = inputs_float + gate_first * attended
    norm_second, inverse_second = rms_norm(middle)
    second_input = (norm_second * (1.0 + scale_second) + shift_second).astype(jnp.bfloat16)
    gate_linear = jnp.dot(second_input, gate_weight, preferred_element_type=jnp.float32)
    up_linear = jnp.dot(second_input, up_weight, preferred_element_type=jnp.float32)
    gate_act = jax.nn.silu(gate_linear)
    hidden = (gate_act * up_linear).astype(jnp.bfloat16)
    branch = jnp.dot(hidden, down_weight, preferred_element_type=jnp.float32)
    layer_out = (middle + gate_second * branch).astype(jnp.bfloat16)
    upstream = cotangent.astype(jnp.float32)
    grad_gate_second = upstream * branch
    grad_branch = (upstream * gate_second).astype(jnp.bfloat16)
    grad_hidden = inner_cols(grad_branch, down_weight)
    grad_gate_linear = (grad_hidden * up_linear * silu_slope(gate_linear)).astype(jnp.bfloat16)
    grad_up_linear = (grad_hidden * gate_act).astype(jnp.bfloat16)
    grad_second = inner_cols(grad_gate_linear, gate_weight) + inner_cols(grad_up_linear, up_weight)
    grad_scale_second = grad_second * norm_second
    grad_middle = upstream + norm_back(
        grad_second * (1.0 + scale_second), norm_second, inverse_second
    )
    grad_gate_first = grad_middle * attended
    grad_attended = (grad_middle * gate_first).astype(jnp.bfloat16)
    grad_context = inner_cols(grad_attended, out_weight).astype(jnp.bfloat16).reshape(split_shape)
    scores_again = masked_scores(queries, memory_keys, allowed, score_scale)
    attention = jnp.exp(scores_again - log_total)
    attention_again = attention.astype(jnp.bfloat16)
    grad_attention = jnp.einsum(
        "thd,shd->hts", grad_context, memory_values, preferred_element_type=jnp.float32
    )
    grad_values = jnp.einsum(
        "hts,thd->shd", attention_again, grad_context, preferred_element_type=jnp.float32
    )
    row_dot = jnp.sum(attention * grad_attention, axis=-1, keepdims=True)
    grad_scores = (attention * (grad_attention - row_dot)).astype(jnp.bfloat16)
    grad_queries = (
        jnp.einsum("hts,shd->thd", grad_scores, memory_keys, preferred_element_type=jnp.float32)
        * score_scale
    )
    grad_keys = (
        jnp.einsum("hts,thd->shd", grad_scores, queries, preferred_element_type=jnp.float32)
        * score_scale
    )
    query_unrot = rotate(grad_queries, cosine, -sine)
    key_unrot = rotate(grad_keys, cosine, -sine)
    grad_query_gain = jnp.sum(query_unrot * query_hat, axis=(0, 1))
    grad_key_gain = jnp.sum(key_unrot * key_hat, axis=(0, 1))
    grad_query_raw = norm_back(query_unrot * query_gain, query_hat, query_inverse)
    grad_key_raw = norm_back(key_unrot * key_gain, key_hat, key_inverse)
    grad_projected = jnp.concatenate(
        [
            grad_query_raw.reshape(tok_count, model_width),
            grad_key_raw.reshape(tok_count, model_width),
            grad_values.reshape(tok_count, model_width),
        ],
        axis=1,
    ).astype(jnp.bfloat16)
    grad_first = inner_cols(grad_projected, qkv_weight)
    grad_scale_first = grad_first * norm_first
    grad_tokens = grad_middle + norm_back(
        grad_first * (1.0 + scale_first), norm_first, inverse_first
    )
    grad_per_token = jnp.concatenate(
        [
            grad_first,
            grad_scale_first,
            grad_gate_first,
            grad_second,
            grad_scale_second,
            grad_gate_second,
        ],
        axis=1,
    )
    grad_mod_own = lax.dot_general(
        onehot.astype(jnp.float32),
        grad_per_token,
        (((0,), (0,)), ((), ())),
        precision=HIGHEST,
        preferred_element_type=jnp.float32,
    ).astype(jnp.bfloat16)
    grad_mod_pair = lax.all_to_all(grad_mod_own, "mod", split_axis=1, concat_axis=0, tiled=True)
    grad_condition_act = lax.psum_scatter(
        inner_cols(grad_mod_pair, mod_weight).astype(jnp.bfloat16),
        "mod",
        scatter_dimension=0,
        tiled=True,
    ).astype(jnp.float32)
    grad_condition = grad_condition_act * silu_slope(condition.astype(jnp.float32))
    shares = reduce_products(
        first_input,
        context,
        second_input,
        hidden,
        grad_projected,
        grad_attended,
        grad_gate_linear,
        grad_up_linear,
        grad_branch,
    )
    mod_rows = lax.all_gather(grad_mod_pair, "dp", axis=0, tiled=True)
    act_rows = lax.all_gather(condition_act, "dp", axis=0, tiled=True)
    dp_rank = lax.axis_index("dp")
    share_rows = model_width // lax.axis_size("dp")
    act_share = lax.dynamic_slice_in_dim(act_rows, dp_rank * share_rows, share_rows, axis=1)
    grad_mod_weight = inner_rows(act_share, mod_rows)
    bias_half = jnp.sum(mod_rows.astype(jnp.float32), axis=0)
    grad_mod_bias = lax.all_gather(bias_half, "mod", axis=0, tiled=True)
    grad_query_gain, grad_key_gain = lax.psum((grad_query_gain, grad_key_gain), ("dp", "mod"))
    return (
        layer_out,
        grad_tokens,
        grad_condition,
        grad_mod_weight,
        grad_mod_bias,
        shares[4],
        grad_query_gain,
        grad_key_gain,
        shares[3],
        shares[1],
        shares[2],
        shares[0],
    )


def solution(mesh):
    placed = (
        P(("dp", "mod"), None),
        P(("dp", "mod"), None),
        P(("dp", "mod")),
        P(None, "mod"),
        P("mod"),
        P(),
        P(),
        P(),
        P(),
        P(),
        P(),
        P(),
        P(("dp", "mod"), None),
    )
    return jax.shard_map(
        body,
        mesh=mesh,
        in_specs=placed,
        out_specs=(
            P(("dp", "mod"), None),
            P(("dp", "mod"), None),
            P(("dp", "mod"), None),
            P("dp", "mod"),
            P(),
            P(("dp", "mod"), None),
            P(),
            P(),
            P(("dp", "mod"), None),
            P(("dp", "mod"), None),
            P(("dp", "mod"), None),
            P(("dp", "mod"), None),
        ),
        check_vma=False,
    )
```

```python
import jax
import jax.numpy as jnp
import numpy as np
from jax import lax
from jax.experimental import pallas as pl
from jax.experimental.pallas import tpu as pltpu
from jax.sharding import PartitionSpec as P

SIDE = 12


EPSILON = 1e-06
HIGHEST = lax.Precision.HIGHEST


def rms_norm(values):
    inverse = lax.rsqrt(jnp.mean(values * values, axis=-1, keepdims=True) + EPSILON)
    return (values * inverse, inverse)


def norm_back(upstream, normed, inverse):
    return inverse * (upstream - normed * jnp.mean(upstream * normed, axis=-1, keepdims=True))


def rotate(values, cosine, sine):
    half_dim = values.shape[-1] // 2
    leading = values[..., :half_dim]
    trailing = values[..., half_dim:]
    cosine = cosine[:, None, :]
    sine = sine[:, None, :]
    return jnp.concatenate(
        [leading * cosine - trailing * sine, trailing * cosine + leading * sine], axis=-1
    )


def rope_tables(segments, slot_count, side_big, head_dim):
    tok_count = segments.shape[0]
    onehot = (segments[:, None] == jnp.arange(slot_count, dtype=jnp.int32)[None, :]).astype(
        jnp.int32
    )
    counts = jnp.sum(onehot, axis=0)
    starts = jnp.cumsum(counts) - counts
    first_tok = jnp.sum(onehot * starts[None, :], axis=1)
    extent = jnp.sum(onehot * counts[None, :], axis=1)
    position = jnp.arange(tok_count, dtype=jnp.int32) - first_tok
    side_len = jnp.where(extent == tok_count, side_big, side_big // 2).astype(jnp.int32)
    row_pos = (position // side_len).astype(jnp.float32)
    col_pos = (position % side_len).astype(jnp.float32)
    quarter = head_dim // 4
    frequency = 10000.0 ** (-jnp.arange(quarter, dtype=jnp.float32) / quarter)
    angles = jnp.concatenate(
        [row_pos[:, None] * frequency[None, :], col_pos[:, None] * frequency[None, :]], axis=1
    )
    return (jnp.cos(angles), jnp.sin(angles))


def silu_slope(values):
    logistic = jax.nn.sigmoid(values)
    return logistic * (1.0 + values * (1.0 - logistic))


def inner_rows(left, right):
    return lax.dot_general(
        left, right, (((0,), (0,)), ((), ())), preferred_element_type=jnp.float32
    )


def inner_cols(left, right):
    return lax.dot_general(
        left, right, (((1,), (1,)), ((), ())), preferred_element_type=jnp.float32
    )


def masked_scores(queries, memory_keys, allowed, score_scale):
    scores = (
        jnp.einsum("thd,shd->hts", queries, memory_keys, preferred_element_type=jnp.float32)
        * score_scale
    )
    return jnp.where(allowed[None], scores, -1e30)


TOK = 144
PAIR = 2 * TOK
WIDE = 1152
HID = 3072
RING = 4
AXES = ((0, 1, 2), (1, 2, 0), (2, 0, 1))
JOBS = (
    ("down", 24, 384, 384, 256),
    ("gate", 9, 1024, 256, 512),
    ("up", 9, 1024, 256, 512),
    ("out", 9, 384, 384, 256),
    ("qkv", 9, 1152, 384, 640),
)
COPIES = 15
PARTNER_COPIES = 9


def sixteen(rows):
    return (rows + 15) // 16 * 16


def position():
    dp = lax.axis_index("dp")
    x_hi = lax.axis_index("mod")
    core = lax.rem(dp, 2)
    y = lax.rem(dp // 2, 4)
    z = lax.rem(dp // 8, 4)
    return (x_hi * 2 + dp // 32, y, z), core


def device_at(place, core):
    x, y, z = place
    return (((lax.rem(x, 2) * 4 + z) * 4 + y) * 2 + core, x // 2)


def moved(place, axis, value):
    return tuple(value if index == axis else kept for index, kept in enumerate(place))


def row_sources():
    tables = []
    for order in AXES:
        table = np.zeros((4, 4, 4, 9), np.int32)
        for first in range(4):
            for second in range(4):
                for third in range(4):
                    place = [0, 0, 0]
                    for axis, value in zip(order, (first, second, third)):
                        place[axis] = value
                    x, y, z = place
                    owner = (x % 2) * 64 + z * 16 + y * 4 + x // 2
                    table[first, second, third] = owner * 9 + np.arange(9)
        tables.append(table.reshape(576, 1))
    return np.stack(tables)


def reduce_kernel(
    src9_ref,
    src24_ref,
    hidden_in,
    second_in,
    context_in,
    first_in,
    gbranch_in,
    ggate_in,
    gup_in,
    gatt_in,
    gproj_in,
    gmod_in,
    act_in,
    condition_in,
    mod_weight_in,
    down_out,
    gate_out,
    up_out,
    out_out,
    qkv_out,
    mod_out,
    special_out,
    condition_out,
    hidden_s,
    second_s,
    context_s,
    first_s,
    gbranch_s,
    ggate_s,
    gup_s,
    gatt_s,
    gproj_s,
    perm9,
    xt9,
    perm24,
    t32,
    xt24,
    acc,
    fold32,
    fold_own,
    fold_other,
    other32,
    pair32,
    across32,
    rows32,
    gathered_a,
    gathered_b,
    product_own,
    product_send,
    product_other,
    final_other,
    special_other,
    part_own,
    part_other,
    weights,
    *rest,
):
    bufs = [rest[7 * index : 7 * index + 7] for index in range(len(JOBS))]
    send_sem, recv_sem, local_sem = rest[7 * len(JOBS) :]
    place, core = position()
    partner = device_at(place, 1 - core)
    near = []
    for axis in range(3):
        here = place[axis]
        near.append(
            (here, lax.rem(here + 1, 4), lax.rem(here + 3, 4), lax.rem(here + 2, 4))
        )

    barrier = pltpu.get_barrier_semaphore()
    pl.semaphore_signal(barrier, inc=1, device_id=partner, device_id_type=pl.DeviceIdType.MESH)
    for axis in range(3):
        for value in near[axis][1:]:
            pl.semaphore_signal(
                barrier,
                inc=1,
                device_id=device_at(moved(place, axis, value), core),
                device_id_type=pl.DeviceIdType.MESH,
            )
    twin = moved(place, 0, near[0][3])
    pl.semaphore_signal(
        barrier, inc=1, device_id=device_at(twin, 1 - core), device_id_type=pl.DeviceIdType.MESH
    )
    pl.semaphore_wait(barrier, 11)

    def remote(src, dst, index, target):
        return pltpu.make_async_remote_copy(
            src_ref=src,
            dst_ref=dst,
            send_sem=send_sem.at[index],
            recv_sem=recv_sem.at[index],
            device_id=target,
            device_id_type=pl.DeviceIdType.MESH,
        )

    sent = []
    pairs = {}
    ins = (gbranch_in, hidden_in, second_in, ggate_in, gup_in, context_in, gatt_in, first_in, gproj_in)
    stacks = (gbranch_s, hidden_s, second_s, ggate_s, gup_s, context_s, gatt_s, first_s, gproj_s)
    for index, (own, stack) in enumerate(zip(ins, stacks)):
        local = pltpu.make_async_copy(own, stack.at[pl.ds(0, TOK)], local_sem.at[index])
        local.start()
        across = remote(own, stack.at[pl.ds(TOK, TOK)], index, partner)
        across.start()
        sent.append(across)
        pairs[index] = (local, across)

    def arrived(*indices):
        for index in indices:
            local, across = pairs[index]
            local.wait()
            across.wait_recv()

    lane = lax.broadcasted_iota(jnp.int32, (192, 384), 1)
    perm24[...] = (lane == src24_ref[...] + core * 48).astype(jnp.float32).astype(jnp.bfloat16)

    def pick9(part, stack):
        @pl.loop(0, 9)
        def _(block):
            columns = lax.broadcasted_iota(jnp.int32, (576, 128), 1) + block * 128
            perm9[:, pl.ds(pl.multiple_of(block * 128, 128), 128)] = (
                (columns == src9_ref[part] + core * 18).astype(jnp.float32).astype(jnp.bfloat16)
            )

        xt9[...] = inner_cols(perm9[...], stack[...]).astype(jnp.bfloat16)

    def pick24(part):
        order = AXES[part]
        weight = [0, 0, 0]
        for axis, value in zip(order, (16, 4, 1)):
            weight[axis] = value

        @pl.loop(0, 8)
        def _(block):
            columns = pl.ds(pl.multiple_of(block * 384, 128), 384)
            rows = inner_cols(perm24[...], hidden_s[:, columns])
            base = (block // 4) * weight[0] + lax.rem(block, 4) * weight[2]
            for y in range(4):
                for x_hi in range(2):
                    unit = base + y * weight[1] + x_hi * 2 * weight[0]
                    at = (y * 2 + x_hi) * 24
                    t32[pl.ds(pl.multiple_of(unit * 24, 8), 24), :] = rows[at : at + 24]

        xt24[...] = t32[...].astype(jnp.bfloat16)

    def multiply(job, part, left, right):
        _, _, width, lanes, _ = JOBS[job]
        target = bufs[job][0]

        @pl.loop(0, width // lanes)
        def _(step):
            to = pl.multiple_of(step * lanes, 128)
            columns = pl.ds(pl.multiple_of(part * width + to, 128), lanes)
            target[part, :, pl.ds(to, lanes)] = jnp.dot(
                left[...], right[:, columns], preferred_element_type=jnp.float32
            ).astype(jnp.bfloat16)

    copies = {}

    def begin(job, part, slot, src, dst, target):
        index = PARTNER_COPIES + (job * 3 + part) * COPIES + slot
        copy = remote(src, dst, index, target)
        copy.start()
        sent.append(copy)
        copies[job, part, slot] = copy

    def arrive(job, part, *slots):
        for slot in slots:
            copies[job, part, slot].wait_recv()

    def ring(part, phase):
        axis = AXES[part][phase]
        here, right, left, opposite = near[axis]
        return (
            here,
            right,
            left,
            opposite,
            device_at(moved(place, axis, right), core),
            device_at(moved(place, axis, left), core),
            device_at(moved(place, axis, opposite), core),
        )

    def first_send(job, part):
        own, half, whole = bufs[job][:3]
        big = 16 * JOBS[job][1]
        cut = sixteen(big // 2)
        here, right, left, opposite, to_right, to_left, _ = ring(part, 0)

        def rows(chunk, start, count):
            return own.at[part, pl.ds(pl.multiple_of(chunk * big + start, 16), count)]

        begin(job, part, 0, rows(opposite, 0, cut), half.at[part, pl.ds(0, cut)], to_right)
        begin(job, part, 1, rows(opposite, cut, big - cut), half.at[part, pl.ds(cut, big - cut)], to_left)
        begin(job, part, 2, rows(right, cut, big - cut), whole.at[part, 0, pl.ds(cut, big - cut)], to_right)
        begin(job, part, 3, rows(left, 0, cut), whole.at[part, 1, pl.ds(0, cut)], to_left)

    def first_add(job, part):
        own, half, whole = bufs[job][:3]
        _, each, width, lanes, _ = JOBS[job]
        big = 16 * each
        cut = sixteen(big // 2)
        here, right, left, opposite, to_right, to_left, _ = ring(part, 0)
        for slot, chunk, start, count, target, side in (
            (0, right, 0, cut, to_right, 0),
            (1, left, cut, big - cut, to_left, 1),
        ):
            arrive(job, part, slot)
            rows = pl.ds(pl.multiple_of(chunk * big + start, 16), count)

            @pl.loop(0, width // 128)
            def _(step):
                columns = pl.ds(pl.multiple_of(step * 128, 128), 128)
                total = own[part, rows, columns].astype(jnp.float32) + half[
                    part, pl.ds(start, count), columns
                ].astype(jnp.float32)
                own[part, rows, columns] = total.astype(jnp.bfloat16)

            begin(
                job,
                part,
                4 + side,
                own.at[part, rows],
                whole.at[part, side, pl.ds(start, count)],
                target,
            )

    def second_send(job, part):
        own, _, whole, mid, mid_half, mid_whole, _ = bufs[job]
        _, each, width, lanes, cut = JOBS[job]
        big, small = 16 * each, 4 * each
        padded = sixteen(small)
        here, right, left, opposite, to_right, to_left, _ = ring(part, 0)
        arrive(job, part, 2, 3, 4, 5)
        rows = pl.ds(pl.multiple_of(here * big, 16), big)

        @pl.loop(0, width // 128)
        def _(step):
            columns = pl.ds(pl.multiple_of(step * 128, 128), 128)
            acc[pl.ds(0, big), :] = (
                own[part, rows, columns].astype(jnp.float32)
                + whole[part, 0, :, columns].astype(jnp.float32)
                + whole[part, 1, :, columns].astype(jnp.float32)
            )
            for chunk in range(4):
                mid[part, chunk, :, columns] = acc[pl.ds(chunk * small, padded), :].astype(jnp.bfloat16)

        here, right, left, opposite, to_right, to_left, _ = ring(part, 1)
        low, high = pl.ds(0, cut), pl.ds(cut, width - cut)
        begin(job, part, 6, mid.at[part, opposite, :, low], mid_half.at[part, :, low], to_right)
        begin(job, part, 7, mid.at[part, opposite, :, high], mid_half.at[part, :, high], to_left)
        begin(job, part, 8, mid.at[part, right, :, high], mid_whole.at[part, 0, :, high], to_right)
        begin(job, part, 9, mid.at[part, left, :, low], mid_whole.at[part, 1, :, low], to_left)

    def second_add(job, part):
        _, _, _, mid, mid_half, mid_whole, _ = bufs[job]
        _, each, width, lanes, cut = JOBS[job]
        here, right, left, opposite, to_right, to_left, _ = ring(part, 1)
        for slot, chunk, start, count, target, side in (
            (6, right, 0, cut, to_right, 0),
            (7, left, cut, width - cut, to_left, 1),
        ):
            arrive(job, part, slot)

            @pl.loop(0, count // 128)
            def _(step):
                columns = pl.ds(pl.multiple_of(start + step * 128, 128), 128)
                total = mid[part, chunk, :, columns].astype(jnp.float32) + mid_half[
                    part, :, columns
                ].astype(jnp.float32)
                mid[part, chunk, :, columns] = total.astype(jnp.bfloat16)

            columns = pl.ds(start, count)
            begin(
                job,
                part,
                10 + side,
                mid.at[part, chunk, :, columns],
                mid_whole.at[part, side, :, columns],
                target,
            )

    def third_send(job, part):
        _, _, _, mid, _, mid_whole, last = bufs[job]
        _, each, width, lanes, cut = JOBS[job]
        small = sixteen(4 * each)
        padded = sixteen(each)
        here = ring(part, 1)[0]
        arrive(job, part, 8, 9, 10, 11)

        @pl.loop(0, width // 128)
        def _(step):
            columns = pl.ds(pl.multiple_of(step * 128, 128), 128)
            acc[pl.ds(0, small), :] = (
                mid[part, here, :, columns].astype(jnp.float32)
                + mid_whole[part, 0, :, columns].astype(jnp.float32)
                + mid_whole[part, 1, :, columns].astype(jnp.float32)
            )
            for chunk in range(4):
                last[part, chunk, :, columns] = acc[pl.ds(chunk * each, padded), :].astype(jnp.bfloat16)

        here, right, left, opposite, to_right, to_left, to_opposite = ring(part, 2)
        for slot, chunk, target in ((0, right, to_right), (1, left, to_left), (2, opposite, to_opposite)):
            begin(job, part, 12 + slot, last.at[part, chunk], last.at[part, 4 + slot], target)

    mod = lax.axis_index("mod")
    mod_base = PARTNER_COPIES + 3 * COPIES * len(JOBS)
    mod_copies = {}

    def mod_send(slot, src, dst, target):
        copy = remote(src, dst, mod_base + slot, target)
        copy.start()
        sent.append(copy)
        mod_copies[slot] = copy

    def mod_arrive(*slots):
        for slot in slots:
            mod_copies[slot].wait_recv()

    def weight_chunk(index):
        return pltpu.make_async_copy(
            mod_weight_in.at[:, pl.ds(index * 384, 384)],
            weights.at[index % 2],
            local_sem.at[PARTNER_COPIES + index % 2],
        )

    def mod_pair():
        weight_chunk(0).start()
        weight_chunk(1).start()
        for quarter in range(4):
            fold32[4 * quarter : 4 * quarter + 4, :] = gmod_in[
                1 - mod, 0:4, quarter * 896 : (quarter + 1) * 896
            ]
        fold_own[...] = fold32[...].astype(jnp.bfloat16)
        mod_send(0, fold_own, fold_other, device_at(twin, core))

    def mod_cores():
        mod_arrive(0)
        fold32[...] = fold_other[...].astype(jnp.float32)
        for quarter in range(4):
            other32[0:4, quarter * 896 : (quarter + 1) * 896] = fold32[4 * quarter : 4 * quarter + 4, :]
        own, other = gmod_in[mod, 0:4, :], other32[0:4, :]
        pair32[0:4, :] = jnp.where(mod == 0, own, other)
        pair32[4:8, :] = jnp.where(mod == 0, other, own)
        there = pl.ds(pl.multiple_of((1 - core) * 1792, 128), 1792)
        mod_send(1, pair32.at[:, there], across32, partner)

    def condition_part():
        total = jnp.zeros((8, WIDE), jnp.float32)
        for index in range(9):
            weight_chunk(index).wait()
            total = total + inner_cols(
                pair32[:, index * 384 : (index + 1) * 384].astype(jnp.bfloat16),
                weights[index % 2],
            )
            if index + 2 < 9:
                weight_chunk(index + 2).start()
        part_own[...] = total
        mod_send(2, part_own, part_other, device_at(twin, core))

    def mod_gather_first():
        mod_arrive(1)
        here = pl.ds(pl.multiple_of(core * 1792, 128), 1792)
        own, other = pair32[:, here], across32[...]
        rows32[0:8, :] = jnp.where(core == 0, own, other)
        rows32[8:16, :] = jnp.where(core == 0, other, own)
        _, y, z = place
        gathered_a[z, y] = rows32[:, 0:896].astype(jnp.bfloat16)
        gathered_b[z, y] = rows32[:, 896:1792].astype(jnp.bfloat16)
        for step in range(3):
            to_y = device_at(moved(place, 1, near[1][1 + step]), core)
            to_z = device_at(moved(place, 2, near[2][1 + step]), core)
            mod_send(3 + step, gathered_a.at[z, y], gathered_a.at[z, y], to_y)
            mod_send(6 + step, gathered_b.at[z, y], gathered_b.at[z, y], to_z)

    def mod_gather_second():
        _, y, z = place
        mod_arrive(3, 4, 5)
        for step in range(3):
            to_z = device_at(moved(place, 2, near[2][1 + step]), core)
            mod_send(9 + step, gathered_a.at[z], gathered_a.at[z], to_z)
        mod_arrive(6, 7, 8)
        for step in range(3):
            to_y = device_at(moved(place, 1, near[1][1 + step]), core)
            mod_send(12 + step, gathered_b.at[:, y], gathered_b.at[:, y], to_y)

    def mod_product():
        mod_arrive(9, 10, 11)
        mod_arrive(12, 13, 14)
        for side, gathered in ((0, gathered_a), (1, gathered_b)):
            columns = slice(side * 896, (side + 1) * 896)
            rows = gathered[...].reshape(256, 896)
            product_send[:, columns] = jnp.dot(
                act_in[1], rows, preferred_element_type=jnp.float32
            ).astype(jnp.bfloat16)
            product_own[:, columns] = jnp.dot(act_in[0], rows, preferred_element_type=jnp.float32)
        x = place[0]
        beside = moved(place, 0, x + 1 - 2 * lax.rem(x, 2))
        mod_send(15, product_send, product_other, device_at(beside, core))

    def mod_sum():
        mod_arrive(15)
        product_own[...] = product_own[...] + product_other[...].astype(jnp.float32)
        mod_send(16, product_own, final_other, partner)
        special = product_own.at[pl.ds(40, 8)]
        mod_send(17, special, special_other.at[core], device_at(twin, core))
        mod_send(18, special, special_other.at[core], device_at(twin, 1 - core))

    def mod_finish():
        here = pl.ds(pl.multiple_of(core * 1792, 128), 1792)
        there = pl.ds(pl.multiple_of((1 - core) * 1792, 128), 1792)
        mod_arrive(2)
        total = part_own[...] + part_other[...]
        raw = condition_in[...].astype(jnp.float32)
        condition_out[...] = jnp.where(mod == 0, total[0:4], total[4:8]) * silu_slope(raw)
        mod_arrive(16)
        for source, columns in ((product_own, here), (final_other, there)):
            mod_out[:, columns] = jnp.where(core == 0, source[0:18, :], source[18:36, :])
            special_out[mod, :, columns] = source[40:48, :]
        mod_arrive(17, 18)
        for side in range(2):
            special_out[1 - mod, :, side * 1792 : (side + 1) * 1792] = special_other[side]

    outs = (down_out, gate_out, up_out, out_out, qkv_out)

    def finish(job, part):
        last = bufs[job][6]
        _, each, width, lanes, cut = JOBS[job]
        here = ring(part, 2)[0]
        arrive(job, part, 12, 13, 14)

        @pl.loop(0, width // 128)
        def _(step):
            to = pl.multiple_of(step * 128, 128)
            columns = pl.ds(to, 128)
            total = last[part, here, :, columns].astype(jnp.float32)
            for slot in range(3):
                total = total + last[part, 4 + slot, :, columns].astype(jnp.float32)
            outs[job][:, pl.ds(pl.multiple_of(part * width + to, 128), 128)] = total[:each]

    def products(job):
        name = JOBS[job][0]
        if name == "down":
            arrived(0, 1)
            for part in range(3):
                pick24(part)
                multiply(job, part, xt24, gbranch_s)
                first_send(job, part)
            return
        stack, right, indices = {
            "gate": (second_s, ggate_s, (2, 3)),
            "up": (second_s, gup_s, (4,)),
            "out": (context_s, gatt_s, (5, 6)),
            "qkv": (first_s, gproj_s, (7, 8)),
        }[name]
        arrived(*indices)
        for part in range(3):
            pick9(part, stack)
            multiply(job, part, xt9, right)
            first_send(job, part)

    extra = {
        0: (mod_pair,),
        1: (mod_cores, condition_part),
        2: (mod_gather_first,),
        3: (mod_gather_second,),
        5: (mod_product,),
        6: (mod_sum,),
        8: (mod_finish,),
    }
    stages = (products, first_add, second_send, second_add, third_send, finish)
    for step in range(len(JOBS) + len(stages) - 1):
        for piece in extra.get(step, ()):
            piece()
        for number, stage in enumerate(stages):
            job = step - number
            if 0 <= job < len(JOBS):
                if number == 0:
                    stage(job)
                else:
                    for part in range(3):
                        stage(job, part)
    for copy in sent:
        copy.wait_send()


def reduce_products(first, context, second, hidden, gproj, gatt, ggate, gup, gbranch, gmod, act, condition, mod_weight):
    src9 = jnp.asarray(row_sources())
    src24 = np.arange(192)
    src24 = jnp.asarray((src24 // 48 * 96 + src24 % 48).reshape(192, 1).astype(np.int32))
    vmem = pl.BlockSpec(memory_space=pltpu.VMEM)
    anywhere = pl.BlockSpec(memory_space=pl.ANY)
    scratch = [
        pltpu.VMEM((PAIR, HID), jnp.bfloat16),
        pltpu.VMEM((PAIR, WIDE), jnp.bfloat16),
        pltpu.VMEM((PAIR, WIDE), jnp.bfloat16),
        pltpu.VMEM((PAIR, WIDE), jnp.bfloat16),
        pltpu.VMEM((PAIR, WIDE), jnp.bfloat16),
        pltpu.VMEM((PAIR, HID), jnp.bfloat16),
        pltpu.VMEM((PAIR, HID), jnp.bfloat16),
        pltpu.VMEM((PAIR, WIDE), jnp.bfloat16),
        pltpu.VMEM((PAIR, 3 * WIDE), jnp.bfloat16),
        pltpu.VMEM((576, WIDE), jnp.bfloat16),
        pltpu.VMEM((576, PAIR), jnp.bfloat16),
        pltpu.VMEM((192, 384), jnp.bfloat16),
        pltpu.VMEM((1536, PAIR), jnp.float32),
        pltpu.VMEM((1536, PAIR), jnp.bfloat16),
        pltpu.VMEM((400, 128), jnp.float32),
        pltpu.VMEM((16, 896), jnp.float32),
        pltpu.VMEM((16, 896), jnp.bfloat16),
        pltpu.VMEM((16, 896), jnp.bfloat16),
        pltpu.VMEM((8, 3584), jnp.float32),
        pltpu.VMEM((8, 3584), jnp.float32),
        pltpu.VMEM((8, 1792), jnp.float32),
        pltpu.VMEM((16, 1792), jnp.float32),
        pltpu.VMEM((4, 4, 16, 896), jnp.bfloat16),
        pltpu.VMEM((4, 4, 16, 896), jnp.bfloat16),
        pltpu.VMEM((48, 1792), jnp.float32),
        pltpu.VMEM((48, 1792), jnp.bfloat16),
        pltpu.VMEM((48, 1792), jnp.bfloat16),
        pltpu.VMEM((48, 1792), jnp.float32),
        pltpu.VMEM((2, 8, 1792), jnp.float32),
        pltpu.VMEM((8, WIDE), jnp.float32),
        pltpu.VMEM((8, WIDE), jnp.float32),
        pltpu.VMEM((2, WIDE, 384), jnp.bfloat16),
    ]
    for _, each, width, _, _ in JOBS:
        big, small, tiny = 16 * each, sixteen(4 * each), sixteen(each)
        scratch += [
            pltpu.VMEM((3, 4 * big, width), jnp.bfloat16),
            pltpu.VMEM((3, big, width), jnp.bfloat16),
            pltpu.VMEM((3, 2, big, width), jnp.bfloat16),
            pltpu.VMEM((3, 4, small, width), jnp.bfloat16),
            pltpu.VMEM((3, small, width), jnp.bfloat16),
            pltpu.VMEM((3, 2, small, width), jnp.bfloat16),
            pltpu.VMEM((3, 7, tiny, width), jnp.bfloat16),
        ]
    count = PARTNER_COPIES + 3 * COPIES * len(JOBS) + 19
    scratch += [
        pltpu.SemaphoreType.DMA((count,)),
        pltpu.SemaphoreType.DMA((count,)),
        pltpu.SemaphoreType.DMA((PARTNER_COPIES + 2,)),
    ]
    return pl.pallas_call(
        reduce_kernel,
        out_shape=[
            jax.ShapeDtypeStruct((each, 3 * width), jnp.float32) for _, each, width, _, _ in JOBS
        ]
        + [
            jax.ShapeDtypeStruct((18, 3584), jnp.float32),
            jax.ShapeDtypeStruct((2, 8, 3584), jnp.float32),
            jax.ShapeDtypeStruct((4, WIDE), jnp.float32),
        ],
        in_specs=[vmem, vmem] + [anywhere] * 9 + [vmem] * 3 + [anywhere],
        out_specs=[vmem] * 8,
        scratch_shapes=scratch,
        compiler_params=pltpu.CompilerParams(
            collective_id=1, has_side_effects=True, vmem_limit_bytes=62 * 1024 * 1024
        ),
        cost_estimate=pl.CostEstimate(
            flops=5_000_000_000, bytes_accessed=10_000_000, transcendentals=0
        ),
    )(src9, src24, hidden, second, context, first, gbranch, ggate, gup, gatt, gproj, gmod, act, condition, mod_weight)

def gathered_act(condition_act):
    rows = lax.all_gather(condition_act, "dp", axis=0, tiled=True)
    dp = lax.axis_index("dp")
    own = lax.dynamic_slice_in_dim(rows, dp // 32 * 256, 256, axis=0)
    slot = np.arange(256)
    ones = np.stack([slot >= 0, slot % 4 == 0, slot % 4 == 1]).astype(jnp.bfloat16)
    tables = []
    for shift in (0, 32):
        start = (dp // 2 * 2 + shift) % 64 * 18
        part = lax.dynamic_slice_in_dim(own, start, 36, axis=1).T
        tables.append(jnp.concatenate([jnp.pad(part, ((0, 4), (0, 0))), jnp.pad(ones, ((0, 5), (0, 0)))]))
    return jnp.stack(tables)


def body(
    tokens,
    condition,
    segments,
    mod_weight,
    mod_bias,
    qkv_weight,
    query_gain,
    key_gain,
    out_weight,
    gate_weight,
    up_weight,
    down_weight,
    cotangent,
):
    tok_count, model_width = tokens.shape
    slot_count = condition.shape[0]
    head_dim = query_gain.shape[0]
    head_count = model_width // head_dim
    split_shape = (tok_count, head_count, head_dim)
    score_scale = head_dim ** (-0.5)
    inputs_float = tokens.astype(jnp.float32)
    condition_pair = lax.all_gather(condition, "mod", axis=0, tiled=True)
    condition_act = jax.nn.silu(condition_pair.astype(jnp.float32)).astype(jnp.bfloat16)
    mod_half = (
        jnp.dot(condition_act, mod_weight, preferred_element_type=jnp.float32)
        + mod_bias.astype(jnp.float32)
    ).astype(jnp.bfloat16)
    modulation = lax.all_to_all(mod_half, "mod", split_axis=0, concat_axis=1, tiled=True)
    onehot = segments[:, None] == jnp.arange(slot_count, dtype=jnp.int32)[None, :]
    per_token = jnp.dot(onehot.astype(jnp.bfloat16), modulation, preferred_element_type=jnp.float32)
    pieces = [
        per_token[:, column * model_width : (column + 1) * model_width] for column in range(6)
    ]
    shift_first, scale_first, gate_first, shift_second, scale_second, gate_second = pieces
    norm_first, inverse_first = rms_norm(inputs_float)
    first_input = (norm_first * (1.0 + scale_first) + shift_first).astype(jnp.bfloat16)
    projected = jnp.dot(first_input, qkv_weight, preferred_element_type=jnp.float32)
    cosine, sine = rope_tables(segments, slot_count, SIDE, head_dim)
    query_hat, query_inverse = rms_norm(projected[:, :model_width].reshape(split_shape))
    key_hat, key_inverse = rms_norm(
        projected[:, model_width : 2 * model_width].reshape(split_shape)
    )
    queries = rotate(query_hat * query_gain, cosine, sine).astype(jnp.bfloat16)
    memory_keys = rotate(key_hat * key_gain, cosine, sine).astype(jnp.bfloat16)
    memory_values = projected[:, 2 * model_width :].reshape(split_shape).astype(jnp.bfloat16)
    allowed = segments[:, None] == segments[None, :]
    scores = masked_scores(queries, memory_keys, allowed, score_scale)
    row_top = jnp.max(scores, axis=-1, keepdims=True)
    log_total = row_top + jnp.log(jnp.sum(jnp.exp(scores - row_top), axis=-1, keepdims=True))
    attention_lo = jnp.exp(scores - log_total).astype(jnp.bfloat16)
    context = (
        jnp.einsum("hts,shd->thd", attention_lo, memory_values, preferred_element_type=jnp.float32)
        .astype(jnp.bfloat16)
        .reshape(tok_count, model_width)
    )
    attended = jnp.dot(context, out_weight, preferred_element_type=jnp.float32)
    middle = inputs_float + gate_first * attended
    norm_second, inverse_second = rms_norm(middle)
    second_input = (norm_second * (1.0 + scale_second) + shift_second).astype(jnp.bfloat16)
    gate_linear = jnp.dot(second_input, gate_weight, preferred_element_type=jnp.float32)
    up_linear = jnp.dot(second_input, up_weight, preferred_element_type=jnp.float32)
    gate_act = jax.nn.silu(gate_linear)
    hidden = (gate_act * up_linear).astype(jnp.bfloat16)
    branch = jnp.dot(hidden, down_weight, preferred_element_type=jnp.float32)
    layer_out = (middle + gate_second * branch).astype(jnp.bfloat16)
    upstream = cotangent.astype(jnp.float32)
    grad_gate_second = upstream * branch
    grad_branch = (upstream * gate_second).astype(jnp.bfloat16)
    grad_hidden = inner_cols(grad_branch, down_weight)
    grad_gate_linear = (grad_hidden * up_linear * silu_slope(gate_linear)).astype(jnp.bfloat16)
    grad_up_linear = (grad_hidden * gate_act).astype(jnp.bfloat16)
    grad_second = inner_cols(grad_gate_linear, gate_weight) + inner_cols(grad_up_linear, up_weight)
    grad_scale_second = grad_second * norm_second
    grad_middle = upstream + norm_back(
        grad_second * (1.0 + scale_second), norm_second, inverse_second
    )
    grad_gate_first = grad_middle * attended
    grad_attended = (grad_middle * gate_first).astype(jnp.bfloat16)
    grad_context = inner_cols(grad_attended, out_weight).astype(jnp.bfloat16).reshape(split_shape)
    scores_again = masked_scores(queries, memory_keys, allowed, score_scale)
    attention = jnp.exp(scores_again - log_total)
    attention_again = attention.astype(jnp.bfloat16)
    grad_attention = jnp.einsum(
        "thd,shd->hts", grad_context, memory_values, preferred_element_type=jnp.float32
    )
    grad_values = jnp.einsum(
        "hts,thd->shd", attention_again, grad_context, preferred_element_type=jnp.float32
    )
    row_dot = jnp.sum(attention * grad_attention, axis=-1, keepdims=True)
    grad_scores = (attention * (grad_attention - row_dot)).astype(jnp.bfloat16)
    grad_queries = (
        jnp.einsum("hts,shd->thd", grad_scores, memory_keys, preferred_element_type=jnp.float32)
        * score_scale
    )
    grad_keys = (
        jnp.einsum("hts,thd->shd", grad_scores, queries, preferred_element_type=jnp.float32)
        * score_scale
    )
    query_unrot = rotate(grad_queries, cosine, -sine)
    key_unrot = rotate(grad_keys, cosine, -sine)
    grad_query_gain = jnp.sum(query_unrot * query_hat, axis=(0, 1))
    grad_key_gain = jnp.sum(key_unrot * key_hat, axis=(0, 1))
    grad_query_raw = norm_back(query_unrot * query_gain, query_hat, query_inverse)
    grad_key_raw = norm_back(key_unrot * key_gain, key_hat, key_inverse)
    grad_projected = jnp.concatenate(
        [
            grad_query_raw.reshape(tok_count, model_width),
            grad_key_raw.reshape(tok_count, model_width),
            grad_values.reshape(tok_count, model_width),
        ],
        axis=1,
    ).astype(jnp.bfloat16)
    grad_first = inner_cols(grad_projected, qkv_weight)
    grad_scale_first = grad_first * norm_first
    grad_tokens = grad_middle + norm_back(
        grad_first * (1.0 + scale_first), norm_first, inverse_first
    )
    grad_per_token = jnp.concatenate(
        [
            grad_first,
            grad_scale_first,
            grad_gate_first,
            grad_second,
            grad_scale_second,
            grad_gate_second,
        ],
        axis=1,
    )
    grad_mod_own = lax.dot_general(
        onehot.astype(jnp.float32),
        grad_per_token,
        (((0,), (0,)), ((), ())),
        precision=HIGHEST,
        preferred_element_type=jnp.float32,
    ).astype(jnp.bfloat16)
    halves = grad_mod_own.astype(jnp.float32).reshape(slot_count, 2, 3 * model_width)
    gains = jnp.stack([grad_query_gain, grad_key_gain])
    gains = jnp.pad(gains[:, None, :], ((0, 2), (0, 1), (0, 128 - head_dim)))
    gmod = jnp.pad(jnp.concatenate([halves, gains], axis=2).transpose(1, 0, 2), ((0, 0), (0, 4), (0, 0)))
    shares = reduce_products(
        first_input,
        context,
        second_input,
        hidden,
        grad_projected,
        grad_attended,
        grad_gate_linear,
        grad_up_linear,
        grad_branch,
        gmod,
        gathered_act(condition_act),
        condition,
        mod_weight,
    )
    grad_mod_weight = shares[5][:, : 3 * model_width]
    grad_mod_bias = shares[6][:, 0, : 3 * model_width].reshape(-1)
    gain_rows = (shares[6][0] + shares[6][1])[:, 3 * model_width : 3 * model_width + head_dim]
    grad_query_gain, grad_key_gain = gain_rows[1], gain_rows[2]
    grad_condition = shares[7]
    return (
        layer_out,
        grad_tokens,
        grad_condition,
        grad_mod_weight,
        grad_mod_bias,
        shares[4],
        grad_query_gain,
        grad_key_gain,
        shares[3],
        shares[1],
        shares[2],
        shares[0],
    )


def solution(mesh):
    placed = (
        P(("dp", "mod"), None),
        P(("dp", "mod"), None),
        P(("dp", "mod")),
        P(None, "mod"),
        P("mod"),
        P(),
        P(),
        P(),
        P(),
        P(),
        P(),
        P(),
        P(("dp", "mod"), None),
    )
    return jax.shard_map(
        body,
        mesh=mesh,
        in_specs=placed,
        out_specs=(
            P(("dp", "mod"), None),
            P(("dp", "mod"), None),
            P(("dp", "mod"), None),
            P("dp", "mod"),
            P(),
            P(("dp", "mod"), None),
            P(),
            P(),
            P(("dp", "mod"), None),
            P(("dp", "mod"), None),
            P(("dp", "mod"), None),
            P(("dp", "mod"), None),
        ),
        check_vma=False,
    )
```

```python
import jax
import jax.numpy as jnp
import numpy as np
from jax import lax
from jax.experimental import pallas as pl
from jax.experimental.pallas import tpu as pltpu
from jax.sharding import PartitionSpec as P

SIDE = 12


EPSILON = 1e-06
HIGHEST = lax.Precision.HIGHEST


def rms_norm(values):
    inverse = lax.rsqrt(jnp.mean(values * values, axis=-1, keepdims=True) + EPSILON)
    return (values * inverse, inverse)


def norm_back(upstream, normed, inverse):
    return inverse * (upstream - normed * jnp.mean(upstream * normed, axis=-1, keepdims=True))


def rotate(values, cosine, sine):
    half_dim = values.shape[-1] // 2
    leading = values[..., :half_dim]
    trailing = values[..., half_dim:]
    cosine = cosine[:, None, :]
    sine = sine[:, None, :]
    return jnp.concatenate(
        [leading * cosine - trailing * sine, trailing * cosine + leading * sine], axis=-1
    )


def rope_tables(segments, slot_count, side_big, head_dim):
    tok_count = segments.shape[0]
    onehot = (segments[:, None] == jnp.arange(slot_count, dtype=jnp.int32)[None, :]).astype(
        jnp.int32
    )
    counts = jnp.sum(onehot, axis=0)
    starts = jnp.cumsum(counts) - counts
    first_tok = jnp.sum(onehot * starts[None, :], axis=1)
    extent = jnp.sum(onehot * counts[None, :], axis=1)
    position = jnp.arange(tok_count, dtype=jnp.int32) - first_tok
    side_len = jnp.where(extent == tok_count, side_big, side_big // 2).astype(jnp.int32)
    row_pos = (position // side_len).astype(jnp.float32)
    col_pos = (position % side_len).astype(jnp.float32)
    quarter = head_dim // 4
    frequency = 10000.0 ** (-jnp.arange(quarter, dtype=jnp.float32) / quarter)
    angles = jnp.concatenate(
        [row_pos[:, None] * frequency[None, :], col_pos[:, None] * frequency[None, :]], axis=1
    )
    return (jnp.cos(angles), jnp.sin(angles))


def silu_slope(values):
    logistic = jax.nn.sigmoid(values)
    return logistic * (1.0 + values * (1.0 - logistic))


def inner_rows(left, right):
    return lax.dot_general(
        left, right, (((0,), (0,)), ((), ())), preferred_element_type=jnp.float32
    )


def inner_cols(left, right):
    return lax.dot_general(
        left, right, (((1,), (1,)), ((), ())), preferred_element_type=jnp.float32
    )


TOK = 144
PAIR = 2 * TOK
WIDE = 1152
HID = 3072
RING = 4
AXES = ((0, 1, 2), (1, 2, 0), (2, 0, 1))
JOBS = (
    ("down", 24, 384, 384, 256),
    ("gate", 9, 1024, 256, 512),
    ("up", 9, 1024, 256, 512),
    ("out", 9, 384, 384, 256),
    ("qkv", 9, 1152, 384, 640),
)
COPIES = 15
PARTNER_COPIES = 9


def sixteen(rows):
    return (rows + 15) // 16 * 16


def position():
    dp = lax.axis_index("dp")
    x_hi = lax.axis_index("mod")
    core = lax.rem(dp, 2)
    y = lax.rem(dp // 2, 4)
    z = lax.rem(dp // 8, 4)
    return (x_hi * 2 + dp // 32, y, z), core


def device_at(place, core):
    x, y, z = place
    return (((lax.rem(x, 2) * 4 + z) * 4 + y) * 2 + core, x // 2)


def moved(place, axis, value):
    return tuple(value if index == axis else kept for index, kept in enumerate(place))


def row_sources():
    tables = []
    for order in AXES:
        table = np.zeros((4, 4, 4, 9), np.int32)
        for first in range(4):
            for second in range(4):
                for third in range(4):
                    place = [0, 0, 0]
                    for axis, value in zip(order, (first, second, third)):
                        place[axis] = value
                    x, y, z = place
                    owner = (x % 2) * 64 + z * 16 + y * 4 + x // 2
                    table[first, second, third] = owner * 9 + np.arange(9)
        tables.append(table.reshape(576, 1))
    return np.stack(tables)


def reduce_kernel(
    src9_ref,
    src24_ref,
    hidden_in,
    second_in,
    context_in,
    first_in,
    gbranch_in,
    ggate_in,
    gup_in,
    gatt_in,
    gproj_in,
    gmod_in,
    act_in,
    condition_in,
    mod_weight_in,
    down_out,
    gate_out,
    up_out,
    out_out,
    qkv_out,
    mod_out,
    special_out,
    condition_out,
    hidden_s,
    second_s,
    context_s,
    first_s,
    gbranch_s,
    ggate_s,
    gup_s,
    gatt_s,
    gproj_s,
    perm9,
    xt9,
    perm24,
    t32,
    xt24,
    acc,
    fold32,
    fold_own,
    fold_other,
    other32,
    pair32,
    across32,
    rows32,
    gathered_a,
    gathered_b,
    product_own,
    product_send,
    product_other,
    final_other,
    special_other,
    part_own,
    part_other,
    weights,
    *rest,
):
    bufs = [rest[7 * index : 7 * index + 7] for index in range(len(JOBS))]
    send_sem, recv_sem, local_sem = rest[7 * len(JOBS) :]
    place, core = position()
    partner = device_at(place, 1 - core)
    near = []
    for axis in range(3):
        here = place[axis]
        near.append(
            (here, lax.rem(here + 1, 4), lax.rem(here + 3, 4), lax.rem(here + 2, 4))
        )

    barrier = pltpu.get_barrier_semaphore()
    pl.semaphore_signal(barrier, inc=1, device_id=partner, device_id_type=pl.DeviceIdType.MESH)
    for axis in range(3):
        for value in near[axis][1:]:
            pl.semaphore_signal(
                barrier,
                inc=1,
                device_id=device_at(moved(place, axis, value), core),
                device_id_type=pl.DeviceIdType.MESH,
            )
    twin = moved(place, 0, near[0][3])
    pl.semaphore_signal(
        barrier, inc=1, device_id=device_at(twin, 1 - core), device_id_type=pl.DeviceIdType.MESH
    )
    pl.semaphore_wait(barrier, 11)

    def remote(src, dst, index, target):
        return pltpu.make_async_remote_copy(
            src_ref=src,
            dst_ref=dst,
            send_sem=send_sem.at[index],
            recv_sem=recv_sem.at[index],
            device_id=target,
            device_id_type=pl.DeviceIdType.MESH,
        )

    sent = []
    pairs = {}
    ins = (gbranch_in, hidden_in, second_in, ggate_in, gup_in, context_in, gatt_in, first_in, gproj_in)
    stacks = (gbranch_s, hidden_s, second_s, ggate_s, gup_s, context_s, gatt_s, first_s, gproj_s)
    for index, (own, stack) in enumerate(zip(ins, stacks)):
        local = pltpu.make_async_copy(own, stack.at[pl.ds(0, TOK)], local_sem.at[index])
        local.start()
        across = remote(own, stack.at[pl.ds(TOK, TOK)], index, partner)
        across.start()
        sent.append(across)
        pairs[index] = (local, across)

    def arrived(*indices):
        for index in indices:
            local, across = pairs[index]
            local.wait()
            across.wait_recv()

    lane = lax.broadcasted_iota(jnp.int32, (192, 384), 1)
    perm24[...] = (lane == src24_ref[...] + core * 48).astype(jnp.float32).astype(jnp.bfloat16)

    def pick9(part, stack):
        @pl.loop(0, 9)
        def _(block):
            columns = lax.broadcasted_iota(jnp.int32, (576, 128), 1) + block * 128
            perm9[:, pl.ds(pl.multiple_of(block * 128, 128), 128)] = (
                (columns == src9_ref[part] + core * 18).astype(jnp.float32).astype(jnp.bfloat16)
            )

        xt9[...] = inner_cols(perm9[...], stack[...]).astype(jnp.bfloat16)

    def pick24(part):
        order = AXES[part]
        weight = [0, 0, 0]
        for axis, value in zip(order, (16, 4, 1)):
            weight[axis] = value

        @pl.loop(0, 8)
        def _(block):
            columns = pl.ds(pl.multiple_of(block * 384, 128), 384)
            rows = inner_cols(perm24[...], hidden_s[:, columns])
            base = (block // 4) * weight[0] + lax.rem(block, 4) * weight[2]
            for y in range(4):
                for x_hi in range(2):
                    unit = base + y * weight[1] + x_hi * 2 * weight[0]
                    at = (y * 2 + x_hi) * 24
                    t32[pl.ds(pl.multiple_of(unit * 24, 8), 24), :] = rows[at : at + 24]

        xt24[...] = t32[...].astype(jnp.bfloat16)

    def multiply(job, part, left, right):
        _, _, width, lanes, _ = JOBS[job]
        target = bufs[job][0]

        @pl.loop(0, width // lanes)
        def _(step):
            to = pl.multiple_of(step * lanes, 128)
            columns = pl.ds(pl.multiple_of(part * width + to, 128), lanes)
            target[part, :, pl.ds(to, lanes)] = jnp.dot(
                left[...], right[:, columns], preferred_element_type=jnp.float32
            ).astype(jnp.bfloat16)

    copies = {}

    def begin(job, part, slot, src, dst, target):
        index = PARTNER_COPIES + (job * 3 + part) * COPIES + slot
        copy = remote(src, dst, index, target)
        copy.start()
        sent.append(copy)
        copies[job, part, slot] = copy

    def arrive(job, part, *slots):
        for slot in slots:
            copies[job, part, slot].wait_recv()

    def ring(part, phase):
        axis = AXES[part][phase]
        here, right, left, opposite = near[axis]
        return (
            here,
            right,
            left,
            opposite,
            device_at(moved(place, axis, right), core),
            device_at(moved(place, axis, left), core),
            device_at(moved(place, axis, opposite), core),
        )

    def first_send(job, part):
        own, half, whole = bufs[job][:3]
        big = 16 * JOBS[job][1]
        cut = sixteen(big // 2)
        here, right, left, opposite, to_right, to_left, _ = ring(part, 0)

        def rows(chunk, start, count):
            return own.at[part, pl.ds(pl.multiple_of(chunk * big + start, 16), count)]

        begin(job, part, 0, rows(opposite, 0, cut), half.at[part, pl.ds(0, cut)], to_right)
        begin(job, part, 1, rows(opposite, cut, big - cut), half.at[part, pl.ds(cut, big - cut)], to_left)
        begin(job, part, 2, rows(right, cut, big - cut), whole.at[part, 0, pl.ds(cut, big - cut)], to_right)
        begin(job, part, 3, rows(left, 0, cut), whole.at[part, 1, pl.ds(0, cut)], to_left)

    def first_add(job, part):
        own, half, whole = bufs[job][:3]
        _, each, width, lanes, _ = JOBS[job]
        big = 16 * each
        cut = sixteen(big // 2)
        here, right, left, opposite, to_right, to_left, _ = ring(part, 0)
        for slot, chunk, start, count, target, side in (
            (0, right, 0, cut, to_right, 0),
            (1, left, cut, big - cut, to_left, 1),
        ):
            arrive(job, part, slot)
            rows = pl.ds(pl.multiple_of(chunk * big + start, 16), count)

            @pl.loop(0, width // 128)
            def _(step):
                columns = pl.ds(pl.multiple_of(step * 128, 128), 128)
                total = own[part, rows, columns].astype(jnp.float32) + half[
                    part, pl.ds(start, count), columns
                ].astype(jnp.float32)
                own[part, rows, columns] = total.astype(jnp.bfloat16)

            begin(
                job,
                part,
                4 + side,
                own.at[part, rows],
                whole.at[part, side, pl.ds(start, count)],
                target,
            )

    def second_send(job, part):
        own, _, whole, mid, mid_half, mid_whole, _ = bufs[job]
        _, each, width, lanes, cut = JOBS[job]
        big, small = 16 * each, 4 * each
        padded = sixteen(small)
        here, right, left, opposite, to_right, to_left, _ = ring(part, 0)
        arrive(job, part, 2, 3, 4, 5)
        rows = pl.ds(pl.multiple_of(here * big, 16), big)

        @pl.loop(0, width // 128)
        def _(step):
            columns = pl.ds(pl.multiple_of(step * 128, 128), 128)
            acc[pl.ds(0, big), :] = (
                own[part, rows, columns].astype(jnp.float32)
                + whole[part, 0, :, columns].astype(jnp.float32)
                + whole[part, 1, :, columns].astype(jnp.float32)
            )
            for chunk in range(4):
                mid[part, chunk, :, columns] = acc[pl.ds(chunk * small, padded), :].astype(jnp.bfloat16)

        here, right, left, opposite, to_right, to_left, _ = ring(part, 1)
        low, high = pl.ds(0, cut), pl.ds(cut, width - cut)
        begin(job, part, 6, mid.at[part, opposite, :, low], mid_half.at[part, :, low], to_right)
        begin(job, part, 7, mid.at[part, opposite, :, high], mid_half.at[part, :, high], to_left)
        begin(job, part, 8, mid.at[part, right, :, high], mid_whole.at[part, 0, :, high], to_right)
        begin(job, part, 9, mid.at[part, left, :, low], mid_whole.at[part, 1, :, low], to_left)

    def second_add(job, part):
        _, _, _, mid, mid_half, mid_whole, _ = bufs[job]
        _, each, width, lanes, cut = JOBS[job]
        here, right, left, opposite, to_right, to_left, _ = ring(part, 1)
        for slot, chunk, start, count, target, side in (
            (6, right, 0, cut, to_right, 0),
            (7, left, cut, width - cut, to_left, 1),
        ):
            arrive(job, part, slot)

            @pl.loop(0, count // 128)
            def _(step):
                columns = pl.ds(pl.multiple_of(start + step * 128, 128), 128)
                total = mid[part, chunk, :, columns].astype(jnp.float32) + mid_half[
                    part, :, columns
                ].astype(jnp.float32)
                mid[part, chunk, :, columns] = total.astype(jnp.bfloat16)

            columns = pl.ds(start, count)
            begin(
                job,
                part,
                10 + side,
                mid.at[part, chunk, :, columns],
                mid_whole.at[part, side, :, columns],
                target,
            )

    def third_send(job, part):
        _, _, _, mid, _, mid_whole, last = bufs[job]
        _, each, width, lanes, cut = JOBS[job]
        small = sixteen(4 * each)
        padded = sixteen(each)
        here = ring(part, 1)[0]
        arrive(job, part, 8, 9, 10, 11)

        @pl.loop(0, width // 128)
        def _(step):
            columns = pl.ds(pl.multiple_of(step * 128, 128), 128)
            acc[pl.ds(0, small), :] = (
                mid[part, here, :, columns].astype(jnp.float32)
                + mid_whole[part, 0, :, columns].astype(jnp.float32)
                + mid_whole[part, 1, :, columns].astype(jnp.float32)
            )
            for chunk in range(4):
                last[part, chunk, :, columns] = acc[pl.ds(chunk * each, padded), :].astype(jnp.bfloat16)

        here, right, left, opposite, to_right, to_left, to_opposite = ring(part, 2)
        for slot, chunk, target in ((0, right, to_right), (1, left, to_left), (2, opposite, to_opposite)):
            begin(job, part, 12 + slot, last.at[part, chunk], last.at[part, 4 + slot], target)

    mod = lax.axis_index("mod")
    mod_base = PARTNER_COPIES + 3 * COPIES * len(JOBS)
    mod_copies = {}

    def mod_send(slot, src, dst, target):
        copy = remote(src, dst, mod_base + slot, target)
        copy.start()
        sent.append(copy)
        mod_copies[slot] = copy

    def mod_arrive(*slots):
        for slot in slots:
            mod_copies[slot].wait_recv()

    def weight_chunk(index):
        return pltpu.make_async_copy(
            mod_weight_in.at[:, pl.ds(index * 384, 384)],
            weights.at[index % 2],
            local_sem.at[PARTNER_COPIES + index % 2],
        )

    def mod_pair():
        weight_chunk(0).start()
        weight_chunk(1).start()
        for quarter in range(4):
            fold32[4 * quarter : 4 * quarter + 4, :] = gmod_in[
                1 - mod, 0:4, quarter * 896 : (quarter + 1) * 896
            ]
        fold_own[...] = fold32[...].astype(jnp.bfloat16)
        mod_send(0, fold_own, fold_other, device_at(twin, core))

    def mod_cores():
        mod_arrive(0)
        fold32[...] = fold_other[...].astype(jnp.float32)
        for quarter in range(4):
            other32[0:4, quarter * 896 : (quarter + 1) * 896] = fold32[4 * quarter : 4 * quarter + 4, :]
        own, other = gmod_in[mod, 0:4, :], other32[0:4, :]
        pair32[0:4, :] = jnp.where(mod == 0, own, other)
        pair32[4:8, :] = jnp.where(mod == 0, other, own)
        there = pl.ds(pl.multiple_of((1 - core) * 1792, 128), 1792)
        mod_send(1, pair32.at[:, there], across32, partner)

    def condition_part():
        total = jnp.zeros((8, WIDE), jnp.float32)
        for index in range(9):
            weight_chunk(index).wait()
            total = total + inner_cols(
                pair32[:, index * 384 : (index + 1) * 384].astype(jnp.bfloat16),
                weights[index % 2],
            )
            if index + 2 < 9:
                weight_chunk(index + 2).start()
        part_own[...] = total
        mod_send(2, part_own, part_other, device_at(twin, core))

    def mod_gather_first():
        mod_arrive(1)
        here = pl.ds(pl.multiple_of(core * 1792, 128), 1792)
        own, other = pair32[:, here], across32[...]
        rows32[0:8, :] = jnp.where(core == 0, own, other)
        rows32[8:16, :] = jnp.where(core == 0, other, own)
        _, y, z = place
        gathered_a[z, y] = rows32[:, 0:896].astype(jnp.bfloat16)
        gathered_b[z, y] = rows32[:, 896:1792].astype(jnp.bfloat16)
        for step in range(3):
            to_y = device_at(moved(place, 1, near[1][1 + step]), core)
            to_z = device_at(moved(place, 2, near[2][1 + step]), core)
            mod_send(3 + step, gathered_a.at[z, y], gathered_a.at[z, y], to_y)
            mod_send(6 + step, gathered_b.at[z, y], gathered_b.at[z, y], to_z)

    def mod_gather_second():
        _, y, z = place
        mod_arrive(3, 4, 5)
        for step in range(3):
            to_z = device_at(moved(place, 2, near[2][1 + step]), core)
            mod_send(9 + step, gathered_a.at[z], gathered_a.at[z], to_z)
        mod_arrive(6, 7, 8)
        for step in range(3):
            to_y = device_at(moved(place, 1, near[1][1 + step]), core)
            mod_send(12 + step, gathered_b.at[:, y], gathered_b.at[:, y], to_y)

    def mod_product():
        mod_arrive(9, 10, 11)
        mod_arrive(12, 13, 14)
        for side, gathered in ((0, gathered_a), (1, gathered_b)):
            columns = slice(side * 896, (side + 1) * 896)
            rows = gathered[...].reshape(256, 896)
            product_send[:, columns] = jnp.dot(
                act_in[1], rows, preferred_element_type=jnp.float32
            ).astype(jnp.bfloat16)
            product_own[:, columns] = jnp.dot(act_in[0], rows, preferred_element_type=jnp.float32)
        x = place[0]
        beside = moved(place, 0, x + 1 - 2 * lax.rem(x, 2))
        mod_send(15, product_send, product_other, device_at(beside, core))

    def mod_sum():
        mod_arrive(15)
        product_own[...] = product_own[...] + product_other[...].astype(jnp.float32)
        mod_send(16, product_own, final_other, partner)
        special = product_own.at[pl.ds(40, 8)]
        mod_send(17, special, special_other.at[core], device_at(twin, core))
        mod_send(18, special, special_other.at[core], device_at(twin, 1 - core))

    def mod_finish():
        here = pl.ds(pl.multiple_of(core * 1792, 128), 1792)
        there = pl.ds(pl.multiple_of((1 - core) * 1792, 128), 1792)
        mod_arrive(2)
        total = part_own[...] + part_other[...]
        raw = condition_in[...].astype(jnp.float32)
        condition_out[...] = jnp.where(mod == 0, total[0:4], total[4:8]) * silu_slope(raw)
        mod_arrive(16)
        for source, columns in ((product_own, here), (final_other, there)):
            mod_out[:, columns] = jnp.where(core == 0, source[0:18, :], source[18:36, :])
            special_out[mod, :, columns] = source[40:48, :]
        mod_arrive(17, 18)
        for side in range(2):
            special_out[1 - mod, :, side * 1792 : (side + 1) * 1792] = special_other[side]

    outs = (down_out, gate_out, up_out, out_out, qkv_out)

    def finish(job, part):
        last = bufs[job][6]
        _, each, width, lanes, cut = JOBS[job]
        here = ring(part, 2)[0]
        arrive(job, part, 12, 13, 14)

        @pl.loop(0, width // 128)
        def _(step):
            to = pl.multiple_of(step * 128, 128)
            columns = pl.ds(to, 128)
            total = last[part, here, :, columns].astype(jnp.float32)
            for slot in range(3):
                total = total + last[part, 4 + slot, :, columns].astype(jnp.float32)
            outs[job][:, pl.ds(pl.multiple_of(part * width + to, 128), 128)] = total[:each]

    def products(job):
        name = JOBS[job][0]
        if name == "down":
            arrived(0, 1)
            for part in range(3):
                pick24(part)
                multiply(job, part, xt24, gbranch_s)
                first_send(job, part)
            return
        stack, right, indices = {
            "gate": (second_s, ggate_s, (2, 3)),
            "up": (second_s, gup_s, (4,)),
            "out": (context_s, gatt_s, (5, 6)),
            "qkv": (first_s, gproj_s, (7, 8)),
        }[name]
        arrived(*indices)
        for part in range(3):
            pick9(part, stack)
            multiply(job, part, xt9, right)
            first_send(job, part)

    extra = {
        0: (mod_pair,),
        1: (mod_cores, condition_part),
        2: (mod_gather_first,),
        3: (mod_gather_second,),
        5: (mod_product,),
        6: (mod_sum,),
        8: (mod_finish,),
    }
    stages = (products, first_add, second_send, second_add, third_send, finish)
    for step in range(len(JOBS) + len(stages) - 1):
        for piece in extra.get(step, ()):
            piece()
        for number, stage in enumerate(stages):
            job = step - number
            if 0 <= job < len(JOBS):
                if number == 0:
                    stage(job)
                else:
                    for part in range(3):
                        stage(job, part)
    for copy in sent:
        copy.wait_send()


def reduce_products(first, context, second, hidden, gproj, gatt, ggate, gup, gbranch, gmod, act, condition, mod_weight):
    src9 = jnp.asarray(row_sources())
    src24 = np.arange(192)
    src24 = jnp.asarray((src24 // 48 * 96 + src24 % 48).reshape(192, 1).astype(np.int32))
    vmem = pl.BlockSpec(memory_space=pltpu.VMEM)
    anywhere = pl.BlockSpec(memory_space=pl.ANY)
    scratch = [
        pltpu.VMEM((PAIR, HID), jnp.bfloat16),
        pltpu.VMEM((PAIR, WIDE), jnp.bfloat16),
        pltpu.VMEM((PAIR, WIDE), jnp.bfloat16),
        pltpu.VMEM((PAIR, WIDE), jnp.bfloat16),
        pltpu.VMEM((PAIR, WIDE), jnp.bfloat16),
        pltpu.VMEM((PAIR, HID), jnp.bfloat16),
        pltpu.VMEM((PAIR, HID), jnp.bfloat16),
        pltpu.VMEM((PAIR, WIDE), jnp.bfloat16),
        pltpu.VMEM((PAIR, 3 * WIDE), jnp.bfloat16),
        pltpu.VMEM((576, WIDE), jnp.bfloat16),
        pltpu.VMEM((576, PAIR), jnp.bfloat16),
        pltpu.VMEM((192, 384), jnp.bfloat16),
        pltpu.VMEM((1536, PAIR), jnp.float32),
        pltpu.VMEM((1536, PAIR), jnp.bfloat16),
        pltpu.VMEM((400, 128), jnp.float32),
        pltpu.VMEM((16, 896), jnp.float32),
        pltpu.VMEM((16, 896), jnp.bfloat16),
        pltpu.VMEM((16, 896), jnp.bfloat16),
        pltpu.VMEM((8, 3584), jnp.float32),
        pltpu.VMEM((8, 3584), jnp.float32),
        pltpu.VMEM((8, 1792), jnp.float32),
        pltpu.VMEM((16, 1792), jnp.float32),
        pltpu.VMEM((4, 4, 16, 896), jnp.bfloat16),
        pltpu.VMEM((4, 4, 16, 896), jnp.bfloat16),
        pltpu.VMEM((48, 1792), jnp.float32),
        pltpu.VMEM((48, 1792), jnp.bfloat16),
        pltpu.VMEM((48, 1792), jnp.bfloat16),
        pltpu.VMEM((48, 1792), jnp.float32),
        pltpu.VMEM((2, 8, 1792), jnp.float32),
        pltpu.VMEM((8, WIDE), jnp.float32),
        pltpu.VMEM((8, WIDE), jnp.float32),
        pltpu.VMEM((2, WIDE, 384), jnp.bfloat16),
    ]
    for _, each, width, _, _ in JOBS:
        big, small, tiny = 16 * each, sixteen(4 * each), sixteen(each)
        scratch += [
            pltpu.VMEM((3, 4 * big, width), jnp.bfloat16),
            pltpu.VMEM((3, big, width), jnp.bfloat16),
            pltpu.VMEM((3, 2, big, width), jnp.bfloat16),
            pltpu.VMEM((3, 4, small, width), jnp.bfloat16),
            pltpu.VMEM((3, small, width), jnp.bfloat16),
            pltpu.VMEM((3, 2, small, width), jnp.bfloat16),
            pltpu.VMEM((3, 7, tiny, width), jnp.bfloat16),
        ]
    count = PARTNER_COPIES + 3 * COPIES * len(JOBS) + 19
    scratch += [
        pltpu.SemaphoreType.DMA((count,)),
        pltpu.SemaphoreType.DMA((count,)),
        pltpu.SemaphoreType.DMA((PARTNER_COPIES + 2,)),
    ]
    return pl.pallas_call(
        reduce_kernel,
        out_shape=[
            jax.ShapeDtypeStruct((each, 3 * width), jnp.float32) for _, each, width, _, _ in JOBS
        ]
        + [
            jax.ShapeDtypeStruct((18, 3584), jnp.float32),
            jax.ShapeDtypeStruct((2, 8, 3584), jnp.float32),
            jax.ShapeDtypeStruct((4, WIDE), jnp.float32),
        ],
        in_specs=[vmem, vmem] + [anywhere] * 9 + [vmem] * 3 + [anywhere],
        out_specs=[vmem] * 8,
        scratch_shapes=scratch,
        compiler_params=pltpu.CompilerParams(
            collective_id=1, has_side_effects=True, vmem_limit_bytes=62 * 1024 * 1024
        ),
        cost_estimate=pl.CostEstimate(
            flops=5_000_000_000, bytes_accessed=10_000_000, transcendentals=0
        ),
    )(src9, src24, hidden, second, context, first, gbranch, ggate, gup, gatt, gproj, gmod, act, condition, mod_weight)

FWD_REMOTE = 12
MESH = pl.DeviceIdType.MESH


def rope_flat():
    token = np.arange(TOK)
    frequency = 10000.0 ** (-np.arange(18, dtype=np.float64) / 18)
    tables = []
    for position_in, side in ((token % 36, 6), (token, 12)):
        row, column = position_in // side, position_in % side
        angle = np.concatenate([row[:, None] * frequency, column[:, None] * frequency], axis=1)
        cosine = np.tile(np.concatenate([np.cos(angle), np.cos(angle)], axis=1), (1, 16))
        sine = np.tile(np.concatenate([-np.sin(angle), np.sin(angle)], axis=1), (1, 16))
        tables.append((cosine, sine))
    return (
        np.stack([pair[0] for pair in tables]).astype(np.float32),
        np.stack([pair[1] for pair in tables]).astype(np.float32),
    )


def row_blocks(step):
    @pl.loop(0, TOK // 16)
    def _(index):
        step(pl.ds(pl.multiple_of(index * 16, 16), 16))


def split_two(values):
    high = values.astype(jnp.bfloat16)
    return high, (values - high.astype(jnp.float32)).astype(jnp.bfloat16)


def head_sum(values, heads):
    high, low = split_two(values)
    return inner_cols(high, heads) + inner_cols(low, heads)


def head_spread(values, heads):
    high, low = split_two(values)
    return jnp.dot(high, heads, preferred_element_type=jnp.float32) + jnp.dot(
        low, heads, preferred_element_type=jnp.float32
    )


def head_rows():
    head = lax.broadcasted_iota(jnp.int32, (128, WIDE), 0) * 72
    lane = lax.broadcasted_iota(jnp.int32, (128, WIDE), 1)
    return ((lane >= head) & (lane < head + 72)).astype(jnp.float32).astype(jnp.bfloat16)


def swap_halves(values):
    lane = lax.broadcasted_iota(jnp.int32, values.shape, 1)
    first = lax.rem(lane, 72) < 36
    return jnp.where(first, pltpu.roll(values, WIDE - 36, 1), pltpu.roll(values, 36, 1))


def head_window(head):
    block = jnp.minimum(head * 72 // 128, 7)
    offset = head * 72 - block * 128
    lane = lax.broadcasted_iota(jnp.int32, (1, 256), 1)
    mask = ((lane >= offset) & (lane < offset + 72)).astype(jnp.float32).astype(jnp.bfloat16)
    return pl.ds(pl.multiple_of(block * 128, 128), 256), mask


def forward_kernel(
    segments,
    tokens,
    condition,
    mod_bias,
    gains,
    cos_in,
    sin_in,
    mod_weight,
    qkv_weight,
    out_weight,
    query_out,
    key_out,
    value_out,
    query_hat_out,
    key_hat_out,
    attention_out,
    context_out,
    attended_out,
    middle_out,
    first_out,
    second_out,
    cos_out,
    sin_out,
    gathered_out,
    inverse_out,
    modulation_out,
    mod_w,
    qkv_w,
    out_w,
    cos2,
    sin2,
    cond32,
    cond_other,
    act32,
    act_across,
    gathered,
    half32,
    fold32,
    fold_own,
    fold_other,
    mods32,
    per_token,
    norm,
    first,
    projected,
    query,
    key,
    value,
    query_hat,
    key_hat,
    attention,
    context32,
    context,
    attended,
    middle,
    second,
    cosine,
    sine,
    heads,
    send_sem,
    recv_sem,
    in_sem,
    out_sem,
):
    place, core = position()
    mod = lax.axis_index("mod")
    partner = device_at(place, 1 - core)
    twin = device_at(moved(place, 0, lax.rem(place[0] + 2, 4)), core)
    peers = [
        [device_at(moved(place, axis, lax.rem(place[axis] + step, 4)), core) for step in (1, 2, 3)]
        for axis in (1, 2)
    ]
    loads = {}

    def load(name, index, src, dst, slot):
        copy = pltpu.make_async_copy(src, dst, in_sem.at[slot])
        copy.start()
        loads[name, index] = copy

    for index in range(9):
        columns = pl.ds(index * 384, 384)
        load("mod", index, mod_weight.at[:, columns], mod_w.at[:, columns], index)
    load("cos", 0, cos_in, cos2, 21)
    load("sin", 0, sin_in, sin2, 22)
    for index in range(9):
        columns = pl.ds(index * 384, 384)
        load("qkv", index, qkv_weight.at[:, columns], qkv_w.at[:, columns], 9 + index)
    for index in range(3):
        columns = pl.ds(index * 384, 384)
        load("out", index, out_weight.at[:, columns], out_w.at[:, columns], 18 + index)

    sent = []
    copies = {}

    def send(slot, src, dst, target):
        copy = pltpu.make_async_remote_copy(
            src_ref=src,
            dst_ref=dst,
            send_sem=send_sem.at[slot],
            recv_sem=recv_sem.at[slot],
            device_id=target,
            device_id_type=MESH,
        )
        copy.start()
        sent.append(copy)
        copies[slot] = copy

    stores = []

    def store(src, dst):
        copy = pltpu.make_async_copy(src, dst, out_sem.at[len(stores)])
        copy.start()
        stores.append(copy)

    barrier = pltpu.get_barrier_semaphore()
    for target in [partner, twin] + peers[0] + peers[1]:
        pl.semaphore_signal(barrier, inc=1, device_id=target, device_id_type=MESH)
    cond32[...] = jnp.zeros_like(cond32)
    cond32[0:4, :] = condition[...].astype(jnp.float32)
    pl.semaphore_wait(barrier, 8)
    send(0, cond32, cond_other, twin)

    kind = segments[TOK - 1] == 0
    row = lax.broadcasted_iota(jnp.int32, (TOK, 16), 0)
    slot = lax.broadcasted_iota(jnp.int32, (TOK, 16), 1)
    onehot = (slot == jnp.where(kind, 0, row // 36)).astype(jnp.float32).astype(jnp.bfloat16)
    heads[...] = head_rows()

    def first_norm(rows):
        values = tokens[rows, :].astype(jnp.float32)
        norm[rows, :] = rms_norm(values)[0]

    row_blocks(first_norm)

    copies[0].wait_recv()
    own, other = cond32[0:4, :], cond_other[0:4, :]
    act32[0:4, :] = jnp.where(mod == 0, own, other)
    act32[4:8, :] = jnp.where(mod == 0, other, own)
    act32[...] = jax.nn.silu(act32[...]).astype(jnp.bfloat16).astype(jnp.float32)
    send(1, act32, act_across, partner)
    act = act32[...].astype(jnp.bfloat16)
    half32[...] = jnp.zeros_like(half32)
    for index in range(9):
        columns = slice(index * 384, (index + 1) * 384)
        loads["mod", index].wait()
        half32[:, columns] = (
            (
                jnp.dot(act, mod_w[:, columns], preferred_element_type=jnp.float32)
                + mod_bias[:, columns].astype(jnp.float32)
            )
            .astype(jnp.bfloat16)
            .astype(jnp.float32)
        )
    for quarter in range(4):
        columns = slice(quarter * 896, (quarter + 1) * 896)
        fold32[4 * quarter : 4 * quarter + 4, :] = jnp.where(
            mod == 0, half32[4:8, columns], half32[0:4, columns]
        )
    fold_own[...] = fold32[...].astype(jnp.bfloat16)
    send(2, fold_own, fold_other, twin)

    copies[1].wait_recv()
    _, y, z = place
    rows16 = jnp.concatenate(
        [
            jnp.where(core == 0, act32[...], act_across[...]),
            jnp.where(core == 0, act_across[...], act32[...]),
        ]
    )
    gathered[z, y] = rows16.astype(jnp.bfloat16)
    for step in range(3):
        send(3 + step, gathered.at[z, y], gathered.at[z, y], peers[0][step])
    loads["cos", 0].wait()
    loads["sin", 0].wait()

    def pick_table(rows):
        cosine[rows, :] = jnp.where(kind, cos2[1, rows, :], cos2[0, rows, :])
        sine[rows, :] = jnp.where(kind, sin2[1, rows, :], sin2[0, rows, :])

    row_blocks(pick_table)
    store(cosine, cos_out)
    store(sine, sin_out)
    for slot_ in (3, 4, 5):
        copies[slot_].wait_recv()
    for step in range(3):
        send(6 + step, gathered.at[z], gathered.at[z], peers[1][step])

    copies[2].wait_recv()
    mods32[...] = jnp.zeros_like(mods32)
    fold32[...] = fold_other[...].astype(jnp.float32)
    for quarter in range(4):
        width = 896 if quarter < 3 else 768
        mods32[0:4, pl.ds(pl.multiple_of((1 - mod) * 3456 + quarter * 896, 128), width)] = fold32[
            4 * quarter : 4 * quarter + 4, 0:width
        ]
    mods32[0:4, pl.ds(pl.multiple_of(mod * 3456, 128), 3456)] = jnp.where(
        mod == 0, half32[0:4, 0:3456], half32[4:8, 0:3456]
    )
    modulation_out[...] = mods32[...].astype(jnp.bfloat16)
    for index in range(18):
        columns = slice(index * 384, (index + 1) * 384)
        per_token[:, columns] = jnp.dot(
            onehot, modulation_out[:, columns], preferred_element_type=jnp.float32
        ).astype(jnp.bfloat16)

    def piece(rows, index):
        return per_token[rows, index * WIDE : (index + 1) * WIDE].astype(jnp.float32)

    def first_input(rows):
        first[rows, :] = (norm[rows, :] * (1.0 + piece(rows, 1)) + piece(rows, 0)).astype(jnp.bfloat16)

    row_blocks(first_input)
    store(first, first_out)

    for index in range(9):
        loads["qkv", index].wait()
        columns = slice(index * 384, (index + 1) * 384)
        result = jnp.dot(first[...], qkv_w[:, columns], preferred_element_type=jnp.float32)
        if index < 6:
            projected[:, columns] = result
        else:
            value[:, (index - 6) * 384 : (index - 5) * 384] = result.astype(jnp.bfloat16)
    store(value, value_out)

    def head_norm(which, hat, result):
        base = which * WIDE

        def steps(rows):
            raw = projected[rows, base : base + WIDE]
            total = head_sum(raw * raw, heads[...])
            inverse = lax.rsqrt(total * (1.0 / 72.0) + EPSILON)
            inverse_out[which, rows, :] = inverse
            normed = raw * head_spread(inverse, heads[...])
            hat[rows, :] = normed
            scaled = normed * gains[which : which + 1, :]
            turned = scaled * cosine[rows, :] + swap_halves(scaled) * sine[rows, :]
            result[rows, :] = turned.astype(jnp.bfloat16)

        @pl.loop(0, 3)
        def _(index):
            steps(pl.ds(pl.multiple_of(index * 48, 16), 48))

    head_norm(0, query_hat, query)
    store(query_hat, query_hat_out)
    store(query, query_out)
    head_norm(1, key_hat, key)
    store(key_hat, key_hat_out)
    store(key, key_out)

    left = lax.broadcasted_iota(jnp.int32, (TOK, TOK), 0) // 36
    right = lax.broadcasted_iota(jnp.int32, (TOK, TOK), 1) // 36
    shut = jnp.where(kind | (left == right), 0.0, -1e30)
    context32[...] = jnp.zeros_like(context32)

    @pl.loop(0, 4)
    def _(group):
        for member in range(4):
            head = group * 4 + member
            window, mask = head_window(head)
            scores = inner_cols(query[:, window] * mask, key[:, window]) * (72**-0.5) + shut
            top = jnp.max(scores, axis=-1, keepdims=True)
            weight = jnp.exp(scores - top)
            weight = weight * (1.0 / jnp.sum(weight, axis=-1, keepdims=True))
            attention[head] = weight
            context32[:, window] += jnp.dot(
                weight.astype(jnp.bfloat16), value[:, window] * mask, preferred_element_type=jnp.float32
            )

    store(attention, attention_out)
    context[...] = context32[...].astype(jnp.bfloat16)
    store(context, context_out)
    for index in range(3):
        loads["out", index].wait()
        columns = slice(index * 384, (index + 1) * 384)
        attended[:, columns] = jnp.dot(context[...], out_w[:, columns], preferred_element_type=jnp.float32)
    store(attended, attended_out)

    def second_input(rows):
        total = tokens[rows, :].astype(jnp.float32) + piece(rows, 2) * attended[rows, :]
        middle[rows, :] = total
        normed = rms_norm(total)[0]
        second[rows, :] = (normed * (1.0 + piece(rows, 4)) + piece(rows, 3)).astype(jnp.bfloat16)

    row_blocks(second_input)
    store(middle, middle_out)
    store(second, second_out)
    for slot_ in (6, 7, 8):
        copies[slot_].wait_recv()
    store(gathered, gathered_out)
    for copy in sent:
        copy.wait_send()
    for copy in stores:
        copy.wait()


def forward(tokens, condition, segments, mod_weight, mod_bias, qkv_weight, query_gain, key_gain, out_weight):
    cos_table, sin_table = rope_flat()
    gains = jnp.tile(jnp.stack([query_gain, key_gain]), (1, 16))
    vmem = pl.BlockSpec(memory_space=pltpu.VMEM)
    anywhere = pl.BlockSpec(memory_space=pl.ANY)
    low, full = jnp.bfloat16, jnp.float32
    wide_low = ((TOK, WIDE), low)
    wide_full = ((TOK, WIDE), full)
    outs = (
        [wide_low] * 3
        + [wide_full] * 2
        + [((16, TOK, TOK), full), wide_low, wide_full, wide_full, wide_low, wide_low]
        + [wide_full] * 2
        + [((4, 4, 16, WIDE), low)]
        + [((2, TOK, 128), full), ((16, 6 * WIDE), low)]
    )
    scratch = [
        ((WIDE, 3456), low),
        ((WIDE, 3456), low),
        ((WIDE, WIDE), low),
        ((2, TOK, WIDE), full),
        ((2, TOK, WIDE), full),
        ((8, WIDE), full),
        ((8, WIDE), full),
        ((8, WIDE), full),
        ((8, WIDE), full),
        ((4, 4, 16, WIDE), low),
        ((8, 3584), full),
        ((16, 896), full),
        ((16, 896), low),
        ((16, 896), low),
        ((16, 6912), full),
        ((TOK, 6912), low),
        wide_full,
        wide_low,
        ((TOK, 2304), full),
        wide_low,
        wide_low,
        wide_low,
        wide_full,
        wide_full,
        ((16, TOK, TOK), full),
        wide_full,
        wide_low,
        wide_full,
        wide_full,
        wide_low,
        wide_full,
        wide_full,
        ((128, WIDE), low),
    ]
    return pl.pallas_call(
        forward_kernel,
        out_shape=[jax.ShapeDtypeStruct(*out) for out in outs],
        in_specs=[pl.BlockSpec(memory_space=pltpu.SMEM)] + [vmem] * 4 + [anywhere] * 5,
        out_specs=[anywhere] * 14 + [vmem] * 2,
        scratch_shapes=[pltpu.VMEM(*item) for item in scratch]
        + [
            pltpu.SemaphoreType.DMA((FWD_REMOTE,)),
            pltpu.SemaphoreType.DMA((FWD_REMOTE,)),
            pltpu.SemaphoreType.DMA((23,)),
            pltpu.SemaphoreType.DMA((16,)),
        ],
        compiler_params=pltpu.CompilerParams(
            collective_id=2, has_side_effects=True, vmem_limit_bytes=56 * 1024 * 1024
        ),
        cost_estimate=pl.CostEstimate(flops=2_000_000_000, bytes_accessed=30_000_000, transcendentals=0),
    )(
        segments,
        tokens,
        condition,
        mod_bias.reshape(1, -1),
        gains,
        jnp.asarray(cos_table),
        jnp.asarray(sin_table),
        mod_weight,
        qkv_weight,
        out_weight,
    )

def gathered_act(act_gathered):
    dp = lax.axis_index("dp")
    own = act_gathered.reshape(256, -1)
    slot = np.arange(256)
    ones = np.stack([slot >= 0, slot % 4 == 0, slot % 4 == 1]).astype(jnp.bfloat16)
    tables = []
    for shift in (0, 32):
        start = (dp // 2 * 2 + shift) % 64 * 18
        part = lax.dynamic_slice_in_dim(own, start, 36, axis=1).T
        tables.append(jnp.concatenate([jnp.pad(part, ((0, 4), (0, 0))), jnp.pad(ones, ((0, 5), (0, 0)))]))
    return jnp.stack(tables)


def body(
    tokens,
    condition,
    segments,
    mod_weight,
    mod_bias,
    qkv_weight,
    query_gain,
    key_gain,
    out_weight,
    gate_weight,
    up_weight,
    down_weight,
    cotangent,
):
    tok_count, model_width = tokens.shape
    slot_count = condition.shape[0]
    head_dim = query_gain.shape[0]
    head_count = model_width // head_dim
    split_shape = (tok_count, head_count, head_dim)
    score_scale = head_dim ** (-0.5)
    inputs_float = tokens.astype(jnp.float32)
    (
        queries,
        memory_keys,
        memory_values,
        query_hat,
        key_hat,
        attention,
        context,
        attended,
        middle,
        first_input,
        second_input,
        cosine,
        sine,
        act_gathered,
        inverses,
        modulation,
    ) = forward(
        tokens, condition, segments, mod_weight, mod_bias, qkv_weight, query_gain, key_gain, out_weight
    )
    modulation = modulation[:slot_count]
    onehot = segments[:, None] == jnp.arange(slot_count, dtype=jnp.int32)[None, :]
    per_token = jnp.dot(onehot.astype(jnp.bfloat16), modulation, preferred_element_type=jnp.float32)
    pieces = [
        per_token[:, column * model_width : (column + 1) * model_width] for column in range(6)
    ]
    shift_first, scale_first, gate_first, shift_second, scale_second, gate_second = pieces
    norm_first, inverse_first = rms_norm(inputs_float)
    cosine, sine = rope_tables(segments, slot_count, SIDE, head_dim)
    queries, memory_keys, memory_values, query_hat, key_hat = (
        part.reshape(split_shape) for part in (queries, memory_keys, memory_values, query_hat, key_hat)
    )
    query_inverse, key_inverse = inverses[0, :, :head_count, None], inverses[1, :, :head_count, None]
    norm_second, inverse_second = rms_norm(middle)
    gate_linear = jnp.dot(second_input, gate_weight, preferred_element_type=jnp.float32)
    up_linear = jnp.dot(second_input, up_weight, preferred_element_type=jnp.float32)
    gate_act = jax.nn.silu(gate_linear)
    hidden = (gate_act * up_linear).astype(jnp.bfloat16)
    branch = jnp.dot(hidden, down_weight, preferred_element_type=jnp.float32)
    layer_out = (middle + gate_second * branch).astype(jnp.bfloat16)
    upstream = cotangent.astype(jnp.float32)
    grad_gate_second = upstream * branch
    grad_branch = (upstream * gate_second).astype(jnp.bfloat16)
    grad_hidden = inner_cols(grad_branch, down_weight)
    grad_gate_linear = (grad_hidden * up_linear * silu_slope(gate_linear)).astype(jnp.bfloat16)
    grad_up_linear = (grad_hidden * gate_act).astype(jnp.bfloat16)
    grad_second = inner_cols(grad_gate_linear, gate_weight) + inner_cols(grad_up_linear, up_weight)
    grad_scale_second = grad_second * norm_second
    grad_middle = upstream + norm_back(
        grad_second * (1.0 + scale_second), norm_second, inverse_second
    )
    grad_gate_first = grad_middle * attended
    grad_attended = (grad_middle * gate_first).astype(jnp.bfloat16)
    grad_context = inner_cols(grad_attended, out_weight).astype(jnp.bfloat16).reshape(split_shape)
    attention_again = attention.astype(jnp.bfloat16)
    grad_attention = jnp.einsum(
        "thd,shd->hts", grad_context, memory_values, preferred_element_type=jnp.float32
    )
    grad_values = jnp.einsum(
        "hts,thd->shd", attention_again, grad_context, preferred_element_type=jnp.float32
    )
    row_dot = jnp.sum(attention * grad_attention, axis=-1, keepdims=True)
    grad_scores = (attention * (grad_attention - row_dot)).astype(jnp.bfloat16)
    grad_queries = (
        jnp.einsum("hts,shd->thd", grad_scores, memory_keys, preferred_element_type=jnp.float32)
        * score_scale
    )
    grad_keys = (
        jnp.einsum("hts,thd->shd", grad_scores, queries, preferred_element_type=jnp.float32)
        * score_scale
    )
    query_unrot = rotate(grad_queries, cosine, -sine)
    key_unrot = rotate(grad_keys, cosine, -sine)
    grad_query_gain = jnp.sum(query_unrot * query_hat, axis=(0, 1))
    grad_key_gain = jnp.sum(key_unrot * key_hat, axis=(0, 1))
    grad_query_raw = norm_back(query_unrot * query_gain, query_hat, query_inverse)
    grad_key_raw = norm_back(key_unrot * key_gain, key_hat, key_inverse)
    grad_projected = jnp.concatenate(
        [
            grad_query_raw.reshape(tok_count, model_width),
            grad_key_raw.reshape(tok_count, model_width),
            grad_values.reshape(tok_count, model_width),
        ],
        axis=1,
    ).astype(jnp.bfloat16)
    grad_first = inner_cols(grad_projected, qkv_weight)
    grad_scale_first = grad_first * norm_first
    grad_tokens = grad_middle + norm_back(
        grad_first * (1.0 + scale_first), norm_first, inverse_first
    )
    grad_per_token = jnp.concatenate(
        [
            grad_first,
            grad_scale_first,
            grad_gate_first,
            grad_second,
            grad_scale_second,
            grad_gate_second,
        ],
        axis=1,
    )
    grad_mod_own = lax.dot_general(
        onehot.astype(jnp.float32),
        grad_per_token,
        (((0,), (0,)), ((), ())),
        precision=HIGHEST,
        preferred_element_type=jnp.float32,
    ).astype(jnp.bfloat16)
    halves = grad_mod_own.astype(jnp.float32).reshape(slot_count, 2, 3 * model_width)
    gains = jnp.stack([grad_query_gain, grad_key_gain])
    gains = jnp.pad(gains[:, None, :], ((0, 2), (0, 1), (0, 128 - head_dim)))
    gmod = jnp.pad(jnp.concatenate([halves, gains], axis=2).transpose(1, 0, 2), ((0, 0), (0, 4), (0, 0)))
    shares = reduce_products(
        first_input,
        context,
        second_input,
        hidden,
        grad_projected,
        grad_attended,
        grad_gate_linear,
        grad_up_linear,
        grad_branch,
        gmod,
        gathered_act(act_gathered),
        condition,
        mod_weight,
    )
    grad_mod_weight = shares[5][:, : 3 * model_width]
    grad_mod_bias = shares[6][:, 0, : 3 * model_width].reshape(-1)
    gain_rows = (shares[6][0] + shares[6][1])[:, 3 * model_width : 3 * model_width + head_dim]
    grad_query_gain, grad_key_gain = gain_rows[1], gain_rows[2]
    grad_condition = shares[7]
    return (
        layer_out,
        grad_tokens,
        grad_condition,
        grad_mod_weight,
        grad_mod_bias,
        shares[4],
        grad_query_gain,
        grad_key_gain,
        shares[3],
        shares[1],
        shares[2],
        shares[0],
    )


def solution(mesh):
    placed = (
        P(("dp", "mod"), None),
        P(("dp", "mod"), None),
        P(("dp", "mod")),
        P(None, "mod"),
        P("mod"),
        P(),
        P(),
        P(),
        P(),
        P(),
        P(),
        P(),
        P(("dp", "mod"), None),
    )
    return jax.shard_map(
        body,
        mesh=mesh,
        in_specs=placed,
        out_specs=(
            P(("dp", "mod"), None),
            P(("dp", "mod"), None),
            P(("dp", "mod"), None),
            P("dp", "mod"),
            P(),
            P(("dp", "mod"), None),
            P(),
            P(),
            P(("dp", "mod"), None),
            P(("dp", "mod"), None),
            P(("dp", "mod"), None),
            P(("dp", "mod"), None),
        ),
        check_vma=False,
    )
```

```python
import jax
import jax.numpy as jnp
import numpy as np
from jax import lax
from jax.experimental import pallas as pl
from jax.experimental.pallas import tpu as pltpu
from jax.sharding import PartitionSpec as P

EPSILON = 1e-06


def rms_norm(values):
    inverse = lax.rsqrt(jnp.mean(values * values, axis=-1, keepdims=True) + EPSILON)
    return (values * inverse, inverse)


def norm_back(upstream, normed, inverse):
    return inverse * (upstream - normed * jnp.mean(upstream * normed, axis=-1, keepdims=True))


def silu_slope(values):
    logistic = jax.nn.sigmoid(values)
    return logistic * (1.0 + values * (1.0 - logistic))


def inner_rows(left, right):
    return lax.dot_general(
        left, right, (((0,), (0,)), ((), ())), preferred_element_type=jnp.float32
    )


def inner_cols(left, right):
    return lax.dot_general(
        left, right, (((1,), (1,)), ((), ())), preferred_element_type=jnp.float32
    )


TOK = 144
PAIR = 2 * TOK
WIDE = 1152
HID = 3072
RING = 4
AXES = ((0, 1, 2), (1, 2, 0), (2, 0, 1))
JOBS = (
    ("gate", 9, 1024, 256, 512),
    ("up", 9, 1024, 256, 512),
    ("down", 24, 384, 384, 256),
    ("out", 9, 384, 384, 256),
    ("qkv", 9, 1152, 384, 640),
)
COPIES = 15
PARTNER_COPIES = 17
MOD_COPIES = 19
CHUNK = 256


def sixteen(rows):
    return (rows + 15) // 16 * 16


def position():
    dp = lax.axis_index("dp")
    x_hi = lax.axis_index("mod")
    core = lax.rem(dp, 2)
    y = lax.rem(dp // 2, 4)
    z = lax.rem(dp // 8, 4)
    return (x_hi * 2 + dp // 32, y, z), core


def device_at(place, core):
    x, y, z = place
    return (((lax.rem(x, 2) * 4 + z) * 4 + y) * 2 + core, x // 2)


def moved(place, axis, value):
    return tuple(value if index == axis else kept for index, kept in enumerate(place))


def row_sources(part):
    row = lax.broadcasted_iota(jnp.int32, (576, 1), 0)
    unit = row // 9
    place = [None] * 3
    for axis, value in zip(AXES[part], (unit // 16, lax.rem(unit // 4, 4), lax.rem(unit, 4))):
        place[axis] = value
    x, y, z = place
    return (lax.rem(x, 2) * 64 + z * 16 + y * 4 + x // 2 - unit) * 9 + row


FWD_REMOTE = 12
MESH = pl.DeviceIdType.MESH


def rope_flat():
    token = np.arange(TOK)
    frequency = 10000.0 ** (-np.arange(18, dtype=np.float64) / 18)
    tables = []
    for position_in, side in ((token % 36, 6), (token, 12)):
        row, column = position_in // side, position_in % side
        angle = np.concatenate([row[:, None] * frequency, column[:, None] * frequency], axis=1)
        cosine = np.tile(np.concatenate([np.cos(angle), np.cos(angle)], axis=1), (1, 16))
        sine = np.tile(np.concatenate([-np.sin(angle), np.sin(angle)], axis=1), (1, 16))
        tables.append((cosine, sine))
    return (
        np.stack([pair[0] for pair in tables]).astype(np.float32),
        np.stack([pair[1] for pair in tables]).astype(np.float32),
    )


def row_blocks(step):
    @pl.loop(0, TOK // 16)
    def _(index):
        step(pl.ds(pl.multiple_of(index * 16, 16), 16))


def split_two(values):
    high = values.astype(jnp.bfloat16)
    return high, (values - high.astype(jnp.float32)).astype(jnp.bfloat16)


def head_sum(values, heads):
    high, low = split_two(values)
    return inner_cols(high, heads) + inner_cols(low, heads)


def head_spread(values, heads):
    high, low = split_two(values)
    return jnp.dot(high, heads, preferred_element_type=jnp.float32) + jnp.dot(
        low, heads, preferred_element_type=jnp.float32
    )


def head_rows():
    head = lax.broadcasted_iota(jnp.int32, (128, WIDE), 0) * 72
    lane = lax.broadcasted_iota(jnp.int32, (128, WIDE), 1)
    return ((lane >= head) & (lane < head + 72)).astype(jnp.float32).astype(jnp.bfloat16)


def swap_halves(values):
    lane = lax.broadcasted_iota(jnp.int32, values.shape, 1)
    first = lax.rem(lane, 72) < 36
    return jnp.where(first, pltpu.roll(values, WIDE - 36, 1), pltpu.roll(values, 36, 1))


def head_window(head):
    block = jnp.minimum(head * 72 // 128, 7)
    offset = head * 72 - block * 128
    lane = lax.broadcasted_iota(jnp.int32, (1, 256), 1)
    mask = ((lane >= offset) & (lane < offset + 72)).astype(jnp.float32).astype(jnp.bfloat16)
    return pl.ds(pl.multiple_of(block * 128, 128), 256), mask


def forward_kernel(
    segments,
    tokens,
    condition,
    mod_bias,
    gains,
    cos_in,
    sin_in,
    mod_weight,
    qkv_weight,
    out_weight,
    query_out,
    key_out,
    value_out,
    query_hat_out,
    key_hat_out,
    context_out,
    attended_out,
    middle_out,
    first_out,
    second_out,
    cos_out,
    sin_out,
    gathered_out,
    inverse_out,
    modulation_out,
    mod_w,
    qkv_w,
    out_w,
    cos2,
    sin2,
    cond32,
    cond_other,
    act32,
    act_across,
    gathered,
    half32,
    fold32,
    fold_own,
    fold_other,
    mods32,
    per_token,
    norm,
    first,
    projected,
    query,
    key,
    value,
    query_hat,
    key_hat,
    context32,
    context,
    attended,
    middle,
    second,
    cosine,
    sine,
    heads,
    send_sem,
    recv_sem,
    in_sem,
    out_sem,
):
    place, core = position()
    mod = lax.axis_index("mod")
    partner = device_at(place, 1 - core)
    twin = device_at(moved(place, 0, lax.rem(place[0] + 2, 4)), core)
    peers = [
        [device_at(moved(place, axis, lax.rem(place[axis] + step, 4)), core) for step in (1, 2, 3)]
        for axis in (1, 2)
    ]
    loads = {}

    def load(name, index, src, dst, slot):
        copy = pltpu.make_async_copy(src, dst, in_sem.at[slot])
        copy.start()
        loads[name, index] = copy

    for index in range(9):
        columns = pl.ds(index * 384, 384)
        load("mod", index, mod_weight.at[:, columns], mod_w.at[:, columns], index)
    load("cos", 0, cos_in, cos2, 21)
    load("sin", 0, sin_in, sin2, 22)
    for index in range(9):
        columns = pl.ds(index * 384, 384)
        load("qkv", index, qkv_weight.at[:, columns], qkv_w.at[:, columns], 9 + index)
    for index in range(3):
        columns = pl.ds(index * 384, 384)
        load("out", index, out_weight.at[:, columns], out_w.at[:, columns], 18 + index)

    sent = []
    copies = {}

    def send(slot, src, dst, target):
        copy = pltpu.make_async_remote_copy(
            src_ref=src,
            dst_ref=dst,
            send_sem=send_sem.at[slot],
            recv_sem=recv_sem.at[slot],
            device_id=target,
            device_id_type=MESH,
        )
        copy.start()
        sent.append(copy)
        copies[slot] = copy

    stores = []

    def store(src, dst):
        copy = pltpu.make_async_copy(src, dst, out_sem.at[len(stores)])
        copy.start()
        stores.append(copy)

    barrier = pltpu.get_barrier_semaphore()
    for target in [partner, twin] + peers[0] + peers[1]:
        pl.semaphore_signal(barrier, inc=1, device_id=target, device_id_type=MESH)
    cond32[...] = jnp.zeros_like(cond32)
    cond32[0:4, :] = condition[...].astype(jnp.float32)
    pl.semaphore_wait(barrier, 8)
    send(0, cond32, cond_other, twin)

    kind = segments[TOK - 1] == 0
    row = lax.broadcasted_iota(jnp.int32, (TOK, 16), 0)
    slot = lax.broadcasted_iota(jnp.int32, (TOK, 16), 1)
    onehot = (slot == jnp.where(kind, 0, row // 36)).astype(jnp.float32).astype(jnp.bfloat16)
    heads[...] = head_rows()

    def first_norm(rows):
        values = tokens[rows, :].astype(jnp.float32)
        norm[rows, :] = rms_norm(values)[0]

    row_blocks(first_norm)

    copies[0].wait_recv()
    own, other = cond32[0:4, :], cond_other[0:4, :]
    act32[0:4, :] = jnp.where(mod == 0, own, other)
    act32[4:8, :] = jnp.where(mod == 0, other, own)
    act32[...] = jax.nn.silu(act32[...]).astype(jnp.bfloat16).astype(jnp.float32)
    send(1, act32, act_across, partner)
    act = act32[...].astype(jnp.bfloat16)
    half32[...] = jnp.zeros_like(half32)
    for index in range(9):
        columns = slice(index * 384, (index + 1) * 384)
        loads["mod", index].wait()
        half32[:, columns] = (
            (
                jnp.dot(act, mod_w[:, columns], preferred_element_type=jnp.float32)
                + mod_bias[:, columns].astype(jnp.float32)
            )
            .astype(jnp.bfloat16)
            .astype(jnp.float32)
        )
    for quarter in range(4):
        columns = slice(quarter * 896, (quarter + 1) * 896)
        fold32[4 * quarter : 4 * quarter + 4, :] = jnp.where(
            mod == 0, half32[4:8, columns], half32[0:4, columns]
        )
    fold_own[...] = fold32[...].astype(jnp.bfloat16)
    send(2, fold_own, fold_other, twin)

    copies[1].wait_recv()
    _, y, z = place
    rows16 = jnp.concatenate(
        [
            jnp.where(core == 0, act32[...], act_across[...]),
            jnp.where(core == 0, act_across[...], act32[...]),
        ]
    )
    gathered[z, y] = rows16.astype(jnp.bfloat16)
    for step in range(3):
        send(3 + step, gathered.at[z, y], gathered.at[z, y], peers[0][step])
    loads["cos", 0].wait()
    loads["sin", 0].wait()

    def pick_table(rows):
        cosine[rows, :] = jnp.where(kind, cos2[1, rows, :], cos2[0, rows, :])
        sine[rows, :] = jnp.where(kind, sin2[1, rows, :], sin2[0, rows, :])

    row_blocks(pick_table)
    store(cosine, cos_out)
    store(sine, sin_out)
    for slot_ in (3, 4, 5):
        copies[slot_].wait_recv()
    for step in range(3):
        send(6 + step, gathered.at[z], gathered.at[z], peers[1][step])

    copies[2].wait_recv()
    mods32[...] = jnp.zeros_like(mods32)
    fold32[...] = fold_other[...].astype(jnp.float32)
    for quarter in range(4):
        width = 896 if quarter < 3 else 768
        mods32[0:4, pl.ds(pl.multiple_of((1 - mod) * 3456 + quarter * 896, 128), width)] = fold32[
            4 * quarter : 4 * quarter + 4, 0:width
        ]
    mods32[0:4, pl.ds(pl.multiple_of(mod * 3456, 128), 3456)] = jnp.where(
        mod == 0, half32[0:4, 0:3456], half32[4:8, 0:3456]
    )
    modulation_out[...] = mods32[...].astype(jnp.bfloat16)
    for index in range(18):
        columns = slice(index * 384, (index + 1) * 384)
        per_token[:, columns] = jnp.dot(
            onehot, modulation_out[:, columns], preferred_element_type=jnp.float32
        ).astype(jnp.bfloat16)

    def piece(rows, index):
        return per_token[rows, index * WIDE : (index + 1) * WIDE].astype(jnp.float32)

    def first_input(rows):
        first[rows, :] = (norm[rows, :] * (1.0 + piece(rows, 1)) + piece(rows, 0)).astype(jnp.bfloat16)

    row_blocks(first_input)
    store(first, first_out)

    for index in range(9):
        loads["qkv", index].wait()
        columns = slice(index * 384, (index + 1) * 384)
        result = jnp.dot(first[...], qkv_w[:, columns], preferred_element_type=jnp.float32)
        if index < 6:
            projected[:, columns] = result
        else:
            value[:, (index - 6) * 384 : (index - 5) * 384] = result.astype(jnp.bfloat16)
    store(value, value_out)

    def head_norm(which, hat, result):
        base = which * WIDE

        def steps(rows):
            raw = projected[rows, base : base + WIDE]
            total = head_sum(raw * raw, heads[...])
            inverse = lax.rsqrt(total * (1.0 / 72.0) + EPSILON)
            inverse_out[which, rows, :] = inverse
            normed = raw * head_spread(inverse, heads[...])
            hat[rows, :] = normed
            scaled = normed * gains[which : which + 1, :]
            turned = scaled * cosine[rows, :] + swap_halves(scaled) * sine[rows, :]
            result[rows, :] = turned.astype(jnp.bfloat16)

        @pl.loop(0, 3)
        def _(index):
            steps(pl.ds(pl.multiple_of(index * 48, 16), 48))

    head_norm(0, query_hat, query)
    store(query_hat, query_hat_out)
    store(query, query_out)
    head_norm(1, key_hat, key)
    store(key_hat, key_hat_out)
    store(key, key_out)

    left = lax.broadcasted_iota(jnp.int32, (TOK, TOK), 0) // 36
    right = lax.broadcasted_iota(jnp.int32, (TOK, TOK), 1) // 36
    shut = jnp.where(kind | (left == right), 0.0, -1e30)
    context32[...] = jnp.zeros_like(context32)

    @pl.loop(0, 4)
    def _(group):
        for member in range(4):
            head = group * 4 + member
            window, mask = head_window(head)
            scores = inner_cols(query[:, window] * mask, key[:, window]) * (72**-0.5) + shut
            top = jnp.max(scores, axis=-1, keepdims=True)
            weight = jnp.exp(scores - top)
            weight = weight * (1.0 / jnp.sum(weight, axis=-1, keepdims=True))
            context32[:, window] += jnp.dot(
                weight.astype(jnp.bfloat16), value[:, window] * mask, preferred_element_type=jnp.float32
            )

    context[...] = context32[...].astype(jnp.bfloat16)
    store(context, context_out)
    for index in range(3):
        loads["out", index].wait()
        columns = slice(index * 384, (index + 1) * 384)
        attended[:, columns] = jnp.dot(context[...], out_w[:, columns], preferred_element_type=jnp.float32)
    store(attended, attended_out)

    def second_input(rows):
        total = tokens[rows, :].astype(jnp.float32) + piece(rows, 2) * attended[rows, :]
        middle[rows, :] = total
        normed = rms_norm(total)[0]
        second[rows, :] = (normed * (1.0 + piece(rows, 4)) + piece(rows, 3)).astype(jnp.bfloat16)

    row_blocks(second_input)
    store(middle, middle_out)
    store(second, second_out)
    for slot_ in (6, 7, 8):
        copies[slot_].wait_recv()
    store(gathered, gathered_out)
    for copy in sent:
        copy.wait_send()
    for copy in stores:
        copy.wait()


def forward(tokens, condition, segments, mod_weight, mod_bias, qkv_weight, gains, out_weight):
    cos_table, sin_table = rope_flat()
    vmem = pl.BlockSpec(memory_space=pltpu.VMEM)
    anywhere = pl.BlockSpec(memory_space=pl.ANY)
    low, full = jnp.bfloat16, jnp.float32
    wide_low = ((TOK, WIDE), low)
    wide_full = ((TOK, WIDE), full)
    outs = (
        [wide_low] * 3
        + [wide_full] * 2
        + [wide_low, wide_full, wide_full, wide_low, wide_low]
        + [wide_full] * 2
        + [((4, 4, 16, WIDE), low)]
        + [((2, TOK, 128), full), ((16, 6 * WIDE), low)]
    )
    scratch = [
        ((WIDE, 3456), low),
        ((WIDE, 3456), low),
        ((WIDE, WIDE), low),
        ((2, TOK, WIDE), full),
        ((2, TOK, WIDE), full),
        ((8, WIDE), full),
        ((8, WIDE), full),
        ((8, WIDE), full),
        ((8, WIDE), full),
        ((4, 4, 16, WIDE), low),
        ((8, 3584), full),
        ((16, 896), full),
        ((16, 896), low),
        ((16, 896), low),
        ((16, 6912), full),
        ((TOK, 6912), low),
        wide_full,
        wide_low,
        ((TOK, 2304), full),
        wide_low,
        wide_low,
        wide_low,
        wide_full,
        wide_full,
        wide_full,
        wide_low,
        wide_full,
        wide_full,
        wide_low,
        wide_full,
        wide_full,
        ((128, WIDE), low),
    ]
    return pl.pallas_call(
        forward_kernel,
        out_shape=[jax.ShapeDtypeStruct(*out) for out in outs],
        in_specs=[pl.BlockSpec(memory_space=pltpu.SMEM)] + [vmem] * 4 + [anywhere] * 5,
        out_specs=[anywhere] * 13 + [vmem] * 2,
        scratch_shapes=[pltpu.VMEM(*item) for item in scratch]
        + [
            pltpu.SemaphoreType.DMA((FWD_REMOTE,)),
            pltpu.SemaphoreType.DMA((FWD_REMOTE,)),
            pltpu.SemaphoreType.DMA((23,)),
            pltpu.SemaphoreType.DMA((16,)),
        ],
        compiler_params=pltpu.CompilerParams(
            collective_id=2, has_side_effects=True, vmem_limit_bytes=56 * 1024 * 1024
        ),
        cost_estimate=pl.CostEstimate(flops=2_000_000_000, bytes_accessed=30_000_000, transcendentals=0),
    )(
        segments,
        tokens,
        condition,
        mod_bias.reshape(1, -1),
        gains,
        jnp.asarray(cos_table),
        jnp.asarray(sin_table),
        mod_weight,
        qkv_weight,
        out_weight,
    )


def backward_kernel(
    segments,
    cotangent,
    tokens,
    modulation,
    condition,
    gains,
    inverses,
    acts,
    second_in,
    first_in,
    context_in,
    middle_in,
    attended_in,
    query_in,
    key_in,
    value_in,
    query_hat_in,
    key_hat_in,
    cos_in,
    sin_in,
    gate_weight,
    up_weight,
    down_weight,
    out_weight,
    qkv_weight,
    mod_weight,
    layer_out,
    tokens_out,
    gate_out,
    up_out,
    down_out,
    out_out,
    qkv_out,
    mod_out,
    special_out,
    condition_out,
    hidden_s,
    second_s,
    first_s,
    gbranch_s,
    ggate_s,
    gup_s,
    gatt_s,
    perm9,
    perm24,
    xt24,
    acc,
    heads,
    folds,
    per_token,
    branch,
    gsecond,
    attended,
    query,
    key,
    value,
    gcontext,
    gquery,
    gkey,
    gvalue,
    cosine,
    gain_sum,
    ring_gate,
    ring_up,
    ring_down,
    gmod,
    act_rows,
    fold32,
    fold_own,
    fold_other,
    other32,
    pair32,
    across32,
    rows32,
    gathered_a,
    gathered_b,
    product_own,
    product_send,
    product_other,
    final_other,
    special_other,
    part_own,
    part_other,
    *rest,
):
    bufs = [list(rest[7 * index : 7 * index + 7]) for index in range(len(JOBS))]
    for index in range(4):
        bufs[0][index] = bufs[4][index]
    xt9 = xt24.at[pl.ds(0, 576)]
    send_sem, recv_sem, local_sem, ring_sem = rest[7 * len(JOBS) :]
    gproj_s, middle = ggate_s, tokens_out
    place, core = position()
    mod = lax.axis_index("mod")
    partner = device_at(place, 1 - core)
    near = []
    for axis in range(3):
        here = place[axis]
        near.append(
            (here, lax.rem(here + 1, 4), lax.rem(here + 3, 4), lax.rem(here + 2, 4))
        )
    twin = moved(place, 0, near[0][3])

    def ff_chunk(index, slot):
        columns = pl.ds(pl.multiple_of(index * CHUNK, CHUNK), CHUNK)
        return (
            pltpu.make_async_copy(gate_weight.at[:, columns], ring_gate.at[slot], ring_sem.at[0, slot]),
            pltpu.make_async_copy(up_weight.at[:, columns], ring_up.at[slot], ring_sem.at[1, slot]),
            pltpu.make_async_copy(down_weight.at[columns, :], ring_down.at[slot], ring_sem.at[2, slot]),
        )

    def out_chunk(index, slot):
        rows = pl.ds(pl.multiple_of(index * CHUNK, CHUNK), CHUNK)
        return pltpu.make_async_copy(out_weight.at[rows, :], ring_down.at[slot], ring_sem.at[2, slot])

    def wide_chunk(source, index, slot):
        columns = pl.ds(pl.multiple_of(index * CHUNK, CHUNK), CHUNK)
        return pltpu.make_async_copy(source.at[:, columns], ring_gate.at[slot], ring_sem.at[0, slot])

    def narrow_chunk(source):
        return pltpu.make_async_copy(
            source.at[:, pl.ds(13 * CHUNK, 128)], ring_up.at[0, :, pl.ds(0, 128)], ring_sem.at[1, 0]
        )

    def wide_columns(source, start, stop):
        for index in range(start, stop):
            wide_chunk(source, index, index).start()
        narrow_chunk(source).start()

    for index in range(2):
        for copy in ff_chunk(index, index):
            copy.start()
    loads = {}

    def load(name, src, dst):
        copy = pltpu.make_async_copy(src, dst, local_sem.at[len(loads)])
        copy.start()
        loads[name] = copy

    own_rows, other_rows = pl.ds(0, TOK), pl.ds(TOK, TOK)
    load("second", second_in, second_s.at[own_rows])
    load("middle", middle_in, middle)
    load("attended", attended_in, attended)
    load("query", query_in, query)
    load("key", key_in, key)
    load("value", value_in, value)
    load("first", first_in, first_s.at[own_rows])

    barrier = pltpu.get_barrier_semaphore()
    pl.semaphore_signal(barrier, inc=1, device_id=partner, device_id_type=MESH)
    for axis in range(3):
        for far in near[axis][1:]:
            pl.semaphore_signal(
                barrier,
                inc=1,
                device_id=device_at(moved(place, axis, far), core),
                device_id_type=MESH,
            )
    pl.semaphore_signal(barrier, inc=1, device_id=device_at(twin, 1 - core), device_id_type=MESH)

    kind = segments[TOK - 1] == 0
    token = lax.broadcasted_iota(jnp.int32, (TOK, 16), 0)
    slot_of = lax.broadcasted_iota(jnp.int32, (TOK, 16), 1)
    onehot = (slot_of == jnp.where(kind, 0, token // 36)).astype(jnp.float32).astype(jnp.bfloat16)
    token_t = lax.broadcasted_iota(jnp.int32, (16, TOK), 1)
    slot_t = lax.broadcasted_iota(jnp.int32, (16, TOK), 0)
    onehot_t = (slot_t == jnp.where(kind, 0, token_t // 36)).astype(jnp.float32).astype(jnp.bfloat16)
    for index, block in enumerate((5, 4, 2, 1)):
        for third in range(3):
            to = index * WIDE + third * 384
            at = block * WIDE + third * 384
            per_token[:, to : to + 384] = jnp.dot(
                onehot, modulation[:, at : at + 384], preferred_element_type=jnp.float32
            ).astype(jnp.bfloat16)

    def piece(rows, block):
        base = (5, 4, 2, 1).index(block) * WIDE
        return per_token[rows, base : base + WIDE].astype(jnp.float32)

    def first_rows(rows):
        upstream = cotangent[rows, :].astype(jnp.float32)
        gbranch_s[rows, :] = (upstream * piece(rows, 5)).astype(jnp.bfloat16)
        zero = jnp.zeros((16, WIDE), jnp.float32)
        branch[rows, :] = zero
        gsecond[rows, :] = zero

    row_blocks(first_rows)
    gmod[...] = jnp.zeros_like(gmod)
    gain_sum[...] = jnp.zeros_like(gain_sum)
    pl.semaphore_wait(barrier, 11)

    def remote(src, dst, index, target):
        return pltpu.make_async_remote_copy(
            src_ref=src,
            dst_ref=dst,
            send_sem=send_sem.at[index],
            recv_sem=recv_sem.at[index],
            device_id=target,
            device_id_type=MESH,
        )

    sent = []
    pairs = {}

    def exchange(name, src, dst):
        copy = remote(src, dst, len(pairs), partner)
        copy.start()
        pairs[name] = copy

    exchange("gbranch", gbranch_s.at[own_rows], gbranch_s.at[other_rows])
    exchange("second", second_in, second_s.at[other_rows])
    exchange("first", first_in, first_s.at[other_rows])

    def arrived(*names):
        for name in names:
            pairs[name].wait_recv()

    lane24 = lax.broadcasted_iota(jnp.int32, (192, 384), 1)
    row24 = lax.broadcasted_iota(jnp.int32, (192, 384), 0)
    perm24[...] = (
        (lane24 == row24 // 48 * 96 + lax.rem(row24, 48) + core * 48)
        .astype(jnp.float32)
        .astype(jnp.bfloat16)
    )
    heads[...] = head_rows()
    folded = lax.rem(lax.broadcasted_iota(jnp.int32, (128, WIDE), 1), 72)
    folds[...] = (
        (folded == lax.broadcasted_iota(jnp.int32, (128, WIDE), 0)).astype(jnp.float32).astype(jnp.bfloat16)
    )

    def pick9(part, stack):
        wanted = row_sources(part) + core * 18

        @pl.loop(0, 9)
        def _(block):
            columns = lax.broadcasted_iota(jnp.int32, (576, 128), 1) + block * 128
            perm9[:, pl.ds(pl.multiple_of(block * 128, 128), 128)] = (
                (columns == wanted)
                .astype(jnp.float32)
                .astype(jnp.bfloat16)
            )

        @pl.loop(0, 3)
        def _(index):
            rows = pl.ds(pl.multiple_of(index * 192, 16), 192)
            xt9[rows, :] = inner_cols(perm9[rows, :], stack[...]).astype(jnp.bfloat16)

    def pick24(part):
        def block_rows(block):
            columns = pl.ds(pl.multiple_of(block * 384, 128), 384)
            return inner_cols(perm24[...], hidden_s[:, columns])

        def put(unit, upper, lower):
            rows = jnp.concatenate([upper, lower]).astype(jnp.bfloat16)
            xt24[pl.ds(pl.multiple_of(unit * 24, 16), 48), :] = rows

        def unit_rows(rows, y, x_hi):
            at = (y * 2 + x_hi) * 24
            return rows[at : at + 24]

        @pl.loop(0, 8 if part == 2 else 4)
        def _(index):
            if part == 0:
                x_lo, z = index // 2, lax.rem(index, 2) * 2
                upper, lower = block_rows(x_lo * 4 + z), block_rows(x_lo * 4 + z + 1)
                for y in range(4):
                    for x_hi in range(2):
                        unit = (x_hi * 2 + x_lo) * 16 + y * 4 + z
                        put(unit, unit_rows(upper, y, x_hi), unit_rows(lower, y, x_hi))
            elif part == 1:
                upper, lower = block_rows(index), block_rows(4 + index)
                for y in range(4):
                    for x_hi in range(2):
                        unit = y * 16 + index * 4 + x_hi * 2
                        put(unit, unit_rows(upper, y, x_hi), unit_rows(lower, y, x_hi))
            else:
                x_lo, z = index // 4, lax.rem(index, 4)
                rows = block_rows(index)
                for y in (0, 2):
                    for x_hi in range(2):
                        unit = z * 16 + (x_hi * 2 + x_lo) * 4 + y
                        put(unit, unit_rows(rows, y, x_hi), unit_rows(rows, y + 1, x_hi))

    def multiply(job, part, left, right):
        _, _, width, lanes, _ = JOBS[job]
        target = bufs[job][0]

        @pl.loop(0, width // lanes)
        def _(step):
            to = pl.multiple_of(step * lanes, 128)
            columns = pl.ds(pl.multiple_of(part * width + to, 128), lanes)

            @pl.loop(0, left.shape[0] // 192)
            def _(index):
                rows = pl.ds(pl.multiple_of(index * 192, 16), 192)
                target[part, rows, pl.ds(to, lanes)] = jnp.dot(
                    left[rows, :], right[:, columns], preferred_element_type=jnp.float32
                ).astype(jnp.bfloat16)

    copies = {}
    drained = set()

    def begin(job, part, slot, src, dst, target):
        index = PARTNER_COPIES + (job * 3 + part) * COPIES + slot
        copy = remote(src, dst, index, target)
        copy.start()
        copies[job, part, slot] = copy

    def arrive(job, part, *slots):
        for slot in slots:
            copies[job, part, slot].wait_recv()

    def ring(part, phase):
        axis = AXES[part][phase]
        here, right, left, opposite = near[axis]
        return (
            here,
            right,
            left,
            opposite,
            device_at(moved(place, axis, right), core),
            device_at(moved(place, axis, left), core),
            device_at(moved(place, axis, opposite), core),
        )

    def sent_out(job, part, *slots):
        for slot in slots:
            if (job, part, slot) not in drained:
                drained.add((job, part, slot))
                copies[job, part, slot].wait_send()

    def first_send(job, part):
        own, half, whole = bufs[job][:3]
        big = 16 * JOBS[job][1]
        cut = sixteen(big // 2)
        here, right, left, opposite, to_right, to_left, _ = ring(part, 0)

        full = pl.ds(0, JOBS[job][2])

        def rows(chunk, start, count):
            return own.at[
                part, pl.ds(pl.multiple_of(chunk * big + start, 16), count), pl.ds(0, JOBS[job][2])
            ]

        begin(job, part, 0, rows(opposite, 0, cut), half.at[part, pl.ds(0, cut), full], to_right)
        begin(job, part, 1, rows(opposite, cut, big - cut), half.at[part, pl.ds(cut, big - cut), full], to_left)
        begin(job, part, 2, rows(right, cut, big - cut), whole.at[part, 0, pl.ds(cut, big - cut), full], to_right)
        begin(job, part, 3, rows(left, 0, cut), whole.at[part, 1, pl.ds(0, cut), full], to_left)

    def first_add(job, part):
        own, half, whole = bufs[job][:3]
        _, each, width, lanes, _ = JOBS[job]
        big = 16 * each
        cut = sixteen(big // 2)
        here, right, left, opposite, to_right, to_left, _ = ring(part, 0)
        for slot, chunk, start, count, target, side in (
            (0, right, 0, cut, to_right, 0),
            (1, left, cut, big - cut, to_left, 1),
        ):
            arrive(job, part, slot)
            rows = pl.ds(pl.multiple_of(chunk * big + start, 16), count)

            @pl.loop(0, width // 128)
            def _(step):
                columns = pl.ds(pl.multiple_of(step * 128, 128), 128)
                total = own[part, rows, columns].astype(jnp.float32) + half[
                    part, pl.ds(start, count), columns
                ].astype(jnp.float32)
                own[part, rows, columns] = total.astype(jnp.bfloat16)

            begin(
                job,
                part,
                4 + side,
                own.at[part, rows, pl.ds(0, width)],
                whole.at[part, side, pl.ds(start, count), pl.ds(0, width)],
                target,
            )

    def second_send(job, part):
        own, _, whole, mid, mid_half, mid_whole, _ = bufs[job]
        _, each, width, lanes, cut = JOBS[job]
        big, small = 16 * each, 4 * each
        padded = sixteen(small)
        here, right, left, opposite, to_right, to_left, _ = ring(part, 0)
        arrive(job, part, 2, 3, 4, 5)
        if JOBS[job][0] == "qkv":
            sent_out(0, part, 6, 7, 8, 9, 10, 11)
        rows = pl.ds(pl.multiple_of(here * big, 16), big)

        @pl.loop(0, width // 128)
        def _(step):
            columns = pl.ds(pl.multiple_of(step * 128, 128), 128)
            acc[pl.ds(0, big), :] = (
                own[part, rows, columns].astype(jnp.float32)
                + whole[part, 0, :, columns].astype(jnp.float32)
                + whole[part, 1, :, columns].astype(jnp.float32)
            )
            for chunk in range(4):
                mid[part, chunk, :, columns] = acc[pl.ds(chunk * small, padded), :].astype(jnp.bfloat16)

        here, right, left, opposite, to_right, to_left, _ = ring(part, 1)
        low, high = pl.ds(0, cut), pl.ds(cut, width - cut)
        begin(job, part, 6, mid.at[part, opposite, :, low], mid_half.at[part, :, low], to_right)
        begin(job, part, 7, mid.at[part, opposite, :, high], mid_half.at[part, :, high], to_left)
        begin(job, part, 8, mid.at[part, right, :, high], mid_whole.at[part, 0, :, high], to_right)
        begin(job, part, 9, mid.at[part, left, :, low], mid_whole.at[part, 1, :, low], to_left)

    def second_add(job, part):
        _, _, _, mid, mid_half, mid_whole, _ = bufs[job]
        _, each, width, lanes, cut = JOBS[job]
        here, right, left, opposite, to_right, to_left, _ = ring(part, 1)
        for slot, chunk, start, count, target, side in (
            (6, right, 0, cut, to_right, 0),
            (7, left, cut, width - cut, to_left, 1),
        ):
            arrive(job, part, slot)

            @pl.loop(0, count // 128)
            def _(step):
                columns = pl.ds(pl.multiple_of(start + step * 128, 128), 128)
                total = mid[part, chunk, :, columns].astype(jnp.float32) + mid_half[
                    part, :, columns
                ].astype(jnp.float32)
                mid[part, chunk, :, columns] = total.astype(jnp.bfloat16)

            columns = pl.ds(start, count)
            begin(
                job,
                part,
                10 + side,
                mid.at[part, chunk, :, columns],
                mid_whole.at[part, side, :, columns],
                target,
            )

    def third_send(job, part):
        _, _, _, mid, _, mid_whole, last = bufs[job]
        _, each, width, lanes, cut = JOBS[job]
        small = sixteen(4 * each)
        padded = sixteen(each)
        here = ring(part, 1)[0]
        arrive(job, part, 8, 9, 10, 11)

        @pl.loop(0, width // 128)
        def _(step):
            columns = pl.ds(pl.multiple_of(step * 128, 128), 128)
            acc[pl.ds(0, small), :] = (
                mid[part, here, :, columns].astype(jnp.float32)
                + mid_whole[part, 0, :, columns].astype(jnp.float32)
                + mid_whole[part, 1, :, columns].astype(jnp.float32)
            )
            for chunk in range(4):
                last[part, chunk, :, columns] = acc[pl.ds(chunk * each, padded), :].astype(jnp.bfloat16)

        here, right, left, opposite, to_right, to_left, to_opposite = ring(part, 2)
        for slot, chunk, target in ((0, right, to_right), (1, left, to_left), (2, opposite, to_opposite)):
            begin(job, part, 12 + slot, last.at[part, chunk], last.at[part, 4 + slot], target)

    mod_base = PARTNER_COPIES + 3 * COPIES * len(JOBS)
    mod_copies = {}

    def mod_send(slot, src, dst, target):
        copy = remote(src, dst, mod_base + slot, target)
        copy.start()
        sent.append(copy)
        mod_copies[slot] = copy

    def mod_arrive(*slots):
        for slot in slots:
            mod_copies[slot].wait_recv()

    def mod_pair():
        for quarter in range(4):
            fold32[4 * quarter : 4 * quarter + 4, :] = gmod[
                1 - mod, 0:4, quarter * 896 : (quarter + 1) * 896
            ]
        fold_own[...] = fold32[...].astype(jnp.bfloat16)
        mod_send(0, fold_own, fold_other, device_at(twin, core))

    def mod_cores():
        mod_arrive(0)
        fold32[...] = fold_other[...].astype(jnp.float32)
        for quarter in range(4):
            other32[0:4, quarter * 896 : (quarter + 1) * 896] = fold32[4 * quarter : 4 * quarter + 4, :]
        own, other = gmod[mod, 0:4, :], other32[0:4, :]
        pair32[0:4, :] = jnp.where(mod == 0, own, other)
        pair32[4:8, :] = jnp.where(mod == 0, other, own)
        there = pl.ds(pl.multiple_of((1 - core) * 1792, 128), 1792)
        mod_send(1, pair32.at[:, there], across32, partner)

    def condition_part():
        wide_columns(mod_weight, 0, 2)
        part_own[...] = jnp.zeros_like(part_own)

        @pl.loop(0, 13)
        def _(index):
            slot = lax.rem(index, 2)
            wide_chunk(mod_weight, index, slot).wait()
            columns = pl.ds(pl.multiple_of(index * CHUNK, CHUNK), CHUNK)
            part_own[...] += inner_cols(pair32[:, columns].astype(jnp.bfloat16), ring_gate[slot])

            @pl.when(index + 2 < 13)
            def _():
                wide_chunk(mod_weight, index + 2, slot).start()

        narrow_chunk(mod_weight).wait()
        part_own[...] += inner_cols(
            pair32[:, 13 * CHUNK : 3456].astype(jnp.bfloat16), ring_up[0, :, 0:128]
        )
        mod_send(2, part_own, part_other, device_at(twin, core))

    def mod_gather_first():
        mod_arrive(1)
        here = pl.ds(pl.multiple_of(core * 1792, 128), 1792)
        own, other = pair32[:, here], across32[...]
        rows32[0:8, :] = jnp.where(core == 0, own, other)
        rows32[8:16, :] = jnp.where(core == 0, other, own)
        _, y, z = place
        gathered_a[z, y] = rows32[:, 0:896].astype(jnp.bfloat16)
        gathered_b[z, y] = rows32[:, 896:1792].astype(jnp.bfloat16)
        for step in range(3):
            to_y = device_at(moved(place, 1, near[1][1 + step]), core)
            to_z = device_at(moved(place, 2, near[2][1 + step]), core)
            mod_send(3 + step, gathered_a.at[z, y], gathered_a.at[z, y], to_y)
            mod_send(6 + step, gathered_b.at[z, y], gathered_b.at[z, y], to_z)

    def mod_gather_second():
        _, y, z = place
        mod_arrive(3, 4, 5)
        for step in range(3):
            to_z = device_at(moved(place, 2, near[2][1 + step]), core)
            mod_send(9 + step, gathered_a.at[z], gathered_a.at[z], to_z)
        mod_arrive(6, 7, 8)
        for step in range(3):
            to_y = device_at(moved(place, 1, near[1][1 + step]), core)
            mod_send(12 + step, gathered_b.at[:, y], gathered_b.at[:, y], to_y)

    def mod_table():
        x, y, z = place
        row = lax.broadcasted_iota(jnp.int32, (48, WIDE), 0)
        lane = lax.broadcasted_iota(jnp.int32, (48, WIDE), 1)
        line = lax.broadcasted_iota(jnp.int32, (48, 256), 0)
        slot = lax.rem(lax.broadcasted_iota(jnp.int32, (48, 256), 1), 4)
        ones = (line == 40) | ((line == 41) & (slot == 0)) | ((line == 42) & (slot == 1))
        for index in range(2):
            half = lax.rem(lax.rem(x, 2) + index, 2)
            start = (half * 32 + z * 8 + y * 2) * 18
            pick = ((row < 36) & (lane == row + start)).astype(jnp.float32).astype(jnp.bfloat16)
            rows = inner_cols(pick, perm9[0:256, :])
            act_rows[index] = (rows + ones.astype(jnp.float32)).astype(jnp.bfloat16)

    def mod_product():
        mod_arrive(9, 10, 11)
        mod_arrive(12, 13, 14)
        for side, gathered in ((0, gathered_a), (1, gathered_b)):
            columns = slice(side * 896, (side + 1) * 896)
            rows = gathered[...].reshape(256, 896)
            product_send[:, columns] = jnp.dot(
                act_rows[1], rows, preferred_element_type=jnp.float32
            ).astype(jnp.bfloat16)
            product_own[:, columns] = jnp.dot(act_rows[0], rows, preferred_element_type=jnp.float32)
        x = place[0]
        beside = moved(place, 0, x + 1 - 2 * lax.rem(x, 2))
        mod_send(15, product_send, product_other, device_at(beside, core))

    def mod_sum():
        mod_arrive(15)
        product_own[...] = product_own[...] + product_other[...].astype(jnp.float32)
        mod_send(16, product_own, final_other, partner)
        special = product_own.at[pl.ds(40, 8)]
        mod_send(17, special, special_other.at[core], device_at(twin, core))
        mod_send(18, special, special_other.at[core], device_at(twin, 1 - core))

    def mod_finish():
        here = pl.ds(pl.multiple_of(core * 1792, 128), 1792)
        there = pl.ds(pl.multiple_of((1 - core) * 1792, 128), 1792)
        mod_arrive(2)
        total = part_own[...] + part_other[...]
        raw = condition[...].astype(jnp.float32)
        condition_out[...] = jnp.where(mod == 0, total[0:4], total[4:8]) * silu_slope(raw)
        mod_arrive(16)
        for source, columns in ((product_own, here), (final_other, there)):
            mod_out[:, columns] = jnp.where(core == 0, source[0:18, :], source[18:36, :])
            special_out[mod, :, columns] = source[40:48, :]
        mod_arrive(17, 18)
        for side in range(2):
            special_out[1 - mod, :, side * 1792 : (side + 1) * 1792] = special_other[side]

    outs = {"gate": gate_out, "up": up_out, "down": down_out, "out": out_out, "qkv": qkv_out}

    def finish(job, part):
        last = bufs[job][6]
        _, each, width, lanes, cut = JOBS[job]
        here = ring(part, 2)[0]
        arrive(job, part, 12, 13, 14)

        @pl.loop(0, width // 128)
        def _(step):
            to = pl.multiple_of(step * 128, 128)
            columns = pl.ds(to, 128)
            total = last[part, here, :, columns].astype(jnp.float32)
            for slot in range(3):
                total = total + last[part, 4 + slot, :, columns].astype(jnp.float32)
            outs[JOBS[job][0]][:, pl.ds(pl.multiple_of(part * width + to, 128), 128)] = total[:each]

    gate_job, up_job, down_job, out_job, qkv_job = range(5)

    def slot_sum(block, source):
        for third in range(3):
            columns = slice(third * 384, (third + 1) * 384)
            high, low = split_two(source[:, columns])
            total = jnp.dot(onehot_t, high, preferred_element_type=jnp.float32) + jnp.dot(
                onehot_t, low, preferred_element_type=jnp.float32
            )
            base = block % 3 * WIDE + third * 384
            gmod[block // 3, :, base : base + 384] = (
                total[0:8].astype(jnp.bfloat16).astype(jnp.float32)
            )

    def stages(stage, job):
        for part in range(3):
            stage(job, part)

    def ff_part(part):
        @pl.loop(0, 4)
        def _(step):
            index = part * 4 + step
            slot = lax.rem(index, 2)
            for copy in ff_chunk(index, slot):
                copy.wait()
            columns = pl.ds(pl.multiple_of(index * CHUNK, CHUNK), CHUNK)
            second = second_s[0:TOK, :]
            gate_linear = jnp.dot(second, ring_gate[slot], preferred_element_type=jnp.float32)
            up_linear = jnp.dot(second, ring_up[slot], preferred_element_type=jnp.float32)
            ghidden = inner_cols(gbranch_s[0:TOK, :], ring_down[slot])
            logistic = jax.nn.sigmoid(gate_linear)
            gate_act = gate_linear * logistic
            hidden = (gate_act * up_linear).astype(jnp.bfloat16)
            slope = logistic * (1.0 + gate_linear * (1.0 - logistic))
            ggate = (ghidden * up_linear * slope).astype(jnp.bfloat16)
            gup = (ghidden * gate_act).astype(jnp.bfloat16)
            hidden_s[0:TOK, columns] = hidden
            ggate_s[0:TOK, columns] = ggate
            gup_s[0:TOK, columns] = gup
            for third in range(3):
                at = slice(third * 384, (third + 1) * 384)
                branch[:, at] += jnp.dot(hidden, ring_down[slot, :, at], preferred_element_type=jnp.float32)
                gsecond[:, at] += inner_cols(ggate, ring_gate[slot, at, :]) + inner_cols(
                    gup, ring_up[slot, at, :]
                )

            @pl.when(index + 2 < 12)
            def _():
                for copy in ff_chunk(index + 2, slot):
                    copy.start()

        columns = pl.ds(part * 1024, 1024)
        exchange("ggate%d" % part, ggate_s.at[own_rows, columns], ggate_s.at[other_rows, columns])
        exchange("gup%d" % part, gup_s.at[own_rows, columns], gup_s.at[other_rows, columns])
        exchange("hidden%d" % part, hidden_s.at[own_rows, columns], hidden_s.at[other_rows, columns])

    def ff_products(part):
        arrived("ggate%d" % part, "gup%d" % part)
        pick9(part, second_s)
        multiply(gate_job, part, xt9, ggate_s)
        first_send(gate_job, part)
        multiply(up_job, part, xt9, gup_s)
        first_send(up_job, part)

    loads["second"].wait()
    ff_part(0)
    arrived("second")
    ff_part(1)
    ff_products(0)
    ff_part(2)
    for index in range(2):
        out_chunk(index, index).start()
    ff_products(1)

    loads["middle"].wait()
    loads["attended"].wait()

    def second_rows(rows):
        upstream = cotangent[rows, :].astype(jnp.float32)
        kept = middle[rows, :]
        result = branch[rows, :]
        layer_out[rows, :] = (kept + piece(rows, 5) * result).astype(jnp.bfloat16)
        branch[rows, :] = upstream * result
        normed, inverse = rms_norm(kept)
        grad = gsecond[rows, :]
        gquery[rows, :] = grad * normed
        total = upstream + norm_back(grad * (1.0 + piece(rows, 4)), normed, inverse)
        middle[rows, :] = total
        attended_row = attended[rows, :]
        attended[rows, :] = total * attended_row
        gatt_s[rows, :] = (total * piece(rows, 2)).astype(jnp.bfloat16)

    row_blocks(second_rows)
    ff_products(2)
    exchange("gatt", gatt_s.at[own_rows], gatt_s.at[other_rows])
    context_s = second_s
    load("context", context_in, context_s.at[own_rows])

    arrived("gbranch", "hidden0", "hidden1", "hidden2")
    for part in range(3):
        pick24(part)
        multiply(down_job, part, xt24, gbranch_s)
        first_send(down_job, part)
    arrived("gatt")
    exchange("context", context_in, context_s.at[other_rows])

    @pl.loop(0, 4)
    def _(index):
        slot = lax.rem(index, 2)
        out_chunk(index, slot).wait()
        columns = pl.ds(pl.multiple_of(index * CHUNK, CHUNK), CHUNK)
        gcontext[:, columns] = inner_cols(gatt_s[0:TOK, :], ring_down[slot]).astype(jnp.bfloat16)

        @pl.when(index + 2 < 4)
        def _():
            out_chunk(index + 2, slot).start()

    tail = pltpu.make_async_copy(
        out_weight.at[pl.ds(1024, 128), :], ring_down.at[0, pl.ds(0, 128), :], ring_sem.at[2, 0]
    )
    tail.start()
    slot_sum(5, branch)
    slot_sum(4, gquery)
    slot_sum(3, gsecond)
    slot_sum(2, attended)
    tail.wait()
    gcontext[:, 1024:WIDE] = inner_cols(gatt_s[0:TOK, :], ring_down[0, 0:128, :]).astype(jnp.bfloat16)
    load("query_hat", query_hat_in, branch)
    load("key_hat", key_hat_in, attended)
    load("cos", cos_in, cosine)
    load("sin", sin_in, gsecond)
    query_hat, key_hat, sine = branch, attended, gsecond
    wide_columns(qkv_weight, 0, 2)

    loads["context"].wait()
    arrived("context")
    for part in range(3):
        pick9(part, context_s)
        multiply(out_job, part, xt9, gatt_s)
        first_send(out_job, part)
    stages(first_add, gate_job)
    stages(first_add, up_job)

    gquery[...] = jnp.zeros_like(gquery)
    gkey[...] = jnp.zeros_like(gkey)
    gvalue[...] = jnp.zeros_like(gvalue)
    for name in ("query", "key", "value"):
        loads[name].wait()

    def attention_group(group):
        @pl.loop(0, 2)
        def _(pair):
            left = lax.broadcasted_iota(jnp.int32, (TOK, TOK), 0) // 36
            right = lax.broadcasted_iota(jnp.int32, (TOK, TOK), 1) // 36
            shut = jnp.where(kind | (left == right), 0.0, -1e30)
            for member in range(2):
                window, mask = head_window(group * 4 + pair * 2 + member)
                query_w, key_w = query[:, window] * mask, key[:, window] * mask
                value_w, grad_w = value[:, window], gcontext[:, window] * mask
                scores = inner_cols(query_w, key_w) * (72**-0.5) + shut
                weight = jnp.exp(scores - jnp.max(scores, axis=-1, keepdims=True))
                weight = weight * (1.0 / jnp.sum(weight, axis=-1, keepdims=True))
                gattention = inner_cols(grad_w, value_w)
                gvalue[:, window] += inner_rows(weight.astype(jnp.bfloat16), grad_w)
                dots = jnp.sum(weight * gattention, axis=-1, keepdims=True)
                gscores = (weight * (gattention - dots)).astype(jnp.bfloat16)
                gquery[:, window] += jnp.dot(gscores, key_w, preferred_element_type=jnp.float32)
                gkey[:, window] += inner_rows(gscores, query_w)

    attention_group(0)
    stages(second_send, gate_job)
    attention_group(1)
    stages(second_send, up_job)
    stages(first_add, down_job)
    attention_group(2)
    stages(second_add, gate_job)
    stages(first_add, out_job)
    attention_group(3)
    stages(second_add, up_job)
    stages(second_send, down_job)

    for part in range(3):
        for name in ("ggate",):
            pairs["ggate%d" % part].wait_send()

    def project_back(which, grads, hat):
        base = which * WIDE

        @pl.loop(0, 3)
        def _(index):
            rows = pl.ds(pl.multiple_of(index * 48, 16), 48)
            grad = grads[rows, :] * (72**-0.5)
            normed = hat[rows, :]
            turned = grad * cosine[rows, :] - swap_halves(grad) * sine[rows, :]
            gain_sum[which] += jnp.sum((turned * normed).reshape(6, 8, WIDE), axis=0)
            scaled = turned * gains[which : which + 1, :]
            inverse = inverses[which, rows, :]
            mean = head_sum(scaled * normed, heads[...]) * (1.0 / 72.0)
            raw = scaled * head_spread(inverse, heads[...]) - normed * head_spread(
                inverse * mean, heads[...]
            )
            gproj_s[rows, base : base + WIDE] = raw.astype(jnp.bfloat16)

    def exchange_projected(part):
        columns = pl.ds(part * WIDE, WIDE)
        exchange("gproj%d" % part, gproj_s.at[own_rows, columns], gproj_s.at[other_rows, columns])

    def value_rows(rows):
        gproj_s[rows, 2 * WIDE : 3 * WIDE] = gvalue[rows, :].astype(jnp.bfloat16)

    row_blocks(value_rows)
    exchange_projected(2)
    for name in ("query_hat", "key_hat", "cos", "sin"):
        loads[name].wait()
    project_back(0, gquery, query_hat)
    exchange_projected(0)
    project_back(1, gkey, key_hat)
    exchange_projected(1)
    loads["first"].wait()
    arrived("first")
    for part in (2, 0, 1):
        arrived("gproj%d" % part)
        pick9(part, first_s)
        sent_out(gate_job, part, 0, 1, 2, 3, 4, 5)
        multiply(qkv_job, part, xt9, gproj_s)
        first_send(qkv_job, part)

    load("acts", acts, perm9.at[pl.ds(0, 256)])
    gfirst, scaled_first = gquery, gkey
    gfirst[...] = jnp.zeros_like(gfirst)

    @pl.loop(0, 13)
    def _(index):
        slot = lax.rem(index, 2)
        wide_chunk(qkv_weight, index, slot).wait()
        columns = pl.ds(pl.multiple_of(index * CHUNK, CHUNK), CHUNK)
        for third in range(3):
            at = slice(third * 384, (third + 1) * 384)
            gfirst[:, at] += inner_cols(gproj_s[0:TOK, columns], ring_gate[slot, at, :])

        @pl.when(index + 2 < 13)
        def _():
            wide_chunk(qkv_weight, index + 2, slot).start()

    narrow_chunk(qkv_weight).wait()
    for third in range(3):
        at = slice(third * 384, (third + 1) * 384)
        gfirst[:, at] += inner_cols(gproj_s[0:TOK, 13 * CHUNK : 3456], ring_up[0, at, 0:128])

    def last_rows(rows):
        normed, inverse = rms_norm(tokens[rows, :].astype(jnp.float32))
        grad = gfirst[rows, :]
        scaled_first[rows, :] = grad * normed
        tokens_out[rows, :] = middle[rows, :] + norm_back(
            grad * (1.0 + piece(rows, 1)), normed, inverse
        )

    row_blocks(last_rows)
    slot_sum(0, gfirst)
    slot_sum(1, scaled_first)
    for which in range(2):
        high, low = split_two(gain_sum[which])
        total = jnp.sum(inner_cols(high, folds[...]) + inner_cols(low, folds[...]), axis=0, keepdims=True)
        gmod[0, which : which + 1, 3456:3584] = total
    mod_pair()
    stages(second_add, down_job)
    stages(third_send, gate_job)
    stages(first_add, qkv_job)
    mod_cores()
    condition_part()
    stages(second_send, out_job)
    mod_gather_first()
    stages(third_send, up_job)
    stages(third_send, down_job)
    loads["acts"].wait()
    mod_table()
    stages(second_add, out_job)
    mod_gather_second()
    stages(second_send, qkv_job)
    stages(finish, gate_job)
    stages(third_send, out_job)
    stages(second_add, qkv_job)
    mod_product()
    stages(finish, up_job)
    stages(finish, down_job)
    stages(third_send, qkv_job)
    mod_sum()
    stages(finish, out_job)
    stages(finish, qkv_job)
    mod_finish()
    for name, copy in pairs.items():
        if not name.startswith("ggate"):
            copy.wait_send()
    for (job, part, slot) in list(copies):
        sent_out(job, part, slot)
    for copy in sent:
        copy.wait_send()


def write_kernel(*refs):
    count = len(refs) // 2
    for source, target in zip(refs[:count], refs[count:]):
        if len(source.shape) == 3:
            target[...] = source[:, 0:1, 0:3456]
        else:
            target[...] = source[:, 0 : target.shape[1]]


def backward(
    cotangent, tokens, condition, segments, gains, saved, gate_weight, up_weight, down_weight, out_weight, qkv_weight, mod_weight
):
    (query, key, value, query_hat, key_hat, context, attended, middle, first, second, cosine, sine, acts, inverses, modulation) = saved
    vmem = pl.BlockSpec(memory_space=pltpu.VMEM)
    anywhere = pl.BlockSpec(memory_space=pl.ANY)
    low, full = jnp.bfloat16, jnp.float32
    wide_low, wide_full = ((TOK, WIDE), low), ((TOK, WIDE), full)
    outs = (
        [wide_low, wide_full]
        + [((each, 3 * width), full) for _, each, width, _, _ in JOBS]
        + [((18, 3584), full), ((2, 8, 3584), full), ((4, WIDE), full)]
    )
    scratch = [
        ((PAIR, HID), low),
        ((PAIR, WIDE), low),
        ((PAIR, WIDE), low),
        ((PAIR, WIDE), low),
        ((PAIR, 3456), low),
        ((PAIR, HID), low),
        ((PAIR, WIDE), low),
        ((576, WIDE), low),
        ((192, 384), low),
        ((1536, PAIR), low),
        ((400, 128), full),
        ((128, WIDE), low),
        ((128, WIDE), low),
        ((TOK, 4 * WIDE), low),
        wide_full,
        wide_full,
        wide_full,
        wide_low,
        wide_low,
        wide_low,
        wide_low,
        wide_full,
        wide_full,
        wide_full,
        wide_full,
        ((2, 8, WIDE), full),
        ((2, WIDE, CHUNK), low),
        ((2, WIDE, CHUNK), low),
        ((2, CHUNK, WIDE), low),
        ((2, 8, 3584), full),
        ((2, 48, 256), low),
        ((16, 896), full),
        ((16, 896), low),
        ((16, 896), low),
        ((8, 3584), full),
        ((8, 3584), full),
        ((8, 1792), full),
        ((16, 1792), full),
        ((4, 4, 16, 896), low),
        ((4, 4, 16, 896), low),
        ((48, 1792), full),
        ((48, 1792), low),
        ((48, 1792), low),
        ((48, 1792), full),
        ((2, 8, 1792), full),
        ((8, WIDE), full),
        ((8, WIDE), full),
    ]
    for name, each, width, _, _ in JOBS:
        big, small, tiny = 16 * each, sixteen(4 * each), sixteen(each)
        unused = name == "gate"
        scratch += [
            ((1, 16, 128) if unused else (3, 4 * big, width), low),
            ((1, 16, 128) if unused else (3, big, width), low),
            ((1, 1, 16, 128) if unused else (3, 2, big, width), low),
            ((1, 1, 16, 128) if unused else (3, 4, small, width), low),
            ((3, small, width), low),
            ((3, 2, small, width), low),
            ((3, 7, tiny, width), low),
        ]
    count = PARTNER_COPIES + 3 * COPIES * len(JOBS) + MOD_COPIES
    results = pl.pallas_call(
        backward_kernel,
        out_shape=[jax.ShapeDtypeStruct(*out) for out in outs],
        in_specs=[pl.BlockSpec(memory_space=pltpu.SMEM)] + [vmem] * 6 + [anywhere] * 19,
        out_specs=[vmem] * 10,
        scratch_shapes=[pltpu.VMEM(*item) for item in scratch]
        + [
            pltpu.SemaphoreType.DMA((count,)),
            pltpu.SemaphoreType.DMA((count,)),
            pltpu.SemaphoreType.DMA((13,)),
            pltpu.SemaphoreType.DMA((3, 2)),
        ],
        compiler_params=pltpu.CompilerParams(
            collective_id=1, has_side_effects=True, vmem_limit_bytes=64 * 1024 * 1024 - 65536
        ),
        cost_estimate=pl.CostEstimate(
            flops=12_000_000_000, bytes_accessed=50_000_000, transcendentals=0
        ),
    )(
        segments,
        cotangent,
        tokens,
        modulation,
        condition,
        gains,
        inverses,
        acts.reshape(256, WIDE),
        second,
        first,
        context,
        middle,
        attended,
        query,
        key,
        value,
        query_hat,
        key_hat,
        cosine,
        sine,
        gate_weight,
        up_weight,
        down_weight,
        out_weight,
        qkv_weight,
        mod_weight,
    )
    special = results[8]
    kept = list(results[:8]) + [results[9]]
    shapes = [
        jax.ShapeDtypeStruct((item.shape[0], min(item.shape[1], 3456)), item.dtype) for item in kept
    ]
    written = pl.pallas_call(
        write_kernel,
        out_shape=shapes + [jax.ShapeDtypeStruct((2, 1, 3456), full)],
        in_specs=[vmem] * 10,
        out_specs=[vmem] * 10,
    )(*kept, special)
    return written, special


def body(
    tokens,
    condition,
    segments,
    mod_weight,
    mod_bias,
    qkv_weight,
    query_gain,
    key_gain,
    out_weight,
    gate_weight,
    up_weight,
    down_weight,
    cotangent,
):
    gains = jnp.tile(jnp.stack([query_gain, key_gain]), (1, 16))
    saved = forward(tokens, condition, segments, mod_weight, mod_bias, qkv_weight, gains, out_weight)
    written, special = backward(
        cotangent,
        tokens,
        condition,
        segments,
        gains,
        saved,
        gate_weight,
        up_weight,
        down_weight,
        out_weight,
        qkv_weight,
        mod_weight,
    )
    layer_out, grad_tokens, gate, up, down, out, qkv, mod_rows, grad_condition, bias = written
    gain_rows = special[0, 1:3, 3456:3528] + special[1, 1:3, 3456:3528]
    return (
        layer_out,
        grad_tokens,
        grad_condition,
        mod_rows,
        bias.reshape(-1),
        qkv,
        gain_rows[0],
        gain_rows[1],
        out,
        gate,
        up,
        down,
    )


def solution(mesh):
    placed = (
        P(("dp", "mod"), None),
        P(("dp", "mod"), None),
        P(("dp", "mod")),
        P(None, "mod"),
        P("mod"),
        P(),
        P(),
        P(),
        P(),
        P(),
        P(),
        P(),
        P(("dp", "mod"), None),
    )
    return jax.shard_map(
        body,
        mesh=mesh,
        in_specs=placed,
        out_specs=(
            P(("dp", "mod"), None),
            P(("dp", "mod"), None),
            P(("dp", "mod"), None),
            P("dp", "mod"),
            P(),
            P(("dp", "mod"), None),
            P(),
            P(),
            P(("dp", "mod"), None),
            P(("dp", "mod"), None),
            P(("dp", "mod"), None),
            P(("dp", "mod"), None),
        ),
        check_vma=False,
    )
```

```python
import jax
import jax.numpy as jnp
import numpy as np
from jax import lax
from jax.experimental import pallas as pl
from jax.experimental.pallas import tpu as pltpu
from jax.sharding import PartitionSpec as P

EPSILON = 1e-06


def rms_norm(values):
    inverse = lax.rsqrt(jnp.mean(values * values, axis=-1, keepdims=True) + EPSILON)
    return (values * inverse, inverse)


def norm_back(upstream, normed, inverse):
    return inverse * (upstream - normed * jnp.mean(upstream * normed, axis=-1, keepdims=True))


def silu_slope(values):
    logistic = jax.nn.sigmoid(values)
    return logistic * (1.0 + values * (1.0 - logistic))


def inner_rows(left, right):
    return lax.dot_general(
        left, right, (((0,), (0,)), ((), ())), preferred_element_type=jnp.float32
    )


def inner_cols(left, right):
    return lax.dot_general(
        left, right, (((1,), (1,)), ((), ())), preferred_element_type=jnp.float32
    )


TOK = 144
PAIR = 2 * TOK
WIDE = 1152
HID = 3072
RING = 4
AXES = ((0, 2, 1), (1, 0, 2), (2, 1, 0))
JOBS = (
    ("gate", 9, 1024, 256, 512),
    ("up", 9, 1024, 256, 512),
    ("down", 24, 384, 384, 256),
    ("out", 9, 384, 384, 256),
    ("qkv", 9, 1152, 384, 640),
)
COPIES = 15
PARTNER_COPIES = 17
MOD_COPIES = 19
CHUNK = 512


def sixteen(rows):
    return (rows + 15) // 16 * 16


def position():
    dp = lax.axis_index("dp")
    x_hi = lax.axis_index("mod")
    core = lax.rem(dp, 2)
    y = lax.rem(dp // 2, 4)
    z = lax.rem(dp // 8, 4)
    return (x_hi * 2 + dp // 32, y, z), core


def device_at(place, core):
    x, y, z = place
    return (((lax.rem(x, 2) * 4 + z) * 4 + y) * 2 + core, x // 2)


def moved(place, axis, value):
    return tuple(value if index == axis else kept for index, kept in enumerate(place))


def line_of(axis, value):
    return value % 2 * 2 + value // 2 if axis == 0 else value


FWD_REMOTE = 12
MESH = pl.DeviceIdType.MESH


def rope_flat():
    token = np.arange(TOK)
    frequency = 10000.0 ** (-np.arange(18, dtype=np.float64) / 18)
    tables = []
    for position_in, side in ((token % 36, 6), (token, 12)):
        row, column = position_in // side, position_in % side
        angle = np.concatenate([row[:, None] * frequency, column[:, None] * frequency], axis=1)
        cosine = np.tile(np.concatenate([np.cos(angle), np.cos(angle)], axis=1), (1, 16))
        sine = np.tile(np.concatenate([-np.sin(angle), np.sin(angle)], axis=1), (1, 16))
        tables.append((cosine, sine))
    return (
        np.stack([pair[0] for pair in tables]).astype(np.float32),
        np.stack([pair[1] for pair in tables]).astype(np.float32),
    )


def row_blocks(step):
    @pl.loop(0, TOK // 16)
    def _(index):
        step(pl.ds(pl.multiple_of(index * 16, 16), 16))


def split_two(values):
    high = values.astype(jnp.bfloat16)
    return high, (values - high.astype(jnp.float32)).astype(jnp.bfloat16)


def head_sum(values, heads):
    high, low = split_two(values)
    return inner_cols(high, heads) + inner_cols(low, heads)


def head_spread(values, heads):
    high, low = split_two(values)
    return jnp.dot(high, heads, preferred_element_type=jnp.float32) + jnp.dot(
        low, heads, preferred_element_type=jnp.float32
    )


def head_rows():
    head = lax.broadcasted_iota(jnp.int32, (128, WIDE), 0) * 72
    lane = lax.broadcasted_iota(jnp.int32, (128, WIDE), 1)
    return ((lane >= head) & (lane < head + 72)).astype(jnp.float32).astype(jnp.bfloat16)


def swap_halves(values):
    lane = lax.broadcasted_iota(jnp.int32, values.shape, 1)
    first = lax.rem(lane, 72) < 36
    return jnp.where(first, pltpu.roll(values, WIDE - 36, 1), pltpu.roll(values, 36, 1))


def head_window(head):
    block = jnp.minimum(head * 72 // 128, 7)
    offset = head * 72 - block * 128
    lane = lax.broadcasted_iota(jnp.int32, (1, 256), 1)
    mask = ((lane >= offset) & (lane < offset + 72)).astype(jnp.float32).astype(jnp.bfloat16)
    return pl.ds(pl.multiple_of(block * 128, 128), 256), mask


def forward_kernel(
    segments,
    tokens,
    condition,
    mod_bias,
    gains,
    cos_in,
    sin_in,
    mod_weight,
    qkv_weight,
    out_weight,
    query_out,
    key_out,
    value_out,
    query_hat_out,
    key_hat_out,
    context_out,
    attended_out,
    middle_out,
    first_out,
    second_out,
    cos_out,
    sin_out,
    gathered_out,
    inverse_out,
    modulation_out,
    mod_w,
    qkv_w,
    out_w,
    cos2,
    sin2,
    cond32,
    cond_other,
    act32,
    act_across,
    gathered,
    half32,
    fold32,
    fold_own,
    fold_other,
    mods32,
    per_token,
    norm,
    first,
    projected,
    query,
    key,
    value,
    query_hat,
    key_hat,
    context32,
    context,
    attended,
    middle,
    second,
    cosine,
    sine,
    heads,
    send_sem,
    recv_sem,
    in_sem,
    out_sem,
):
    place, core = position()
    mod = lax.axis_index("mod")
    partner = device_at(place, 1 - core)
    twin = device_at(moved(place, 0, lax.rem(place[0] + 2, 4)), core)
    peers = [
        [device_at(moved(place, axis, lax.rem(place[axis] + step, 4)), core) for step in (1, 2, 3)]
        for axis in (1, 2)
    ]
    loads = {}

    def load(name, index, src, dst, slot):
        copy = pltpu.make_async_copy(src, dst, in_sem.at[slot])
        copy.start()
        loads[name, index] = copy

    for index in range(9):
        columns = pl.ds(index * 384, 384)
        load("mod", index, mod_weight.at[:, columns], mod_w.at[:, columns], index)
    load("cos", 0, cos_in, cos2, 21)
    load("sin", 0, sin_in, sin2, 22)
    for index in range(9):
        columns = pl.ds(index * 384, 384)
        load("qkv", index, qkv_weight.at[:, columns], qkv_w.at[:, columns], 9 + index)
    for index in range(3):
        columns = pl.ds(index * 384, 384)
        load("out", index, out_weight.at[:, columns], out_w.at[:, columns], 18 + index)

    sent = []
    copies = {}

    def send(slot, src, dst, target):
        copy = pltpu.make_async_remote_copy(
            src_ref=src,
            dst_ref=dst,
            send_sem=send_sem.at[slot],
            recv_sem=recv_sem.at[slot],
            device_id=target,
            device_id_type=MESH,
        )
        copy.start()
        sent.append(copy)
        copies[slot] = copy

    stores = []

    def store(src, dst):
        copy = pltpu.make_async_copy(src, dst, out_sem.at[len(stores)])
        copy.start()
        stores.append(copy)

    barrier = pltpu.get_barrier_semaphore()
    for target in [partner, twin] + peers[0] + peers[1]:
        pl.semaphore_signal(barrier, inc=1, device_id=target, device_id_type=MESH)
    cond32[...] = jnp.zeros_like(cond32)
    cond32[0:4, :] = condition[...].astype(jnp.float32)
    pl.semaphore_wait(barrier, 8)
    send(0, cond32, cond_other, twin)

    kind = segments[TOK - 1] == 0
    row = lax.broadcasted_iota(jnp.int32, (TOK, 16), 0)
    slot = lax.broadcasted_iota(jnp.int32, (TOK, 16), 1)
    onehot = (slot == jnp.where(kind, 0, row // 36)).astype(jnp.float32).astype(jnp.bfloat16)
    heads[...] = head_rows()

    def first_norm(rows):
        values = tokens[rows, :].astype(jnp.float32)
        norm[rows, :] = rms_norm(values)[0]

    row_blocks(first_norm)

    copies[0].wait_recv()
    own, other = cond32[0:4, :], cond_other[0:4, :]
    act32[0:4, :] = jnp.where(mod == 0, own, other)
    act32[4:8, :] = jnp.where(mod == 0, other, own)
    act32[...] = jax.nn.silu(act32[...]).astype(jnp.bfloat16).astype(jnp.float32)
    send(1, act32, act_across, partner)
    act = act32[...].astype(jnp.bfloat16)
    half32[...] = jnp.zeros_like(half32)
    for index in range(9):
        columns = slice(index * 384, (index + 1) * 384)
        loads["mod", index].wait()
        half32[:, columns] = (
            (
                jnp.dot(act, mod_w[:, columns], preferred_element_type=jnp.float32)
                + mod_bias[:, columns].astype(jnp.float32)
            )
            .astype(jnp.bfloat16)
            .astype(jnp.float32)
        )
    for quarter in range(4):
        columns = slice(quarter * 896, (quarter + 1) * 896)
        fold32[4 * quarter : 4 * quarter + 4, :] = jnp.where(
            mod == 0, half32[4:8, columns], half32[0:4, columns]
        )
    fold_own[...] = fold32[...].astype(jnp.bfloat16)
    send(2, fold_own, fold_other, twin)

    copies[1].wait_recv()
    _, y, z = place
    rows16 = jnp.concatenate(
        [
            jnp.where(core == 0, act32[...], act_across[...]),
            jnp.where(core == 0, act_across[...], act32[...]),
        ]
    )
    gathered[z, y] = rows16.astype(jnp.bfloat16)
    for step in range(3):
        send(3 + step, gathered.at[z, y], gathered.at[z, y], peers[0][step])
    loads["cos", 0].wait()
    loads["sin", 0].wait()

    def pick_table(rows):
        cosine[rows, :] = jnp.where(kind, cos2[1, rows, :], cos2[0, rows, :])
        sine[rows, :] = jnp.where(kind, sin2[1, rows, :], sin2[0, rows, :])

    row_blocks(pick_table)
    store(cosine, cos_out)
    store(sine, sin_out)
    for slot_ in (3, 4, 5):
        copies[slot_].wait_recv()
    for step in range(3):
        send(6 + step, gathered.at[z], gathered.at[z], peers[1][step])

    copies[2].wait_recv()
    mods32[...] = jnp.zeros_like(mods32)
    fold32[...] = fold_other[...].astype(jnp.float32)
    for quarter in range(4):
        width = 896 if quarter < 3 else 768
        mods32[0:4, pl.ds(pl.multiple_of((1 - mod) * 3456 + quarter * 896, 128), width)] = fold32[
            4 * quarter : 4 * quarter + 4, 0:width
        ]
    mods32[0:4, pl.ds(pl.multiple_of(mod * 3456, 128), 3456)] = jnp.where(
        mod == 0, half32[0:4, 0:3456], half32[4:8, 0:3456]
    )
    modulation_out[...] = mods32[...].astype(jnp.bfloat16)
    for index in range(18):
        columns = slice(index * 384, (index + 1) * 384)
        per_token[:, columns] = jnp.dot(
            onehot, modulation_out[:, columns], preferred_element_type=jnp.float32
        ).astype(jnp.bfloat16)

    def piece(rows, index):
        return per_token[rows, index * WIDE : (index + 1) * WIDE].astype(jnp.float32)

    def first_input(rows):
        first[rows, :] = (norm[rows, :] * (1.0 + piece(rows, 1)) + piece(rows, 0)).astype(jnp.bfloat16)

    row_blocks(first_input)
    store(first, first_out)

    for index in range(9):
        loads["qkv", index].wait()
        columns = slice(index * 384, (index + 1) * 384)
        result = jnp.dot(first[...], qkv_w[:, columns], preferred_element_type=jnp.float32)
        if index < 6:
            projected[:, columns] = result
        else:
            value[:, (index - 6) * 384 : (index - 5) * 384] = result.astype(jnp.bfloat16)
    store(value, value_out)

    def head_norm(which, hat, result):
        base = which * WIDE

        def steps(rows):
            raw = projected[rows, base : base + WIDE]
            total = head_sum(raw * raw, heads[...])
            inverse = lax.rsqrt(total * (1.0 / 72.0) + EPSILON)
            inverse_out[which, rows, :] = inverse
            normed = raw * head_spread(inverse, heads[...])
            hat[rows, :] = normed
            scaled = normed * gains[which : which + 1, :]
            turned = scaled * cosine[rows, :] + swap_halves(scaled) * sine[rows, :]
            result[rows, :] = turned.astype(jnp.bfloat16)

        @pl.loop(0, 3)
        def _(index):
            steps(pl.ds(pl.multiple_of(index * 48, 16), 48))

    head_norm(0, query_hat, query)
    store(query_hat, query_hat_out)
    store(query, query_out)
    head_norm(1, key_hat, key)
    store(key_hat, key_hat_out)
    store(key, key_out)

    left = lax.broadcasted_iota(jnp.int32, (TOK, TOK), 0) // 36
    right = lax.broadcasted_iota(jnp.int32, (TOK, TOK), 1) // 36
    shut = jnp.where(kind | (left == right), 0.0, -1e30)
    context32[...] = jnp.zeros_like(context32)

    @pl.loop(0, 4)
    def _(group):
        for member in range(4):
            head = group * 4 + member
            window, mask = head_window(head)
            scores = inner_cols(query[:, window] * mask, key[:, window]) * (72**-0.5) + shut
            top = jnp.max(scores, axis=-1, keepdims=True)
            weight = jnp.exp(scores - top)
            weight = weight * (1.0 / jnp.sum(weight, axis=-1, keepdims=True))
            context32[:, window] += jnp.dot(
                weight.astype(jnp.bfloat16), value[:, window] * mask, preferred_element_type=jnp.float32
            )

    context[...] = context32[...].astype(jnp.bfloat16)
    store(context, context_out)
    for index in range(3):
        loads["out", index].wait()
        columns = slice(index * 384, (index + 1) * 384)
        attended[:, columns] = jnp.dot(context[...], out_w[:, columns], preferred_element_type=jnp.float32)
    store(attended, attended_out)

    def second_input(rows):
        total = tokens[rows, :].astype(jnp.float32) + piece(rows, 2) * attended[rows, :]
        middle[rows, :] = total
        normed = rms_norm(total)[0]
        second[rows, :] = (normed * (1.0 + piece(rows, 4)) + piece(rows, 3)).astype(jnp.bfloat16)

    row_blocks(second_input)
    store(middle, middle_out)
    store(second, second_out)
    for slot_ in (6, 7, 8):
        copies[slot_].wait_recv()
    store(gathered, gathered_out)
    for copy in sent:
        copy.wait_send()
    for copy in stores:
        copy.wait()


def forward(tokens, condition, segments, mod_weight, mod_bias, qkv_weight, gains, out_weight):
    cos_table, sin_table = rope_flat()
    vmem = pl.BlockSpec(memory_space=pltpu.VMEM)
    anywhere = pl.BlockSpec(memory_space=pl.ANY)
    low, full = jnp.bfloat16, jnp.float32
    wide_low = ((TOK, WIDE), low)
    wide_full = ((TOK, WIDE), full)
    outs = (
        [wide_low] * 3
        + [wide_full] * 2
        + [wide_low, wide_full, wide_full, wide_low, wide_low]
        + [wide_full] * 2
        + [((4, 4, 16, WIDE), low)]
        + [((2, TOK, 128), full), ((16, 6 * WIDE), low)]
    )
    scratch = [
        ((WIDE, 3456), low),
        ((WIDE, 3456), low),
        ((WIDE, WIDE), low),
        ((2, TOK, WIDE), full),
        ((2, TOK, WIDE), full),
        ((8, WIDE), full),
        ((8, WIDE), full),
        ((8, WIDE), full),
        ((8, WIDE), full),
        ((4, 4, 16, WIDE), low),
        ((8, 3584), full),
        ((16, 896), full),
        ((16, 896), low),
        ((16, 896), low),
        ((16, 6912), full),
        ((TOK, 6912), low),
        wide_full,
        wide_low,
        ((TOK, 2304), full),
        wide_low,
        wide_low,
        wide_low,
        wide_full,
        wide_full,
        wide_full,
        wide_low,
        wide_full,
        wide_full,
        wide_low,
        wide_full,
        wide_full,
        ((128, WIDE), low),
    ]
    return pl.pallas_call(
        forward_kernel,
        out_shape=[jax.ShapeDtypeStruct(*out) for out in outs],
        in_specs=[pl.BlockSpec(memory_space=pltpu.SMEM)] + [vmem] * 4 + [anywhere] * 5,
        out_specs=[anywhere] * 13 + [vmem] * 2,
        scratch_shapes=[pltpu.VMEM(*item) for item in scratch]
        + [
            pltpu.SemaphoreType.DMA((FWD_REMOTE,)),
            pltpu.SemaphoreType.DMA((FWD_REMOTE,)),
            pltpu.SemaphoreType.DMA((23,)),
            pltpu.SemaphoreType.DMA((16,)),
        ],
        compiler_params=pltpu.CompilerParams(
            collective_id=2, has_side_effects=True, vmem_limit_bytes=56 * 1024 * 1024
        ),
        cost_estimate=pl.CostEstimate(flops=2_000_000_000, bytes_accessed=30_000_000, transcendentals=0),
    )(
        segments,
        tokens,
        condition,
        mod_bias.reshape(1, -1),
        gains,
        jnp.asarray(cos_table),
        jnp.asarray(sin_table),
        mod_weight,
        qkv_weight,
        out_weight,
    )


def backward_kernel(
    segments,
    cotangent,
    tokens,
    modulation,
    condition,
    gains,
    inverses,
    acts,
    second_in,
    first_in,
    context_in,
    middle_in,
    attended_in,
    query_in,
    key_in,
    value_in,
    query_hat_in,
    key_hat_in,
    cos_in,
    sin_in,
    gate_weight,
    up_weight,
    down_weight,
    out_weight,
    qkv_weight,
    mod_weight,
    layer_out,
    tokens_out,
    gate_out,
    up_out,
    down_out,
    out_out,
    qkv_out,
    mod_out,
    special_out,
    condition_out,
    hidden_s,
    second_s,
    gbranch_s,
    ggate_s,
    gup_s,
    gatt_s,
    pick_x,
    pick_y,
    pick_z,
    acts_s,
    perm24,
    xt24,
    acc,
    heads,
    folds,
    per_token,
    branch,
    gsecond,
    attended,
    query,
    key,
    value,
    gcontext,
    gquery,
    gkey,
    gvalue,
    cosine,
    gain_sum,
    out_w,
    narrow_w,
    gmod,
    act_rows,
    fold32,
    fold_own,
    fold_other,
    other32,
    pair32,
    across32,
    rows32,
    gathered_a,
    gathered_b,
    product_own,
    product_send,
    product_other,
    final_other,
    special_other,
    part_own,
    part_other,
    *rest,
):
    bufs = [list(rest[7 * index : 7 * index + 7]) for index in range(len(JOBS))]
    for index in range(4):
        bufs[0][index] = bufs[4][index]
    xt9 = xt24.at[pl.ds(0, 576)]
    send_sem, recv_sem, local_sem, ring_sem = rest[7 * len(JOBS) :]
    gproj_s, middle = ggate_s, tokens_out
    place, core = position()
    mod = lax.axis_index("mod")
    partner = device_at(place, 1 - core)
    near = []
    for axis in range(3):
        here = place[axis]
        near.append(
            (here, lax.rem(here + 1, 4), lax.rem(here + 3, 4), lax.rem(here + 2, 4))
        )
    twin = moved(place, 0, near[0][3])

    ring_a, ring_b, ring_c = bufs[0][0], bufs[1][0], bufs[2][0]

    def ff_slots(slot):
        columns = pl.ds(pl.multiple_of(slot * CHUNK, CHUNK), CHUNK)
        return (
            ring_a.at[pl.ds(0, WIDE), columns],
            ring_b.at[pl.ds(0, WIDE), columns],
            ring_c.at[columns, :],
        )

    def ff_chunk(index, slot):
        columns = pl.ds(pl.multiple_of(index * CHUNK, CHUNK), CHUNK)
        sources = (gate_weight.at[:, columns], up_weight.at[:, columns], down_weight.at[columns, :])
        return [
            pltpu.make_async_copy(source, target, ring_sem.at[number, slot])
            for number, (source, target) in enumerate(zip(sources, ff_slots(slot)))
        ]

    wide_loads = {}

    def wide_load(name, index, source, target, number):
        copy = pltpu.make_async_copy(source, target, ring_sem.at[3, number])
        copy.start()
        wide_loads[name, index] = copy

    for index in range(2):
        for copy in ff_chunk(index, index):
            copy.start()
    wide_load("out", 0, out_weight, out_w, 0)
    third_w = ring_c.at[pl.ds(0, WIDE), :]
    fourth_w = ring_b.at[pl.ds(0, WIDE), :]

    def wide_parts(name, source, number):
        if number == 0:
            wide_load(name, 0, source.at[:, pl.ds(0, WIDE)], out_w, 0)
        elif number == 1:
            wide_load(name, 1, source.at[:, pl.ds(WIDE, WIDE)], third_w, 1)
        else:
            wide_load(name, 2, source.at[:, pl.ds(2 * WIDE, 1024)], fourth_w, 2)
            wide_load(name, 3, source.at[:, pl.ds(3328, 128)], narrow_w, 3)

    loads = {}

    def load(name, src, dst):
        copy = pltpu.make_async_copy(src, dst, local_sem.at[len(loads)])
        copy.start()
        loads[name] = copy

    own_rows, other_rows = pl.ds(0, TOK), pl.ds(TOK, TOK)
    load("second", second_in, second_s.at[own_rows])
    load("middle", middle_in, middle)
    load("attended", attended_in, attended)
    load("query", query_in, query)
    load("acts", acts, acts_s)
    load("key", key_in, key)
    load("value", value_in, value)

    barrier = pltpu.get_barrier_semaphore()
    pl.semaphore_signal(barrier, inc=1, device_id=partner, device_id_type=MESH)
    for axis in range(3):
        for far in near[axis][1:]:
            pl.semaphore_signal(
                barrier,
                inc=1,
                device_id=device_at(moved(place, axis, far), core),
                device_id_type=MESH,
            )
    pl.semaphore_signal(barrier, inc=1, device_id=device_at(twin, 1 - core), device_id_type=MESH)

    kind = segments[TOK - 1] == 0
    token = lax.broadcasted_iota(jnp.int32, (TOK, 16), 0)
    slot_of = lax.broadcasted_iota(jnp.int32, (TOK, 16), 1)
    onehot = (slot_of == jnp.where(kind, 0, token // 36)).astype(jnp.float32).astype(jnp.bfloat16)
    token_t = lax.broadcasted_iota(jnp.int32, (16, TOK), 1)
    slot_t = lax.broadcasted_iota(jnp.int32, (16, TOK), 0)
    onehot_t = (slot_t == jnp.where(kind, 0, token_t // 36)).astype(jnp.float32).astype(jnp.bfloat16)
    for index, block in enumerate((5, 4, 2, 1)):
        for third in range(3):
            to = index * WIDE + third * 384
            at = block * WIDE + third * 384
            per_token[:, to : to + 384] = jnp.dot(
                onehot, modulation[:, at : at + 384], preferred_element_type=jnp.float32
            ).astype(jnp.bfloat16)

    def piece(rows, block):
        base = (5, 4, 2, 1).index(block) * WIDE
        return per_token[rows, base : base + WIDE].astype(jnp.float32)

    def first_rows(rows):
        upstream = cotangent[rows, :].astype(jnp.float32)
        gbranch_s[rows, :] = (upstream * piece(rows, 5)).astype(jnp.bfloat16)
        zero = jnp.zeros((16, WIDE), jnp.float32)
        branch[rows, :] = zero
        gsecond[rows, :] = zero

    row_blocks(first_rows)
    gmod[...] = jnp.zeros_like(gmod)
    gain_sum[...] = jnp.zeros_like(gain_sum)
    pl.semaphore_wait(barrier, 11)

    def remote(src, dst, index, target):
        return pltpu.make_async_remote_copy(
            src_ref=src,
            dst_ref=dst,
            send_sem=send_sem.at[index],
            recv_sem=recv_sem.at[index],
            device_id=target,
            device_id_type=MESH,
        )

    sent = []
    pairs, landed = {}, set()

    def exchange(name, src, dst):
        copy = remote(src, dst, len(pairs), partner)
        copy.start()
        pairs[name] = copy

    exchange("gbranch", gbranch_s.at[own_rows], gbranch_s.at[other_rows])
    exchange("second", second_in, second_s.at[other_rows])

    def arrived(*names):
        for name in names:
            if name not in landed:
                landed.add(name)
                pairs[name].wait_recv()

    lane24 = lax.broadcasted_iota(jnp.int32, (192, 384), 1)
    row24 = lax.broadcasted_iota(jnp.int32, (192, 384), 0)
    perm24[...] = (
        (lane24 == row24 // 48 * 96 + lax.rem(row24, 48) + core * 48)
        .astype(jnp.float32)
        .astype(jnp.bfloat16)
    )
    heads[...] = head_rows()
    folded = lax.rem(lax.broadcasted_iota(jnp.int32, (128, WIDE), 1), 72)
    folds[...] = (
        (folded == lax.broadcasted_iota(jnp.int32, (128, WIDE), 0)).astype(jnp.float32).astype(jnp.bfloat16)
    )

    row = lax.broadcasted_iota(jnp.int32, (288, 640), 0)
    lane = lax.broadcasted_iota(jnp.int32, (288, 640), 1)
    unit, entry = row // 9, lax.rem(row, 9)
    for_x = unit // 16 * 9 + lax.rem(unit // 4, 4) * 144 + lax.rem(unit, 4) * 36 + entry + core * 18
    for_y = unit // 8 * 36 + lax.rem(unit // 4, 2) * 9 + lax.rem(unit, 4) * 144 + entry + core * 18
    for x_lo in range(2):
        pick_x[x_lo] = (lane == for_x + x_lo * 64).astype(jnp.float32).astype(jnp.bfloat16)
        pick_y[x_lo] = (lane == for_y + x_lo * 64).astype(jnp.float32).astype(jnp.bfloat16)
    row = lax.broadcasted_iota(jnp.int32, (80, 256), 0)
    lane = lax.broadcasted_iota(jnp.int32, (80, 256), 1)
    unit = row // 9
    for_z = unit // 2 * 36 + lax.rem(unit, 2) * 9 + lax.rem(row, 9) + core * 18
    for block in range(8):
        pick_z[block] = (
            ((row < 72) & (lane == for_z + block * 16)).astype(jnp.float32).astype(jnp.bfloat16)
        )

    def pick9(part, stack):
        if part == 2:
            for z in range(4):
                halves = []
                for x_lo in range(2):
                    block = x_lo * 4 + z
                    rows = inner_cols(pick_z[block], stack[:, block * 128 : block * 128 + 256])
                    halves.append(rows[0:72])
                xt9[z * 144 : (z + 1) * 144, :] = jnp.concatenate(halves).astype(jnp.bfloat16)
            return
        table = (pick_x, pick_y)[part]
        low = inner_cols(table[0], stack[:, 0:640])
        high = inner_cols(table[1], stack[:, 512:WIDE])
        for value_ in range(4):
            if part == 0:
                half = (low, high)[value_ % 2]
                rows = half[value_ // 2 * 144 : value_ // 2 * 144 + 144]
            else:
                at = slice(value_ * 72, (value_ + 1) * 72)
                rows = jnp.concatenate([low[at], high[at]])
            xt9[value_ * 144 : (value_ + 1) * 144, :] = rows.astype(jnp.bfloat16)

    def pick24(part):
        def block_rows(block):
            columns = pl.ds(pl.multiple_of(block * 384, 128), 384)
            return inner_cols(perm24[...], hidden_s[:, columns])

        def put(unit, rows):
            xt24[pl.ds(pl.multiple_of(unit * 24, 16), 48), :] = rows.astype(jnp.bfloat16)

        def unit_rows(rows, y, x_hi):
            at = (y * 2 + x_hi) * 24
            return rows[at : at + 24]

        @pl.loop(0, 2)
        def _(x_lo):
            blocks = [block_rows(x_lo * 4 + z) for z in range(4)]
            for z in range(4):
                for y in range(4):
                    for x_hi in range(2):
                        upper = unit_rows(blocks[z], y, x_hi)
                        if part == 0 and y % 2 == 0:
                            unit = (x_hi * 2 + x_lo) * 16 + z * 4 + y
                            put(unit, jnp.concatenate([upper, unit_rows(blocks[z], y + 1, x_hi)]))
                        elif part == 1 and z % 2 == 0:
                            unit = y * 16 + (x_lo * 2 + x_hi) * 4 + z
                            put(unit, jnp.concatenate([upper, unit_rows(blocks[z + 1], y, x_hi)]))
                        elif part == 2 and x_hi == 0:
                            unit = z * 16 + y * 4 + x_lo * 2
                            put(unit, jnp.concatenate([upper, unit_rows(blocks[z], y, 1)]))

    def multiply(job, part, left, right):
        width = JOBS[job][2]
        own_view(job, part)[...] = jnp.dot(
            left[...], right[:, part * width : (part + 1) * width], preferred_element_type=jnp.float32
        ).astype(jnp.bfloat16)

    copies = {}
    drained = set()

    def begin(job, part, slot, src, dst, target):
        index = PARTNER_COPIES + (job * 3 + part) * COPIES + slot
        copy = remote(src, dst, index, target)
        copy.start()
        copies[job, part, slot] = copy

    def arrive(job, part, *slots):
        for slot in slots:
            copies[job, part, slot].wait_recv()

    def ring(part, phase):
        axis = AXES[part][phase]
        here, right, left, opposite = near[axis]
        return (
            here,
            right,
            left,
            opposite,
            device_at(moved(place, axis, right), core),
            device_at(moved(place, axis, left), core),
            device_at(moved(place, axis, opposite), core),
        )

    def sent_out(job, part, *slots):
        for slot in slots:
            if (job, part, slot) not in drained:
                drained.add((job, part, slot))
                copies[job, part, slot].wait_send()

    def own_view(job, part):
        base, width = bufs[job][0], JOBS[job][2]
        if JOBS[job][0] == "down":
            return base.at[:, pl.ds(part * width, width)]
        return base.at[pl.ds(part * 576, 576), pl.ds(0, width)]

    def first_send(job, part):
        half, whole = bufs[job][1:3]
        own = own_view(job, part)
        big = 16 * JOBS[job][1]
        cut = sixteen(big // 2)
        here, right, left, opposite, to_right, to_left, _ = ring(part, 0)

        full = pl.ds(0, JOBS[job][2])

        def rows(chunk, start, count):
            return own.at[pl.ds(pl.multiple_of(chunk * big + start, 16), count)]

        begin(job, part, 0, rows(opposite, 0, cut), half.at[part, pl.ds(0, cut), full], to_right)
        begin(job, part, 1, rows(opposite, cut, big - cut), half.at[part, pl.ds(cut, big - cut), full], to_left)
        begin(job, part, 2, rows(right, cut, big - cut), whole.at[part, 0, pl.ds(cut, big - cut), full], to_right)
        begin(job, part, 3, rows(left, 0, cut), whole.at[part, 1, pl.ds(0, cut), full], to_left)

    def first_add(job, part):
        half, whole = bufs[job][1:3]
        own = own_view(job, part)
        _, each, width, lanes, _ = JOBS[job]
        big = 16 * each
        cut = sixteen(big // 2)
        here, right, left, opposite, to_right, to_left, _ = ring(part, 0)
        for slot, chunk, start, count, target, side in (
            (0, right, 0, cut, to_right, 0),
            (1, left, cut, big - cut, to_left, 1),
        ):
            arrive(job, part, slot)
            rows = pl.ds(pl.multiple_of(chunk * big + start, 16), count)

            @pl.loop(0, width // 128)
            def _(step):
                columns = pl.ds(pl.multiple_of(step * 128, 128), 128)
                total = own[rows, columns].astype(jnp.float32) + half[
                    part, pl.ds(start, count), columns
                ].astype(jnp.float32)
                own[rows, columns] = total.astype(jnp.bfloat16)

            begin(
                job,
                part,
                4 + side,
                own.at[rows],
                whole.at[part, side, pl.ds(start, count), pl.ds(0, width)],
                target,
            )

    def second_send(job, part):
        _, _, whole, mid, mid_half, mid_whole, _ = bufs[job]
        own = own_view(job, part)
        _, each, width, lanes, cut = JOBS[job]
        big, small = 16 * each, 4 * each
        padded = sixteen(small)
        here, right, left, opposite, to_right, to_left, _ = ring(part, 0)
        arrive(job, part, 2, 3, 4, 5)
        if JOBS[job][0] == "qkv":
            sent_out(0, part, 6, 7, 8, 9, 10, 11)
        rows = pl.ds(pl.multiple_of(here * big, 16), big)

        @pl.loop(0, width // 128)
        def _(step):
            columns = pl.ds(pl.multiple_of(step * 128, 128), 128)
            total = (
                own[rows, columns].astype(jnp.float32)
                + whole[part, 0, :, columns].astype(jnp.float32)
                + whole[part, 1, :, columns].astype(jnp.float32)
            )
            if part == 2 and each == 9:
                for x_lo in range(2):
                    for y in range(4):
                        piece_at = x_lo * 72 + y * 18
                        acc[y * 36 + x_lo * 18 : y * 36 + x_lo * 18 + 18, :] = total[piece_at : piece_at + 18]
            else:
                acc[pl.ds(0, big), :] = total
            for chunk in range(4):
                line = line_of(AXES[part][1], chunk)
                mid[part, chunk, :, columns] = acc[pl.ds(line * small, padded), :].astype(jnp.bfloat16)

        here, right, left, opposite, to_right, to_left, _ = ring(part, 1)
        low, high = pl.ds(0, cut), pl.ds(cut, width - cut)
        begin(job, part, 6, mid.at[part, opposite, :, low], mid_half.at[part, :, low], to_right)
        begin(job, part, 7, mid.at[part, opposite, :, high], mid_half.at[part, :, high], to_left)
        begin(job, part, 8, mid.at[part, right, :, high], mid_whole.at[part, 0, :, high], to_right)
        begin(job, part, 9, mid.at[part, left, :, low], mid_whole.at[part, 1, :, low], to_left)

    def second_add(job, part):
        _, _, _, mid, mid_half, mid_whole, _ = bufs[job]
        _, each, width, lanes, cut = JOBS[job]
        here, right, left, opposite, to_right, to_left, _ = ring(part, 1)
        for slot, chunk, start, count, target, side in (
            (6, right, 0, cut, to_right, 0),
            (7, left, cut, width - cut, to_left, 1),
        ):
            arrive(job, part, slot)

            @pl.loop(0, count // 128)
            def _(step):
                columns = pl.ds(pl.multiple_of(start + step * 128, 128), 128)
                total = mid[part, chunk, :, columns].astype(jnp.float32) + mid_half[
                    part, :, columns
                ].astype(jnp.float32)
                mid[part, chunk, :, columns] = total.astype(jnp.bfloat16)

            columns = pl.ds(start, count)
            begin(
                job,
                part,
                10 + side,
                mid.at[part, chunk, :, columns],
                mid_whole.at[part, side, :, columns],
                target,
            )

    def third_send(job, part):
        _, _, _, mid, _, mid_whole, last = bufs[job]
        _, each, width, lanes, cut = JOBS[job]
        small = sixteen(4 * each)
        padded = sixteen(each)
        here = ring(part, 1)[0]
        arrive(job, part, 8, 9, 10, 11)

        @pl.loop(0, width // 128)
        def _(step):
            columns = pl.ds(pl.multiple_of(step * 128, 128), 128)
            acc[pl.ds(0, small), :] = (
                mid[part, here, :, columns].astype(jnp.float32)
                + mid_whole[part, 0, :, columns].astype(jnp.float32)
                + mid_whole[part, 1, :, columns].astype(jnp.float32)
            )
            for chunk in range(4):
                line = line_of(AXES[part][2], chunk)
                last[part, chunk, :, columns] = acc[pl.ds(line * each, padded), :].astype(jnp.bfloat16)

        here, right, left, opposite, to_right, to_left, to_opposite = ring(part, 2)
        for slot, chunk, target in ((0, right, to_right), (1, left, to_left), (2, opposite, to_opposite)):
            begin(job, part, 12 + slot, last.at[part, chunk], last.at[part, 4 + slot], target)

    mod_base = PARTNER_COPIES + 3 * COPIES * len(JOBS)
    mod_copies = {}

    def mod_send(slot, src, dst, target):
        copy = remote(src, dst, mod_base + slot, target)
        copy.start()
        sent.append(copy)
        mod_copies[slot] = copy

    def mod_arrive(*slots):
        for slot in slots:
            mod_copies[slot].wait_recv()

    def mod_pair():
        for quarter in range(4):
            fold32[4 * quarter : 4 * quarter + 4, :] = gmod[
                1 - mod, 0:4, quarter * 896 : (quarter + 1) * 896
            ]
        fold_own[...] = fold32[...].astype(jnp.bfloat16)
        mod_send(0, fold_own, fold_other, device_at(twin, core))

    def mod_cores():
        mod_arrive(0)
        fold32[...] = fold_other[...].astype(jnp.float32)
        for quarter in range(4):
            other32[0:4, quarter * 896 : (quarter + 1) * 896] = fold32[4 * quarter : 4 * quarter + 4, :]
        own, other = gmod[mod, 0:4, :], other32[0:4, :]
        pair32[0:4, :] = jnp.where(mod == 0, own, other)
        pair32[4:8, :] = jnp.where(mod == 0, other, own)
        there = pl.ds(pl.multiple_of((1 - core) * 1792, 128), 1792)
        mod_send(1, pair32.at[:, there], across32, partner)

    def condition_part():
        first = pair32[:, 0:WIDE].astype(jnp.bfloat16)
        wide_loads["mod", 0].wait()
        part_own[...] = inner_cols(first, out_w[...])
        wide_loads["mod", 1].wait()
        part_own[...] += inner_cols(pair32[:, WIDE : 2 * WIDE].astype(jnp.bfloat16), third_w[...])
        wide_loads["mod", 2].wait()
        wide_loads["mod", 3].wait()
        part_own[...] += inner_cols(pair32[:, 2 * WIDE : 3328].astype(jnp.bfloat16), fourth_w[...])
        part_own[...] += inner_cols(pair32[:, 3328:3456].astype(jnp.bfloat16), narrow_w[...])
        mod_send(2, part_own, part_other, device_at(twin, core))

    def mod_gather_first():
        mod_arrive(1)
        here = pl.ds(pl.multiple_of(core * 1792, 128), 1792)
        own, other = pair32[:, here], across32[...]
        rows32[0:8, :] = jnp.where(core == 0, own, other)
        rows32[8:16, :] = jnp.where(core == 0, other, own)
        _, y, z = place
        gathered_a[z, y] = rows32[:, 0:896].astype(jnp.bfloat16)
        gathered_b[z, y] = rows32[:, 896:1792].astype(jnp.bfloat16)
        for step in range(3):
            to_y = device_at(moved(place, 1, near[1][1 + step]), core)
            to_z = device_at(moved(place, 2, near[2][1 + step]), core)
            mod_send(3 + step, gathered_a.at[z, y], gathered_a.at[z, y], to_y)
            mod_send(6 + step, gathered_b.at[z, y], gathered_b.at[z, y], to_z)

    def mod_gather_second():
        _, y, z = place
        mod_arrive(3, 4, 5)
        for step in range(3):
            to_z = device_at(moved(place, 2, near[2][1 + step]), core)
            mod_send(9 + step, gathered_a.at[z], gathered_a.at[z], to_z)
        mod_arrive(6, 7, 8)
        for step in range(3):
            to_y = device_at(moved(place, 1, near[1][1 + step]), core)
            mod_send(12 + step, gathered_b.at[:, y], gathered_b.at[:, y], to_y)

    def mod_table():
        x, y, z = place
        row = lax.broadcasted_iota(jnp.int32, (48, WIDE), 0)
        lane = lax.broadcasted_iota(jnp.int32, (48, WIDE), 1)
        line = lax.broadcasted_iota(jnp.int32, (48, 256), 0)
        slot = lax.rem(lax.broadcasted_iota(jnp.int32, (48, 256), 1), 4)
        ones = (line == 40) | ((line == 41) & (slot == 0)) | ((line == 42) & (slot == 1))
        for index in range(2):
            half = lax.rem(lax.rem(x, 2) + index, 2)
            start = (half * 32 + z * 8 + y * 2) * 18
            pick = ((row < 36) & (lane == row + start)).astype(jnp.float32).astype(jnp.bfloat16)
            rows = inner_cols(pick, acts_s[...])
            act_rows[index] = (rows + ones.astype(jnp.float32)).astype(jnp.bfloat16)

    def mod_product():
        mod_arrive(9, 10, 11)
        mod_arrive(12, 13, 14)
        for side, gathered in ((0, gathered_a), (1, gathered_b)):
            columns = slice(side * 896, (side + 1) * 896)
            rows = gathered[...].reshape(256, 896)
            product_send[:, columns] = jnp.dot(
                act_rows[1], rows, preferred_element_type=jnp.float32
            ).astype(jnp.bfloat16)
            product_own[:, columns] = jnp.dot(act_rows[0], rows, preferred_element_type=jnp.float32)
        x = place[0]
        beside = moved(place, 0, x + 1 - 2 * lax.rem(x, 2))
        mod_send(15, product_send, product_other, device_at(beside, core))

    def mod_sum():
        mod_arrive(15)
        product_own[...] = product_own[...] + product_other[...].astype(jnp.float32)
        mod_send(16, product_own, final_other, partner)
        special = product_own.at[pl.ds(40, 8)]
        mod_send(17, special, special_other.at[core], device_at(twin, core))
        mod_send(18, special, special_other.at[core], device_at(twin, 1 - core))

    def mod_finish():
        here = pl.ds(pl.multiple_of(core * 1792, 128), 1792)
        there = pl.ds(pl.multiple_of((1 - core) * 1792, 128), 1792)
        mod_arrive(2)
        total = part_own[...] + part_other[...]
        raw = condition[...].astype(jnp.float32)
        condition_out[...] = jnp.where(mod == 0, total[0:4], total[4:8]) * silu_slope(raw)
        mod_arrive(16)
        for source, columns in ((product_own, here), (final_other, there)):
            mod_out[:, columns] = jnp.where(core == 0, source[0:18, :], source[18:36, :])
            special_out[mod, :, columns] = source[40:48, :]
        mod_arrive(17, 18)
        for side in range(2):
            special_out[1 - mod, :, side * 1792 : (side + 1) * 1792] = special_other[side]

    outs = {"gate": gate_out, "up": up_out, "down": down_out, "out": out_out, "qkv": qkv_out}

    def finish(job, part):
        last = bufs[job][6]
        _, each, width, lanes, cut = JOBS[job]
        here = ring(part, 2)[0]
        arrive(job, part, 12, 13, 14)

        @pl.loop(0, width // 128)
        def _(step):
            to = pl.multiple_of(step * 128, 128)
            columns = pl.ds(to, 128)
            total = last[part, here, :, columns].astype(jnp.float32)
            for slot in range(3):
                total = total + last[part, 4 + slot, :, columns].astype(jnp.float32)
            outs[JOBS[job][0]][:, pl.ds(pl.multiple_of(part * width + to, 128), 128)] = total[:each]

    gate_job, up_job, down_job, out_job, qkv_job = range(5)

    def slot_sum(block, source):
        for third in range(3):
            columns = slice(third * 384, (third + 1) * 384)
            high, low = split_two(source[:, columns])
            total = jnp.dot(onehot_t, high, preferred_element_type=jnp.float32) + jnp.dot(
                onehot_t, low, preferred_element_type=jnp.float32
            )
            base = block % 3 * WIDE + third * 384
            gmod[block // 3, :, base : base + 384] = (
                total[0:8].astype(jnp.bfloat16).astype(jnp.float32)
            )

    def stages(stage, job):
        for part in range(3):
            stage(job, part)

    def ff_products(part):
        pick9(part, second_s)
        arrived("ggate", "gup")
        multiply(gate_job, part, xt9, ggate_s)
        first_send(gate_job, part)
        multiply(up_job, part, xt9, gup_s)
        first_send(up_job, part)

    loads["second"].wait()

    @pl.loop(0, 6)
    def _(index):
        slot = lax.rem(index, 2)
        for copy in ff_chunk(index, slot):
            copy.wait()
        gate_w, up_w, down_w = ff_slots(slot)
        columns = pl.ds(pl.multiple_of(index * CHUNK, CHUNK), CHUNK)
        gate_linear = jnp.dot(second_s[0:TOK, :], gate_w[...], preferred_element_type=jnp.float32)
        up_linear = jnp.dot(second_s[0:TOK, :], up_w[...], preferred_element_type=jnp.float32)
        ghidden = inner_cols(gbranch_s[0:TOK, :], down_w[...])
        logistic = jax.nn.sigmoid(gate_linear)
        gate_act = gate_linear * logistic
        hidden = (gate_act * up_linear).astype(jnp.bfloat16)
        slope = logistic * (1.0 + gate_linear * (1.0 - logistic))
        ggate = (ghidden * up_linear * slope).astype(jnp.bfloat16)
        gup = (ghidden * gate_act).astype(jnp.bfloat16)
        hidden_s[0:TOK, columns] = hidden
        ggate_s[0:TOK, columns] = ggate
        gup_s[0:TOK, columns] = gup
        branch[...] += jnp.dot(hidden, down_w[...], preferred_element_type=jnp.float32)
        gsecond[...] += inner_cols(ggate, gate_w[...])
        gsecond[...] += inner_cols(gup, up_w[...])

        @pl.when(index + 2 < 6)
        def _():
            for copy in ff_chunk(index + 2, slot):
                copy.start()

    exchange("ggate", ggate_s.at[own_rows, pl.ds(0, HID)], ggate_s.at[other_rows, pl.ds(0, HID)])
    exchange("gup", gup_s.at[own_rows], gup_s.at[other_rows])
    exchange("hidden", hidden_s.at[own_rows], hidden_s.at[other_rows])
    loads["middle"].wait()
    loads["attended"].wait()

    def second_rows(rows):
        upstream = cotangent[rows, :].astype(jnp.float32)
        kept = middle[rows, :]
        result = branch[rows, :]
        layer_out[rows, :] = (kept + piece(rows, 5) * result).astype(jnp.bfloat16)
        branch[rows, :] = upstream * result
        normed, inverse = rms_norm(kept)
        grad = gsecond[rows, :]
        gquery[rows, :] = grad * normed
        total = upstream + norm_back(grad * (1.0 + piece(rows, 4)), normed, inverse)
        middle[rows, :] = total
        attended_row = attended[rows, :]
        attended[rows, :] = total * attended_row
        gatt_s[rows, :] = (total * piece(rows, 2)).astype(jnp.bfloat16)

    row_blocks(second_rows)
    arrived("second")
    for part in range(3):
        ff_products(part)
    exchange("gatt", gatt_s.at[own_rows], gatt_s.at[other_rows])
    context_s = second_s
    load("context", context_in, context_s.at[own_rows])

    arrived("gbranch", "hidden")
    for part in range(3):
        pick24(part)
        multiply(down_job, part, xt24, gbranch_s)
        first_send(down_job, part)
    arrived("gatt")
    exchange("context", context_in, context_s.at[other_rows])

    wide_loads["out", 0].wait()
    gcontext[...] = inner_cols(gatt_s[0:TOK, :], out_w[...]).astype(jnp.bfloat16)
    wide_parts("qkv", qkv_weight, 0)
    slot_sum(5, branch)
    slot_sum(4, gquery)
    slot_sum(3, gsecond)
    slot_sum(2, attended)
    load("query_hat", query_hat_in, branch)
    load("key_hat", key_hat_in, attended)
    load("cos", cos_in, cosine)
    load("sin", sin_in, gsecond)
    query_hat, key_hat, sine = branch, attended, gsecond

    loads["context"].wait()
    arrived("context")
    for part in range(3):
        pick9(part, context_s)
        multiply(out_job, part, xt9, gatt_s)
        first_send(out_job, part)
    stages(first_add, gate_job)
    stages(first_add, up_job)

    gquery[...] = jnp.zeros_like(gquery)
    gkey[...] = jnp.zeros_like(gkey)
    gvalue[...] = jnp.zeros_like(gvalue)
    for name in ("query", "key", "value"):
        loads[name].wait()

    def attention_group(group):
        @pl.loop(0, 2)
        def _(pair):
            left = lax.broadcasted_iota(jnp.int32, (TOK, TOK), 0) // 36
            right = lax.broadcasted_iota(jnp.int32, (TOK, TOK), 1) // 36
            shut = jnp.where(kind | (left == right), 0.0, -1e30)
            for member in range(2):
                window, mask = head_window(group * 4 + pair * 2 + member)
                query_w, key_w = query[:, window] * mask, key[:, window] * mask
                value_w, grad_w = value[:, window], gcontext[:, window] * mask
                scores = inner_cols(query_w, key_w) * (72**-0.5) + shut
                weight = jnp.exp(scores - jnp.max(scores, axis=-1, keepdims=True))
                weight = weight * (1.0 / jnp.sum(weight, axis=-1, keepdims=True))
                gattention = inner_cols(grad_w, value_w)
                gvalue[:, window] += inner_rows(weight.astype(jnp.bfloat16), grad_w)
                dots = jnp.sum(weight * gattention, axis=-1, keepdims=True)
                gscores = (weight * (gattention - dots)).astype(jnp.bfloat16)
                gquery[:, window] += jnp.dot(gscores, key_w, preferred_element_type=jnp.float32)
                gkey[:, window] += inner_rows(gscores, query_w)

    attention_group(0)
    stages(second_send, gate_job)
    attention_group(1)
    stages(second_send, up_job)
    stages(first_add, down_job)
    attention_group(2)
    stages(second_add, gate_job)
    stages(first_add, out_job)
    attention_group(3)
    stages(second_add, up_job)
    stages(second_send, down_job)

    for part in range(3):
        sent_out(down_job, part, 0, 1, 2, 3, 4, 5)
        sent_out(up_job, part, 0, 1, 2, 3, 4, 5)
    wide_parts("qkv", qkv_weight, 1)
    wide_parts("qkv", qkv_weight, 2)
    pairs["ggate"].wait_send()

    def project_back(which, grads, hat):
        base = which * WIDE

        @pl.loop(0, 3)
        def _(index):
            rows = pl.ds(pl.multiple_of(index * 48, 16), 48)
            grad = grads[rows, :] * (72**-0.5)
            normed = hat[rows, :]
            turned = grad * cosine[rows, :] - swap_halves(grad) * sine[rows, :]
            gain_sum[which] += jnp.sum((turned * normed).reshape(6, 8, WIDE), axis=0)
            scaled = turned * gains[which : which + 1, :]
            inverse = inverses[which, rows, :]
            mean = head_sum(scaled * normed, heads[...]) * (1.0 / 72.0)
            raw = scaled * head_spread(inverse, heads[...]) - normed * head_spread(
                inverse * mean, heads[...]
            )
            gproj_s[rows, base : base + WIDE] = raw.astype(jnp.bfloat16)

    def exchange_projected(part):
        columns = pl.ds(part * WIDE, WIDE)
        exchange("gproj%d" % part, gproj_s.at[own_rows, columns], gproj_s.at[other_rows, columns])

    def value_rows(rows):
        gproj_s[rows, 2 * WIDE : 3 * WIDE] = gvalue[rows, :].astype(jnp.bfloat16)

    row_blocks(value_rows)
    exchange_projected(2)
    for name in ("query_hat", "key_hat", "cos", "sin"):
        loads[name].wait()
    project_back(0, gquery, query_hat)
    exchange_projected(0)
    arrived("gproj2")
    first_s = second_s
    load("first", first_in, first_s.at[own_rows])
    exchange("first", first_in, first_s.at[other_rows])
    project_back(1, gkey, key_hat)
    exchange_projected(1)
    loads["first"].wait()
    arrived("first")
    for part in (2, 0, 1):
        pick9(part, first_s)
        if part != 2:
            arrived("gproj%d" % part)
        sent_out(gate_job, part, 0, 1, 2, 3, 4, 5)
        multiply(qkv_job, part, xt9, gproj_s)
        first_send(qkv_job, part)

    gfirst, scaled_first = gquery, gkey
    wide_loads["qkv", 0].wait()
    gfirst[...] = inner_cols(gproj_s[0:TOK, 0:WIDE], out_w[...])
    wide_parts("mod", mod_weight, 0)
    wide_loads["qkv", 1].wait()
    gfirst[...] += inner_cols(gproj_s[0:TOK, WIDE : 2 * WIDE], third_w[...])
    wide_parts("mod", mod_weight, 1)
    wide_loads["qkv", 2].wait()
    wide_loads["qkv", 3].wait()
    gfirst[...] += inner_cols(gproj_s[0:TOK, 2 * WIDE : 3328], fourth_w[...])
    gfirst[...] += inner_cols(gproj_s[0:TOK, 3328:3456], narrow_w[...])
    wide_parts("mod", mod_weight, 2)

    def last_rows(rows):
        normed, inverse = rms_norm(tokens[rows, :].astype(jnp.float32))
        grad = gfirst[rows, :]
        scaled_first[rows, :] = grad * normed
        tokens_out[rows, :] = middle[rows, :] + norm_back(
            grad * (1.0 + piece(rows, 1)), normed, inverse
        )

    row_blocks(last_rows)
    slot_sum(0, gfirst)
    slot_sum(1, scaled_first)
    for which in range(2):
        high, low = split_two(gain_sum[which])
        total = jnp.sum(inner_cols(high, folds[...]) + inner_cols(low, folds[...]), axis=0, keepdims=True)
        gmod[0, which : which + 1, 3456:3584] = total
    mod_pair()
    stages(second_add, down_job)
    stages(third_send, gate_job)
    stages(first_add, qkv_job)
    mod_cores()
    condition_part()
    stages(second_send, out_job)
    mod_gather_first()
    stages(third_send, up_job)
    stages(third_send, down_job)
    loads["acts"].wait()
    mod_table()
    stages(second_add, out_job)
    mod_gather_second()
    stages(second_send, qkv_job)
    stages(finish, gate_job)
    stages(third_send, out_job)
    stages(second_add, qkv_job)
    mod_product()
    stages(finish, up_job)
    stages(finish, down_job)
    stages(third_send, qkv_job)
    mod_sum()
    stages(finish, out_job)
    stages(finish, qkv_job)
    mod_finish()
    for name, copy in pairs.items():
        if name != "ggate":
            copy.wait_send()
    for (job, part, slot) in list(copies):
        sent_out(job, part, slot)
    for copy in sent:
        copy.wait_send()


def write_kernel(*refs):
    count = len(refs) // 2
    for source, target in zip(refs[:count], refs[count:]):
        if len(source.shape) == 3:
            target[...] = source[:, 0:1, 0:3456]
        else:
            target[...] = source[:, 0 : target.shape[1]]


def backward(
    cotangent, tokens, condition, segments, gains, saved, gate_weight, up_weight, down_weight, out_weight, qkv_weight, mod_weight
):
    (query, key, value, query_hat, key_hat, context, attended, middle, first, second, cosine, sine, acts, inverses, modulation) = saved
    vmem = pl.BlockSpec(memory_space=pltpu.VMEM)
    anywhere = pl.BlockSpec(memory_space=pl.ANY)
    low, full = jnp.bfloat16, jnp.float32
    wide_low, wide_full = ((TOK, WIDE), low), ((TOK, WIDE), full)
    outs = (
        [wide_low, wide_full]
        + [((each, 3 * width), full) for _, each, width, _, _ in JOBS]
        + [((18, 3584), full), ((2, 8, 3584), full), ((4, WIDE), full)]
    )
    scratch = [
        ((PAIR, HID), low),
        ((PAIR, WIDE), low),
        ((PAIR, WIDE), low),
        ((PAIR, 3456), low),
        ((PAIR, HID), low),
        ((PAIR, WIDE), low),
        ((2, 288, 640), low),
        ((2, 288, 640), low),
        ((8, 80, 256), low),
        ((256, WIDE), low),
        ((192, 384), low),
        ((1536, PAIR), low),
        ((400, 128), full),
        ((128, WIDE), low),
        ((128, WIDE), low),
        ((TOK, 4 * WIDE), low),
        wide_full,
        wide_full,
        wide_full,
        wide_low,
        wide_low,
        wide_low,
        wide_low,
        wide_full,
        wide_full,
        wide_full,
        wide_full,
        ((2, 8, WIDE), full),
        ((WIDE, WIDE), low),
        ((WIDE, 128), low),
        ((2, 8, 3584), full),
        ((2, 48, 256), low),
        ((16, 896), full),
        ((16, 896), low),
        ((16, 896), low),
        ((8, 3584), full),
        ((8, 3584), full),
        ((8, 1792), full),
        ((16, 1792), full),
        ((4, 4, 16, 896), low),
        ((4, 4, 16, 896), low),
        ((48, 1792), full),
        ((48, 1792), low),
        ((48, 1792), low),
        ((48, 1792), full),
        ((2, 8, 1792), full),
        ((8, WIDE), full),
        ((8, WIDE), full),
    ]
    sums = {
        "gate": (16, 128),
        "up": (1728, 1024),
        "down": (1536, WIDE),
        "out": (1728, 384),
        "qkv": (1728, WIDE),
    }
    for name, each, width, _, _ in JOBS:
        big, small, tiny = 16 * each, sixteen(4 * each), sixteen(each)
        unused = name == "gate"
        scratch += [
            (sums[name], low),
            ((1, 16, 128) if unused else (3, big, width), low),
            ((1, 1, 16, 128) if unused else (3, 2, big, width), low),
            ((1, 1, 16, 128) if unused else (3, 4, small, width), low),
            ((3, small, width), low),
            ((3, 2, small, width), low),
            ((3, 7, tiny, width), low),
        ]
    count = PARTNER_COPIES + 3 * COPIES * len(JOBS) + MOD_COPIES
    results = pl.pallas_call(
        backward_kernel,
        out_shape=[jax.ShapeDtypeStruct(*out) for out in outs],
        in_specs=[pl.BlockSpec(memory_space=pltpu.SMEM)] + [vmem] * 6 + [anywhere] * 19,
        out_specs=[vmem] * 10,
        scratch_shapes=[pltpu.VMEM(*item) for item in scratch]
        + [
            pltpu.SemaphoreType.DMA((count,)),
            pltpu.SemaphoreType.DMA((count,)),
            pltpu.SemaphoreType.DMA((13,)),
            pltpu.SemaphoreType.DMA((4, 4)),
        ],
        compiler_params=pltpu.CompilerParams(
            collective_id=1, has_side_effects=True, vmem_limit_bytes=64 * 1024 * 1024 - 65536
        ),
        cost_estimate=pl.CostEstimate(
            flops=12_000_000_000, bytes_accessed=50_000_000, transcendentals=0
        ),
    )(
        segments,
        cotangent,
        tokens,
        modulation,
        condition,
        gains,
        inverses,
        acts.reshape(256, WIDE),
        second,
        first,
        context,
        middle,
        attended,
        query,
        key,
        value,
        query_hat,
        key_hat,
        cosine,
        sine,
        gate_weight,
        up_weight,
        down_weight,
        out_weight,
        qkv_weight,
        mod_weight,
    )
    special = results[8]
    kept = list(results[:8]) + [results[9]]
    shapes = [
        jax.ShapeDtypeStruct((item.shape[0], min(item.shape[1], 3456)), item.dtype) for item in kept
    ]
    written = pl.pallas_call(
        write_kernel,
        out_shape=shapes + [jax.ShapeDtypeStruct((2, 1, 3456), full)],
        in_specs=[vmem] * 10,
        out_specs=[vmem] * 10,
    )(*kept, special)
    return written, special


def body(
    tokens,
    condition,
    segments,
    mod_weight,
    mod_bias,
    qkv_weight,
    query_gain,
    key_gain,
    out_weight,
    gate_weight,
    up_weight,
    down_weight,
    cotangent,
):
    gains = jnp.tile(jnp.stack([query_gain, key_gain]), (1, 16))
    saved = forward(tokens, condition, segments, mod_weight, mod_bias, qkv_weight, gains, out_weight)
    written, special = backward(
        cotangent,
        tokens,
        condition,
        segments,
        gains,
        saved,
        gate_weight,
        up_weight,
        down_weight,
        out_weight,
        qkv_weight,
        mod_weight,
    )
    layer_out, grad_tokens, gate, up, down, out, qkv, mod_rows, grad_condition, bias = written
    gain_rows = special[0, 1:3, 3456:3528] + special[1, 1:3, 3456:3528]
    return (
        layer_out,
        grad_tokens,
        grad_condition,
        mod_rows,
        bias.reshape(-1),
        qkv,
        gain_rows[0],
        gain_rows[1],
        out,
        gate,
        up,
        down,
    )


def solution(mesh):
    placed = (
        P(("dp", "mod"), None),
        P(("dp", "mod"), None),
        P(("dp", "mod")),
        P(None, "mod"),
        P("mod"),
        P(),
        P(),
        P(),
        P(),
        P(),
        P(),
        P(),
        P(("dp", "mod"), None),
    )
    return jax.shard_map(
        body,
        mesh=mesh,
        in_specs=placed,
        out_specs=(
            P(("dp", "mod"), None),
            P(("dp", "mod"), None),
            P(("dp", "mod"), None),
            P("dp", "mod"),
            P(),
            P(("dp", "mod"), None),
            P(),
            P(),
            P(("dp", "mod"), None),
            P(("dp", "mod"), None),
            P(("dp", "mod"), None),
            P(("dp", "mod"), None),
        ),
        check_vma=False,
    )
```

```python
import jax
import jax.numpy as jnp
import numpy as np
from jax import lax
from jax.experimental import pallas as pl
from jax.experimental.pallas import tpu as pltpu
from jax.sharding import PartitionSpec as P

EPSILON = 1e-06


def rms_norm(values):
    inverse = lax.rsqrt(jnp.mean(values * values, axis=-1, keepdims=True) + EPSILON)
    return (values * inverse, inverse)


def norm_back(upstream, normed, inverse):
    return inverse * (upstream - normed * jnp.mean(upstream * normed, axis=-1, keepdims=True))


def silu_slope(values):
    logistic = jax.nn.sigmoid(values)
    return logistic * (1.0 + values * (1.0 - logistic))


def inner_rows(left, right):
    return lax.dot_general(
        left, right, (((0,), (0,)), ((), ())), preferred_element_type=jnp.float32
    )


def inner_cols(left, right):
    return lax.dot_general(
        left, right, (((1,), (1,)), ((), ())), preferred_element_type=jnp.float32
    )


TOK = 144
PAIR = 2 * TOK
WIDE = 1152
HID = 3072
RING = 4
AXES = ((0, 2, 1), (1, 0, 2), (2, 1, 0))
JOBS = (
    ("gate", 9, 1024, 256, 512),
    ("up", 9, 1024, 256, 512),
    ("down", 24, 384, 384, 256),
    ("out", 9, 384, 384, 256),
    ("qkv", 9, 1152, 384, 640),
)
COPIES = 15
PARTNER_COPIES = 17
MOD_COPIES = 20
CHUNK = 512


def sixteen(rows):
    return (rows + 15) // 16 * 16


def position():
    dp = lax.axis_index("dp")
    x_hi = lax.axis_index("mod")
    core = lax.rem(dp, 2)
    y = lax.rem(dp // 2, 4)
    z = lax.rem(dp // 8, 4)
    return (x_hi * 2 + dp // 32, y, z), core


def device_at(place, core):
    x, y, z = place
    return (((lax.rem(x, 2) * 4 + z) * 4 + y) * 2 + core, x // 2)


def moved(place, axis, value):
    return tuple(value if index == axis else kept for index, kept in enumerate(place))


def line_of(axis, value):
    return value % 2 * 2 + value // 2 if axis == 0 else value


FWD_REMOTE = 12
MESH = pl.DeviceIdType.MESH


def rope_flat():
    token = np.arange(TOK)
    frequency = 10000.0 ** (-np.arange(18, dtype=np.float64) / 18)
    tables = []
    for position_in, side in ((token % 36, 6), (token, 12)):
        row, column = position_in // side, position_in % side
        angle = np.concatenate([row[:, None] * frequency, column[:, None] * frequency], axis=1)
        cosine = np.tile(np.concatenate([np.cos(angle), np.cos(angle)], axis=1), (1, 16))
        sine = np.tile(np.concatenate([-np.sin(angle), np.sin(angle)], axis=1), (1, 16))
        tables.append((cosine, sine))
    return (
        np.stack([pair[0] for pair in tables]).astype(np.float32),
        np.stack([pair[1] for pair in tables]).astype(np.float32),
    )


def row_blocks(step, size=16):
    @pl.loop(0, TOK // size)
    def _(index):
        step(pl.ds(pl.multiple_of(index * size, 16), size))


def split_two(values):
    high = values.astype(jnp.bfloat16)
    return high, (values - high.astype(jnp.float32)).astype(jnp.bfloat16)


def head_sum(values, heads):
    high, low = split_two(values)
    return inner_cols(high, heads) + inner_cols(low, heads)


def head_spread(values, heads):
    high, low = split_two(values)
    return jnp.dot(high, heads, preferred_element_type=jnp.float32) + jnp.dot(
        low, heads, preferred_element_type=jnp.float32
    )


def head_rows():
    head = lax.broadcasted_iota(jnp.int32, (128, WIDE), 0) * 72
    lane = lax.broadcasted_iota(jnp.int32, (128, WIDE), 1)
    return ((lane >= head) & (lane < head + 72)).astype(jnp.float32).astype(jnp.bfloat16)


def swap_halves(values):
    lane = lax.broadcasted_iota(jnp.int32, values.shape, 1)
    first = lax.rem(lane, 72) < 36
    return jnp.where(first, pltpu.roll(values, WIDE - 36, 1), pltpu.roll(values, 36, 1))


def head_window(head):
    block = jnp.minimum(head * 72 // 128, 7)
    offset = head * 72 - block * 128
    lane = lax.broadcasted_iota(jnp.int32, (1, 256), 1)
    mask = ((lane >= offset) & (lane < offset + 72)).astype(jnp.float32).astype(jnp.bfloat16)
    return pl.ds(pl.multiple_of(block * 128, 128), 256), mask


def forward_kernel(
    segments,
    tokens,
    condition,
    mod_bias,
    query_gain,
    key_gain,
    cos_in,
    sin_in,
    mod_weight,
    qkv_weight,
    out_weight,
    query_out,
    key_out,
    value_out,
    query_hat_out,
    key_hat_out,
    context_out,
    attended_out,
    middle_out,
    first_out,
    second_out,
    cos_out,
    sin_out,
    gathered_out,
    inverse_out,
    modulation_out,
    gains,
    mod_w,
    qkv_w,
    out_w,
    cos2,
    sin2,
    cond32,
    cond_other,
    act32,
    act_across,
    gathered,
    half32,
    fold32,
    fold_own,
    fold_other,
    mods32,
    per_token,
    norm,
    first,
    projected,
    query,
    key,
    value,
    query_hat,
    key_hat,
    context32,
    context,
    attended,
    middle,
    second,
    cosine,
    sine,
    heads,
    send_sem,
    recv_sem,
    in_sem,
    out_sem,
):
    place, core = position()
    mod = lax.axis_index("mod")
    partner = device_at(place, 1 - core)
    twin = device_at(moved(place, 0, lax.rem(place[0] + 2, 4)), core)
    peers = [
        [device_at(moved(place, axis, lax.rem(place[axis] + step, 4)), core) for step in (1, 2, 3)]
        for axis in (1, 2)
    ]
    loads = {}

    def load(name, index, src, dst, slot):
        copy = pltpu.make_async_copy(src, dst, in_sem.at[slot])
        copy.start()
        loads[name, index] = copy

    for index in range(3):
        columns = pl.ds(index * WIDE, WIDE)
        load("mod", index, mod_weight.at[:, columns], mod_w.at[:, columns], index)
    load("cos", 0, cos_in, cos2, 21)
    load("sin", 0, sin_in, sin2, 22)
    for index in range(3):
        columns = pl.ds(index * WIDE, WIDE)
        load("qkv", index, qkv_weight.at[:, columns], qkv_w.at[:, columns], 9 + index)
    load("out", 0, out_weight, out_w, 18)

    sent = []
    copies = {}

    def send(slot, src, dst, target):
        copy = pltpu.make_async_remote_copy(
            src_ref=src,
            dst_ref=dst,
            send_sem=send_sem.at[slot],
            recv_sem=recv_sem.at[slot],
            device_id=target,
            device_id_type=MESH,
        )
        copy.start()
        sent.append(copy)
        copies[slot] = copy

    stores = []

    def store(src, dst):
        copy = pltpu.make_async_copy(src, dst, out_sem.at[len(stores)])
        copy.start()
        stores.append(copy)

    barrier = pltpu.get_barrier_semaphore()
    for target in [partner, twin] + peers[0] + peers[1]:
        pl.semaphore_signal(barrier, inc=1, device_id=target, device_id_type=MESH)
    cond32[...] = jnp.zeros_like(cond32)
    cond32[0:4, :] = condition[...].astype(jnp.float32)
    pl.semaphore_wait(barrier, 8)
    send(0, cond32, cond_other, twin)

    for which, source in enumerate((query_gain, key_gain)):
        gains[which : which + 1, :] = jnp.concatenate([source[...].reshape(1, 72)] * 16, axis=1)
    kind = segments[TOK - 1] == 0
    row = lax.broadcasted_iota(jnp.int32, (TOK, 16), 0)
    slot = lax.broadcasted_iota(jnp.int32, (TOK, 16), 1)
    onehot = (slot == jnp.where(kind, 0, row // 36)).astype(jnp.float32).astype(jnp.bfloat16)
    heads[...] = head_rows()

    def first_norm(rows):
        values = tokens[rows, :].astype(jnp.float32)
        norm[rows, :] = rms_norm(values)[0]

    row_blocks(first_norm, 48)

    copies[0].wait_recv()
    own, other = cond32[0:4, :], cond_other[0:4, :]
    act32[0:4, :] = jnp.where(mod == 0, own, other)
    act32[4:8, :] = jnp.where(mod == 0, other, own)
    act32[...] = jax.nn.silu(act32[...]).astype(jnp.bfloat16).astype(jnp.float32)
    send(1, act32, act_across, partner)
    act = act32[...].astype(jnp.bfloat16)
    half32[...] = jnp.zeros_like(half32)
    for index in range(3):
        columns = slice(index * WIDE, (index + 1) * WIDE)
        loads["mod", index].wait()
        half32[:, columns] = (
            (
                jnp.dot(act, mod_w[:, columns], preferred_element_type=jnp.float32)
                + mod_bias[columns].astype(jnp.float32).reshape(1, WIDE)
            )
            .astype(jnp.bfloat16)
            .astype(jnp.float32)
        )
    for quarter in range(4):
        columns = slice(quarter * 896, (quarter + 1) * 896)
        fold32[4 * quarter : 4 * quarter + 4, :] = jnp.where(
            mod == 0, half32[4:8, columns], half32[0:4, columns]
        )
    fold_own[...] = fold32[...].astype(jnp.bfloat16)
    send(2, fold_own, fold_other, twin)

    copies[1].wait_recv()
    _, y, z = place
    rows16 = jnp.concatenate(
        [
            jnp.where(core == 0, act32[...], act_across[...]),
            jnp.where(core == 0, act_across[...], act32[...]),
        ]
    )
    gathered[z, y] = rows16.astype(jnp.bfloat16)
    for step in range(3):
        send(3 + step, gathered.at[z, y], gathered.at[z, y], peers[0][step])
    loads["cos", 0].wait()
    loads["sin", 0].wait()

    def pick_table(rows):
        cosine[rows, :] = jnp.where(kind, cos2[1, rows, :], cos2[0, rows, :])
        sine[rows, :] = jnp.where(kind, sin2[1, rows, :], sin2[0, rows, :])

    row_blocks(pick_table)
    store(cosine, cos_out)
    store(sine, sin_out)
    for slot_ in (3, 4, 5):
        copies[slot_].wait_recv()
    for step in range(3):
        send(6 + step, gathered.at[z], gathered.at[z], peers[1][step])

    copies[2].wait_recv()
    mods32[...] = jnp.zeros_like(mods32)
    fold32[...] = fold_other[...].astype(jnp.float32)
    for quarter in range(4):
        width = 896 if quarter < 3 else 768
        mods32[0:4, pl.ds(pl.multiple_of((1 - mod) * 3456 + quarter * 896, 128), width)] = fold32[
            4 * quarter : 4 * quarter + 4, 0:width
        ]
    mods32[0:4, pl.ds(pl.multiple_of(mod * 3456, 128), 3456)] = jnp.where(
        mod == 0, half32[0:4, 0:3456], half32[4:8, 0:3456]
    )
    modulation_out[...] = mods32[...].astype(jnp.bfloat16)
    for index in range(5):
        columns = slice(index * WIDE, (index + 1) * WIDE)
        per_token[:, columns] = jnp.dot(
            onehot, modulation_out[:, columns], preferred_element_type=jnp.float32
        ).astype(jnp.bfloat16)

    def piece(rows, index):
        return per_token[rows, index * WIDE : (index + 1) * WIDE].astype(jnp.float32)

    def first_input(rows):
        first[rows, :] = (norm[rows, :] * (1.0 + piece(rows, 1)) + piece(rows, 0)).astype(jnp.bfloat16)

    row_blocks(first_input, 48)
    store(first, first_out)

    for index in range(3):
        loads["qkv", index].wait()
        columns = slice(index * WIDE, (index + 1) * WIDE)
        result = jnp.dot(first[...], qkv_w[:, columns], preferred_element_type=jnp.float32)
        if index < 2:
            projected[:, columns] = result
        else:
            value[...] = result.astype(jnp.bfloat16)
    store(value, value_out)

    def head_norm(which, hat, result, rows):
        raw = projected[rows, which * WIDE : (which + 1) * WIDE]
        total = head_sum(raw * raw, heads[...])
        inverse = lax.rsqrt(total * (1.0 / 72.0) + EPSILON)
        inverse_out[which, rows, :] = inverse
        normed = raw * head_spread(inverse, heads[...])
        hat[rows, :] = normed
        scaled = normed * gains[which : which + 1, :]
        turned = scaled * cosine[rows, :] + swap_halves(scaled) * sine[rows, :]
        result[rows, :] = turned.astype(jnp.bfloat16)

    def head_rows_step(rows):
        head_norm(0, query_hat, query, rows)
        head_norm(1, key_hat, key, rows)

    row_blocks(head_rows_step, 48)
    store(query_hat, query_hat_out)
    store(query, query_out)
    store(key_hat, key_hat_out)
    store(key, key_out)

    left = lax.broadcasted_iota(jnp.int32, (TOK, TOK), 0) // 36
    right = lax.broadcasted_iota(jnp.int32, (TOK, TOK), 1) // 36
    shut = jnp.where(kind | (left == right), 0.0, -1e30)
    context32[...] = jnp.zeros_like(context32)

    @pl.loop(0, 4)
    def _(group):
        for member in range(4):
            head = group * 4 + member
            window, mask = head_window(head)
            scores = inner_cols(query[:, window] * mask, key[:, window]) * (72**-0.5) + shut
            top = jnp.max(scores, axis=-1, keepdims=True)
            weight = jnp.exp(scores - top)
            weight = weight * (1.0 / jnp.sum(weight, axis=-1, keepdims=True))
            context32[:, window] += jnp.dot(
                weight.astype(jnp.bfloat16), value[:, window] * mask, preferred_element_type=jnp.float32
            )

    context[...] = context32[...].astype(jnp.bfloat16)
    store(context, context_out)
    loads["out", 0].wait()
    attended[...] = jnp.dot(context[...], out_w[...], preferred_element_type=jnp.float32)
    store(attended, attended_out)

    def second_input(rows):
        total = tokens[rows, :].astype(jnp.float32) + piece(rows, 2) * attended[rows, :]
        middle[rows, :] = total
        normed = rms_norm(total)[0]
        second[rows, :] = (normed * (1.0 + piece(rows, 4)) + piece(rows, 3)).astype(jnp.bfloat16)

    row_blocks(second_input, 48)
    store(middle, middle_out)
    store(second, second_out)
    for slot_ in (6, 7, 8):
        copies[slot_].wait_recv()
    store(gathered, gathered_out)
    for copy in sent:
        copy.wait_send()
    for copy in stores:
        copy.wait()


def forward(tokens, condition, segments, mod_weight, mod_bias, qkv_weight, query_gain, key_gain, out_weight):
    cos_table, sin_table = rope_flat()
    vmem = pl.BlockSpec(memory_space=pltpu.VMEM)
    anywhere = pl.BlockSpec(memory_space=pl.ANY)
    low, full = jnp.bfloat16, jnp.float32
    wide_low = ((TOK, WIDE), low)
    wide_full = ((TOK, WIDE), full)
    outs = (
        [wide_low] * 3
        + [wide_full] * 2
        + [wide_low, wide_full, wide_full, wide_low, wide_low]
        + [wide_full] * 2
        + [((4, 4, 16, WIDE), low)]
        + [((2, TOK, 128), full), ((16, 6 * WIDE), low), ((2, WIDE), full)]
    )
    scratch = [
        ((WIDE, 3456), low),
        ((WIDE, 3456), low),
        ((WIDE, WIDE), low),
        ((2, TOK, WIDE), full),
        ((2, TOK, WIDE), full),
        ((8, WIDE), full),
        ((8, WIDE), full),
        ((8, WIDE), full),
        ((8, WIDE), full),
        ((4, 4, 16, WIDE), low),
        ((8, 3584), full),
        ((16, 896), full),
        ((16, 896), low),
        ((16, 896), low),
        ((16, 6912), full),
        ((TOK, 6912), low),
        wide_full,
        wide_low,
        ((TOK, 2304), full),
        wide_low,
        wide_low,
        wide_low,
        wide_full,
        wide_full,
        wide_full,
        wide_low,
        wide_full,
        wide_full,
        wide_low,
        wide_full,
        wide_full,
        ((128, WIDE), low),
    ]
    return pl.pallas_call(
        forward_kernel,
        out_shape=[jax.ShapeDtypeStruct(*out) for out in outs],
        in_specs=[pl.BlockSpec(memory_space=pltpu.SMEM)] + [vmem] * 5 + [anywhere] * 5,
        out_specs=[anywhere] * 13 + [vmem] * 3,
        scratch_shapes=[pltpu.VMEM(*item) for item in scratch]
        + [
            pltpu.SemaphoreType.DMA((FWD_REMOTE,)),
            pltpu.SemaphoreType.DMA((FWD_REMOTE,)),
            pltpu.SemaphoreType.DMA((23,)),
            pltpu.SemaphoreType.DMA((16,)),
        ],
        compiler_params=pltpu.CompilerParams(
            collective_id=2, has_side_effects=True, vmem_limit_bytes=56 * 1024 * 1024
        ),
        cost_estimate=pl.CostEstimate(flops=2_000_000_000, bytes_accessed=30_000_000, transcendentals=0),
    )(
        segments,
        tokens,
        condition,
        mod_bias,
        query_gain,
        key_gain,
        jnp.asarray(cos_table),
        jnp.asarray(sin_table),
        mod_weight,
        qkv_weight,
        out_weight,
    )


def backward_kernel(
    segments,
    cotangent,
    tokens,
    modulation,
    condition,
    gains,
    inverses,
    acts,
    second_in,
    first_in,
    context_in,
    middle_in,
    attended_in,
    query_in,
    key_in,
    value_in,
    query_hat_in,
    key_hat_in,
    cos_in,
    sin_in,
    gate_weight,
    up_weight,
    down_weight,
    out_weight,
    qkv_weight,
    mod_weight,
    layer_out,
    tokens_out,
    gate_out,
    up_out,
    down_out,
    out_out,
    qkv_out,
    mod_out,
    special_out,
    condition_out,
    hidden_s,
    second_s,
    gbranch_s,
    ggate_s,
    gup_s,
    gatt_s,
    pick_x,
    pick_y,
    pick_z,
    acts_s,
    perm24,
    xt24,
    acc,
    heads,
    folds,
    per_token,
    branch,
    gsecond,
    attended,
    query,
    key,
    value,
    gcontext,
    gquery,
    gkey,
    gvalue,
    cosine,
    gain_sum,
    out_w,
    narrow_w,
    gmod,
    act_rows,
    fold32,
    fold_own,
    fold_other,
    other32,
    pair32,
    turned32,
    side_own,
    side_other,
    cross_other,
    rows32,
    gathered_a,
    gathered_b,
    product_own,
    product_send,
    product_other,
    final_other,
    special_other,
    part_own,
    part_other,
    *rest,
):
    bufs = [list(rest[7 * index : 7 * index + 7]) for index in range(len(JOBS))]
    for index in range(4):
        bufs[0][index] = bufs[4][index]
    xt9 = xt24.at[pl.ds(0, 576)]
    send_sem, recv_sem, local_sem, ring_sem = rest[7 * len(JOBS) :]
    gproj_s, middle = ggate_s, tokens_out
    place, core = position()
    mod = lax.axis_index("mod")
    partner = device_at(place, 1 - core)
    near = []
    for axis in range(3):
        here = place[axis]
        near.append(
            (here, lax.rem(here + 1, 4), lax.rem(here + 3, 4), lax.rem(here + 2, 4))
        )
    twin = moved(place, 0, near[0][3])

    ring_a, ring_b, ring_c = bufs[0][0], bufs[1][0], bufs[2][0]

    def ff_slots(slot):
        columns = pl.ds(pl.multiple_of(slot * CHUNK, CHUNK), CHUNK)
        return (
            ring_a.at[pl.ds(0, WIDE), columns],
            ring_b.at[pl.ds(0, WIDE), columns],
            ring_c.at[columns, :],
        )

    def ff_chunk(index, slot):
        columns = pl.ds(pl.multiple_of(index * CHUNK, CHUNK), CHUNK)
        sources = (gate_weight.at[:, columns], up_weight.at[:, columns], down_weight.at[columns, :])
        return [
            pltpu.make_async_copy(source, target, ring_sem.at[number, slot])
            for number, (source, target) in enumerate(zip(sources, ff_slots(slot)))
        ]

    wide_loads = {}

    def wide_load(name, index, source, target, number):
        copy = pltpu.make_async_copy(source, target, ring_sem.at[3, number])
        copy.start()
        wide_loads[name, index] = copy

    for index in range(2):
        for copy in ff_chunk(index, index):
            copy.start()
    wide_load("out", 0, out_weight, out_w, 0)
    third_w = ring_c.at[pl.ds(0, WIDE), :]
    fourth_w = ring_b.at[pl.ds(0, WIDE), :]

    def wide_parts(name, source, number):
        if number == 0:
            wide_load(name, 0, source.at[:, pl.ds(0, WIDE)], out_w, 0)
        elif number == 1:
            wide_load(name, 1, source.at[:, pl.ds(WIDE, WIDE)], third_w, 1)
        else:
            wide_load(name, 2, source.at[:, pl.ds(2 * WIDE, 1024)], fourth_w, 2)
            wide_load(name, 3, source.at[:, pl.ds(3328, 128)], narrow_w, 3)

    loads = {}

    def load(name, src, dst):
        copy = pltpu.make_async_copy(src, dst, local_sem.at[len(loads)])
        copy.start()
        loads[name] = copy

    own_rows, other_rows = pl.ds(0, TOK), pl.ds(TOK, TOK)
    load("second", second_in, second_s.at[own_rows])
    load("middle", middle_in, middle)
    load("attended", attended_in, attended)
    load("query", query_in, query)
    load("acts", acts, acts_s)
    load("key", key_in, key)
    load("value", value_in, value)

    barrier = pltpu.get_barrier_semaphore()
    pl.semaphore_signal(barrier, inc=1, device_id=partner, device_id_type=MESH)
    for axis in range(3):
        for far in near[axis][1:]:
            pl.semaphore_signal(
                barrier,
                inc=1,
                device_id=device_at(moved(place, axis, far), core),
                device_id_type=MESH,
            )
    pl.semaphore_signal(barrier, inc=1, device_id=device_at(twin, 1 - core), device_id_type=MESH)

    kind = segments[TOK - 1] == 0
    token = lax.broadcasted_iota(jnp.int32, (TOK, 16), 0)
    slot_of = lax.broadcasted_iota(jnp.int32, (TOK, 16), 1)
    onehot = (slot_of == jnp.where(kind, 0, token // 36)).astype(jnp.float32).astype(jnp.bfloat16)
    token_t = lax.broadcasted_iota(jnp.int32, (16, TOK), 1)
    slot_t = lax.broadcasted_iota(jnp.int32, (16, TOK), 0)
    onehot_t = (slot_t == jnp.where(kind, 0, token_t // 36)).astype(jnp.float32).astype(jnp.bfloat16)
    for index, block in enumerate((5, 4, 2, 1)):
        per_token[:, index * WIDE : (index + 1) * WIDE] = jnp.dot(
            onehot, modulation[:, block * WIDE : (block + 1) * WIDE], preferred_element_type=jnp.float32
        ).astype(jnp.bfloat16)

    def piece(rows, block):
        base = (5, 4, 2, 1).index(block) * WIDE
        return per_token[rows, base : base + WIDE].astype(jnp.float32)

    def first_rows(rows):
        upstream = cotangent[rows, :].astype(jnp.float32)
        gbranch_s[rows, :] = (upstream * piece(rows, 5)).astype(jnp.bfloat16)
        zero = jnp.zeros((48, WIDE), jnp.float32)
        branch[rows, :] = zero
        gsecond[rows, :] = zero

    row_blocks(first_rows, 48)
    gmod[...] = jnp.zeros_like(gmod)
    gain_sum[...] = jnp.zeros_like(gain_sum)
    pl.semaphore_wait(barrier, 11)

    def remote(src, dst, index, target):
        return pltpu.make_async_remote_copy(
            src_ref=src,
            dst_ref=dst,
            send_sem=send_sem.at[index],
            recv_sem=recv_sem.at[index],
            device_id=target,
            device_id_type=MESH,
        )

    sent = []
    pairs, landed = {}, set()

    def exchange(name, src, dst):
        copy = remote(src, dst, len(pairs), partner)
        copy.start()
        pairs[name] = copy

    exchange("gbranch", gbranch_s.at[own_rows], gbranch_s.at[other_rows])
    exchange("second", second_in, second_s.at[other_rows])

    def arrived(*names):
        for name in names:
            if name not in landed:
                landed.add(name)
                pairs[name].wait_recv()

    lane24 = lax.broadcasted_iota(jnp.int32, (192, 384), 1)
    row24 = lax.broadcasted_iota(jnp.int32, (192, 384), 0)
    perm24[...] = (
        (lane24 == row24 // 48 * 96 + lax.rem(row24, 48) + core * 48)
        .astype(jnp.float32)
        .astype(jnp.bfloat16)
    )
    heads[...] = head_rows()
    folded = lax.rem(lax.broadcasted_iota(jnp.int32, (128, WIDE), 1), 72)
    folds[...] = (
        (folded == lax.broadcasted_iota(jnp.int32, (128, WIDE), 0)).astype(jnp.float32).astype(jnp.bfloat16)
    )

    row = lax.broadcasted_iota(jnp.int32, (288, 640), 0)
    lane = lax.broadcasted_iota(jnp.int32, (288, 640), 1)
    unit, entry = row // 9, lax.rem(row, 9)
    for_x = unit // 16 * 9 + lax.rem(unit // 4, 4) * 144 + lax.rem(unit, 4) * 36 + entry + core * 18
    for_y = unit // 8 * 36 + lax.rem(unit // 4, 2) * 9 + lax.rem(unit, 4) * 144 + entry + core * 18
    for x_lo in range(2):
        pick_x[x_lo] = (lane == for_x + x_lo * 64).astype(jnp.float32).astype(jnp.bfloat16)
        pick_y[x_lo] = (lane == for_y + x_lo * 64).astype(jnp.float32).astype(jnp.bfloat16)
    row = lax.broadcasted_iota(jnp.int32, (80, 256), 0)
    lane = lax.broadcasted_iota(jnp.int32, (80, 256), 1)
    unit = row // 9
    for_z = unit // 2 * 36 + lax.rem(unit, 2) * 9 + lax.rem(row, 9) + core * 18
    for block in range(8):
        pick_z[block] = (
            ((row < 72) & (lane == for_z + block * 16)).astype(jnp.float32).astype(jnp.bfloat16)
        )

    def pick9(part, stack):
        if part == 2:
            for z in range(4):
                halves = []
                for x_lo in range(2):
                    block = x_lo * 4 + z
                    rows = inner_cols(pick_z[block], stack[:, block * 128 : block * 128 + 256])
                    halves.append(rows[0:72])
                xt9[z * 144 : (z + 1) * 144, :] = jnp.concatenate(halves).astype(jnp.bfloat16)
            return
        table = (pick_x, pick_y)[part]
        low = inner_cols(table[0], stack[:, 0:640])
        high = inner_cols(table[1], stack[:, 512:WIDE])
        for value_ in range(4):
            if part == 0:
                half = (low, high)[value_ % 2]
                rows = half[value_ // 2 * 144 : value_ // 2 * 144 + 144]
            else:
                at = slice(value_ * 72, (value_ + 1) * 72)
                rows = jnp.concatenate([low[at], high[at]])
            xt9[value_ * 144 : (value_ + 1) * 144, :] = rows.astype(jnp.bfloat16)

    def pick24(part):
        def block_rows(block):
            columns = pl.ds(pl.multiple_of(block * 384, 128), 384)
            return inner_cols(perm24[...], hidden_s[:, columns])

        def put(unit, rows):
            xt24[pl.ds(pl.multiple_of(unit * 24, 16), 48), :] = rows.astype(jnp.bfloat16)

        def unit_rows(rows, y, x_hi):
            at = (y * 2 + x_hi) * 24
            return rows[at : at + 24]

        @pl.loop(0, 2)
        def _(x_lo):
            blocks = [block_rows(x_lo * 4 + z) for z in range(4)]
            for z in range(4):
                for y in range(4):
                    for x_hi in range(2):
                        upper = unit_rows(blocks[z], y, x_hi)
                        if part == 0 and y % 2 == 0:
                            unit = (x_hi * 2 + x_lo) * 16 + z * 4 + y
                            put(unit, jnp.concatenate([upper, unit_rows(blocks[z], y + 1, x_hi)]))
                        elif part == 1 and z % 2 == 0:
                            unit = y * 16 + (x_lo * 2 + x_hi) * 4 + z
                            put(unit, jnp.concatenate([upper, unit_rows(blocks[z + 1], y, x_hi)]))
                        elif part == 2 and x_hi == 0:
                            unit = z * 16 + y * 4 + x_lo * 2
                            put(unit, jnp.concatenate([upper, unit_rows(blocks[z], y, 1)]))

    def multiply(job, part, left, right):
        width = JOBS[job][2]
        own_view(job, part)[...] = jnp.dot(
            left[...], right[:, part * width : (part + 1) * width], preferred_element_type=jnp.float32
        ).astype(jnp.bfloat16)

    copies = {}
    drained = set()

    def begin(job, part, slot, src, dst, target):
        index = PARTNER_COPIES + (job * 3 + part) * COPIES + slot
        copy = remote(src, dst, index, target)
        copy.start()
        copies[job, part, slot] = copy

    def arrive(job, part, *slots):
        for slot in slots:
            copies[job, part, slot].wait_recv()

    def ring(part, phase):
        axis = AXES[part][phase]
        here, right, left, opposite = near[axis]
        return (
            here,
            right,
            left,
            opposite,
            device_at(moved(place, axis, right), core),
            device_at(moved(place, axis, left), core),
            device_at(moved(place, axis, opposite), core),
        )

    def sent_out(job, part, *slots):
        for slot in slots:
            if (job, part, slot) not in drained:
                drained.add((job, part, slot))
                copies[job, part, slot].wait_send()

    def own_view(job, part):
        base, width = bufs[job][0], JOBS[job][2]
        if JOBS[job][0] == "down":
            return base.at[:, pl.ds(part * width, width)]
        return base.at[pl.ds(part * 576, 576), pl.ds(0, width)]

    def first_send(job, part):
        half, whole = bufs[job][1:3]
        own = own_view(job, part)
        big = 16 * JOBS[job][1]
        cut = sixteen(big // 2) if job % 2 == 0 else big // 32 * 16
        here, right, left, opposite, to_right, to_left, _ = ring(part, 0)

        full = pl.ds(0, JOBS[job][2])

        def rows(chunk, start, count):
            return own.at[pl.ds(pl.multiple_of(chunk * big + start, 16), count)]

        begin(job, part, 0, rows(opposite, 0, cut), half.at[part, pl.ds(0, cut), full], to_right)
        begin(job, part, 1, rows(opposite, cut, big - cut), half.at[part, pl.ds(cut, big - cut), full], to_left)
        begin(job, part, 2, rows(right, cut, big - cut), whole.at[part, 0, pl.ds(cut, big - cut), full], to_right)
        begin(job, part, 3, rows(left, 0, cut), whole.at[part, 1, pl.ds(0, cut), full], to_left)

    def first_add(job, part):
        half, whole = bufs[job][1:3]
        own = own_view(job, part)
        _, each, width, lanes, _ = JOBS[job]
        big = 16 * each
        cut = sixteen(big // 2) if job % 2 == 0 else big // 32 * 16
        here, right, left, opposite, to_right, to_left, _ = ring(part, 0)
        for slot, chunk, start, count, target, side in (
            (0, right, 0, cut, to_right, 0),
            (1, left, cut, big - cut, to_left, 1),
        ):
            arrive(job, part, slot)
            rows = pl.ds(pl.multiple_of(chunk * big + start, 16), count)

            @pl.loop(0, width // 128)
            def _(step):
                columns = pl.ds(pl.multiple_of(step * 128, 128), 128)
                total = own[rows, columns].astype(jnp.float32) + half[
                    part, pl.ds(start, count), columns
                ].astype(jnp.float32)
                own[rows, columns] = total.astype(jnp.bfloat16)

            begin(
                job,
                part,
                4 + side,
                own.at[rows],
                whole.at[part, side, pl.ds(start, count), pl.ds(0, width)],
                target,
            )

    def second_send(job, part):
        _, _, whole, mid, mid_half, mid_whole, _ = bufs[job]
        own = own_view(job, part)
        _, each, width, lanes, cut = JOBS[job]
        big, small = 16 * each, 4 * each
        padded = sixteen(small)
        here, right, left, opposite, to_right, to_left, _ = ring(part, 0)
        arrive(job, part, 2, 3, 4, 5)
        if JOBS[job][0] == "qkv":
            sent_out(0, part, 6, 7, 8, 9, 10, 11)
        rows = pl.ds(pl.multiple_of(here * big, 16), big)

        @pl.loop(0, width // 128)
        def _(step):
            columns = pl.ds(pl.multiple_of(step * 128, 128), 128)
            total = (
                own[rows, columns].astype(jnp.float32)
                + whole[part, 0, :, columns].astype(jnp.float32)
                + whole[part, 1, :, columns].astype(jnp.float32)
            )
            if part == 2 and each == 9:
                for x_lo in range(2):
                    for y in range(4):
                        piece_at = x_lo * 72 + y * 18
                        acc[y * 36 + x_lo * 18 : y * 36 + x_lo * 18 + 18, :] = total[piece_at : piece_at + 18]
            else:
                acc[pl.ds(0, big), :] = total
            for chunk in range(4):
                line = line_of(AXES[part][1], chunk)
                mid[part, chunk, :, columns] = acc[pl.ds(line * small, padded), :].astype(jnp.bfloat16)

        here, right, left, opposite, to_right, to_left, _ = ring(part, 1)
        low, high = pl.ds(0, cut), pl.ds(cut, width - cut)
        begin(job, part, 6, mid.at[part, opposite, :, low], mid_half.at[part, :, low], to_right)
        begin(job, part, 7, mid.at[part, opposite, :, high], mid_half.at[part, :, high], to_left)
        begin(job, part, 8, mid.at[part, right, :, high], mid_whole.at[part, 0, :, high], to_right)
        begin(job, part, 9, mid.at[part, left, :, low], mid_whole.at[part, 1, :, low], to_left)

    def second_add(job, part):
        _, _, _, mid, mid_half, mid_whole, _ = bufs[job]
        _, each, width, lanes, cut = JOBS[job]
        here, right, left, opposite, to_right, to_left, _ = ring(part, 1)
        for slot, chunk, start, count, target, side in (
            (6, right, 0, cut, to_right, 0),
            (7, left, cut, width - cut, to_left, 1),
        ):
            arrive(job, part, slot)

            @pl.loop(0, count // 128)
            def _(step):
                columns = pl.ds(pl.multiple_of(start + step * 128, 128), 128)
                total = mid[part, chunk, :, columns].astype(jnp.float32) + mid_half[
                    part, :, columns
                ].astype(jnp.float32)
                mid[part, chunk, :, columns] = total.astype(jnp.bfloat16)

            columns = pl.ds(start, count)
            begin(
                job,
                part,
                10 + side,
                mid.at[part, chunk, :, columns],
                mid_whole.at[part, side, :, columns],
                target,
            )

    def third_send(job, part):
        _, _, _, mid, _, mid_whole, last = bufs[job]
        _, each, width, lanes, cut = JOBS[job]
        small = sixteen(4 * each)
        padded = sixteen(each)
        here = ring(part, 1)[0]
        arrive(job, part, 8, 9, 10, 11)

        @pl.loop(0, width // 128)
        def _(step):
            columns = pl.ds(pl.multiple_of(step * 128, 128), 128)
            acc[pl.ds(0, small), :] = (
                mid[part, here, :, columns].astype(jnp.float32)
                + mid_whole[part, 0, :, columns].astype(jnp.float32)
                + mid_whole[part, 1, :, columns].astype(jnp.float32)
            )
            for chunk in range(4):
                line = line_of(AXES[part][2], chunk)
                last[part, chunk, :, columns] = acc[pl.ds(line * each, padded), :].astype(jnp.bfloat16)

        here, right, left, opposite, to_right, to_left, to_opposite = ring(part, 2)
        for slot, chunk, target in ((0, right, to_right), (1, left, to_left), (2, opposite, to_opposite)):
            begin(job, part, 12 + slot, last.at[part, chunk], last.at[part, 4 + slot], target)

    mod_base = PARTNER_COPIES + 3 * COPIES * len(JOBS)
    mod_copies = {}

    def mod_send(slot, src, dst, target):
        copy = remote(src, dst, mod_base + slot, target)
        copy.start()
        sent.append(copy)
        mod_copies[slot] = copy

    def mod_arrive(*slots):
        for slot in slots:
            mod_copies[slot].wait_recv()

    def mod_pair():
        for quarter in range(4):
            fold32[4 * quarter : 4 * quarter + 4, :] = gmod[
                1 - mod, 0:4, quarter * 896 : (quarter + 1) * 896
            ]
        start = (1 - core) * 1792
        for half in range(2):
            columns = pl.ds(pl.multiple_of(start + half * 896, 128), 896)
            side_own[4 * half : 4 * half + 4, :] = gmod[mod, 0:4, columns]
        fold_own[...] = fold32[...].astype(jnp.bfloat16)
        there = pl.ds(pl.multiple_of((1 - core) * 8, 8), 8)
        mod_send(19, fold32.at[there], cross_other, device_at(twin, 1 - core))
        mod_send(0, fold_own, fold_other, device_at(twin, core))
        mod_send(1, side_own, side_other, partner)

    def condition_part():
        for quarter in range(4):
            other32[0:4, quarter * 896 : (quarter + 1) * 896] = turned32[4 * quarter : 4 * quarter + 4, :]
        own, other = gmod[mod, 0:4, :], other32[0:4, :]
        pair32[0:4, :] = jnp.where(mod == 0, own, other)
        pair32[4:8, :] = jnp.where(mod == 0, other, own)
        first = pair32[:, 0:WIDE].astype(jnp.bfloat16)
        wide_loads["mod", 0].wait()
        part_own[...] = inner_cols(first, out_w[...])
        wide_loads["mod", 1].wait()
        part_own[...] += inner_cols(pair32[:, WIDE : 2 * WIDE].astype(jnp.bfloat16), third_w[...])
        wide_loads["mod", 2].wait()
        wide_loads["mod", 3].wait()
        part_own[...] += inner_cols(pair32[:, 2 * WIDE : 3328].astype(jnp.bfloat16), fourth_w[...])
        part_own[...] += inner_cols(pair32[:, 3328:3456].astype(jnp.bfloat16), narrow_w[...])
        mod_send(2, part_own, part_other, device_at(twin, core))

    def mod_gather_first():
        mod_arrive(0, 1, 19)
        turned32[...] = fold_other[...].astype(jnp.float32)
        twin_rows = turned32[pl.ds(pl.multiple_of(core * 8, 8), 8), :]
        for half in range(2):
            columns = pl.ds(pl.multiple_of(core * 1792 + half * 896, 128), 896)
            at = slice(4 * half, 4 * half + 4)
            own, other = gmod[mod, 0:4, columns], twin_rows[at]
            beside, cross = side_other[at, :], cross_other[at, :]
            mine = (jnp.where(mod == 0, own, other), jnp.where(mod == 0, other, own))
            theirs = (jnp.where(mod == 0, beside, cross), jnp.where(mod == 0, cross, beside))
            to = slice(half * 896, (half + 1) * 896)
            for which in range(2):
                rows32[4 * which : 4 * which + 4, to] = jnp.where(core == 0, mine[which], theirs[which])
                rows32[8 + 4 * which : 12 + 4 * which, to] = jnp.where(core == 0, theirs[which], mine[which])
        _, y, z = place
        gathered_a[z, y] = rows32[:, 0:896].astype(jnp.bfloat16)
        gathered_b[z, y] = rows32[:, 896:1792].astype(jnp.bfloat16)
        for step in range(3):
            to_y = device_at(moved(place, 1, near[1][1 + step]), core)
            to_z = device_at(moved(place, 2, near[2][1 + step]), core)
            mod_send(3 + step, gathered_a.at[z, y], gathered_a.at[z, y], to_y)
            mod_send(6 + step, gathered_b.at[z, y], gathered_b.at[z, y], to_z)

    def mod_gather_second():
        _, y, z = place
        mod_arrive(3, 4, 5)
        for step in range(3):
            to_z = device_at(moved(place, 2, near[2][1 + step]), core)
            mod_send(9 + step, gathered_a.at[z], gathered_a.at[z], to_z)
        mod_arrive(6, 7, 8)
        for step in range(3):
            to_y = device_at(moved(place, 1, near[1][1 + step]), core)
            mod_send(12 + step, gathered_b.at[:, y], gathered_b.at[:, y], to_y)

    def mod_table():
        x, y, z = place
        row = lax.broadcasted_iota(jnp.int32, (48, WIDE), 0)
        lane = lax.broadcasted_iota(jnp.int32, (48, WIDE), 1)
        line = lax.broadcasted_iota(jnp.int32, (48, 256), 0)
        slot = lax.rem(lax.broadcasted_iota(jnp.int32, (48, 256), 1), 4)
        ones = (line == 40) | ((line == 41) & (slot == 0)) | ((line == 42) & (slot == 1))
        for index in range(2):
            half = lax.rem(lax.rem(x, 2) + index, 2)
            start = (half * 32 + z * 8 + y * 2) * 18
            pick = ((row < 36) & (lane == row + start)).astype(jnp.float32).astype(jnp.bfloat16)
            rows = inner_cols(pick, acts_s[...])
            act_rows[index] = (rows + ones.astype(jnp.float32)).astype(jnp.bfloat16)

    def mod_product():
        mod_arrive(9, 10, 11)
        mod_arrive(12, 13, 14)
        for side, gathered in ((0, gathered_a), (1, gathered_b)):
            columns = slice(side * 896, (side + 1) * 896)
            rows = gathered[...].reshape(256, 896)
            product_send[:, columns] = jnp.dot(
                act_rows[1], rows, preferred_element_type=jnp.float32
            ).astype(jnp.bfloat16)
            product_own[:, columns] = jnp.dot(act_rows[0], rows, preferred_element_type=jnp.float32)
        x = place[0]
        beside = moved(place, 0, x + 1 - 2 * lax.rem(x, 2))
        mod_send(15, product_send, product_other, device_at(beside, core))

    def mod_sum():
        mod_arrive(15)
        product_own[...] = product_own[...] + product_other[...].astype(jnp.float32)
        mod_send(16, product_own, final_other, partner)
        special = product_own.at[pl.ds(40, 8)]
        mod_send(17, special, special_other.at[core], device_at(twin, core))
        mod_send(18, special, special_other.at[core], device_at(twin, 1 - core))

    def mod_finish():
        here = pl.ds(pl.multiple_of(core * 1792, 128), 1792)
        there = pl.ds(pl.multiple_of((1 - core) * 1792, 128), 1792)
        mod_arrive(2)
        total = part_own[...] + part_other[...]
        raw = condition[...].astype(jnp.float32)
        condition_out[...] = jnp.where(mod == 0, total[0:4], total[4:8]) * silu_slope(raw)
        mod_arrive(16)
        for source, columns in ((product_own, here), (final_other, there)):
            mod_out[:, columns] = jnp.where(core == 0, source[0:18, :], source[18:36, :])
            special_out[mod, :, columns] = source[40:48, :]
        mod_arrive(17, 18)
        for side in range(2):
            special_out[1 - mod, :, side * 1792 : (side + 1) * 1792] = special_other[side]

    outs = {"gate": gate_out, "up": up_out, "down": down_out, "out": out_out, "qkv": qkv_out}

    def finish(job, part):
        last = bufs[job][6]
        _, each, width, lanes, cut = JOBS[job]
        here = ring(part, 2)[0]
        arrive(job, part, 12, 13, 14)

        @pl.loop(0, width // 128)
        def _(step):
            to = pl.multiple_of(step * 128, 128)
            columns = pl.ds(to, 128)
            total = last[part, here, :, columns].astype(jnp.float32)
            for slot in range(3):
                total = total + last[part, 4 + slot, :, columns].astype(jnp.float32)
            outs[JOBS[job][0]][:, pl.ds(pl.multiple_of(part * width + to, 128), 128)] = total[:each]

    gate_job, up_job, down_job, out_job, qkv_job = range(5)

    def slot_sum(block, source):
        for third in range(3):
            columns = slice(third * 384, (third + 1) * 384)
            high, low = split_two(source[:, columns])
            total = jnp.dot(onehot_t, high, preferred_element_type=jnp.float32) + jnp.dot(
                onehot_t, low, preferred_element_type=jnp.float32
            )
            base = block % 3 * WIDE + third * 384
            gmod[block // 3, :, base : base + 384] = (
                total[0:8].astype(jnp.bfloat16).astype(jnp.float32)
            )

    def stages(stage, job):
        for part in range(3):
            stage(job, part)

    def ff_products(part):
        pick9(part, second_s)
        arrived("ggate", "gup")
        multiply(gate_job, part, xt9, ggate_s)
        first_send(gate_job, part)
        multiply(up_job, part, xt9, gup_s)
        first_send(up_job, part)

    loads["second"].wait()

    @pl.loop(0, 6)
    def _(index):
        slot = lax.rem(index, 2)
        for copy in ff_chunk(index, slot):
            copy.wait()
        gate_w, up_w, down_w = ff_slots(slot)
        columns = pl.ds(pl.multiple_of(index * CHUNK, CHUNK), CHUNK)
        gate_linear = jnp.dot(second_s[0:TOK, :], gate_w[...], preferred_element_type=jnp.float32)
        up_linear = jnp.dot(second_s[0:TOK, :], up_w[...], preferred_element_type=jnp.float32)
        ghidden = inner_cols(gbranch_s[0:TOK, :], down_w[...])
        logistic = jax.nn.sigmoid(gate_linear)
        gate_act = gate_linear * logistic
        hidden = (gate_act * up_linear).astype(jnp.bfloat16)
        slope = logistic * (1.0 + gate_linear * (1.0 - logistic))
        ggate = (ghidden * up_linear * slope).astype(jnp.bfloat16)
        gup = (ghidden * gate_act).astype(jnp.bfloat16)
        hidden_s[0:TOK, columns] = hidden
        ggate_s[0:TOK, columns] = ggate
        gup_s[0:TOK, columns] = gup
        branch[...] += jnp.dot(hidden, down_w[...], preferred_element_type=jnp.float32)
        gsecond[...] += inner_cols(ggate, gate_w[...])
        gsecond[...] += inner_cols(gup, up_w[...])

        @pl.when(index + 2 < 6)
        def _():
            for copy in ff_chunk(index + 2, slot):
                copy.start()

    exchange("ggate", ggate_s.at[own_rows, pl.ds(0, HID)], ggate_s.at[other_rows, pl.ds(0, HID)])
    exchange("gup", gup_s.at[own_rows], gup_s.at[other_rows])
    exchange("hidden", hidden_s.at[own_rows], hidden_s.at[other_rows])
    arrived("second")
    for part in range(3):
        ff_products(part)
    loads["middle"].wait()
    loads["attended"].wait()

    def second_rows(rows):
        upstream = cotangent[rows, :].astype(jnp.float32)
        kept = middle[rows, :]
        result = branch[rows, :]
        layer_out[rows, :] = (kept + piece(rows, 5) * result).astype(jnp.bfloat16)
        branch[rows, :] = upstream * result
        normed, inverse = rms_norm(kept)
        grad = gsecond[rows, :]
        gquery[rows, :] = grad * normed
        total = upstream + norm_back(grad * (1.0 + piece(rows, 4)), normed, inverse)
        middle[rows, :] = total
        attended_row = attended[rows, :]
        attended[rows, :] = total * attended_row
        gatt_s[rows, :] = (total * piece(rows, 2)).astype(jnp.bfloat16)

    row_blocks(second_rows, 48)
    exchange("gatt", gatt_s.at[own_rows], gatt_s.at[other_rows])
    context_s = second_s
    load("context", context_in, context_s.at[own_rows])
    stages(first_add, gate_job)

    arrived("gbranch", "hidden")
    for part in range(3):
        pick24(part)
        multiply(down_job, part, xt24, gbranch_s)
        first_send(down_job, part)
    stages(first_add, up_job)
    arrived("gatt")
    exchange("context", context_in, context_s.at[other_rows])

    wide_loads["out", 0].wait()
    gcontext[...] = inner_cols(gatt_s[0:TOK, :], out_w[...]).astype(jnp.bfloat16)
    wide_parts("qkv", qkv_weight, 0)
    stages(second_send, gate_job)
    loads["context"].wait()
    arrived("context")
    for part in range(3):
        pick9(part, context_s)
        multiply(out_job, part, xt9, gatt_s)
        first_send(out_job, part)
    slot_sum(5, branch)
    slot_sum(4, gquery)
    slot_sum(3, gsecond)
    slot_sum(2, attended)
    load("query_hat", query_hat_in, branch)
    load("key_hat", key_hat_in, attended)
    load("cos", cos_in, cosine)
    load("sin", sin_in, gsecond)
    query_hat, key_hat, sine = branch, attended, gsecond
    stages(second_send, up_job)

    gquery[...] = jnp.zeros_like(gquery)
    gkey[...] = jnp.zeros_like(gkey)
    gvalue[...] = jnp.zeros_like(gvalue)
    for name in ("query", "key", "value"):
        loads[name].wait()

    def attention_group(group):
        @pl.loop(0, 1)
        def _(pair):
            left = lax.broadcasted_iota(jnp.int32, (TOK, TOK), 0) // 36
            right = lax.broadcasted_iota(jnp.int32, (TOK, TOK), 1) // 36
            shut = jnp.where(kind | (left == right), 0.0, -1e30)
            for member in range(4):
                window, mask = head_window(group * 4 + pair + member)
                query_w, key_w = query[:, window] * mask, key[:, window] * mask
                value_w, grad_w = value[:, window], gcontext[:, window] * mask
                scores = inner_cols(query_w, key_w) * (72**-0.5) + shut
                weight = jnp.exp(scores - jnp.max(scores, axis=-1, keepdims=True))
                weight = weight * (1.0 / jnp.sum(weight, axis=-1, keepdims=True))
                gattention = inner_cols(grad_w, value_w)
                gvalue[:, window] += inner_rows(weight.astype(jnp.bfloat16), grad_w)
                dots = jnp.sum(weight * gattention, axis=-1, keepdims=True)
                gscores = (weight * (gattention - dots)).astype(jnp.bfloat16)
                gquery[:, window] += jnp.dot(gscores, key_w, preferred_element_type=jnp.float32)
                gkey[:, window] += inner_rows(gscores, query_w)

    attention_group(0)
    stages(first_add, down_job)
    attention_group(1)
    stages(second_add, gate_job)
    attention_group(2)
    stages(second_send, down_job)
    stages(first_add, out_job)
    attention_group(3)
    stages(second_add, up_job)
    for part in range(3):
        sent_out(down_job, part, 0, 1, 2, 3, 4, 5)
        sent_out(up_job, part, 0, 1, 2, 3, 4, 5)
    wide_parts("qkv", qkv_weight, 1)
    wide_parts("qkv", qkv_weight, 2)
    pairs["ggate"].wait_send()

    def project_back(which, grads, hat, rows):
        base = which * WIDE
        grad = grads[rows, :] * (72**-0.5)
        normed = hat[rows, :]
        turned = grad * cosine[rows, :] - swap_halves(grad) * sine[rows, :]
        gain_sum[which] += jnp.sum((turned * normed).reshape(6, 8, WIDE), axis=0)
        scaled = turned * gains[which : which + 1, :]
        inverse = inverses[which, rows, :]
        mean = head_sum(scaled * normed, heads[...]) * (1.0 / 72.0)
        raw = scaled * head_spread(inverse, heads[...]) - normed * head_spread(
            inverse * mean, heads[...]
        )
        gproj_s[rows, base : base + WIDE] = raw.astype(jnp.bfloat16)

    def project_rows(rows):
        project_back(0, gquery, query_hat, rows)
        project_back(1, gkey, key_hat, rows)

    def exchange_projected(part):
        columns = pl.ds(part * WIDE, WIDE)
        exchange("gproj%d" % part, gproj_s.at[own_rows, columns], gproj_s.at[other_rows, columns])

    def value_rows(rows):
        gproj_s[rows, 2 * WIDE : 3 * WIDE] = gvalue[rows, :].astype(jnp.bfloat16)

    row_blocks(value_rows)
    exchange_projected(2)
    for name in ("query_hat", "key_hat", "cos", "sin"):
        loads[name].wait()
    arrived("gproj2")
    first_s = second_s
    load("first", first_in, first_s.at[own_rows])
    exchange("first", first_in, first_s.at[other_rows])
    row_blocks(project_rows, 48)
    exchange_projected(0)
    exchange_projected(1)
    loads["first"].wait()
    arrived("first")
    for part in (2, 0, 1):
        pick9(part, first_s)
        if part != 2:
            arrived("gproj%d" % part)
        sent_out(gate_job, part, 0, 1, 2, 3, 4, 5)
        multiply(qkv_job, part, xt9, gproj_s)
        first_send(qkv_job, part)
    stages(third_send, gate_job)
    stages(second_send, out_job)
    stages(second_add, down_job)
    stages(third_send, up_job)

    gfirst, scaled_first = gquery, gkey
    wide_loads["qkv", 0].wait()
    gfirst[...] = inner_cols(gproj_s[0:TOK, 0:WIDE], out_w[...])
    wide_parts("mod", mod_weight, 0)
    wide_loads["qkv", 1].wait()
    gfirst[...] += inner_cols(gproj_s[0:TOK, WIDE : 2 * WIDE], third_w[...])
    wide_parts("mod", mod_weight, 1)
    wide_loads["qkv", 2].wait()
    wide_loads["qkv", 3].wait()
    gfirst[...] += inner_cols(gproj_s[0:TOK, 2 * WIDE : 3328], fourth_w[...])
    gfirst[...] += inner_cols(gproj_s[0:TOK, 3328:3456], narrow_w[...])
    wide_parts("mod", mod_weight, 2)

    def last_rows(rows):
        normed, inverse = rms_norm(tokens[rows, :].astype(jnp.float32))
        grad = gfirst[rows, :]
        scaled_first[rows, :] = grad * normed
        tokens_out[rows, :] = middle[rows, :] + norm_back(
            grad * (1.0 + piece(rows, 1)), normed, inverse
        )

    row_blocks(last_rows, 48)
    slot_sum(0, gfirst)
    slot_sum(1, scaled_first)
    for which in range(2):
        high, low = split_two(gain_sum[which])
        total = jnp.sum(inner_cols(high, folds[...]) + inner_cols(low, folds[...]), axis=0, keepdims=True)
        gmod[0, which : which + 1, 3456:3584] = total
    mod_pair()
    stages(first_add, qkv_job)
    stages(third_send, down_job)
    stages(second_add, out_job)
    mod_gather_first()
    condition_part()
    stages(finish, gate_job)
    stages(second_send, qkv_job)
    mod_gather_second()
    stages(third_send, out_job)
    loads["acts"].wait()
    mod_table()
    stages(finish, up_job)
    stages(second_add, qkv_job)
    mod_product()
    stages(finish, down_job)
    stages(third_send, qkv_job)
    mod_sum()
    stages(finish, out_job)
    stages(finish, qkv_job)
    mod_finish()
    for name, copy in pairs.items():
        if name != "ggate":
            copy.wait_send()
    for (job, part, slot) in list(copies):
        sent_out(job, part, slot)
    for copy in sent:
        copy.wait_send()


def write_kernel(*refs):
    count = len(refs) // 2 - 1
    for source, target in zip(refs[:count], refs[count:-2]):
        if len(source.shape) == 3:
            for half in range(2):
                target[pl.ds(half * 3456, 3456)] = source[half, 0, 0:3456]
            for which in range(2):
                total = source[0, 1 + which, 3456:3584] + source[1, 1 + which, 3456:3584]
                refs[count * 2 + which][...] = total[0:72]
        else:
            target[...] = source[:, 0 : target.shape[1]]


def backward(
    cotangent, tokens, condition, segments, saved, gate_weight, up_weight, down_weight, out_weight, qkv_weight, mod_weight
):
    (query, key, value, query_hat, key_hat, context, attended, middle, first, second, cosine, sine, acts, inverses, modulation, gains) = saved
    vmem = pl.BlockSpec(memory_space=pltpu.VMEM)
    anywhere = pl.BlockSpec(memory_space=pl.ANY)
    low, full = jnp.bfloat16, jnp.float32
    wide_low, wide_full = ((TOK, WIDE), low), ((TOK, WIDE), full)
    outs = (
        [wide_low, wide_full]
        + [((each, 3 * width), full) for _, each, width, _, _ in JOBS]
        + [((18, 3584), full), ((2, 8, 3584), full), ((4, WIDE), full)]
    )
    scratch = [
        ((PAIR, HID), low),
        ((PAIR, WIDE), low),
        ((PAIR, WIDE), low),
        ((PAIR, 3456), low),
        ((PAIR, HID), low),
        ((PAIR, WIDE), low),
        ((2, 288, 640), low),
        ((2, 288, 640), low),
        ((8, 80, 256), low),
        ((256, WIDE), low),
        ((192, 384), low),
        ((1536, PAIR), low),
        ((400, 128), full),
        ((128, WIDE), low),
        ((128, WIDE), low),
        ((TOK, 4 * WIDE), low),
        wide_full,
        wide_full,
        wide_full,
        wide_low,
        wide_low,
        wide_low,
        wide_low,
        wide_full,
        wide_full,
        wide_full,
        wide_full,
        ((2, 8, WIDE), full),
        ((WIDE, WIDE), low),
        ((WIDE, 128), low),
        ((2, 8, 3584), full),
        ((2, 48, 256), low),
        ((16, 896), full),
        ((16, 896), low),
        ((16, 896), low),
        ((8, 3584), full),
        ((8, 3584), full),
        ((16, 896), full),
        ((8, 896), full),
        ((8, 896), full),
        ((8, 896), full),
        ((16, 1792), full),
        ((4, 4, 16, 896), low),
        ((4, 4, 16, 896), low),
        ((48, 1792), full),
        ((48, 1792), low),
        ((48, 1792), low),
        ((48, 1792), full),
        ((2, 8, 1792), full),
        ((8, WIDE), full),
        ((8, WIDE), full),
    ]
    sums = {
        "gate": (16, 128),
        "up": (1728, 1024),
        "down": (1536, WIDE),
        "out": (1728, 384),
        "qkv": (1728, WIDE),
    }
    for name, each, width, _, _ in JOBS:
        big, small, tiny = 16 * each, sixteen(4 * each), sixteen(each)
        unused = name == "gate"
        scratch += [
            (sums[name], low),
            ((1, 16, 128) if unused else (3, big, width), low),
            ((1, 1, 16, 128) if unused else (3, 2, big, width), low),
            ((1, 1, 16, 128) if unused else (3, 4, small, width), low),
            ((3, small, width), low),
            ((3, 2, small, width), low),
            ((3, 7, tiny, width), low),
        ]
    count = PARTNER_COPIES + 3 * COPIES * len(JOBS) + MOD_COPIES
    results = pl.pallas_call(
        backward_kernel,
        out_shape=[jax.ShapeDtypeStruct(*out) for out in outs],
        in_specs=[pl.BlockSpec(memory_space=pltpu.SMEM)] + [vmem] * 6 + [anywhere] * 19,
        out_specs=[vmem] * 10,
        scratch_shapes=[pltpu.VMEM(*item) for item in scratch]
        + [
            pltpu.SemaphoreType.DMA((count,)),
            pltpu.SemaphoreType.DMA((count,)),
            pltpu.SemaphoreType.DMA((13,)),
            pltpu.SemaphoreType.DMA((4, 4)),
        ],
        compiler_params=pltpu.CompilerParams(
            collective_id=1, has_side_effects=True, vmem_limit_bytes=64 * 1024 * 1024 - 65536
        ),
        cost_estimate=pl.CostEstimate(
            flops=12_000_000_000, bytes_accessed=50_000_000, transcendentals=0
        ),
    )(
        segments,
        cotangent,
        tokens,
        modulation,
        condition,
        gains,
        inverses,
        acts.reshape(256, WIDE),
        second,
        first,
        context,
        middle,
        attended,
        query,
        key,
        value,
        query_hat,
        key_hat,
        cosine,
        sine,
        gate_weight,
        up_weight,
        down_weight,
        out_weight,
        qkv_weight,
        mod_weight,
    )
    special = results[8]
    kept = list(results[:8]) + [results[9]]
    shapes = [
        jax.ShapeDtypeStruct((item.shape[0], min(item.shape[1], 3456)), item.dtype) for item in kept
    ]
    written = pl.pallas_call(
        write_kernel,
        out_shape=shapes + [jax.ShapeDtypeStruct((size,), full) for size in (6912, 72, 72)],
        in_specs=[vmem] * 10,
        out_specs=[vmem] * 12,
    )(*kept, special)
    return written


def body(
    tokens,
    condition,
    segments,
    mod_weight,
    mod_bias,
    qkv_weight,
    query_gain,
    key_gain,
    out_weight,
    gate_weight,
    up_weight,
    down_weight,
    cotangent,
):
    saved = forward(tokens, condition, segments, mod_weight, mod_bias, qkv_weight, query_gain, key_gain, out_weight)
    written = backward(
        cotangent,
        tokens,
        condition,
        segments,
        saved,
        gate_weight,
        up_weight,
        down_weight,
        out_weight,
        qkv_weight,
        mod_weight,
    )
    layer_out, grad_tokens, gate, up, down, out, qkv, mod_rows, grad_condition, bias, query_grad, key_grad = written
    return (
        layer_out,
        grad_tokens,
        grad_condition,
        mod_rows,
        bias,
        qkv,
        query_grad,
        key_grad,
        out,
        gate,
        up,
        down,
    )


def solution(mesh):
    placed = (
        P(("dp", "mod"), None),
        P(("dp", "mod"), None),
        P(("dp", "mod")),
        P(None, "mod"),
        P("mod"),
        P(),
        P(),
        P(),
        P(),
        P(),
        P(),
        P(),
        P(("dp", "mod"), None),
    )
    return jax.shard_map(
        body,
        mesh=mesh,
        in_specs=placed,
        out_specs=(
            P(("dp", "mod"), None),
            P(("dp", "mod"), None),
            P(("dp", "mod"), None),
            P("dp", "mod"),
            P(),
            P(("dp", "mod"), None),
            P(),
            P(),
            P(("dp", "mod"), None),
            P(("dp", "mod"), None),
            P(("dp", "mod"), None),
            P(("dp", "mod"), None),
        ),
        check_vma=False,
    )
```

```python
import jax
import jax.numpy as jnp
import numpy as np
from jax import lax
from jax.experimental import pallas as pl
from jax.experimental.pallas import tpu as pltpu
from jax.sharding import PartitionSpec as P

EPSILON = 1e-06


def rms_norm(values):
    inverse = lax.rsqrt(jnp.mean(values * values, axis=-1, keepdims=True) + EPSILON)
    return (values * inverse, inverse)


def norm_back(upstream, normed, inverse):
    return inverse * (upstream - normed * jnp.mean(upstream * normed, axis=-1, keepdims=True))


def silu_slope(values):
    logistic = jax.nn.sigmoid(values)
    return logistic * (1.0 + values * (1.0 - logistic))


def inner_rows(left, right):
    return lax.dot_general(
        left, right, (((0,), (0,)), ((), ())), preferred_element_type=jnp.float32
    )


def inner_cols(left, right):
    return lax.dot_general(
        left, right, (((1,), (1,)), ((), ())), preferred_element_type=jnp.float32
    )


TOK = 144
PAIR = 2 * TOK
WIDE = 1152
HID = 3072
RING = 4
AXES = ((0, 2, 1), (1, 0, 2), (2, 1, 0))
JOBS = (
    ("gate", 9, 1024, 256, 512),
    ("up", 9, 1024, 256, 512),
    ("down", 24, 384, 384, 256),
    ("out", 9, 384, 384, 256),
    ("qkv", 9, 1152, 384, 640),
)
COPIES = 15
PARTNER_COPIES = 17
MOD_COPIES = 20
CHUNK = 512


def sixteen(rows):
    return (rows + 15) // 16 * 16


def position():
    dp = lax.axis_index("dp")
    x_hi = lax.axis_index("mod")
    core = lax.rem(dp, 2)
    y = lax.rem(dp // 2, 4)
    z = lax.rem(dp // 8, 4)
    return (x_hi * 2 + dp // 32, y, z), core


def device_at(place, core):
    x, y, z = place
    return (((lax.rem(x, 2) * 4 + z) * 4 + y) * 2 + core, x // 2)


def moved(place, axis, value):
    return tuple(value if index == axis else kept for index, kept in enumerate(place))


def line_of(axis, value):
    return value % 2 * 2 + value // 2 if axis == 0 else value


FWD_REMOTE = 12
MESH = pl.DeviceIdType.MESH


def rope_flat():
    token = np.arange(TOK)
    frequency = 10000.0 ** (-np.arange(18, dtype=np.float64) / 18)
    tables = []
    for position_in, side in ((token % 36, 6), (token, 12)):
        row, column = position_in // side, position_in % side
        angle = np.concatenate([row[:, None] * frequency, column[:, None] * frequency], axis=1)
        cosine = np.tile(np.concatenate([np.cos(angle), np.cos(angle)], axis=1), (1, 16))
        sine = np.tile(np.concatenate([-np.sin(angle), np.sin(angle)], axis=1), (1, 16))
        tables.append((cosine, sine))
    return (
        np.stack([pair[0] for pair in tables]).astype(np.float32),
        np.stack([pair[1] for pair in tables]).astype(np.float32),
    )


def row_blocks(step, size=16):
    @pl.loop(0, TOK // size)
    def _(index):
        step(pl.ds(pl.multiple_of(index * size, 16), size))


def split_two(values):
    high = values.astype(jnp.bfloat16)
    return high, (values - high.astype(jnp.float32)).astype(jnp.bfloat16)


def head_sum(values, heads):
    high, low = split_two(values)
    return inner_cols(high, heads) + inner_cols(low, heads)


def head_spread(values, heads):
    high, low = split_two(values)
    return jnp.dot(high, heads, preferred_element_type=jnp.float32) + jnp.dot(
        low, heads, preferred_element_type=jnp.float32
    )


def head_rows():
    head = lax.broadcasted_iota(jnp.int32, (128, WIDE), 0) * 72
    lane = lax.broadcasted_iota(jnp.int32, (128, WIDE), 1)
    return ((lane >= head) & (lane < head + 72)).astype(jnp.float32).astype(jnp.bfloat16)


def swap_halves(values):
    lane = lax.broadcasted_iota(jnp.int32, values.shape, 1)
    first = lax.rem(lane, 72) < 36
    return jnp.where(first, pltpu.roll(values, WIDE - 36, 1), pltpu.roll(values, 36, 1))


def head_window(head):
    block = jnp.minimum(head * 72 // 128, 7)
    offset = head * 72 - block * 128
    lane = lax.broadcasted_iota(jnp.int32, (1, 256), 1)
    mask = ((lane >= offset) & (lane < offset + 72)).astype(jnp.float32).astype(jnp.bfloat16)
    return pl.ds(pl.multiple_of(block * 128, 128), 256), mask


def forward_kernel(
    segments,
    tokens,
    condition,
    mod_bias,
    query_gain,
    key_gain,
    cos_in,
    sin_in,
    mod_weight,
    qkv_weight,
    out_weight,
    query_out,
    key_out,
    value_out,
    query_hat_out,
    key_hat_out,
    context_out,
    attended_out,
    middle_out,
    first_out,
    second_out,
    cos_out,
    sin_out,
    gathered_out,
    inverse_out,
    modulation_out,
    gains,
    mod_w,
    qkv_w,
    out_w,
    cos2,
    sin2,
    cond32,
    cond_other,
    act32,
    act_across,
    gathered,
    half32,
    fold32,
    fold_own,
    fold_other,
    mods32,
    per_token,
    norm,
    first,
    projected,
    query,
    key,
    value,
    query_hat,
    key_hat,
    context32,
    context,
    attended,
    middle,
    second,
    cosine,
    sine,
    heads,
    send_sem,
    recv_sem,
    in_sem,
    out_sem,
):
    place, core = position()
    mod = lax.axis_index("mod")
    partner = device_at(place, 1 - core)
    twin = device_at(moved(place, 0, lax.rem(place[0] + 2, 4)), core)
    peers = [
        [device_at(moved(place, axis, lax.rem(place[axis] + step, 4)), core) for step in (1, 2, 3)]
        for axis in (1, 2)
    ]
    loads = {}

    def load(name, index, src, dst, slot):
        copy = pltpu.make_async_copy(src, dst, in_sem.at[slot])
        copy.start()
        loads[name, index] = copy

    for index in range(3):
        columns = pl.ds(index * WIDE, WIDE)
        load("mod", index, mod_weight.at[:, columns], mod_w.at[:, columns], index)
    load("cos", 0, cos_in, cos2, 21)
    load("sin", 0, sin_in, sin2, 22)
    for index in range(3):
        columns = pl.ds(index * WIDE, WIDE)
        load("qkv", index, qkv_weight.at[:, columns], qkv_w.at[:, columns], 9 + index)
    load("out", 0, out_weight, out_w, 18)

    sent = []
    copies = {}

    def send(slot, src, dst, target):
        copy = pltpu.make_async_remote_copy(
            src_ref=src,
            dst_ref=dst,
            send_sem=send_sem.at[slot],
            recv_sem=recv_sem.at[slot],
            device_id=target,
            device_id_type=MESH,
        )
        copy.start()
        sent.append(copy)
        copies[slot] = copy

    stores = []

    def store(src, dst):
        copy = pltpu.make_async_copy(src, dst, out_sem.at[len(stores)])
        copy.start()
        stores.append(copy)

    barrier = pltpu.get_barrier_semaphore()
    for target in [partner, twin] + peers[0] + peers[1]:
        pl.semaphore_signal(barrier, inc=1, device_id=target, device_id_type=MESH)
    cond32[...] = jnp.zeros_like(cond32)
    cond32[0:4, :] = condition[...].astype(jnp.float32)
    pl.semaphore_wait(barrier, 8)
    send(0, cond32, cond_other, twin)

    for which, source in enumerate((query_gain, key_gain)):
        gains[which : which + 1, :] = jnp.concatenate([source[...].reshape(1, 72)] * 16, axis=1)
    kind = segments[TOK - 1] == 0
    row = lax.broadcasted_iota(jnp.int32, (TOK, 16), 0)
    slot = lax.broadcasted_iota(jnp.int32, (TOK, 16), 1)
    onehot = (slot == jnp.where(kind, 0, row // 36)).astype(jnp.float32).astype(jnp.bfloat16)
    heads[...] = head_rows()

    def first_norm(rows):
        values = tokens[rows, :].astype(jnp.float32)
        norm[rows, :] = rms_norm(values)[0]

    row_blocks(first_norm, 48)

    copies[0].wait_recv()
    own, other = cond32[0:4, :], cond_other[0:4, :]
    act32[0:4, :] = jnp.where(mod == 0, own, other)
    act32[4:8, :] = jnp.where(mod == 0, other, own)
    act32[...] = jax.nn.silu(act32[...]).astype(jnp.bfloat16).astype(jnp.float32)
    send(1, act32, act_across, partner)
    act = act32[...].astype(jnp.bfloat16)
    half32[...] = jnp.zeros_like(half32)
    for index in range(3):
        columns = slice(index * WIDE, (index + 1) * WIDE)
        loads["mod", index].wait()
        half32[:, columns] = (
            (
                jnp.dot(act, mod_w[:, columns], preferred_element_type=jnp.float32)
                + mod_bias[columns].astype(jnp.float32).reshape(1, WIDE)
            )
            .astype(jnp.bfloat16)
            .astype(jnp.float32)
        )
    for quarter in range(4):
        columns = slice(quarter * 896, (quarter + 1) * 896)
        fold32[4 * quarter : 4 * quarter + 4, :] = jnp.where(
            mod == 0, half32[4:8, columns], half32[0:4, columns]
        )
    fold_own[...] = fold32[...].astype(jnp.bfloat16)
    send(2, fold_own, fold_other, twin)

    copies[1].wait_recv()
    _, y, z = place
    rows16 = jnp.concatenate(
        [
            jnp.where(core == 0, act32[...], act_across[...]),
            jnp.where(core == 0, act_across[...], act32[...]),
        ]
    )
    gathered[z, y] = rows16.astype(jnp.bfloat16)
    for step in range(3):
        send(3 + step, gathered.at[z, y], gathered.at[z, y], peers[0][step])
    loads["cos", 0].wait()
    loads["sin", 0].wait()

    def pick_table(rows):
        cosine[rows, :] = jnp.where(kind, cos2[1, rows, :], cos2[0, rows, :])
        sine[rows, :] = jnp.where(kind, sin2[1, rows, :], sin2[0, rows, :])

    row_blocks(pick_table)
    store(cosine, cos_out)
    store(sine, sin_out)
    for slot_ in (3, 4, 5):
        copies[slot_].wait_recv()
    for step in range(3):
        send(6 + step, gathered.at[z], gathered.at[z], peers[1][step])

    copies[2].wait_recv()
    mods32[...] = jnp.zeros_like(mods32)
    fold32[...] = fold_other[...].astype(jnp.float32)
    for quarter in range(4):
        width = 896 if quarter < 3 else 768
        mods32[0:4, pl.ds(pl.multiple_of((1 - mod) * 3456 + quarter * 896, 128), width)] = fold32[
            4 * quarter : 4 * quarter + 4, 0:width
        ]
    mods32[0:4, pl.ds(pl.multiple_of(mod * 3456, 128), 3456)] = jnp.where(
        mod == 0, half32[0:4, 0:3456], half32[4:8, 0:3456]
    )
    modulation_out[...] = mods32[...].astype(jnp.bfloat16)
    for index in range(5):
        columns = slice(index * WIDE, (index + 1) * WIDE)
        per_token[:, columns] = jnp.dot(
            onehot, modulation_out[:, columns], preferred_element_type=jnp.float32
        ).astype(jnp.bfloat16)

    def piece(rows, index):
        return per_token[rows, index * WIDE : (index + 1) * WIDE].astype(jnp.float32)

    def first_input(rows):
        first[rows, :] = (norm[rows, :] * (1.0 + piece(rows, 1)) + piece(rows, 0)).astype(jnp.bfloat16)

    row_blocks(first_input, 48)
    store(first, first_out)

    for index in range(3):
        loads["qkv", index].wait()
        columns = slice(index * WIDE, (index + 1) * WIDE)
        result = jnp.dot(first[...], qkv_w[:, columns], preferred_element_type=jnp.float32)
        if index < 2:
            projected[:, columns] = result
        else:
            value[...] = result.astype(jnp.bfloat16)
    store(value, value_out)

    def head_norm(which, hat, result, rows):
        raw = projected[rows, which * WIDE : (which + 1) * WIDE]
        total = head_sum(raw * raw, heads[...])
        inverse = lax.rsqrt(total * (1.0 / 72.0) + EPSILON)
        inverse_out[which, rows, :] = inverse
        normed = raw * head_spread(inverse, heads[...])
        hat[rows, :] = normed
        scaled = normed * gains[which : which + 1, :]
        turned = scaled * cosine[rows, :] + swap_halves(scaled) * sine[rows, :]
        result[rows, :] = turned.astype(jnp.bfloat16)

    def head_rows_step(rows):
        head_norm(0, query_hat, query, rows)
        head_norm(1, key_hat, key, rows)

    row_blocks(head_rows_step, 48)
    store(query_hat, query_hat_out)
    store(query, query_out)
    store(key_hat, key_hat_out)
    store(key, key_out)

    left = lax.broadcasted_iota(jnp.int32, (TOK, TOK), 0) // 36
    right = lax.broadcasted_iota(jnp.int32, (TOK, TOK), 1) // 36
    shut = jnp.where(kind | (left == right), 0.0, -1e30)
    context32[...] = jnp.zeros_like(context32)

    @pl.loop(0, 4)
    def _(group):
        for member in range(4):
            head = group * 4 + member
            window, mask = head_window(head)
            scores = inner_cols(query[:, window] * mask, key[:, window]) * (72**-0.5) + shut
            top = jnp.max(scores, axis=-1, keepdims=True)
            weight = jnp.exp(scores - top)
            weight = weight * (1.0 / jnp.sum(weight, axis=-1, keepdims=True))
            context32[:, window] += jnp.dot(
                weight.astype(jnp.bfloat16), value[:, window] * mask, preferred_element_type=jnp.float32
            )

    context[...] = context32[...].astype(jnp.bfloat16)
    store(context, context_out)
    loads["out", 0].wait()
    attended[...] = jnp.dot(context[...], out_w[...], preferred_element_type=jnp.float32)
    store(attended, attended_out)

    def second_input(rows):
        total = tokens[rows, :].astype(jnp.float32) + piece(rows, 2) * attended[rows, :]
        middle[rows, :] = total
        normed = rms_norm(total)[0]
        second[rows, :] = (normed * (1.0 + piece(rows, 4)) + piece(rows, 3)).astype(jnp.bfloat16)

    row_blocks(second_input, 48)
    store(middle, middle_out)
    store(second, second_out)
    for slot_ in (6, 7, 8):
        copies[slot_].wait_recv()
    store(gathered, gathered_out)
    for copy in sent:
        copy.wait_send()
    for copy in stores:
        copy.wait()


def forward(tokens, condition, segments, mod_weight, mod_bias, qkv_weight, query_gain, key_gain, out_weight):
    cos_table, sin_table = rope_flat()
    vmem = pl.BlockSpec(memory_space=pltpu.VMEM)
    anywhere = pl.BlockSpec(memory_space=pl.ANY)
    low, full = jnp.bfloat16, jnp.float32
    wide_low = ((TOK, WIDE), low)
    wide_full = ((TOK, WIDE), full)
    outs = (
        [wide_low] * 3
        + [wide_full] * 2
        + [wide_low, wide_full, wide_full, wide_low, wide_low]
        + [wide_full] * 2
        + [((4, 4, 16, WIDE), low)]
        + [((2, TOK, 128), full), ((16, 6 * WIDE), low), ((2, WIDE), full)]
    )
    scratch = [
        ((WIDE, 3456), low),
        ((WIDE, 3456), low),
        ((WIDE, WIDE), low),
        ((2, TOK, WIDE), full),
        ((2, TOK, WIDE), full),
        ((8, WIDE), full),
        ((8, WIDE), full),
        ((8, WIDE), full),
        ((8, WIDE), full),
        ((4, 4, 16, WIDE), low),
        ((8, 3584), full),
        ((16, 896), full),
        ((16, 896), low),
        ((16, 896), low),
        ((16, 6912), full),
        ((TOK, 6912), low),
        wide_full,
        wide_low,
        ((TOK, 2304), full),
        wide_low,
        wide_low,
        wide_low,
        wide_full,
        wide_full,
        wide_full,
        wide_low,
        wide_full,
        wide_full,
        wide_low,
        wide_full,
        wide_full,
        ((128, WIDE), low),
    ]
    return pl.pallas_call(
        forward_kernel,
        out_shape=[jax.ShapeDtypeStruct(*out) for out in outs],
        in_specs=[pl.BlockSpec(memory_space=pltpu.SMEM)] + [vmem] * 5 + [anywhere] * 5,
        out_specs=[anywhere] * 13 + [vmem] * 3,
        scratch_shapes=[pltpu.VMEM(*item) for item in scratch]
        + [
            pltpu.SemaphoreType.DMA((FWD_REMOTE,)),
            pltpu.SemaphoreType.DMA((FWD_REMOTE,)),
            pltpu.SemaphoreType.DMA((23,)),
            pltpu.SemaphoreType.DMA((16,)),
        ],
        compiler_params=pltpu.CompilerParams(
            collective_id=2, has_side_effects=True, vmem_limit_bytes=56 * 1024 * 1024
        ),
        cost_estimate=pl.CostEstimate(flops=2_000_000_000, bytes_accessed=30_000_000, transcendentals=0),
    )(
        segments,
        tokens,
        condition,
        mod_bias,
        query_gain,
        key_gain,
        jnp.asarray(cos_table),
        jnp.asarray(sin_table),
        mod_weight,
        qkv_weight,
        out_weight,
    )


def backward_kernel(
    segments,
    cotangent,
    tokens,
    modulation,
    condition,
    gains,
    inverses,
    acts,
    second_in,
    first_in,
    context_in,
    middle_in,
    attended_in,
    query_in,
    key_in,
    value_in,
    query_hat_in,
    key_hat_in,
    cos_in,
    sin_in,
    gate_weight,
    up_weight,
    down_weight,
    out_weight,
    qkv_weight,
    mod_weight,
    layer_out,
    tokens_out,
    gate_out,
    up_out,
    down_out,
    out_out,
    qkv_out,
    mod_out,
    special_out,
    condition_out,
    hidden_s,
    second_s,
    gbranch_s,
    ggate_s,
    gup_s,
    gatt_s,
    pick_x,
    pick_y,
    pick_z,
    acts_s,
    perm24,
    xt24,
    acc,
    heads,
    folds,
    per_token,
    branch,
    gsecond,
    attended,
    query,
    key,
    value,
    gcontext,
    gquery,
    gkey,
    gvalue,
    cosine,
    gain_sum,
    out_w,
    narrow_w,
    gmod,
    act_rows,
    fold32,
    fold_own,
    fold_other,
    other32,
    pair32,
    turned32,
    side_own,
    side_other,
    cross_other,
    rows32,
    gathered_a,
    gathered_b,
    product_own,
    product_send,
    product_other,
    final_other,
    special_other,
    part_own,
    part_other,
    *rest,
):
    bufs = [list(rest[7 * index : 7 * index + 7]) for index in range(len(JOBS))]
    for index in range(4):
        bufs[0][index] = bufs[4][index]
    xt9 = xt24.at[pl.ds(0, 576)]
    send_sem, recv_sem, local_sem, ring_sem = rest[7 * len(JOBS) :]
    gproj_s, middle = ggate_s, tokens_out
    place, core = position()
    mod = lax.axis_index("mod")
    partner = device_at(place, 1 - core)
    near = []
    for axis in range(3):
        here = place[axis]
        near.append(
            (here, lax.rem(here + 1, 4), lax.rem(here + 3, 4), lax.rem(here + 2, 4))
        )
    twin = moved(place, 0, near[0][3])

    ring_a, ring_b, ring_c = bufs[0][0], bufs[1][0], bufs[2][0]

    def ff_slots(slot):
        columns = pl.ds(pl.multiple_of(slot * CHUNK, CHUNK), CHUNK)
        return (
            ring_a.at[pl.ds(0, WIDE), columns],
            ring_b.at[pl.ds(0, WIDE), columns],
            ring_c.at[columns, :],
        )

    def ff_chunk(index, slot):
        columns = pl.ds(pl.multiple_of(index * CHUNK, CHUNK), CHUNK)
        sources = (gate_weight.at[:, columns], up_weight.at[:, columns], down_weight.at[columns, :])
        return [
            pltpu.make_async_copy(source, target, ring_sem.at[number, slot])
            for number, (source, target) in enumerate(zip(sources, ff_slots(slot)))
        ]

    wide_loads = {}

    def wide_load(name, index, source, target, number):
        copy = pltpu.make_async_copy(source, target, ring_sem.at[3, number])
        copy.start()
        wide_loads[name, index] = copy

    for index in range(2):
        for copy in ff_chunk(index, index):
            copy.start()
    wide_load("out", 0, out_weight, out_w, 0)
    third_w = ring_c.at[pl.ds(0, WIDE), :]
    fourth_w = ring_b.at[pl.ds(0, WIDE), :]

    def wide_parts(name, source, number):
        if number == 0:
            wide_load(name, 0, source.at[:, pl.ds(0, WIDE)], out_w, 0)
        elif number == 1:
            wide_load(name, 1, source.at[:, pl.ds(WIDE, WIDE)], third_w, 1)
        else:
            wide_load(name, 2, source.at[:, pl.ds(2 * WIDE, 1024)], fourth_w, 2)
            wide_load(name, 3, source.at[:, pl.ds(3328, 128)], narrow_w, 3)

    loads = {}

    def load(name, src, dst):
        copy = pltpu.make_async_copy(src, dst, local_sem.at[len(loads)])
        copy.start()
        loads[name] = copy

    own_rows, other_rows = pl.ds(0, TOK), pl.ds(TOK, TOK)
    load("second", second_in, second_s.at[own_rows])
    load("middle", middle_in, middle)
    load("attended", attended_in, attended)
    load("query", query_in, query)
    load("acts", acts, acts_s)
    load("key", key_in, key)
    load("value", value_in, value)

    barrier = pltpu.get_barrier_semaphore()
    pl.semaphore_signal(barrier, inc=1, device_id=partner, device_id_type=MESH)
    for axis in range(3):
        for far in near[axis][1:]:
            pl.semaphore_signal(
                barrier,
                inc=1,
                device_id=device_at(moved(place, axis, far), core),
                device_id_type=MESH,
            )
    pl.semaphore_signal(barrier, inc=1, device_id=device_at(twin, 1 - core), device_id_type=MESH)

    kind = segments[TOK - 1] == 0
    token = lax.broadcasted_iota(jnp.int32, (TOK, 16), 0)
    slot_of = lax.broadcasted_iota(jnp.int32, (TOK, 16), 1)
    onehot = (slot_of == jnp.where(kind, 0, token // 36)).astype(jnp.float32).astype(jnp.bfloat16)
    token_t = lax.broadcasted_iota(jnp.int32, (16, TOK), 1)
    slot_t = lax.broadcasted_iota(jnp.int32, (16, TOK), 0)
    onehot_t = (slot_t == jnp.where(kind, 0, token_t // 36)).astype(jnp.float32).astype(jnp.bfloat16)
    for index, block in enumerate((5, 4, 2, 1)):
        per_token[:, index * WIDE : (index + 1) * WIDE] = jnp.dot(
            onehot, modulation[:, block * WIDE : (block + 1) * WIDE], preferred_element_type=jnp.float32
        ).astype(jnp.bfloat16)

    def piece(rows, block):
        base = (5, 4, 2, 1).index(block) * WIDE
        return per_token[rows, base : base + WIDE].astype(jnp.float32)

    def first_rows(rows):
        upstream = cotangent[rows, :].astype(jnp.float32)
        gbranch_s[rows, :] = (upstream * piece(rows, 5)).astype(jnp.bfloat16)
        zero = jnp.zeros((48, WIDE), jnp.float32)
        branch[rows, :] = zero
        gsecond[rows, :] = zero

    row_blocks(first_rows, 48)
    gmod[...] = jnp.zeros_like(gmod)
    gain_sum[...] = jnp.zeros_like(gain_sum)

    def remote(src, dst, index, target):
        return pltpu.make_async_remote_copy(
            src_ref=src,
            dst_ref=dst,
            send_sem=send_sem.at[index],
            recv_sem=recv_sem.at[index],
            device_id=target,
            device_id_type=MESH,
        )

    sent = []
    pairs, landed = {}, set()

    def exchange(name, src, dst):
        copy = remote(src, dst, len(pairs), partner)
        copy.start()
        pairs[name] = copy


    def arrived(*names):
        for name in names:
            if name not in landed:
                landed.add(name)
                pairs[name].wait_recv()

    lane24 = lax.broadcasted_iota(jnp.int32, (192, 384), 1)
    row24 = lax.broadcasted_iota(jnp.int32, (192, 384), 0)
    perm24[...] = (
        (lane24 == row24 // 48 * 96 + lax.rem(row24, 48) + core * 48)
        .astype(jnp.float32)
        .astype(jnp.bfloat16)
    )
    heads[...] = head_rows()
    folded = lax.rem(lax.broadcasted_iota(jnp.int32, (128, WIDE), 1), 72)
    folds[...] = (
        (folded == lax.broadcasted_iota(jnp.int32, (128, WIDE), 0)).astype(jnp.float32).astype(jnp.bfloat16)
    )

    row = lax.broadcasted_iota(jnp.int32, (288, 640), 0)
    lane = lax.broadcasted_iota(jnp.int32, (288, 640), 1)
    unit, entry = row // 9, lax.rem(row, 9)
    for_x = unit // 16 * 9 + lax.rem(unit // 4, 4) * 144 + lax.rem(unit, 4) * 36 + entry + core * 18
    for_y = unit // 8 * 36 + lax.rem(unit // 4, 2) * 9 + lax.rem(unit, 4) * 144 + entry + core * 18
    for x_lo in range(2):
        pick_x[x_lo] = (lane == for_x + x_lo * 64).astype(jnp.float32).astype(jnp.bfloat16)
        pick_y[x_lo] = (lane == for_y + x_lo * 64).astype(jnp.float32).astype(jnp.bfloat16)
    row = lax.broadcasted_iota(jnp.int32, (80, 256), 0)
    lane = lax.broadcasted_iota(jnp.int32, (80, 256), 1)
    unit = row // 9
    for_z = unit // 2 * 36 + lax.rem(unit, 2) * 9 + lax.rem(row, 9) + core * 18
    for block in range(8):
        pick_z[block] = (
            ((row < 72) & (lane == for_z + block * 16)).astype(jnp.float32).astype(jnp.bfloat16)
        )

    def pick9(part, stack):
        if part == 2:
            for z in range(4):
                halves = []
                for x_lo in range(2):
                    block = x_lo * 4 + z
                    rows = inner_cols(pick_z[block], stack[:, block * 128 : block * 128 + 256])
                    halves.append(rows[0:72])
                xt9[z * 144 : (z + 1) * 144, :] = jnp.concatenate(halves).astype(jnp.bfloat16)
            return
        table = (pick_x, pick_y)[part]
        low = inner_cols(table[0], stack[:, 0:640])
        high = inner_cols(table[1], stack[:, 512:WIDE])
        for value_ in range(4):
            if part == 0:
                half = (low, high)[value_ % 2]
                rows = half[value_ // 2 * 144 : value_ // 2 * 144 + 144]
            else:
                at = slice(value_ * 72, (value_ + 1) * 72)
                rows = jnp.concatenate([low[at], high[at]])
            xt9[value_ * 144 : (value_ + 1) * 144, :] = rows.astype(jnp.bfloat16)

    def pick24(part):
        def block_rows(block):
            columns = pl.ds(pl.multiple_of(block * 384, 128), 384)
            return inner_cols(perm24[...], hidden_s[:, columns])

        def put(unit, rows):
            xt24[pl.ds(pl.multiple_of(unit * 24, 16), 48), :] = rows.astype(jnp.bfloat16)

        def unit_rows(rows, y, x_hi):
            at = (y * 2 + x_hi) * 24
            return rows[at : at + 24]

        @pl.loop(0, 2)
        def _(x_lo):
            blocks = [block_rows(x_lo * 4 + z) for z in range(4)]
            for z in range(4):
                for y in range(4):
                    for x_hi in range(2):
                        upper = unit_rows(blocks[z], y, x_hi)
                        if part == 0 and y % 2 == 0:
                            unit = (x_hi * 2 + x_lo) * 16 + z * 4 + y
                            put(unit, jnp.concatenate([upper, unit_rows(blocks[z], y + 1, x_hi)]))
                        elif part == 1 and z % 2 == 0:
                            unit = y * 16 + (x_lo * 2 + x_hi) * 4 + z
                            put(unit, jnp.concatenate([upper, unit_rows(blocks[z + 1], y, x_hi)]))
                        elif part == 2 and x_hi == 0:
                            unit = z * 16 + y * 4 + x_lo * 2
                            put(unit, jnp.concatenate([upper, unit_rows(blocks[z], y, 1)]))

    def multiply(job, part, left, right):
        width = JOBS[job][2]
        own_view(job, part)[...] = jnp.dot(
            left[...], right[:, part * width : (part + 1) * width], preferred_element_type=jnp.float32
        ).astype(jnp.bfloat16)

    copies = {}
    drained = set()

    def begin(job, part, slot, src, dst, target):
        index = PARTNER_COPIES + (job * 3 + part) * COPIES + slot
        copy = remote(src, dst, index, target)
        copy.start()
        copies[job, part, slot] = copy

    def arrive(job, part, *slots):
        for slot in slots:
            copies[job, part, slot].wait_recv()

    def ring(part, phase):
        axis = AXES[part][phase]
        here, right, left, opposite = near[axis]
        return (
            here,
            right,
            left,
            opposite,
            device_at(moved(place, axis, right), core),
            device_at(moved(place, axis, left), core),
            device_at(moved(place, axis, opposite), core),
        )

    def sent_out(job, part, *slots):
        for slot in slots:
            if (job, part, slot) not in drained:
                drained.add((job, part, slot))
                copies[job, part, slot].wait_send()

    def own_view(job, part):
        base, width = bufs[job][0], JOBS[job][2]
        if JOBS[job][0] == "down":
            return base.at[:, pl.ds(part * width, width)]
        return base.at[pl.ds(part * 576, 576), pl.ds(0, width)]

    def first_send(job, part):
        half, whole = bufs[job][1:3]
        own = own_view(job, part)
        big = 16 * JOBS[job][1]
        cut = sixteen(big // 2) if job % 2 == 0 else big // 32 * 16
        here, right, left, opposite, to_right, to_left, _ = ring(part, 0)

        full = pl.ds(0, JOBS[job][2])

        def rows(chunk, start, count):
            return own.at[pl.ds(pl.multiple_of(chunk * big + start, 16), count)]

        begin(job, part, 0, rows(opposite, 0, cut), half.at[part, pl.ds(0, cut), full], to_right)
        begin(job, part, 1, rows(opposite, cut, big - cut), half.at[part, pl.ds(cut, big - cut), full], to_left)
        begin(job, part, 2, rows(right, cut, big - cut), whole.at[part, 0, pl.ds(cut, big - cut), full], to_right)
        begin(job, part, 3, rows(left, 0, cut), whole.at[part, 1, pl.ds(0, cut), full], to_left)

    def first_add(job, part):
        half, whole = bufs[job][1:3]
        own = own_view(job, part)
        _, each, width, lanes, _ = JOBS[job]
        big = 16 * each
        cut = sixteen(big // 2) if job % 2 == 0 else big // 32 * 16
        here, right, left, opposite, to_right, to_left, _ = ring(part, 0)
        for slot, chunk, start, count, target, side in (
            (0, right, 0, cut, to_right, 0),
            (1, left, cut, big - cut, to_left, 1),
        ):
            arrive(job, part, slot)
            rows = pl.ds(pl.multiple_of(chunk * big + start, 16), count)

            @pl.loop(0, width // 128)
            def _(step):
                columns = pl.ds(pl.multiple_of(step * 128, 128), 128)
                total = own[rows, columns].astype(jnp.float32) + half[
                    part, pl.ds(start, count), columns
                ].astype(jnp.float32)
                own[rows, columns] = total.astype(jnp.bfloat16)

            begin(
                job,
                part,
                4 + side,
                own.at[rows],
                whole.at[part, side, pl.ds(start, count), pl.ds(0, width)],
                target,
            )

    def second_send(job, part):
        _, _, whole, mid, mid_half, mid_whole, _ = bufs[job]
        own = own_view(job, part)
        _, each, width, lanes, cut = JOBS[job]
        big, small = 16 * each, 4 * each
        padded = sixteen(small)
        here, right, left, opposite, to_right, to_left, _ = ring(part, 0)
        arrive(job, part, 2, 3, 4, 5)
        if JOBS[job][0] == "qkv":
            sent_out(0, part, 6, 7, 8, 9, 10, 11)
        rows = pl.ds(pl.multiple_of(here * big, 16), big)

        @pl.loop(0, width // 128)
        def _(step):
            columns = pl.ds(pl.multiple_of(step * 128, 128), 128)
            total = (
                own[rows, columns].astype(jnp.float32)
                + whole[part, 0, :, columns].astype(jnp.float32)
                + whole[part, 1, :, columns].astype(jnp.float32)
            )
            if part == 2 and each == 9:
                for x_lo in range(2):
                    for y in range(4):
                        piece_at = x_lo * 72 + y * 18
                        acc[y * 36 + x_lo * 18 : y * 36 + x_lo * 18 + 18, :] = total[piece_at : piece_at + 18]
            else:
                acc[pl.ds(0, big), :] = total
            for chunk in range(4):
                line = line_of(AXES[part][1], chunk)
                mid[part, chunk, :, columns] = acc[pl.ds(line * small, padded), :].astype(jnp.bfloat16)

        here, right, left, opposite, to_right, to_left, _ = ring(part, 1)
        low, high = pl.ds(0, cut), pl.ds(cut, width - cut)
        begin(job, part, 6, mid.at[part, opposite, :, low], mid_half.at[part, :, low], to_right)
        begin(job, part, 7, mid.at[part, opposite, :, high], mid_half.at[part, :, high], to_left)
        begin(job, part, 8, mid.at[part, right, :, high], mid_whole.at[part, 0, :, high], to_right)
        begin(job, part, 9, mid.at[part, left, :, low], mid_whole.at[part, 1, :, low], to_left)

    def second_add(job, part):
        _, _, _, mid, mid_half, mid_whole, _ = bufs[job]
        _, each, width, lanes, cut = JOBS[job]
        here, right, left, opposite, to_right, to_left, _ = ring(part, 1)
        for slot, chunk, start, count, target, side in (
            (6, right, 0, cut, to_right, 0),
            (7, left, cut, width - cut, to_left, 1),
        ):
            arrive(job, part, slot)

            @pl.loop(0, count // 128)
            def _(step):
                columns = pl.ds(pl.multiple_of(start + step * 128, 128), 128)
                total = mid[part, chunk, :, columns].astype(jnp.float32) + mid_half[
                    part, :, columns
                ].astype(jnp.float32)
                mid[part, chunk, :, columns] = total.astype(jnp.bfloat16)

            columns = pl.ds(start, count)
            begin(
                job,
                part,
                10 + side,
                mid.at[part, chunk, :, columns],
                mid_whole.at[part, side, :, columns],
                target,
            )

    def third_send(job, part):
        _, _, _, mid, _, mid_whole, last = bufs[job]
        _, each, width, lanes, cut = JOBS[job]
        small = sixteen(4 * each)
        padded = sixteen(each)
        here = ring(part, 1)[0]
        arrive(job, part, 8, 9, 10, 11)

        @pl.loop(0, width // 128)
        def _(step):
            columns = pl.ds(pl.multiple_of(step * 128, 128), 128)
            acc[pl.ds(0, small), :] = (
                mid[part, here, :, columns].astype(jnp.float32)
                + mid_whole[part, 0, :, columns].astype(jnp.float32)
                + mid_whole[part, 1, :, columns].astype(jnp.float32)
            )
            for chunk in range(4):
                line = line_of(AXES[part][2], chunk)
                last[part, chunk, :, columns] = acc[pl.ds(line * each, padded), :].astype(jnp.bfloat16)

        here, right, left, opposite, to_right, to_left, to_opposite = ring(part, 2)
        for slot, chunk, target in ((0, right, to_right), (1, left, to_left), (2, opposite, to_opposite)):
            begin(job, part, 12 + slot, last.at[part, chunk], last.at[part, 4 + slot], target)

    mod_base = PARTNER_COPIES + 3 * COPIES * len(JOBS)
    mod_copies = {}

    def mod_send(slot, src, dst, target):
        copy = remote(src, dst, mod_base + slot, target)
        copy.start()
        sent.append(copy)
        mod_copies[slot] = copy

    def mod_arrive(*slots):
        for slot in slots:
            mod_copies[slot].wait_recv()

    def mod_pair():
        for quarter in range(4):
            fold32[4 * quarter : 4 * quarter + 4, :] = gmod[
                1 - mod, 0:4, quarter * 896 : (quarter + 1) * 896
            ]
        start = (1 - core) * 1792
        for half in range(2):
            columns = pl.ds(pl.multiple_of(start + half * 896, 128), 896)
            side_own[4 * half : 4 * half + 4, :] = gmod[mod, 0:4, columns]
        fold_own[...] = fold32[...].astype(jnp.bfloat16)
        there = pl.ds(pl.multiple_of((1 - core) * 8, 8), 8)
        mod_send(19, fold32.at[there], cross_other, device_at(twin, 1 - core))
        mod_send(0, fold_own, fold_other, device_at(twin, core))
        mod_send(1, side_own, side_other, partner)

    def condition_part():
        for quarter in range(4):
            other32[0:4, quarter * 896 : (quarter + 1) * 896] = turned32[4 * quarter : 4 * quarter + 4, :]
        own, other = gmod[mod, 0:4, :], other32[0:4, :]
        pair32[0:4, :] = jnp.where(mod == 0, own, other)
        pair32[4:8, :] = jnp.where(mod == 0, other, own)
        first = pair32[:, 0:WIDE].astype(jnp.bfloat16)
        wide_loads["mod", 0].wait()
        part_own[...] = inner_cols(first, out_w[...])
        wide_loads["mod", 1].wait()
        part_own[...] += inner_cols(pair32[:, WIDE : 2 * WIDE].astype(jnp.bfloat16), third_w[...])
        wide_loads["mod", 2].wait()
        wide_loads["mod", 3].wait()
        part_own[...] += inner_cols(pair32[:, 2 * WIDE : 3328].astype(jnp.bfloat16), fourth_w[...])
        part_own[...] += inner_cols(pair32[:, 3328:3456].astype(jnp.bfloat16), narrow_w[...])
        mod_send(2, part_own, part_other, device_at(twin, core))

    def mod_gather_first():
        mod_arrive(0, 1, 19)
        turned32[...] = fold_other[...].astype(jnp.float32)
        twin_rows = turned32[pl.ds(pl.multiple_of(core * 8, 8), 8), :]
        for half in range(2):
            columns = pl.ds(pl.multiple_of(core * 1792 + half * 896, 128), 896)
            at = slice(4 * half, 4 * half + 4)
            own, other = gmod[mod, 0:4, columns], twin_rows[at]
            beside, cross = side_other[at, :], cross_other[at, :]
            mine = (jnp.where(mod == 0, own, other), jnp.where(mod == 0, other, own))
            theirs = (jnp.where(mod == 0, beside, cross), jnp.where(mod == 0, cross, beside))
            to = slice(half * 896, (half + 1) * 896)
            for which in range(2):
                rows32[4 * which : 4 * which + 4, to] = jnp.where(core == 0, mine[which], theirs[which])
                rows32[8 + 4 * which : 12 + 4 * which, to] = jnp.where(core == 0, theirs[which], mine[which])
        _, y, z = place
        gathered_a[z, y] = rows32[:, 0:896].astype(jnp.bfloat16)
        gathered_b[z, y] = rows32[:, 896:1792].astype(jnp.bfloat16)
        for step in range(3):
            to_y = device_at(moved(place, 1, near[1][1 + step]), core)
            to_z = device_at(moved(place, 2, near[2][1 + step]), core)
            mod_send(3 + step, gathered_a.at[z, y], gathered_a.at[z, y], to_y)
            mod_send(6 + step, gathered_b.at[z, y], gathered_b.at[z, y], to_z)

    def mod_gather_second():
        _, y, z = place
        mod_arrive(3, 4, 5)
        for step in range(3):
            to_z = device_at(moved(place, 2, near[2][1 + step]), core)
            mod_send(9 + step, gathered_a.at[z], gathered_a.at[z], to_z)
        mod_arrive(6, 7, 8)
        for step in range(3):
            to_y = device_at(moved(place, 1, near[1][1 + step]), core)
            mod_send(12 + step, gathered_b.at[:, y], gathered_b.at[:, y], to_y)

    def mod_table():
        x, y, z = place
        row = lax.broadcasted_iota(jnp.int32, (48, WIDE), 0)
        lane = lax.broadcasted_iota(jnp.int32, (48, WIDE), 1)
        line = lax.broadcasted_iota(jnp.int32, (48, 256), 0)
        slot = lax.rem(lax.broadcasted_iota(jnp.int32, (48, 256), 1), 4)
        ones = (line == 40) | ((line == 41) & (slot == 0)) | ((line == 42) & (slot == 1))
        for index in range(2):
            half = lax.rem(lax.rem(x, 2) + index, 2)
            start = (half * 32 + z * 8 + y * 2) * 18
            pick = ((row < 36) & (lane == row + start)).astype(jnp.float32).astype(jnp.bfloat16)
            rows = inner_cols(pick, acts_s[...])
            act_rows[index] = (rows + ones.astype(jnp.float32)).astype(jnp.bfloat16)

    def mod_product():
        mod_arrive(9, 10, 11)
        mod_arrive(12, 13, 14)
        for side, gathered in ((0, gathered_a), (1, gathered_b)):
            columns = slice(side * 896, (side + 1) * 896)
            rows = gathered[...].reshape(256, 896)
            product_send[:, columns] = jnp.dot(
                act_rows[1], rows, preferred_element_type=jnp.float32
            ).astype(jnp.bfloat16)
            product_own[:, columns] = jnp.dot(act_rows[0], rows, preferred_element_type=jnp.float32)
        x = place[0]
        beside = moved(place, 0, x + 1 - 2 * lax.rem(x, 2))
        mod_send(15, product_send, product_other, device_at(beside, core))

    def mod_sum():
        mod_arrive(15)
        product_own[...] = product_own[...] + product_other[...].astype(jnp.float32)
        mod_send(16, product_own, final_other, partner)
        special = product_own.at[pl.ds(40, 8)]
        mod_send(17, special, special_other.at[core], device_at(twin, core))
        mod_send(18, special, special_other.at[core], device_at(twin, 1 - core))

    def mod_finish():
        here = pl.ds(pl.multiple_of(core * 1792, 128), 1792)
        there = pl.ds(pl.multiple_of((1 - core) * 1792, 128), 1792)
        mod_arrive(2)
        total = part_own[...] + part_other[...]
        raw = condition[...].astype(jnp.float32)
        condition_out[...] = jnp.where(mod == 0, total[0:4], total[4:8]) * silu_slope(raw)
        mod_arrive(16)
        for source, columns in ((product_own, here), (final_other, there)):
            mod_out[:, columns] = jnp.where(core == 0, source[0:18, :], source[18:36, :])
            special_out[mod, :, columns] = source[40:48, :]
        mod_arrive(17, 18)
        for side in range(2):
            special_out[1 - mod, :, side * 1792 : (side + 1) * 1792] = special_other[side]

    outs = {"gate": gate_out, "up": up_out, "down": down_out, "out": out_out, "qkv": qkv_out}

    def finish(job, part):
        last = bufs[job][6]
        _, each, width, lanes, cut = JOBS[job]
        here = ring(part, 2)[0]
        arrive(job, part, 12, 13, 14)

        @pl.loop(0, width // 128)
        def _(step):
            to = pl.multiple_of(step * 128, 128)
            columns = pl.ds(to, 128)
            total = last[part, here, :, columns].astype(jnp.float32)
            for slot in range(3):
                total = total + last[part, 4 + slot, :, columns].astype(jnp.float32)
            outs[JOBS[job][0]][:, pl.ds(pl.multiple_of(part * width + to, 128), 128)] = total[:each]

    gate_job, up_job, down_job, out_job, qkv_job = range(5)

    def slot_sum(block, source):
        for third in range(3):
            columns = slice(third * 384, (third + 1) * 384)
            high, low = split_two(source[:, columns])
            total = jnp.dot(onehot_t, high, preferred_element_type=jnp.float32) + jnp.dot(
                onehot_t, low, preferred_element_type=jnp.float32
            )
            base = block % 3 * WIDE + third * 384
            gmod[block // 3, :, base : base + 384] = (
                total[0:8].astype(jnp.bfloat16).astype(jnp.float32)
            )

    def stages(stage, job):
        for part in range(3):
            stage(job, part)

    def ff_products(part):
        pick9(part, second_s)
        arrived("ggate", "gup")
        multiply(gate_job, part, xt9, ggate_s)
        first_send(gate_job, part)
        multiply(up_job, part, xt9, gup_s)
        first_send(up_job, part)

    loads["second"].wait()

    def feed_forward(index):
        slot = lax.rem(index, 2)
        for copy in ff_chunk(index, slot):
            copy.wait()
        gate_w, up_w, down_w = ff_slots(slot)
        columns = pl.ds(pl.multiple_of(index * CHUNK, CHUNK), CHUNK)
        gate_linear = jnp.dot(second_s[0:TOK, :], gate_w[...], preferred_element_type=jnp.float32)
        up_linear = jnp.dot(second_s[0:TOK, :], up_w[...], preferred_element_type=jnp.float32)
        ghidden = inner_cols(gbranch_s[0:TOK, :], down_w[...])
        logistic = jax.nn.sigmoid(gate_linear)
        gate_act = gate_linear * logistic
        hidden = (gate_act * up_linear).astype(jnp.bfloat16)
        slope = logistic * (1.0 + gate_linear * (1.0 - logistic))
        ggate = (ghidden * up_linear * slope).astype(jnp.bfloat16)
        gup = (ghidden * gate_act).astype(jnp.bfloat16)
        hidden_s[0:TOK, columns] = hidden
        ggate_s[0:TOK, columns] = ggate
        gup_s[0:TOK, columns] = gup
        branch[...] += jnp.dot(hidden, down_w[...], preferred_element_type=jnp.float32)
        gsecond[...] += inner_cols(ggate, gate_w[...])
        gsecond[...] += inner_cols(gup, up_w[...])

        @pl.when(index + 2 < 6)
        def _():
            for copy in ff_chunk(index + 2, slot):
                copy.start()

    pl.loop(0, 2)(feed_forward)
    pl.semaphore_wait(barrier, 11)
    exchange("second", second_in, second_s.at[other_rows])
    exchange("gbranch", gbranch_s.at[own_rows], gbranch_s.at[other_rows])
    pl.loop(2, 6)(feed_forward)
    exchange("ggate", ggate_s.at[own_rows, pl.ds(0, HID)], ggate_s.at[other_rows, pl.ds(0, HID)])
    exchange("gup", gup_s.at[own_rows], gup_s.at[other_rows])
    exchange("hidden", hidden_s.at[own_rows], hidden_s.at[other_rows])
    arrived("second")
    for part in range(3):
        ff_products(part)
    loads["middle"].wait()
    loads["attended"].wait()

    def second_rows(rows):
        upstream = cotangent[rows, :].astype(jnp.float32)
        kept = middle[rows, :]
        result = branch[rows, :]
        layer_out[rows, :] = (kept + piece(rows, 5) * result).astype(jnp.bfloat16)
        branch[rows, :] = upstream * result
        normed, inverse = rms_norm(kept)
        grad = gsecond[rows, :]
        gquery[rows, :] = grad * normed
        total = upstream + norm_back(grad * (1.0 + piece(rows, 4)), normed, inverse)
        middle[rows, :] = total
        attended_row = attended[rows, :]
        attended[rows, :] = total * attended_row
        gatt_s[rows, :] = (total * piece(rows, 2)).astype(jnp.bfloat16)

    row_blocks(second_rows, 48)
    exchange("gatt", gatt_s.at[own_rows], gatt_s.at[other_rows])
    context_s = second_s
    load("context", context_in, context_s.at[own_rows])
    stages(first_add, gate_job)

    arrived("gbranch", "hidden")
    for part in range(3):
        pick24(part)
        multiply(down_job, part, xt24, gbranch_s)
        first_send(down_job, part)
    stages(first_add, up_job)
    arrived("gatt")
    exchange("context", context_in, context_s.at[other_rows])

    wide_loads["out", 0].wait()
    gcontext[...] = inner_cols(gatt_s[0:TOK, :], out_w[...]).astype(jnp.bfloat16)
    wide_parts("qkv", qkv_weight, 0)
    stages(second_send, gate_job)
    loads["context"].wait()
    arrived("context")
    for part in range(3):
        pick9(part, context_s)
        multiply(out_job, part, xt9, gatt_s)
        first_send(out_job, part)
    slot_sum(5, branch)
    slot_sum(4, gquery)
    slot_sum(3, gsecond)
    slot_sum(2, attended)
    load("query_hat", query_hat_in, branch)
    load("key_hat", key_hat_in, attended)
    load("cos", cos_in, cosine)
    load("sin", sin_in, gsecond)
    query_hat, key_hat, sine = branch, attended, gsecond
    stages(second_send, up_job)

    gquery[...] = jnp.zeros_like(gquery)
    gkey[...] = jnp.zeros_like(gkey)
    gvalue[...] = jnp.zeros_like(gvalue)
    for name in ("query", "key", "value"):
        loads[name].wait()

    def attention_group(group):
        @pl.loop(0, 1)
        def _(pair):
            left = lax.broadcasted_iota(jnp.int32, (TOK, TOK), 0) // 36
            right = lax.broadcasted_iota(jnp.int32, (TOK, TOK), 1) // 36
            shut = jnp.where(kind | (left == right), 0.0, -1e30)
            for member in range(4):
                window, mask = head_window(group * 4 + pair + member)
                query_w, key_w = query[:, window] * mask, key[:, window] * mask
                value_w, grad_w = value[:, window], gcontext[:, window] * mask
                scores = inner_cols(query_w, key_w) * (72**-0.5) + shut
                weight = jnp.exp(scores - jnp.max(scores, axis=-1, keepdims=True))
                weight = weight * (1.0 / jnp.sum(weight, axis=-1, keepdims=True))
                gattention = inner_cols(grad_w, value_w)
                gvalue[:, window] += inner_rows(weight.astype(jnp.bfloat16), grad_w)
                dots = jnp.sum(weight * gattention, axis=-1, keepdims=True)
                gscores = (weight * (gattention - dots)).astype(jnp.bfloat16)
                gquery[:, window] += jnp.dot(gscores, key_w, preferred_element_type=jnp.float32)
                gkey[:, window] += inner_rows(gscores, query_w)

    attention_group(0)
    stages(first_add, down_job)
    attention_group(1)
    stages(second_add, gate_job)
    attention_group(2)
    stages(first_add, out_job)
    attention_group(3)
    stages(second_add, up_job)
    pairs["ggate"].wait_send()

    def project_back(which, grads, hat, rows):
        base = which * WIDE
        grad = grads[rows, :] * (72**-0.5)
        normed = hat[rows, :]
        turned = grad * cosine[rows, :] - swap_halves(grad) * sine[rows, :]
        gain_sum[which] += jnp.sum((turned * normed).reshape(6, 8, WIDE), axis=0)
        scaled = turned * gains[which : which + 1, :]
        inverse = inverses[which, rows, :]
        mean = head_sum(scaled * normed, heads[...]) * (1.0 / 72.0)
        raw = scaled * head_spread(inverse, heads[...]) - normed * head_spread(
            inverse * mean, heads[...]
        )
        gproj_s[rows, base : base + WIDE] = raw.astype(jnp.bfloat16)

    def project_rows(rows):
        project_back(0, gquery, query_hat, rows)
        project_back(1, gkey, key_hat, rows)

    def exchange_projected(part):
        columns = pl.ds(part * WIDE, WIDE)
        exchange("gproj%d" % part, gproj_s.at[own_rows, columns], gproj_s.at[other_rows, columns])

    def value_rows(rows):
        gproj_s[rows, 2 * WIDE : 3 * WIDE] = gvalue[rows, :].astype(jnp.bfloat16)

    row_blocks(value_rows)
    exchange_projected(2)
    for name in ("query_hat", "key_hat", "cos", "sin"):
        loads[name].wait()
    arrived("gproj2")
    first_s = second_s
    load("first", first_in, first_s.at[own_rows])
    exchange("first", first_in, first_s.at[other_rows])
    row_blocks(project_rows, 48)
    exchange_projected(0)
    exchange_projected(1)
    loads["first"].wait()
    arrived("first")
    for part in (2, 0, 1):
        pick9(part, first_s)
        if part != 2:
            arrived("gproj%d" % part)
        sent_out(gate_job, part, 0, 1, 2, 3, 4, 5)
        multiply(qkv_job, part, xt9, gproj_s)
        first_send(qkv_job, part)
    for part in range(3):
        sent_out(up_job, part, 0, 1, 2, 3, 4, 5)
    wide_parts("qkv", qkv_weight, 2)
    stages(second_send, down_job)
    for part in range(3):
        sent_out(down_job, part, 0, 1, 2, 3, 4, 5)
    wide_parts("qkv", qkv_weight, 1)
    stages(third_send, gate_job)
    stages(second_send, out_job)
    stages(third_send, up_job)

    gfirst, scaled_first = gquery, gkey
    wide_loads["qkv", 0].wait()
    gfirst[...] = inner_cols(gproj_s[0:TOK, 0:WIDE], out_w[...])
    wide_parts("mod", mod_weight, 0)
    wide_loads["qkv", 1].wait()
    gfirst[...] += inner_cols(gproj_s[0:TOK, WIDE : 2 * WIDE], third_w[...])
    wide_parts("mod", mod_weight, 1)
    wide_loads["qkv", 2].wait()
    wide_loads["qkv", 3].wait()
    gfirst[...] += inner_cols(gproj_s[0:TOK, 2 * WIDE : 3328], fourth_w[...])
    gfirst[...] += inner_cols(gproj_s[0:TOK, 3328:3456], narrow_w[...])
    wide_parts("mod", mod_weight, 2)

    def last_rows(rows):
        normed, inverse = rms_norm(tokens[rows, :].astype(jnp.float32))
        grad = gfirst[rows, :]
        scaled_first[rows, :] = grad * normed
        tokens_out[rows, :] = middle[rows, :] + norm_back(
            grad * (1.0 + piece(rows, 1)), normed, inverse
        )

    row_blocks(last_rows, 48)
    slot_sum(0, gfirst)
    slot_sum(1, scaled_first)
    for which in range(2):
        high, low = split_two(gain_sum[which])
        total = jnp.sum(inner_cols(high, folds[...]) + inner_cols(low, folds[...]), axis=0, keepdims=True)
        gmod[0, which : which + 1, 3456:3584] = total
    mod_pair()
    stages(first_add, qkv_job)
    mod_gather_first()
    stages(second_add, down_job)
    stages(second_add, out_job)
    mod_gather_second()
    condition_part()
    stages(finish, gate_job)
    stages(second_send, qkv_job)
    loads["acts"].wait()
    mod_table()
    mod_product()
    stages(third_send, down_job)
    stages(third_send, out_job)
    stages(second_add, qkv_job)
    mod_sum()
    stages(third_send, qkv_job)
    stages(finish, up_job)
    stages(finish, down_job)
    stages(finish, out_job)
    mod_finish()
    stages(finish, qkv_job)
    for name, copy in pairs.items():
        if name != "ggate":
            copy.wait_send()
    for (job, part, slot) in list(copies):
        sent_out(job, part, slot)
    for copy in sent:
        copy.wait_send()


def write_kernel(*refs):
    count = len(refs) // 2 - 1
    for source, target in zip(refs[:count], refs[count:-2]):
        if len(source.shape) == 3:
            for half in range(2):
                target[pl.ds(half * 3456, 3456)] = source[half, 0, 0:3456]
            for which in range(2):
                total = source[0, 1 + which, 3456:3584] + source[1, 1 + which, 3456:3584]
                refs[count * 2 + which][...] = total[0:72]
        else:
            target[...] = source[:, 0 : target.shape[1]]


def backward(
    cotangent, tokens, condition, segments, saved, gate_weight, up_weight, down_weight, out_weight, qkv_weight, mod_weight
):
    (query, key, value, query_hat, key_hat, context, attended, middle, first, second, cosine, sine, acts, inverses, modulation, gains) = saved
    vmem = pl.BlockSpec(memory_space=pltpu.VMEM)
    anywhere = pl.BlockSpec(memory_space=pl.ANY)
    low, full = jnp.bfloat16, jnp.float32
    wide_low, wide_full = ((TOK, WIDE), low), ((TOK, WIDE), full)
    outs = (
        [wide_low, wide_full]
        + [((each, 3 * width), full) for _, each, width, _, _ in JOBS]
        + [((18, 3584), full), ((2, 8, 3584), full), ((4, WIDE), full)]
    )
    scratch = [
        ((PAIR, HID), low),
        ((PAIR, WIDE), low),
        ((PAIR, WIDE), low),
        ((PAIR, 3456), low),
        ((PAIR, HID), low),
        ((PAIR, WIDE), low),
        ((2, 288, 640), low),
        ((2, 288, 640), low),
        ((8, 80, 256), low),
        ((256, WIDE), low),
        ((192, 384), low),
        ((1536, PAIR), low),
        ((400, 128), full),
        ((128, WIDE), low),
        ((128, WIDE), low),
        ((TOK, 4 * WIDE), low),
        wide_full,
        wide_full,
        wide_full,
        wide_low,
        wide_low,
        wide_low,
        wide_low,
        wide_full,
        wide_full,
        wide_full,
        wide_full,
        ((2, 8, WIDE), full),
        ((WIDE, WIDE), low),
        ((WIDE, 128), low),
        ((2, 8, 3584), full),
        ((2, 48, 256), low),
        ((16, 896), full),
        ((16, 896), low),
        ((16, 896), low),
        ((8, 3584), full),
        ((8, 3584), full),
        ((16, 896), full),
        ((8, 896), full),
        ((8, 896), full),
        ((8, 896), full),
        ((16, 1792), full),
        ((4, 4, 16, 896), low),
        ((4, 4, 16, 896), low),
        ((48, 1792), full),
        ((48, 1792), low),
        ((48, 1792), low),
        ((48, 1792), full),
        ((2, 8, 1792), full),
        ((8, WIDE), full),
        ((8, WIDE), full),
    ]
    sums = {
        "gate": (16, 128),
        "up": (1728, 1024),
        "down": (1536, WIDE),
        "out": (1728, 384),
        "qkv": (1728, WIDE),
    }
    for name, each, width, _, _ in JOBS:
        big, small, tiny = 16 * each, sixteen(4 * each), sixteen(each)
        unused = name == "gate"
        scratch += [
            (sums[name], low),
            ((1, 16, 128) if unused else (3, big, width), low),
            ((1, 1, 16, 128) if unused else (3, 2, big, width), low),
            ((1, 1, 16, 128) if unused else (3, 4, small, width), low),
            ((3, small, width), low),
            ((3, 2, small, width), low),
            ((3, 7, tiny, width), low),
        ]
    count = PARTNER_COPIES + 3 * COPIES * len(JOBS) + MOD_COPIES
    results = pl.pallas_call(
        backward_kernel,
        out_shape=[jax.ShapeDtypeStruct(*out) for out in outs],
        in_specs=[pl.BlockSpec(memory_space=pltpu.SMEM)] + [vmem] * 6 + [anywhere] * 19,
        out_specs=[vmem] * 10,
        scratch_shapes=[pltpu.VMEM(*item) for item in scratch]
        + [
            pltpu.SemaphoreType.DMA((count,)),
            pltpu.SemaphoreType.DMA((count,)),
            pltpu.SemaphoreType.DMA((13,)),
            pltpu.SemaphoreType.DMA((4, 4)),
        ],
        compiler_params=pltpu.CompilerParams(
            collective_id=1, has_side_effects=True, vmem_limit_bytes=64 * 1024 * 1024 - 65536
        ),
        cost_estimate=pl.CostEstimate(
            flops=12_000_000_000, bytes_accessed=50_000_000, transcendentals=0
        ),
    )(
        segments,
        cotangent,
        tokens,
        modulation,
        condition,
        gains,
        inverses,
        acts.reshape(256, WIDE),
        second,
        first,
        context,
        middle,
        attended,
        query,
        key,
        value,
        query_hat,
        key_hat,
        cosine,
        sine,
        gate_weight,
        up_weight,
        down_weight,
        out_weight,
        qkv_weight,
        mod_weight,
    )
    special = results[8]
    kept = list(results[:8]) + [results[9]]
    shapes = [
        jax.ShapeDtypeStruct((item.shape[0], min(item.shape[1], 3456)), item.dtype) for item in kept
    ]
    written = pl.pallas_call(
        write_kernel,
        out_shape=shapes + [jax.ShapeDtypeStruct((size,), full) for size in (6912, 72, 72)],
        in_specs=[vmem] * 10,
        out_specs=[vmem] * 12,
    )(*kept, special)
    return written


def body(
    tokens,
    condition,
    segments,
    mod_weight,
    mod_bias,
    qkv_weight,
    query_gain,
    key_gain,
    out_weight,
    gate_weight,
    up_weight,
    down_weight,
    cotangent,
):
    saved = forward(tokens, condition, segments, mod_weight, mod_bias, qkv_weight, query_gain, key_gain, out_weight)
    written = backward(
        cotangent,
        tokens,
        condition,
        segments,
        saved,
        gate_weight,
        up_weight,
        down_weight,
        out_weight,
        qkv_weight,
        mod_weight,
    )
    layer_out, grad_tokens, gate, up, down, out, qkv, mod_rows, grad_condition, bias, query_grad, key_grad = written
    return (
        layer_out,
        grad_tokens,
        grad_condition,
        mod_rows,
        bias,
        qkv,
        query_grad,
        key_grad,
        out,
        gate,
        up,
        down,
    )


def solution(mesh):
    placed = (
        P(("dp", "mod"), None),
        P(("dp", "mod"), None),
        P(("dp", "mod")),
        P(None, "mod"),
        P("mod"),
        P(),
        P(),
        P(),
        P(),
        P(),
        P(),
        P(),
        P(("dp", "mod"), None),
    )
    return jax.shard_map(
        body,
        mesh=mesh,
        in_specs=placed,
        out_specs=(
            P(("dp", "mod"), None),
            P(("dp", "mod"), None),
            P(("dp", "mod"), None),
            P("dp", "mod"),
            P(),
            P(("dp", "mod"), None),
            P(),
            P(),
            P(("dp", "mod"), None),
            P(("dp", "mod"), None),
            P(("dp", "mod"), None),
            P(("dp", "mod"), None),
        ),
        check_vma=False,
    )
```

```python
import jax
import jax.numpy as jnp
import numpy as np
from jax import lax
from jax.experimental import pallas as pl
from jax.experimental.pallas import tpu as pltpu
from jax.sharding import PartitionSpec as P

EPSILON = 1e-06


def rms_norm(values):
    inverse = lax.rsqrt(jnp.mean(values * values, axis=-1, keepdims=True) + EPSILON)
    return (values * inverse, inverse)


def norm_back(upstream, normed, inverse):
    return inverse * (upstream - normed * jnp.mean(upstream * normed, axis=-1, keepdims=True))


def silu_slope(values):
    logistic = jax.nn.sigmoid(values)
    return logistic * (1.0 + values * (1.0 - logistic))


def inner_rows(left, right):
    return lax.dot_general(
        left, right, (((0,), (0,)), ((), ())), preferred_element_type=jnp.float32
    )


def inner_cols(left, right):
    return lax.dot_general(
        left, right, (((1,), (1,)), ((), ())), preferred_element_type=jnp.float32
    )


TOK = 144
PAIR = 2 * TOK
WIDE = 1152
HID = 3072
RING = 4
AXES = ((0, 2, 1), (1, 0, 2), (2, 1, 0))
JOBS = (
    ("gate", 9, 1024, 256, 512),
    ("up", 9, 1024, 256, 512),
    ("down", 24, 384, 384, 256),
    ("out", 9, 384, 384, 256),
    ("qkv", 9, 1152, 384, 640),
)
COPIES = 15
PARTNER_COPIES = 17
MOD_COPIES = 20
CHUNK = 512


def sixteen(rows):
    return (rows + 15) // 16 * 16


def position():
    dp = lax.axis_index("dp")
    x_hi = lax.axis_index("mod")
    core = lax.rem(dp, 2)
    y = lax.rem(dp // 2, 4)
    z = lax.rem(dp // 8, 4)
    return (x_hi * 2 + dp // 32, y, z), core


def device_at(place, core):
    x, y, z = place
    return (((lax.rem(x, 2) * 4 + z) * 4 + y) * 2 + core, x // 2)


def moved(place, axis, value):
    return tuple(value if index == axis else kept for index, kept in enumerate(place))


def line_of(axis, value):
    return value % 2 * 2 + value // 2 if axis == 0 else value


FWD_REMOTE = 12
MESH = pl.DeviceIdType.MESH


def rope_flat():
    token = np.arange(TOK)
    frequency = 10000.0 ** (-np.arange(18, dtype=np.float64) / 18)
    tables = []
    for position_in, side in ((token % 36, 6), (token, 12)):
        row, column = position_in // side, position_in % side
        angle = np.concatenate([row[:, None] * frequency, column[:, None] * frequency], axis=1)
        cosine = np.tile(np.concatenate([np.cos(angle), np.cos(angle)], axis=1), (1, 16))
        sine = np.tile(np.concatenate([-np.sin(angle), np.sin(angle)], axis=1), (1, 16))
        tables.append((cosine, sine))
    return (
        np.stack([pair[0] for pair in tables]).astype(np.float32),
        np.stack([pair[1] for pair in tables]).astype(np.float32),
    )


def row_blocks(step, size=16):
    @pl.loop(0, TOK // size)
    def _(index):
        step(pl.ds(pl.multiple_of(index * size, 16), size))


def split_two(values):
    high = values.astype(jnp.bfloat16)
    return high, (values - high.astype(jnp.float32)).astype(jnp.bfloat16)


def head_sum(values, heads):
    high, low = split_two(values)
    return inner_cols(high, heads) + inner_cols(low, heads)


def head_spread(values, heads):
    high, low = split_two(values)
    return jnp.dot(high, heads, preferred_element_type=jnp.float32) + jnp.dot(
        low, heads, preferred_element_type=jnp.float32
    )


def head_rows():
    head = lax.broadcasted_iota(jnp.int32, (128, WIDE), 0) * 72
    lane = lax.broadcasted_iota(jnp.int32, (128, WIDE), 1)
    return ((lane >= head) & (lane < head + 72)).astype(jnp.float32).astype(jnp.bfloat16)


def swap_halves(values):
    lane = lax.broadcasted_iota(jnp.int32, values.shape, 1)
    first = lax.rem(lane, 72) < 36
    return jnp.where(first, pltpu.roll(values, WIDE - 36, 1), pltpu.roll(values, 36, 1))


def head_window(head):
    block = jnp.minimum(head * 72 // 128, 7)
    offset = head * 72 - block * 128
    lane = lax.broadcasted_iota(jnp.int32, (1, 256), 1)
    mask = ((lane >= offset) & (lane < offset + 72)).astype(jnp.float32).astype(jnp.bfloat16)
    return pl.ds(pl.multiple_of(block * 128, 128), 256), mask


def forward_kernel(
    segments,
    tokens,
    condition,
    mod_bias,
    query_gain,
    key_gain,
    cos_in,
    sin_in,
    mod_weight,
    qkv_weight,
    out_weight,
    query_out,
    key_out,
    value_out,
    query_hat_out,
    key_hat_out,
    context_out,
    attended_out,
    middle_out,
    first_out,
    second_out,
    cos_out,
    sin_out,
    gathered_out,
    inverse_out,
    modulation_out,
    gains,
    mod_w,
    qkv_w,
    out_w,
    cos2,
    sin2,
    cond32,
    cond_other,
    act32,
    act_across,
    gathered,
    half32,
    fold32,
    fold_own,
    fold_other,
    mods32,
    per_token,
    norm,
    first,
    projected,
    query,
    key,
    value,
    query_hat,
    key_hat,
    context32,
    context,
    attended,
    middle,
    second,
    cosine,
    sine,
    heads,
    send_sem,
    recv_sem,
    in_sem,
    out_sem,
):
    place, core = position()
    mod = lax.axis_index("mod")
    partner = device_at(place, 1 - core)
    twin = device_at(moved(place, 0, lax.rem(place[0] + 2, 4)), core)
    peers = [
        [device_at(moved(place, axis, lax.rem(place[axis] + step, 4)), core) for step in (1, 2, 3)]
        for axis in (1, 2)
    ]
    loads = {}

    def load(name, index, src, dst, slot):
        copy = pltpu.make_async_copy(src, dst, in_sem.at[slot])
        copy.start()
        loads[name, index] = copy

    for index in range(3):
        columns = pl.ds(index * WIDE, WIDE)
        load("mod", index, mod_weight.at[:, columns], mod_w.at[:, columns], index)
    load("cos", 0, cos_in, cos2, 21)
    load("sin", 0, sin_in, sin2, 22)
    for index in range(3):
        columns = pl.ds(index * WIDE, WIDE)
        load("qkv", index, qkv_weight.at[:, columns], qkv_w.at[:, columns], 9 + index)
    load("out", 0, out_weight, out_w, 18)

    sent = []
    copies = {}

    def send(slot, src, dst, target):
        copy = pltpu.make_async_remote_copy(
            src_ref=src,
            dst_ref=dst,
            send_sem=send_sem.at[slot],
            recv_sem=recv_sem.at[slot],
            device_id=target,
            device_id_type=MESH,
        )
        copy.start()
        sent.append(copy)
        copies[slot] = copy

    stores = []

    def store(src, dst):
        copy = pltpu.make_async_copy(src, dst, out_sem.at[len(stores)])
        copy.start()
        stores.append(copy)

    barrier = pltpu.get_barrier_semaphore()
    for target in [partner, twin] + peers[0] + peers[1]:
        pl.semaphore_signal(barrier, inc=1, device_id=target, device_id_type=MESH)
    cond32[...] = jnp.zeros_like(cond32)
    cond32[0:4, :] = condition[...].astype(jnp.float32)
    pl.semaphore_wait(barrier, 8)
    send(0, cond32, cond_other, twin)

    for which, source in enumerate((query_gain, key_gain)):
        gains[which : which + 1, :] = jnp.concatenate([source[...].reshape(1, 72)] * 16, axis=1)
    kind = segments[TOK - 1] == 0
    row = lax.broadcasted_iota(jnp.int32, (TOK, 16), 0)
    slot = lax.broadcasted_iota(jnp.int32, (TOK, 16), 1)
    onehot = (slot == jnp.where(kind, 0, row // 36)).astype(jnp.float32).astype(jnp.bfloat16)
    heads[...] = head_rows()

    def first_norm(rows):
        values = tokens[rows, :].astype(jnp.float32)
        norm[rows, :] = rms_norm(values)[0]

    row_blocks(first_norm, 48)

    copies[0].wait_recv()
    own, other = cond32[0:4, :], cond_other[0:4, :]
    act32[0:4, :] = jnp.where(mod == 0, own, other)
    act32[4:8, :] = jnp.where(mod == 0, other, own)
    act32[...] = jax.nn.silu(act32[...]).astype(jnp.bfloat16).astype(jnp.float32)
    send(1, act32, act_across, partner)
    act = act32[...].astype(jnp.bfloat16)
    half32[...] = jnp.zeros_like(half32)
    for index in range(3):
        columns = slice(index * WIDE, (index + 1) * WIDE)
        loads["mod", index].wait()
        half32[:, columns] = (
            (
                jnp.dot(act, mod_w[:, columns], preferred_element_type=jnp.float32)
                + mod_bias[columns].astype(jnp.float32).reshape(1, WIDE)
            )
            .astype(jnp.bfloat16)
            .astype(jnp.float32)
        )
    for quarter in range(4):
        columns = slice(quarter * 896, (quarter + 1) * 896)
        fold32[4 * quarter : 4 * quarter + 4, :] = jnp.where(
            mod == 0, half32[4:8, columns], half32[0:4, columns]
        )
    fold_own[...] = fold32[...].astype(jnp.bfloat16)
    send(2, fold_own, fold_other, twin)

    copies[1].wait_recv()
    _, y, z = place
    rows16 = jnp.concatenate(
        [
            jnp.where(core == 0, act32[...], act_across[...]),
            jnp.where(core == 0, act_across[...], act32[...]),
        ]
    )
    gathered[z, y] = rows16.astype(jnp.bfloat16)
    for step in range(3):
        send(3 + step, gathered.at[z, y], gathered.at[z, y], peers[0][step])
    loads["cos", 0].wait()
    loads["sin", 0].wait()

    def pick_table(rows):
        cosine[rows, :] = jnp.where(kind, cos2[1, rows, :], cos2[0, rows, :])
        sine[rows, :] = jnp.where(kind, sin2[1, rows, :], sin2[0, rows, :])

    row_blocks(pick_table)
    store(cosine, cos_out)
    store(sine, sin_out)
    for slot_ in (3, 4, 5):
        copies[slot_].wait_recv()
    for step in range(3):
        send(6 + step, gathered.at[z], gathered.at[z], peers[1][step])

    copies[2].wait_recv()
    mods32[...] = jnp.zeros_like(mods32)
    fold32[...] = fold_other[...].astype(jnp.float32)
    for quarter in range(4):
        width = 896 if quarter < 3 else 768
        mods32[0:4, pl.ds(pl.multiple_of((1 - mod) * 3456 + quarter * 896, 128), width)] = fold32[
            4 * quarter : 4 * quarter + 4, 0:width
        ]
    mods32[0:4, pl.ds(pl.multiple_of(mod * 3456, 128), 3456)] = jnp.where(
        mod == 0, half32[0:4, 0:3456], half32[4:8, 0:3456]
    )
    modulation_out[...] = mods32[...].astype(jnp.bfloat16)
    for index in range(5):
        columns = slice(index * WIDE, (index + 1) * WIDE)
        per_token[:, columns] = jnp.dot(
            onehot, modulation_out[:, columns], preferred_element_type=jnp.float32
        ).astype(jnp.bfloat16)

    def piece(rows, index):
        return per_token[rows, index * WIDE : (index + 1) * WIDE].astype(jnp.float32)

    def first_input(rows):
        first[rows, :] = (norm[rows, :] * (1.0 + piece(rows, 1)) + piece(rows, 0)).astype(jnp.bfloat16)

    row_blocks(first_input, 48)
    store(first, first_out)

    for index in range(3):
        loads["qkv", index].wait()
        columns = slice(index * WIDE, (index + 1) * WIDE)
        result = jnp.dot(first[...], qkv_w[:, columns], preferred_element_type=jnp.float32)
        if index < 2:
            projected[:, columns] = result
        else:
            value[...] = result.astype(jnp.bfloat16)
    store(value, value_out)

    def head_norm(which, hat, result, rows):
        raw = projected[rows, which * WIDE : (which + 1) * WIDE]
        total = head_sum(raw * raw, heads[...])
        inverse = lax.rsqrt(total * (1.0 / 72.0) + EPSILON)
        inverse_out[which, rows, :] = inverse
        normed = raw * head_spread(inverse, heads[...])
        hat[rows, :] = normed
        scaled = normed * gains[which : which + 1, :]
        turned = scaled * cosine[rows, :] + swap_halves(scaled) * sine[rows, :]
        result[rows, :] = turned.astype(jnp.bfloat16)

    def head_rows_step(rows):
        head_norm(0, query_hat, query, rows)
        head_norm(1, key_hat, key, rows)

    row_blocks(head_rows_step, 48)
    store(query_hat, query_hat_out)
    store(query, query_out)
    store(key_hat, key_hat_out)
    store(key, key_out)

    left = lax.broadcasted_iota(jnp.int32, (TOK, TOK), 0) // 36
    right = lax.broadcasted_iota(jnp.int32, (TOK, TOK), 1) // 36
    shut = jnp.where(kind | (left == right), 0.0, -1e30)
    context32[...] = jnp.zeros_like(context32)

    @pl.loop(0, 4)
    def _(group):
        for member in range(4):
            head = group * 4 + member
            window, mask = head_window(head)
            scores = inner_cols(query[:, window] * mask, key[:, window]) * (72**-0.5) + shut
            top = jnp.max(scores, axis=-1, keepdims=True)
            weight = jnp.exp(scores - top)
            weight = weight * (1.0 / jnp.sum(weight, axis=-1, keepdims=True))
            context32[:, window] += jnp.dot(
                weight.astype(jnp.bfloat16), value[:, window] * mask, preferred_element_type=jnp.float32
            )

    context[...] = context32[...].astype(jnp.bfloat16)
    store(context, context_out)
    loads["out", 0].wait()
    attended[...] = jnp.dot(context[...], out_w[...], preferred_element_type=jnp.float32)
    store(attended, attended_out)

    def second_input(rows):
        total = tokens[rows, :].astype(jnp.float32) + piece(rows, 2) * attended[rows, :]
        middle[rows, :] = total
        normed = rms_norm(total)[0]
        second[rows, :] = (normed * (1.0 + piece(rows, 4)) + piece(rows, 3)).astype(jnp.bfloat16)

    row_blocks(second_input, 48)
    store(middle, middle_out)
    store(second, second_out)
    for slot_ in (6, 7, 8):
        copies[slot_].wait_recv()
    store(gathered, gathered_out)
    for copy in sent:
        copy.wait_send()
    for copy in stores:
        copy.wait()


def forward(tokens, condition, segments, mod_weight, mod_bias, qkv_weight, query_gain, key_gain, out_weight):
    cos_table, sin_table = rope_flat()
    vmem = pl.BlockSpec(memory_space=pltpu.VMEM)
    anywhere = pl.BlockSpec(memory_space=pl.ANY)
    low, full = jnp.bfloat16, jnp.float32
    wide_low = ((TOK, WIDE), low)
    wide_full = ((TOK, WIDE), full)
    outs = (
        [wide_low] * 3
        + [wide_full] * 2
        + [wide_low, wide_full, wide_full, wide_low, wide_low]
        + [wide_full] * 2
        + [((4, 4, 16, WIDE), low)]
        + [((2, TOK, 128), full), ((16, 6 * WIDE), low), ((2, WIDE), full)]
    )
    scratch = [
        ((WIDE, 3456), low),
        ((WIDE, 3456), low),
        ((WIDE, WIDE), low),
        ((2, TOK, WIDE), full),
        ((2, TOK, WIDE), full),
        ((8, WIDE), full),
        ((8, WIDE), full),
        ((8, WIDE), full),
        ((8, WIDE), full),
        ((4, 4, 16, WIDE), low),
        ((8, 3584), full),
        ((16, 896), full),
        ((16, 896), low),
        ((16, 896), low),
        ((16, 6912), full),
        ((TOK, 6912), low),
        wide_full,
        wide_low,
        ((TOK, 2304), full),
        wide_low,
        wide_low,
        wide_low,
        wide_full,
        wide_full,
        wide_full,
        wide_low,
        wide_full,
        wide_full,
        wide_low,
        wide_full,
        wide_full,
        ((128, WIDE), low),
    ]
    return pl.pallas_call(
        forward_kernel,
        out_shape=[jax.ShapeDtypeStruct(*out) for out in outs],
        in_specs=[pl.BlockSpec(memory_space=pltpu.SMEM)] + [vmem] * 5 + [anywhere] * 5,
        out_specs=[anywhere] * 13 + [vmem] * 3,
        scratch_shapes=[pltpu.VMEM(*item) for item in scratch]
        + [
            pltpu.SemaphoreType.DMA((FWD_REMOTE,)),
            pltpu.SemaphoreType.DMA((FWD_REMOTE,)),
            pltpu.SemaphoreType.DMA((23,)),
            pltpu.SemaphoreType.DMA((16,)),
        ],
        compiler_params=pltpu.CompilerParams(
            collective_id=2, has_side_effects=True, vmem_limit_bytes=56 * 1024 * 1024
        ),
        cost_estimate=pl.CostEstimate(flops=2_000_000_000, bytes_accessed=30_000_000, transcendentals=0),
    )(
        segments,
        tokens,
        condition,
        mod_bias,
        query_gain,
        key_gain,
        jnp.asarray(cos_table),
        jnp.asarray(sin_table),
        mod_weight,
        qkv_weight,
        out_weight,
    )


def backward_kernel(
    segments,
    cotangent,
    tokens,
    modulation,
    condition,
    gains,
    inverses,
    acts,
    second_in,
    first_in,
    context_in,
    middle_in,
    attended_in,
    query_in,
    key_in,
    value_in,
    query_hat_in,
    key_hat_in,
    cos_in,
    sin_in,
    gate_weight,
    up_weight,
    down_weight,
    out_weight,
    qkv_weight,
    mod_weight,
    layer_out,
    tokens_out,
    gate_out,
    up_out,
    down_out,
    out_out,
    qkv_out,
    mod_out,
    special_out,
    condition_out,
    hidden_s,
    second_s,
    gbranch_s,
    ggate_s,
    gup_s,
    gatt_s,
    pick_x,
    pick_y,
    pick_z,
    acts_s,
    perm24,
    xt24,
    acc,
    heads,
    folds,
    per_token,
    branch,
    gsecond,
    attended,
    query,
    key,
    value,
    gcontext,
    gquery,
    gkey,
    gvalue,
    cosine,
    gain_sum,
    out_w,
    narrow_w,
    gmod,
    act_rows,
    fold32,
    fold_own,
    fold_other,
    other32,
    pair32,
    turned32,
    side_own,
    side_other,
    cross_other,
    rows32,
    gathered_a,
    gathered_b,
    product_own,
    product_send,
    product_other,
    final_other,
    special_other,
    part_own,
    part_other,
    *rest,
):
    bufs = [list(rest[7 * index : 7 * index + 7]) for index in range(len(JOBS))]
    for index in range(4):
        bufs[0][index] = bufs[4][index]
    xt9 = xt24.at[pl.ds(0, 576)]
    send_sem, recv_sem, local_sem, ring_sem = rest[7 * len(JOBS) :]
    gproj_s, middle = ggate_s, tokens_out
    place, core = position()
    mod = lax.axis_index("mod")
    partner = device_at(place, 1 - core)
    near = []
    for axis in range(3):
        here = place[axis]
        near.append(
            (here, lax.rem(here + 1, 4), lax.rem(here + 3, 4), lax.rem(here + 2, 4))
        )
    twin = moved(place, 0, near[0][3])

    ring_a, ring_b, ring_c = bufs[0][0], bufs[1][0], bufs[2][0]

    def ff_slots(slot):
        columns = pl.ds(pl.multiple_of(slot * CHUNK, CHUNK), CHUNK)
        return (
            ring_a.at[pl.ds(0, WIDE), columns],
            ring_b.at[pl.ds(0, WIDE), columns],
            ring_c.at[columns, :],
        )

    def ff_chunk(index, slot):
        columns = pl.ds(pl.multiple_of(index * CHUNK, CHUNK), CHUNK)
        sources = (gate_weight.at[:, columns], up_weight.at[:, columns], down_weight.at[columns, :])
        return [
            pltpu.make_async_copy(source, target, ring_sem.at[number, slot])
            for number, (source, target) in enumerate(zip(sources, ff_slots(slot)))
        ]

    wide_loads = {}

    def wide_load(name, index, source, target, number):
        copy = pltpu.make_async_copy(source, target, ring_sem.at[3, number])
        copy.start()
        wide_loads[name, index] = copy

    for index in range(2):
        for copy in ff_chunk(index, index):
            copy.start()
    wide_load("out", 0, out_weight, out_w, 0)
    third_w = ring_c.at[pl.ds(0, WIDE), :]
    fourth_w = ring_b.at[pl.ds(0, WIDE), :]

    def wide_parts(name, source, number):
        if number == 0:
            wide_load(name, 0, source.at[:, pl.ds(0, WIDE)], out_w, 0)
        elif number == 1:
            wide_load(name, 1, source.at[:, pl.ds(WIDE, WIDE)], third_w, 1)
        else:
            wide_load(name, 2, source.at[:, pl.ds(2 * WIDE, 1024)], fourth_w, 2)
            wide_load(name, 3, source.at[:, pl.ds(3328, 128)], narrow_w, 3)

    loads = {}

    def load(name, src, dst):
        copy = pltpu.make_async_copy(src, dst, local_sem.at[len(loads)])
        copy.start()
        loads[name] = copy

    own_rows, other_rows = pl.ds(0, TOK), pl.ds(TOK, TOK)
    load("second", second_in, second_s.at[own_rows])
    load("middle", middle_in, middle)
    load("attended", attended_in, attended)
    load("query", query_in, query)
    load("acts", acts, acts_s)
    load("key", key_in, key)
    load("value", value_in, value)

    barrier = pltpu.get_barrier_semaphore()
    pl.semaphore_signal(barrier, inc=1, device_id=partner, device_id_type=MESH)
    for axis in range(3):
        for far in near[axis][1:]:
            pl.semaphore_signal(
                barrier,
                inc=1,
                device_id=device_at(moved(place, axis, far), core),
                device_id_type=MESH,
            )
    pl.semaphore_signal(barrier, inc=1, device_id=device_at(twin, 1 - core), device_id_type=MESH)

    kind = segments[TOK - 1] == 0
    token = lax.broadcasted_iota(jnp.int32, (TOK, 16), 0)
    slot_of = lax.broadcasted_iota(jnp.int32, (TOK, 16), 1)
    onehot = (slot_of == jnp.where(kind, 0, token // 36)).astype(jnp.float32).astype(jnp.bfloat16)
    token_t = lax.broadcasted_iota(jnp.int32, (16, TOK), 1)
    slot_t = lax.broadcasted_iota(jnp.int32, (16, TOK), 0)
    onehot_t = (slot_t == jnp.where(kind, 0, token_t // 36)).astype(jnp.float32).astype(jnp.bfloat16)
    for index, block in enumerate((5, 4, 2, 1)):
        per_token[:, index * WIDE : (index + 1) * WIDE] = jnp.dot(
            onehot, modulation[:, block * WIDE : (block + 1) * WIDE], preferred_element_type=jnp.float32
        ).astype(jnp.bfloat16)

    def piece(rows, block):
        base = (5, 4, 2, 1).index(block) * WIDE
        return per_token[rows, base : base + WIDE].astype(jnp.float32)

    def first_rows(rows):
        upstream = cotangent[rows, :].astype(jnp.float32)
        gbranch_s[rows, :] = (upstream * piece(rows, 5)).astype(jnp.bfloat16)
        zero = jnp.zeros((48, WIDE), jnp.float32)
        branch[rows, :] = zero
        gsecond[rows, :] = zero

    row_blocks(first_rows, 48)
    gmod[...] = jnp.zeros_like(gmod)
    gain_sum[...] = jnp.zeros_like(gain_sum)

    def remote(src, dst, index, target):
        return pltpu.make_async_remote_copy(
            src_ref=src,
            dst_ref=dst,
            send_sem=send_sem.at[index],
            recv_sem=recv_sem.at[index],
            device_id=target,
            device_id_type=MESH,
        )

    sent = []
    pairs, landed = {}, set()

    def exchange(name, src, dst):
        copy = remote(src, dst, len(pairs), partner)
        copy.start()
        pairs[name] = copy


    def arrived(*names):
        for name in names:
            if name not in landed:
                landed.add(name)
                pairs[name].wait_recv()

    lane24 = lax.broadcasted_iota(jnp.int32, (192, 384), 1)
    row24 = lax.broadcasted_iota(jnp.int32, (192, 384), 0)
    perm24[...] = (
        (lane24 == row24 // 48 * 96 + lax.rem(row24, 48) + core * 48)
        .astype(jnp.float32)
        .astype(jnp.bfloat16)
    )
    heads[...] = head_rows()
    folded = lax.rem(lax.broadcasted_iota(jnp.int32, (128, WIDE), 1), 72)
    folds[...] = (
        (folded == lax.broadcasted_iota(jnp.int32, (128, WIDE), 0)).astype(jnp.float32).astype(jnp.bfloat16)
    )

    row = lax.broadcasted_iota(jnp.int32, (288, 640), 0)
    lane = lax.broadcasted_iota(jnp.int32, (288, 640), 1)
    unit, entry = row // 9, lax.rem(row, 9)
    for_x = unit // 16 * 9 + lax.rem(unit // 4, 4) * 144 + lax.rem(unit, 4) * 36 + entry + core * 18
    for_y = unit // 8 * 36 + lax.rem(unit // 4, 2) * 9 + lax.rem(unit, 4) * 144 + entry + core * 18
    for x_lo in range(2):
        pick_x[x_lo] = (lane == for_x + x_lo * 64).astype(jnp.float32).astype(jnp.bfloat16)
        pick_y[x_lo] = (lane == for_y + x_lo * 64).astype(jnp.float32).astype(jnp.bfloat16)
    row = lax.broadcasted_iota(jnp.int32, (80, 256), 0)
    lane = lax.broadcasted_iota(jnp.int32, (80, 256), 1)
    unit = row // 9
    for_z = unit // 2 * 36 + lax.rem(unit, 2) * 9 + lax.rem(row, 9) + core * 18
    for block in range(8):
        pick_z[block] = (
            ((row < 72) & (lane == for_z + block * 16)).astype(jnp.float32).astype(jnp.bfloat16)
        )

    def pick9(part, stack):
        if part == 2:
            for z in range(4):
                halves = []
                for x_lo in range(2):
                    block = x_lo * 4 + z
                    rows = inner_cols(pick_z[block], stack[:, block * 128 : block * 128 + 256])
                    halves.append(rows[0:72])
                xt9[z * 144 : (z + 1) * 144, :] = jnp.concatenate(halves).astype(jnp.bfloat16)
            return
        table = (pick_x, pick_y)[part]
        low = inner_cols(table[0], stack[:, 0:640])
        high = inner_cols(table[1], stack[:, 512:WIDE])
        for value_ in range(4):
            if part == 0:
                half = (low, high)[value_ % 2]
                rows = half[value_ // 2 * 144 : value_ // 2 * 144 + 144]
            else:
                at = slice(value_ * 72, (value_ + 1) * 72)
                rows = jnp.concatenate([low[at], high[at]])
            xt9[value_ * 144 : (value_ + 1) * 144, :] = rows.astype(jnp.bfloat16)

    def pick24(part):
        def block_rows(block):
            columns = pl.ds(pl.multiple_of(block * 384, 128), 384)
            return inner_cols(perm24[...], hidden_s[:, columns])

        def put(unit, rows):
            xt24[pl.ds(pl.multiple_of(unit * 24, 16), 48), :] = rows.astype(jnp.bfloat16)

        def unit_rows(rows, y, x_hi):
            at = (y * 2 + x_hi) * 24
            return rows[at : at + 24]

        @pl.loop(0, 2)
        def _(x_lo):
            blocks = [block_rows(x_lo * 4 + z) for z in range(4)]
            for z in range(4):
                for y in range(4):
                    for x_hi in range(2):
                        upper = unit_rows(blocks[z], y, x_hi)
                        if part == 0 and y % 2 == 0:
                            unit = (x_hi * 2 + x_lo) * 16 + z * 4 + y
                            put(unit, jnp.concatenate([upper, unit_rows(blocks[z], y + 1, x_hi)]))
                        elif part == 1 and z % 2 == 0:
                            unit = y * 16 + (x_lo * 2 + x_hi) * 4 + z
                            put(unit, jnp.concatenate([upper, unit_rows(blocks[z + 1], y, x_hi)]))
                        elif part == 2 and x_hi == 0:
                            unit = z * 16 + y * 4 + x_lo * 2
                            put(unit, jnp.concatenate([upper, unit_rows(blocks[z], y, 1)]))

    def multiply(job, part, left, right):
        width = JOBS[job][2]
        own_view(job, part)[...] = jnp.dot(
            left[...], right[:, part * width : (part + 1) * width], preferred_element_type=jnp.float32
        ).astype(jnp.bfloat16)

    copies = {}
    drained = set()

    def begin(job, part, slot, src, dst, target):
        index = PARTNER_COPIES + (job * 3 + part) * COPIES + slot
        copy = remote(src, dst, index, target)
        copy.start()
        copies[job, part, slot] = copy

    def arrive(job, part, *slots):
        for slot in slots:
            copies[job, part, slot].wait_recv()

    def ring(part, phase):
        axis = AXES[part][phase]
        here, right, left, opposite = near[axis]
        return (
            here,
            right,
            left,
            opposite,
            device_at(moved(place, axis, right), core),
            device_at(moved(place, axis, left), core),
            device_at(moved(place, axis, opposite), core),
        )

    def sent_out(job, part, *slots):
        for slot in slots:
            if (job, part, slot) not in drained:
                drained.add((job, part, slot))
                copies[job, part, slot].wait_send()

    def own_view(job, part):
        base, width = bufs[job][0], JOBS[job][2]
        if JOBS[job][0] == "down":
            return base.at[:, pl.ds(part * width, width)]
        return base.at[pl.ds(part * 576, 576), pl.ds(0, width)]

    def first_send(job, part):
        half, whole = bufs[job][1:3]
        own = own_view(job, part)
        big = 16 * JOBS[job][1]
        cut = sixteen(big // 2) if job % 2 == 0 else big // 32 * 16
        here, right, left, opposite, to_right, to_left, _ = ring(part, 0)

        full = pl.ds(0, JOBS[job][2])

        def rows(chunk, start, count):
            return own.at[pl.ds(pl.multiple_of(chunk * big + start, 16), count)]

        begin(job, part, 0, rows(opposite, 0, cut), half.at[part, pl.ds(0, cut), full], to_right)
        begin(job, part, 1, rows(opposite, cut, big - cut), half.at[part, pl.ds(cut, big - cut), full], to_left)
        begin(job, part, 2, rows(right, cut, big - cut), whole.at[part, 0, pl.ds(cut, big - cut), full], to_right)
        begin(job, part, 3, rows(left, 0, cut), whole.at[part, 1, pl.ds(0, cut), full], to_left)

    def first_add(job, part):
        half, whole = bufs[job][1:3]
        own = own_view(job, part)
        _, each, width, lanes, _ = JOBS[job]
        big = 16 * each
        cut = sixteen(big // 2) if job % 2 == 0 else big // 32 * 16
        here, right, left, opposite, to_right, to_left, _ = ring(part, 0)
        for slot, chunk, start, count, target, side in (
            (0, right, 0, cut, to_right, 0),
            (1, left, cut, big - cut, to_left, 1),
        ):
            arrive(job, part, slot)
            rows = pl.ds(pl.multiple_of(chunk * big + start, 16), count)

            @pl.loop(0, width // 128)
            def _(step):
                columns = pl.ds(pl.multiple_of(step * 128, 128), 128)
                total = own[rows, columns].astype(jnp.float32) + half[
                    part, pl.ds(start, count), columns
                ].astype(jnp.float32)
                own[rows, columns] = total.astype(jnp.bfloat16)

            begin(
                job,
                part,
                4 + side,
                own.at[rows],
                whole.at[part, side, pl.ds(start, count), pl.ds(0, width)],
                target,
            )

    def second_send(job, part):
        _, _, whole, mid, mid_half, mid_whole, _ = bufs[job]
        own = own_view(job, part)
        _, each, width, lanes, cut = JOBS[job]
        big, small = 16 * each, 4 * each
        padded = sixteen(small)
        here, right, left, opposite, to_right, to_left, _ = ring(part, 0)
        arrive(job, part, 2, 3, 4, 5)
        if JOBS[job][0] == "qkv":
            sent_out(0, part, 6, 7, 8, 9, 10, 11)
        rows = pl.ds(pl.multiple_of(here * big, 16), big)

        @pl.loop(0, width // 128)
        def _(step):
            columns = pl.ds(pl.multiple_of(step * 128, 128), 128)
            total = (
                own[rows, columns].astype(jnp.float32)
                + whole[part, 0, :, columns].astype(jnp.float32)
                + whole[part, 1, :, columns].astype(jnp.float32)
            )
            if part == 2 and each == 9:
                for x_lo in range(2):
                    for y in range(4):
                        piece_at = x_lo * 72 + y * 18
                        acc[y * 36 + x_lo * 18 : y * 36 + x_lo * 18 + 18, :] = total[piece_at : piece_at + 18]
            else:
                acc[pl.ds(0, big), :] = total
            for chunk in range(4):
                line = line_of(AXES[part][1], chunk)
                mid[part, chunk, :, columns] = acc[pl.ds(line * small, padded), :].astype(jnp.bfloat16)

        here, right, left, opposite, to_right, to_left, _ = ring(part, 1)
        low, high = pl.ds(0, cut), pl.ds(cut, width - cut)
        begin(job, part, 6, mid.at[part, opposite, :, low], mid_half.at[part, :, low], to_right)
        begin(job, part, 7, mid.at[part, opposite, :, high], mid_half.at[part, :, high], to_left)
        begin(job, part, 8, mid.at[part, right, :, high], mid_whole.at[part, 0, :, high], to_right)
        begin(job, part, 9, mid.at[part, left, :, low], mid_whole.at[part, 1, :, low], to_left)

    def second_add(job, part):
        _, _, _, mid, mid_half, mid_whole, _ = bufs[job]
        _, each, width, lanes, cut = JOBS[job]
        here, right, left, opposite, to_right, to_left, _ = ring(part, 1)
        for slot, chunk, start, count, target, side in (
            (6, right, 0, cut, to_right, 0),
            (7, left, cut, width - cut, to_left, 1),
        ):
            arrive(job, part, slot)

            @pl.loop(0, count // 128)
            def _(step):
                columns = pl.ds(pl.multiple_of(start + step * 128, 128), 128)
                total = mid[part, chunk, :, columns].astype(jnp.float32) + mid_half[
                    part, :, columns
                ].astype(jnp.float32)
                mid[part, chunk, :, columns] = total.astype(jnp.bfloat16)

            columns = pl.ds(start, count)
            begin(
                job,
                part,
                10 + side,
                mid.at[part, chunk, :, columns],
                mid_whole.at[part, side, :, columns],
                target,
            )

    def third_send(job, part):
        _, _, _, mid, _, mid_whole, last = bufs[job]
        _, each, width, lanes, cut = JOBS[job]
        small = sixteen(4 * each)
        padded = sixteen(each)
        here = ring(part, 1)[0]
        arrive(job, part, 8, 9, 10, 11)

        @pl.loop(0, width // 128)
        def _(step):
            columns = pl.ds(pl.multiple_of(step * 128, 128), 128)
            acc[pl.ds(0, small), :] = (
                mid[part, here, :, columns].astype(jnp.float32)
                + mid_whole[part, 0, :, columns].astype(jnp.float32)
                + mid_whole[part, 1, :, columns].astype(jnp.float32)
            )
            for chunk in range(4):
                line = line_of(AXES[part][2], chunk)
                last[part, chunk, :, columns] = acc[pl.ds(line * each, padded), :].astype(jnp.bfloat16)

        here, right, left, opposite, to_right, to_left, to_opposite = ring(part, 2)
        for slot, chunk, target in ((0, right, to_right), (1, left, to_left), (2, opposite, to_opposite)):
            begin(job, part, 12 + slot, last.at[part, chunk], last.at[part, 4 + slot], target)

    mod_base = PARTNER_COPIES + 3 * COPIES * len(JOBS)
    mod_copies = {}

    def mod_send(slot, src, dst, target):
        copy = remote(src, dst, mod_base + slot, target)
        copy.start()
        sent.append(copy)
        mod_copies[slot] = copy

    def mod_arrive(*slots):
        for slot in slots:
            mod_copies[slot].wait_recv()

    def mod_pair():
        for quarter in range(4):
            fold32[4 * quarter : 4 * quarter + 4, :] = gmod[
                1 - mod, 0:4, quarter * 896 : (quarter + 1) * 896
            ]
        start = (1 - core) * 1792
        for half in range(2):
            columns = pl.ds(pl.multiple_of(start + half * 896, 128), 896)
            side_own[4 * half : 4 * half + 4, :] = gmod[mod, 0:4, columns]
        fold_own[...] = fold32[...].astype(jnp.bfloat16)
        there = pl.ds(pl.multiple_of((1 - core) * 8, 8), 8)
        mod_send(19, fold32.at[there], cross_other, device_at(twin, 1 - core))
        mod_send(0, fold_own, fold_other, device_at(twin, core))
        mod_send(1, side_own, side_other, partner)

    def condition_part():
        for quarter in range(4):
            other32[0:4, quarter * 896 : (quarter + 1) * 896] = turned32[4 * quarter : 4 * quarter + 4, :]
        own, other = gmod[mod, 0:4, :], other32[0:4, :]
        pair32[0:4, :] = jnp.where(mod == 0, own, other)
        pair32[4:8, :] = jnp.where(mod == 0, other, own)
        first = pair32[:, 0:WIDE].astype(jnp.bfloat16)
        wide_loads["mod", 0].wait()
        part_own[...] = inner_cols(first, out_w[...])
        wide_loads["mod", 1].wait()
        part_own[...] += inner_cols(pair32[:, WIDE : 2 * WIDE].astype(jnp.bfloat16), third_w[...])
        wide_loads["mod", 2].wait()
        wide_loads["mod", 3].wait()
        part_own[...] += inner_cols(pair32[:, 2 * WIDE : 3328].astype(jnp.bfloat16), fourth_w[...])
        part_own[...] += inner_cols(pair32[:, 3328:3456].astype(jnp.bfloat16), narrow_w[...])
        mod_send(2, part_own, part_other, device_at(twin, core))

    def mod_gather_first():
        mod_arrive(0, 1, 19)
        turned32[...] = fold_other[...].astype(jnp.float32)
        twin_rows = turned32[pl.ds(pl.multiple_of(core * 8, 8), 8), :]
        for half in range(2):
            columns = pl.ds(pl.multiple_of(core * 1792 + half * 896, 128), 896)
            at = slice(4 * half, 4 * half + 4)
            own, other = gmod[mod, 0:4, columns], twin_rows[at]
            beside, cross = side_other[at, :], cross_other[at, :]
            mine = (jnp.where(mod == 0, own, other), jnp.where(mod == 0, other, own))
            theirs = (jnp.where(mod == 0, beside, cross), jnp.where(mod == 0, cross, beside))
            to = slice(half * 896, (half + 1) * 896)
            for which in range(2):
                rows32[4 * which : 4 * which + 4, to] = jnp.where(core == 0, mine[which], theirs[which])
                rows32[8 + 4 * which : 12 + 4 * which, to] = jnp.where(core == 0, theirs[which], mine[which])
        _, y, z = place
        gathered_a[z, y] = rows32[:, 0:896].astype(jnp.bfloat16)
        gathered_b[z, y] = rows32[:, 896:1792].astype(jnp.bfloat16)
        for step in range(3):
            to_y = device_at(moved(place, 1, near[1][1 + step]), core)
            to_z = device_at(moved(place, 2, near[2][1 + step]), core)
            mod_send(3 + step, gathered_a.at[z, y], gathered_a.at[z, y], to_y)
            mod_send(6 + step, gathered_b.at[z, y], gathered_b.at[z, y], to_z)

    def mod_gather_second():
        _, y, z = place
        mod_arrive(3, 4, 5)
        for step in range(3):
            to_z = device_at(moved(place, 2, near[2][1 + step]), core)
            mod_send(9 + step, gathered_a.at[z], gathered_a.at[z], to_z)
        mod_arrive(6, 7, 8)
        for step in range(3):
            to_y = device_at(moved(place, 1, near[1][1 + step]), core)
            mod_send(12 + step, gathered_b.at[:, y], gathered_b.at[:, y], to_y)

    def mod_table():
        x, y, z = place
        row = lax.broadcasted_iota(jnp.int32, (48, WIDE), 0)
        lane = lax.broadcasted_iota(jnp.int32, (48, WIDE), 1)
        line = lax.broadcasted_iota(jnp.int32, (48, 256), 0)
        slot = lax.rem(lax.broadcasted_iota(jnp.int32, (48, 256), 1), 4)
        ones = (line == 40) | ((line == 41) & (slot == 0)) | ((line == 42) & (slot == 1))
        for index in range(2):
            half = lax.rem(lax.rem(x, 2) + index, 2)
            start = (half * 32 + z * 8 + y * 2) * 18
            pick = ((row < 36) & (lane == row + start)).astype(jnp.float32).astype(jnp.bfloat16)
            rows = inner_cols(pick, acts_s[...])
            act_rows[index] = (rows + ones.astype(jnp.float32)).astype(jnp.bfloat16)

    def mod_product():
        mod_arrive(9, 10, 11)
        mod_arrive(12, 13, 14)
        for side, gathered in ((0, gathered_a), (1, gathered_b)):
            columns = slice(side * 896, (side + 1) * 896)
            rows = gathered[...].reshape(256, 896)
            product_send[:, columns] = jnp.dot(
                act_rows[1], rows, preferred_element_type=jnp.float32
            ).astype(jnp.bfloat16)
            product_own[:, columns] = jnp.dot(act_rows[0], rows, preferred_element_type=jnp.float32)
        x = place[0]
        beside = moved(place, 0, x + 1 - 2 * lax.rem(x, 2))
        mod_send(15, product_send, product_other, device_at(beside, core))

    def mod_sum():
        mod_arrive(15)
        product_own[...] = product_own[...] + product_other[...].astype(jnp.float32)
        mod_send(16, product_own, final_other, partner)
        special = product_own.at[pl.ds(40, 8)]
        mod_send(17, special, special_other.at[core], device_at(twin, core))
        mod_send(18, special, special_other.at[core], device_at(twin, 1 - core))

    def mod_finish():
        here = pl.ds(pl.multiple_of(core * 1792, 128), 1792)
        there = pl.ds(pl.multiple_of((1 - core) * 1792, 128), 1792)
        mod_arrive(2)
        total = part_own[...] + part_other[...]
        raw = condition[...].astype(jnp.float32)
        condition_out[...] = jnp.where(mod == 0, total[0:4], total[4:8]) * silu_slope(raw)
        mod_arrive(16)
        for source, columns in ((product_own, here), (final_other, there)):
            mod_out[:, columns] = jnp.where(core == 0, source[0:18, :], source[18:36, :])
            special_out[mod, :, columns] = source[40:48, :]
        mod_arrive(17, 18)
        for side in range(2):
            special_out[1 - mod, :, side * 1792 : (side + 1) * 1792] = special_other[side]

    outs = {"gate": gate_out, "up": up_out, "down": down_out, "out": out_out, "qkv": qkv_out}

    def finish(job, part):
        last = bufs[job][6]
        _, each, width, lanes, cut = JOBS[job]
        here = ring(part, 2)[0]
        arrive(job, part, 12, 13, 14)

        @pl.loop(0, width // 128)
        def _(step):
            to = pl.multiple_of(step * 128, 128)
            columns = pl.ds(to, 128)
            total = last[part, here, :, columns].astype(jnp.float32)
            for slot in range(3):
                total = total + last[part, 4 + slot, :, columns].astype(jnp.float32)
            outs[JOBS[job][0]][:, pl.ds(pl.multiple_of(part * width + to, 128), 128)] = total[:each]

    gate_job, up_job, down_job, out_job, qkv_job = range(5)

    def slot_sum(block, source):
        for third in range(3):
            columns = slice(third * 384, (third + 1) * 384)
            high, low = split_two(source[:, columns])
            total = jnp.dot(onehot_t, high, preferred_element_type=jnp.float32) + jnp.dot(
                onehot_t, low, preferred_element_type=jnp.float32
            )
            base = block % 3 * WIDE + third * 384
            gmod[block // 3, :, base : base + 384] = (
                total[0:8].astype(jnp.bfloat16).astype(jnp.float32)
            )

    def stages(stage, job):
        for part in range(3):
            stage(job, part)

    def ff_products(part):
        pick9(part, second_s)
        arrived("ggate")
        multiply(gate_job, part, xt9, ggate_s)
        first_send(gate_job, part)
        arrived("gup")
        multiply(up_job, part, xt9, gup_s)
        first_send(up_job, part)

    loads["second"].wait()

    def feed_forward(index):
        slot = lax.rem(index, 2)
        for copy in ff_chunk(index, slot):
            copy.wait()
        gate_w, up_w, down_w = ff_slots(slot)
        columns = pl.ds(pl.multiple_of(index * CHUNK, CHUNK), CHUNK)
        gate_linear = jnp.dot(second_s[0:TOK, :], gate_w[...], preferred_element_type=jnp.float32)
        up_linear = jnp.dot(second_s[0:TOK, :], up_w[...], preferred_element_type=jnp.float32)
        ghidden = inner_cols(gbranch_s[0:TOK, :], down_w[...])
        logistic = jax.nn.sigmoid(gate_linear)
        gate_act = gate_linear * logistic
        hidden = (gate_act * up_linear).astype(jnp.bfloat16)
        slope = logistic * (1.0 + gate_linear * (1.0 - logistic))
        ggate = (ghidden * up_linear * slope).astype(jnp.bfloat16)
        gup = (ghidden * gate_act).astype(jnp.bfloat16)
        hidden_s[0:TOK, columns] = hidden
        ggate_s[0:TOK, columns] = ggate
        gup_s[0:TOK, columns] = gup
        branch[...] += jnp.dot(hidden, down_w[...], preferred_element_type=jnp.float32)
        gsecond[...] += inner_cols(ggate, gate_w[...])
        gsecond[...] += inner_cols(gup, up_w[...])

        @pl.when(index + 2 < 6)
        def _():
            for copy in ff_chunk(index + 2, slot):
                copy.start()

    pl.loop(0, 2)(feed_forward)
    pl.semaphore_wait(barrier, 11)
    exchange("second", second_in, second_s.at[other_rows])
    exchange("gbranch", gbranch_s.at[own_rows], gbranch_s.at[other_rows])
    pl.loop(2, 6)(feed_forward)
    exchange("ggate", ggate_s.at[own_rows, pl.ds(0, HID)], ggate_s.at[other_rows, pl.ds(0, HID)])
    exchange("gup", gup_s.at[own_rows], gup_s.at[other_rows])
    exchange("hidden", hidden_s.at[own_rows], hidden_s.at[other_rows])
    arrived("second")
    for part in range(3):
        ff_products(part)
    loads["middle"].wait()
    loads["attended"].wait()

    def second_rows(rows):
        upstream = cotangent[rows, :].astype(jnp.float32)
        kept = middle[rows, :]
        result = branch[rows, :]
        layer_out[rows, :] = (kept + piece(rows, 5) * result).astype(jnp.bfloat16)
        branch[rows, :] = upstream * result
        normed, inverse = rms_norm(kept)
        grad = gsecond[rows, :]
        gquery[rows, :] = grad * normed
        total = upstream + norm_back(grad * (1.0 + piece(rows, 4)), normed, inverse)
        middle[rows, :] = total
        attended_row = attended[rows, :]
        attended[rows, :] = total * attended_row
        gatt_s[rows, :] = (total * piece(rows, 2)).astype(jnp.bfloat16)

    row_blocks(second_rows, 48)
    exchange("gatt", gatt_s.at[own_rows], gatt_s.at[other_rows])
    context_s = second_s
    load("context", context_in, context_s.at[own_rows])
    stages(first_add, gate_job)

    arrived("gbranch", "hidden")
    for part in range(3):
        pick24(part)
        multiply(down_job, part, xt24, gbranch_s)
        first_send(down_job, part)
    stages(first_add, up_job)
    arrived("gatt")
    exchange("context", context_in, context_s.at[other_rows])

    wide_loads["out", 0].wait()
    gcontext[...] = inner_cols(gatt_s[0:TOK, :], out_w[...]).astype(jnp.bfloat16)
    wide_parts("qkv", qkv_weight, 0)
    stages(second_send, gate_job)
    loads["context"].wait()
    arrived("context")
    for part in range(3):
        pick9(part, context_s)
        multiply(out_job, part, xt9, gatt_s)
        first_send(out_job, part)
    slot_sum(5, branch)
    slot_sum(4, gquery)
    slot_sum(3, gsecond)
    slot_sum(2, attended)
    load("query_hat", query_hat_in, branch)
    load("key_hat", key_hat_in, attended)
    load("cos", cos_in, cosine)
    load("sin", sin_in, gsecond)
    query_hat, key_hat, sine = branch, attended, gsecond
    stages(second_send, up_job)

    gquery[...] = jnp.zeros_like(gquery)
    gkey[...] = jnp.zeros_like(gkey)
    gvalue[...] = jnp.zeros_like(gvalue)
    for name in ("query", "key", "value"):
        loads[name].wait()

    def attention_group(group):
        @pl.loop(0, 1)
        def _(pair):
            left = lax.broadcasted_iota(jnp.int32, (TOK, TOK), 0) // 36
            right = lax.broadcasted_iota(jnp.int32, (TOK, TOK), 1) // 36
            shut = jnp.where(kind | (left == right), 0.0, -1e30)
            for member in range(4):
                window, mask = head_window(group * 4 + pair + member)
                query_w, key_w = query[:, window] * mask, key[:, window] * mask
                value_w, grad_w = value[:, window], gcontext[:, window] * mask
                scores = inner_cols(query_w, key_w) * (72**-0.5) + shut
                weight = jnp.exp(scores - jnp.max(scores, axis=-1, keepdims=True))
                weight = weight * (1.0 / jnp.sum(weight, axis=-1, keepdims=True))
                gattention = inner_cols(grad_w, value_w)
                gvalue[:, window] += inner_rows(weight.astype(jnp.bfloat16), grad_w)
                dots = jnp.sum(weight * gattention, axis=-1, keepdims=True)
                gscores = (weight * (gattention - dots)).astype(jnp.bfloat16)
                gquery[:, window] += jnp.dot(gscores, key_w, preferred_element_type=jnp.float32)
                gkey[:, window] += inner_rows(gscores, query_w)

    attention_group(0)
    stages(first_add, down_job)
    attention_group(1)
    stages(second_add, gate_job)
    attention_group(2)
    stages(first_add, out_job)
    attention_group(3)
    stages(second_add, up_job)
    pairs["ggate"].wait_send()

    def project_back(which, grads, hat, rows):
        base = which * WIDE
        grad = grads[rows, :] * (72**-0.5)
        normed = hat[rows, :]
        turned = grad * cosine[rows, :] - swap_halves(grad) * sine[rows, :]
        gain_sum[which] += jnp.sum((turned * normed).reshape(6, 8, WIDE), axis=0)
        scaled = turned * gains[which : which + 1, :]
        inverse = inverses[which, rows, :]
        mean = head_sum(scaled * normed, heads[...]) * (1.0 / 72.0)
        raw = scaled * head_spread(inverse, heads[...]) - normed * head_spread(
            inverse * mean, heads[...]
        )
        gproj_s[rows, base : base + WIDE] = raw.astype(jnp.bfloat16)

    def project_rows(rows):
        project_back(0, gquery, query_hat, rows)
        project_back(1, gkey, key_hat, rows)

    def exchange_projected(part):
        columns = pl.ds(part * WIDE, WIDE)
        exchange("gproj%d" % part, gproj_s.at[own_rows, columns], gproj_s.at[other_rows, columns])

    def value_rows(rows):
        gproj_s[rows, 2 * WIDE : 3 * WIDE] = gvalue[rows, :].astype(jnp.bfloat16)

    row_blocks(value_rows)
    exchange_projected(2)
    for name in ("query_hat", "key_hat", "cos", "sin"):
        loads[name].wait()
    arrived("gproj2")
    first_s = second_s
    load("first", first_in, first_s.at[own_rows])
    exchange("first", first_in, first_s.at[other_rows])
    row_blocks(project_rows, 48)
    exchange_projected(0)
    exchange_projected(1)
    loads["first"].wait()
    arrived("first")
    for part in (2, 0, 1):
        pick9(part, first_s)
        if part != 2:
            arrived("gproj%d" % part)
        sent_out(gate_job, part, 0, 1, 2, 3, 4, 5)
        multiply(qkv_job, part, xt9, gproj_s)
        first_send(qkv_job, part)
    for part in range(3):
        sent_out(up_job, part, 0, 1, 2, 3, 4, 5)
    wide_parts("qkv", qkv_weight, 2)
    stages(second_send, down_job)
    for part in range(3):
        sent_out(down_job, part, 0, 1, 2, 3, 4, 5)
    wide_parts("qkv", qkv_weight, 1)
    stages(third_send, gate_job)
    stages(second_send, out_job)
    stages(third_send, up_job)

    gfirst, scaled_first = gquery, gkey
    wide_loads["qkv", 0].wait()
    gfirst[...] = inner_cols(gproj_s[0:TOK, 0:WIDE], out_w[...])
    wide_parts("mod", mod_weight, 0)
    wide_loads["qkv", 1].wait()
    gfirst[...] += inner_cols(gproj_s[0:TOK, WIDE : 2 * WIDE], third_w[...])
    wide_parts("mod", mod_weight, 1)
    wide_loads["qkv", 2].wait()
    wide_loads["qkv", 3].wait()
    gfirst[...] += inner_cols(gproj_s[0:TOK, 2 * WIDE : 3328], fourth_w[...])
    gfirst[...] += inner_cols(gproj_s[0:TOK, 3328:3456], narrow_w[...])
    wide_parts("mod", mod_weight, 2)

    def last_rows(rows):
        normed, inverse = rms_norm(tokens[rows, :].astype(jnp.float32))
        grad = gfirst[rows, :]
        scaled_first[rows, :] = grad * normed
        tokens_out[rows, :] = middle[rows, :] + norm_back(
            grad * (1.0 + piece(rows, 1)), normed, inverse
        )

    row_blocks(last_rows, 48)
    slot_sum(0, gfirst)
    slot_sum(1, scaled_first)
    for which in range(2):
        high, low = split_two(gain_sum[which])
        total = jnp.sum(inner_cols(high, folds[...]) + inner_cols(low, folds[...]), axis=0, keepdims=True)
        gmod[0, which : which + 1, 3456:3584] = total
    mod_pair()
    stages(first_add, qkv_job)
    mod_gather_first()
    stages(second_add, down_job)
    stages(second_add, out_job)
    mod_gather_second()
    condition_part()
    loads["acts"].wait()
    mod_table()
    stages(finish, gate_job)
    stages(second_send, qkv_job)
    mod_product()
    stages(third_send, down_job)
    stages(third_send, out_job)
    stages(second_add, qkv_job)
    mod_sum()
    stages(third_send, qkv_job)
    stages(finish, up_job)
    stages(finish, down_job)
    stages(finish, out_job)
    mod_finish()
    stages(finish, qkv_job)
    for name, copy in pairs.items():
        if name != "ggate":
            copy.wait_send()
    for (job, part, slot) in list(copies):
        sent_out(job, part, slot)
    for copy in sent:
        copy.wait_send()


def write_kernel(*refs):
    count = len(refs) // 2 - 1
    for source, target in zip(refs[:count], refs[count:-2]):
        if len(source.shape) == 3:
            for half in range(2):
                target[pl.ds(half * 3456, 3456)] = source[half, 0, 0:3456]
            for which in range(2):
                total = source[0, 1 + which, 3456:3584] + source[1, 1 + which, 3456:3584]
                refs[count * 2 + which][...] = total[0:72]
        else:
            target[...] = source[:, 0 : target.shape[1]]


def backward(
    cotangent, tokens, condition, segments, saved, gate_weight, up_weight, down_weight, out_weight, qkv_weight, mod_weight
):
    (query, key, value, query_hat, key_hat, context, attended, middle, first, second, cosine, sine, acts, inverses, modulation, gains) = saved
    vmem = pl.BlockSpec(memory_space=pltpu.VMEM)
    anywhere = pl.BlockSpec(memory_space=pl.ANY)
    low, full = jnp.bfloat16, jnp.float32
    wide_low, wide_full = ((TOK, WIDE), low), ((TOK, WIDE), full)
    outs = (
        [wide_low, wide_full]
        + [((each, 3 * width), full) for _, each, width, _, _ in JOBS]
        + [((18, 3584), full), ((2, 8, 3584), full), ((4, WIDE), full)]
    )
    scratch = [
        ((PAIR, HID), low),
        ((PAIR, WIDE), low),
        ((PAIR, WIDE), low),
        ((PAIR, 3456), low),
        ((PAIR, HID), low),
        ((PAIR, WIDE), low),
        ((2, 288, 640), low),
        ((2, 288, 640), low),
        ((8, 80, 256), low),
        ((256, WIDE), low),
        ((192, 384), low),
        ((1536, PAIR), low),
        ((400, 128), full),
        ((128, WIDE), low),
        ((128, WIDE), low),
        ((TOK, 4 * WIDE), low),
        wide_full,
        wide_full,
        wide_full,
        wide_low,
        wide_low,
        wide_low,
        wide_low,
        wide_full,
        wide_full,
        wide_full,
        wide_full,
        ((2, 8, WIDE), full),
        ((WIDE, WIDE), low),
        ((WIDE, 128), low),
        ((2, 8, 3584), full),
        ((2, 48, 256), low),
        ((16, 896), full),
        ((16, 896), low),
        ((16, 896), low),
        ((8, 3584), full),
        ((8, 3584), full),
        ((16, 896), full),
        ((8, 896), full),
        ((8, 896), full),
        ((8, 896), full),
        ((16, 1792), full),
        ((4, 4, 16, 896), low),
        ((4, 4, 16, 896), low),
        ((48, 1792), full),
        ((48, 1792), low),
        ((48, 1792), low),
        ((48, 1792), full),
        ((2, 8, 1792), full),
        ((8, WIDE), full),
        ((8, WIDE), full),
    ]
    sums = {
        "gate": (16, 128),
        "up": (1728, 1024),
        "down": (1536, WIDE),
        "out": (1728, 384),
        "qkv": (1728, WIDE),
    }
    for name, each, width, _, _ in JOBS:
        big, small, tiny = 16 * each, sixteen(4 * each), sixteen(each)
        unused = name == "gate"
        scratch += [
            (sums[name], low),
            ((1, 16, 128) if unused else (3, big, width), low),
            ((1, 1, 16, 128) if unused else (3, 2, big, width), low),
            ((1, 1, 16, 128) if unused else (3, 4, small, width), low),
            ((3, small, width), low),
            ((3, 2, small, width), low),
            ((3, 7, tiny, width), low),
        ]
    count = PARTNER_COPIES + 3 * COPIES * len(JOBS) + MOD_COPIES
    results = pl.pallas_call(
        backward_kernel,
        out_shape=[jax.ShapeDtypeStruct(*out) for out in outs],
        in_specs=[pl.BlockSpec(memory_space=pltpu.SMEM)] + [vmem] * 6 + [anywhere] * 19,
        out_specs=[vmem] * 10,
        scratch_shapes=[pltpu.VMEM(*item) for item in scratch]
        + [
            pltpu.SemaphoreType.DMA((count,)),
            pltpu.SemaphoreType.DMA((count,)),
            pltpu.SemaphoreType.DMA((13,)),
            pltpu.SemaphoreType.DMA((4, 4)),
        ],
        compiler_params=pltpu.CompilerParams(
            collective_id=1, has_side_effects=True, vmem_limit_bytes=64 * 1024 * 1024 - 65536
        ),
        cost_estimate=pl.CostEstimate(
            flops=12_000_000_000, bytes_accessed=50_000_000, transcendentals=0
        ),
    )(
        segments,
        cotangent,
        tokens,
        modulation,
        condition,
        gains,
        inverses,
        acts.reshape(256, WIDE),
        second,
        first,
        context,
        middle,
        attended,
        query,
        key,
        value,
        query_hat,
        key_hat,
        cosine,
        sine,
        gate_weight,
        up_weight,
        down_weight,
        out_weight,
        qkv_weight,
        mod_weight,
    )
    special = results[8]
    kept = list(results[:8]) + [results[9]]
    shapes = [
        jax.ShapeDtypeStruct((item.shape[0], min(item.shape[1], 3456)), item.dtype) for item in kept
    ]
    written = pl.pallas_call(
        write_kernel,
        out_shape=shapes + [jax.ShapeDtypeStruct((size,), full) for size in (6912, 72, 72)],
        in_specs=[vmem] * 10,
        out_specs=[vmem] * 12,
    )(*kept, special)
    return written


def body(
    tokens,
    condition,
    segments,
    mod_weight,
    mod_bias,
    qkv_weight,
    query_gain,
    key_gain,
    out_weight,
    gate_weight,
    up_weight,
    down_weight,
    cotangent,
):
    saved = forward(tokens, condition, segments, mod_weight, mod_bias, qkv_weight, query_gain, key_gain, out_weight)
    written = backward(
        cotangent,
        tokens,
        condition,
        segments,
        saved,
        gate_weight,
        up_weight,
        down_weight,
        out_weight,
        qkv_weight,
        mod_weight,
    )
    layer_out, grad_tokens, gate, up, down, out, qkv, mod_rows, grad_condition, bias, query_grad, key_grad = written
    return (
        layer_out,
        grad_tokens,
        grad_condition,
        mod_rows,
        bias,
        qkv,
        query_grad,
        key_grad,
        out,
        gate,
        up,
        down,
    )


def solution(mesh):
    placed = (
        P(("dp", "mod"), None),
        P(("dp", "mod"), None),
        P(("dp", "mod")),
        P(None, "mod"),
        P("mod"),
        P(),
        P(),
        P(),
        P(),
        P(),
        P(),
        P(),
        P(("dp", "mod"), None),
    )
    return jax.shard_map(
        body,
        mesh=mesh,
        in_specs=placed,
        out_specs=(
            P(("dp", "mod"), None),
            P(("dp", "mod"), None),
            P(("dp", "mod"), None),
            P("dp", "mod"),
            P(),
            P(("dp", "mod"), None),
            P(),
            P(),
            P(("dp", "mod"), None),
            P(("dp", "mod"), None),
            P(("dp", "mod"), None),
            P(("dp", "mod"), None),
        ),
        check_vma=False,
    )
```
